32 devices in a mesh: tile: 8 (over z, y), chan: 4 (over x, core).
Axes of the slice: x: 2, y: 2, z: 4, core: 2. Of those that a mesh axis runs over, the one named last changes fastest.
Arguments:
- features: bfloat16 [8, 192, 2304], P('tile', 'chan'), may hold values from -6 to 6
- land_mask: int32 [8, 2304], P('tile'), may hold values 0 or 1
- wet_slots: int32 [8], replicated, may hold values from 0 to 15, as said below
- device_of: int32 [8], replicated, may hold values from 0 to 7, as said below
- depth_weight: float32 [2, 192, 49], P(None, 'chan'), may hold values from -0.875 to 0.875
- depth_bias: float32 [2, 192], P(None, 'chan'), may hold values from -1.5 to 1.5
- norm_gain: float32 [2, 192], replicated, may hold values from 0.5 to 1.5
- norm_bias: float32 [2, 192], replicated, may hold values from -1.5 to 1.5
- up_weight: bfloat16 [2, 768, 192], replicated, may hold values from -0.4375 to 0.4375
- up_bias: float32 [2, 768], replicated, may hold values from -2.5 to 2.5
- down_weight: bfloat16 [2, 192, 768], replicated, may hold values from -0.21875 to 0.21875
- down_bias: float32 [2, 192], replicated, may hold values from -1.5 to 1.5
- layer_scale: float32 [2, 192], P(None, 'chan'), may hold values from 0.5 to 1.5
- pool_weight: float32 [192, 4], P('chan'), may hold values from -2.5 to 2.5
- spread_weight: float32 [192, 4], P('chan'), may hold values from -2.5 to 2.5
Outputs:
- merged: bfloat16 [8, 192, 2304], P('tile', 'chan')
The draws below stay inside these ranges and needn't reach their ends.
Inputs may be any that keep to these rules, and one draw needn't show every extreme that they name: `wet_slots`: 8 distinct grid slots in increasing order, among them slots 0, 1 and the last slot. `device_of`: each device along tile holds exactly one wet tile; the tiles in slots 0 and 1 lie 8 / 2 devices apart, counted round. `land_mask`: 1 marks an ocean cell, 0 a land cell.
All inputs are finite; a program needn't handle non-finite values. No bound on the sum of `land_mask` on one device may be relied on, other than what follows from the above.
Results may differ from the reference program's by a relative error of at most 0.011.
Values may be sent and summed in bfloat16 or wider, within the bound.
No kernel may reach another device: no remote copies, remote signals or barrier semaphores. Data moves between devices by JAX's collectives and lax.ppermute only.
A program may use at most 64 MiB of HBM per device.

```python
import jax
import jax.numpy as jnp
from jax import lax

CHANNELS = 192
HIDDEN_SIZE = 768
TILE = 48
GRID_Y = 4
LEVELS = 2
GRID_X = 4
WET = 8


def draw_wet_slots(key, part):
    slot_count = GRID_X * GRID_Y
    scores = jax.random.permutation(key, slot_count).astype(jnp.int32)
    slot_ids = jnp.arange(slot_count, dtype=jnp.int32)
    scores = jnp.where(slot_ids == 0, slot_count, scores)
    scores = jnp.where(slot_ids == 1, slot_count + 2, scores)
    scores = jnp.where(slot_ids == slot_count - 1, slot_count + 1, scores)
    best_scores, chosen = lax.top_k(scores, WET)
    return jnp.sort(chosen).astype(jnp.int32)


def draw_device_of(key, part):
    order = jax.random.permutation(key, WET).astype(jnp.int32)
    positions = jnp.arange(WET, dtype=jnp.int32)
    target = (order[0] + WET // 2) % WET
    where_target = jnp.sum(jnp.where(order == target, positions, 0)).astype(jnp.int32)
    second = order[1]
    swapped = jnp.where(positions == 1, target, order)
    swapped = jnp.where(positions == where_target, second, swapped)
    swapped = jnp.where(positions == 1, target, swapped)
    return swapped.astype(jnp.int32)


def plant(values, key, least, top_value):
    longest = values.shape.index(max(values.shape))
    spots = []
    for shift in (0, 1):
        where = [jax.random.randint(jax.random.fold_in(key, axis), (), 0, length) for axis, length in enumerate(values.shape)]
        where[longest] = (where[longest] + shift) % values.shape[longest]
        spots.append(tuple(where))
    return values.at[spots[0]].set(least).at[spots[1]].set(top_value)


def levels(stream_key, extent, split, least, high):
    def one(dim, parts):
        steps = jax.random.uniform(jax.random.fold_in(jax.random.fold_in(stream_key, 6), dim), (parts,), jnp.float32, least / len(split), high / len(split))
        return jnp.repeat(jnp.exp(steps), extent[dim] // parts).reshape((-1,) + (1,) * (len(extent) - dim - 1))

    factor_of = one(*split[0])
    for cut in split[1:]:
        factor_of = factor_of * one(*cut)
    return factor_of


def noise(stream_key, shape, scale, bound, shards=(), kind=jnp.bfloat16):
    gain = levels(stream_key, shape, shards, -0.22, 0.18) if shards else 1.0
    values = jax.random.normal(stream_key, shape, jnp.float32) * scale * gain
    return jnp.minimum(jnp.maximum(values, -bound), bound).astype(kind)


def setup_inputs(seed: int = 0) -> dict:
    key_list = jax.random.split(jax.random.key(seed), 16)
    return {
        "features": noise(key_list[0], (WET, CHANNELS, TILE * TILE), 1.0, 6.0, ((0, 8), (1, 4))),
        "land_mask": plant((jax.random.randint(key_list[1], (WET, TILE * TILE), 0, 8) < 7).astype(jnp.int32), jax.random.fold_in(key_list[1], 1), 0, 1),
        "wet_slots": draw_wet_slots(jax.random.fold_in(key_list[15], 71), 0),
        "device_of": draw_device_of(jax.random.fold_in(key_list[15], 71), 0),
        "depth_weight": noise(key_list[4], (LEVELS, CHANNELS, 49), 49 ** -0.5, 0.875, ((1, 4),), jnp.float32),
        "depth_bias": noise(key_list[5], (LEVELS, CHANNELS), 0.3, 1.5, ((1, 4),), jnp.float32),
        "norm_gain": jnp.clip(1.0 + 0.1 * jax.random.normal(key_list[6], (LEVELS, CHANNELS), jnp.float32), 0.5, 1.5),
        "norm_bias": noise(key_list[7], (LEVELS, CHANNELS), 0.3, 1.5, (), jnp.float32),
        "up_weight": noise(key_list[8], (LEVELS, HIDDEN_SIZE, CHANNELS), CHANNELS ** -0.5, 0.4375),
        "up_bias": noise(key_list[9], (LEVELS, HIDDEN_SIZE), 0.5, 2.5, (), jnp.float32),
        "down_weight": noise(key_list[10], (LEVELS, CHANNELS, HIDDEN_SIZE), HIDDEN_SIZE ** -0.5, 0.21875),
        "down_bias": noise(key_list[11], (LEVELS, CHANNELS), 0.3, 1.5, (), jnp.float32),
        "layer_scale": jnp.clip(1.0 + 0.1 * jax.random.normal(key_list[12], (LEVELS, CHANNELS), jnp.float32), 0.5, 1.5),
        "pool_weight": noise(key_list[13], (CHANNELS, 4), 0.5, 2.5, ((0, 4),), jnp.float32),
        "spread_weight": noise(key_list[14], (CHANNELS, 4), 0.5, 2.5, ((0, 4),), jnp.float32),
    }


BANDS = ((-1, -1), (-1, 0), (-1, 1), (0, -1), (0, 1), (1, -1), (1, 0), (1, 1))
norm_eps = 1e-06

def neighbour_tables(wet_slots, device_of, grid_x, grid_y):
    tile_count = wet_slots.shape[0]
    devices = jnp.arange(tile_count, dtype=jnp.int32)
    holder = device_of[:, None] == devices[None, :]
    device_slot = lax.optimization_barrier(jnp.sum(jnp.where(holder, wet_slots[:, None], 0), axis=0)).astype(jnp.int32)
    slot_ids = jnp.arange(grid_x * grid_y, dtype=jnp.int32)
    owned = device_slot[:, None] == slot_ids[None, :]
    slot_device = (lax.optimization_barrier(jnp.sum(jnp.where(owned, devices[:, None] + 1, 0), axis=0)) - 1).astype(jnp.int32)
    column = device_slot % grid_x
    tile_row = device_slot // grid_x
    sources = []
    strip_ids = []
    flips = []
    for up_by, right_by in BANDS:
        near_column = (column + right_by) % grid_x
        near_row = tile_row + up_by
        folded = near_row >= grid_y
        source_column = jnp.where(folded, grid_x - 1 - near_column, near_column)
        source_row = jnp.where(folded, grid_y - 1, near_row)
        source_slot = source_row * grid_x + source_column
        matched = source_slot[:, None] == slot_ids[None, :]
        source = (lax.optimization_barrier(jnp.sum(jnp.where(matched, slot_device[None, :] + 1, 0), axis=1)) - 1).astype(jnp.int32)
        source = jnp.where(near_row < 0, -1, source).astype(jnp.int32)
        if up_by == -1:
            strip_id = jnp.full_like(column, 1)
        elif up_by == 1:
            strip_id = jnp.where(folded, 1, 0).astype(jnp.int32)
        elif right_by == -1:
            strip_id = jnp.full_like(column, 3)
        else:
            strip_id = jnp.full_like(column, 2)
        sources.append(source)
        strip_ids.append(strip_id.astype(jnp.int32))
        flips.append(folded)
    return (jnp.stack(sources, axis=1), jnp.stack(strip_ids, axis=1), jnp.stack(flips, axis=1))

def edge_strips(tile_grid):
    tile_side = tile_grid.shape[-1]
    first_rows = tile_grid[..., :3, :]
    last_rows = tile_grid[..., tile_side - 3:, :]
    first_cols = jnp.swapaxes(tile_grid[..., :, :3], -1, -2)
    last_cols = jnp.swapaxes(tile_grid[..., :, tile_side - 3:], -1, -2)
    return jnp.stack([first_rows, last_rows, first_cols, last_cols], axis=-4)

def padded_tile(own_tile, raw_strips, flips):
    tile_side = own_tile.shape[-1]
    band_list = []
    for band_index, (up_by, right_by) in enumerate(BANDS):
        piece_in = raw_strips[band_index]
        if up_by != 0:
            if up_by == 1:
                piece_in = jnp.where(flips[band_index], piece_in[:, ::-1, ::-1], piece_in)
            if right_by == -1:
                piece_in = piece_in[:, :, tile_side - 3:]
            elif right_by == 1:
                piece_in = piece_in[:, :, :3]
        else:
            piece_in = jnp.swapaxes(piece_in, 1, 2)
        band_list.append(piece_in)
    lower_rows = jnp.concatenate([band_list[0], band_list[1], band_list[2]], axis=2)
    middle_rows = jnp.concatenate([band_list[3], own_tile, band_list[4]], axis=2)
    upper_rows = jnp.concatenate([band_list[5], band_list[6], band_list[7]], axis=2)
    return jnp.concatenate([lower_rows, middle_rows, upper_rows], axis=1)

def depthwise(padded, weights, bias_row):
    chan_rows = padded.shape[0]
    padded_side = padded.shape[1]
    tile_side = padded_side - 6
    flat_cells = padded.astype(jnp.float32).reshape(chan_rows, padded_side * padded_side)
    flat_cells = jnp.pad(flat_cells, ((0, 0), (0, 6)))
    span_cells = tile_side * padded_side
    running = jnp.zeros((chan_rows, span_cells), jnp.float32)
    for row_step in range(7):
        for col_step in range(7):
            offset = row_step * padded_side + col_step
            running = running + weights[:, row_step * 7 + col_step][:, None] * flat_cells[:, offset:offset + span_cells]
    conv_out = running.reshape(chan_rows, tile_side, padded_side)[:, :, :tile_side] + bias_row[:, None, None]
    return conv_out.astype(jnp.bfloat16)

def mixed_branch(block_in, params, row_start, row_count):
    values = block_in.astype(jnp.float32)
    cell_mean = lax.optimization_barrier(jnp.mean(values, axis=0, keepdims=True))
    centred = values - cell_mean
    spread = lax.optimization_barrier(jnp.mean(centred * centred, axis=0, keepdims=True))
    normed = (centred * lax.rsqrt(spread + norm_eps) * params[2][:, None] + params[3][:, None]).astype(jnp.bfloat16)
    hidden = jnp.dot(params[4], normed, preferred_element_type=jnp.float32) + params[5][:, None]
    hidden = jax.nn.gelu(hidden, approximate=False).astype(jnp.bfloat16)
    down_rows = lax.dynamic_slice_in_dim(params[6], row_start, row_count, 0)
    bias_rows = lax.dynamic_slice_in_dim(params[7], row_start, row_count, 0)
    return jnp.dot(down_rows, hidden, preferred_element_type=jnp.float32) + bias_rows[:, None]

def pool_cells(tile_grid, weights):
    values = tile_grid.astype(jnp.float32)
    running = weights[:, 0][:, None, None] * values[:, 0::2, 0::2]
    running = running + weights[:, 1][:, None, None] * values[:, 0::2, 1::2]
    running = running + weights[:, 2][:, None, None] * values[:, 1::2, 0::2]
    running = running + weights[:, 3][:, None, None] * values[:, 1::2, 1::2]
    return running.astype(jnp.bfloat16)

def coarse_mask(mask_grid):
    half_side = mask_grid.shape[0] // 2
    return lax.optimization_barrier(jnp.max(mask_grid.reshape(half_side, 2, half_side, 2), axis=(1, 3)))

def join_levels(fine_flat, coarse_flat, weights, cell_mask, tile_side):
    chan_rows = fine_flat.shape[0]
    half_side = tile_side // 2
    coarse_vals = coarse_flat.astype(jnp.float32).reshape(chan_rows, half_side, half_side)
    spread = weights.reshape(chan_rows, 2, 2)
    expanded = coarse_vals[:, :, None, :, None] * spread[:, None, :, None, :]
    expanded = expanded.reshape(chan_rows, tile_side * tile_side)
    return (cell_mask[None, :] * (fine_flat.astype(jnp.float32) + expanded)).astype(jnp.bfloat16)

def level_reference(tiles, tile_side, params, masks, tables):
    tile_count = tiles.shape[0]
    channels_all = tiles.shape[1]
    tile_grid = tiles.reshape(tile_count, channels_all, tile_side, tile_side)
    strip_table = edge_strips(tile_grid)
    sources, strip_ids, flips = tables

    def one_tile(device):
        my_sources = sources[device]
        my_strips = strip_ids[device]
        raw_strips = []
        for band_index in range(8):
            source = my_sources[band_index]
            picked = strip_table[jnp.maximum(source, 0), my_strips[band_index]]
            raw_strips.append(jnp.where(source >= 0, picked, jnp.zeros_like(picked)))
        padded = padded_tile(tile_grid[device], raw_strips, flips[device])
        conv_out = depthwise(padded, params[0], params[1]).reshape(channels_all, tile_side * tile_side)
        branch = mixed_branch(conv_out, params, 0, channels_all)
        return (masks[device][None, :] * (tiles[device].astype(jnp.float32) + params[8][:, None] * branch)).astype(jnp.bfloat16)
    return lax.map(one_tile, jnp.arange(tile_count, dtype=jnp.int32))

def reference(features, land_mask, wet_slots, device_of, depth_weight, depth_bias, norm_gain, norm_bias, up_weight, up_bias, down_weight, down_bias, layer_scale, pool_weight, spread_weight):
    tables = neighbour_tables(wet_slots, device_of, GRID_X, GRID_Y)
    stacks = (depth_weight, depth_bias, norm_gain, norm_bias, up_weight, up_bias, down_weight, down_bias, layer_scale)
    fine_params = tuple((array[0] for array in stacks))
    coarse_params = tuple((array[1] for array in stacks))
    channels_all = features.shape[1]
    half_side = TILE // 2
    fine_masks = land_mask.astype(jnp.float32)
    fine_out = level_reference(features, TILE, fine_params, fine_masks, tables)

    def pool_one(tile_flat):
        return pool_cells(tile_flat.reshape(channels_all, TILE, TILE), pool_weight).reshape(channels_all, half_side * half_side)

    def mask_one(mask_flat):
        return coarse_mask(mask_flat.reshape(TILE, TILE)).reshape(half_side * half_side)
    pooled = jax.vmap(pool_one)(fine_out)
    coarse_masks = jax.vmap(mask_one)(land_mask).astype(jnp.float32)
    coarse = level_reference(pooled, half_side, coarse_params, coarse_masks, tables)

    def join_one(fine_flat, coarse_flat, mask_flat):
        return join_levels(fine_flat, coarse_flat, spread_weight, mask_flat, TILE)
    return jax.vmap(join_one)(fine_out, coarse, fine_masks)
```

```python
import jax
import jax.numpy as jnp
import ml_dtypes
import numpy as np
from jax import lax
from jax.experimental import pallas as pl
from jax.experimental.pallas import tpu as pltpu
from jax.sharding import PartitionSpec as P

TILE = 48
HALF = TILE // 2
GRID_Y = 4
GROUPS = 6
ROWS = 48
FINE_IN = 8 * TILE
FINE_PAD = 8 * 64
BANDS = ((-1, -1), (-1, 0), (-1, 1), (0, -1), (0, 1), (1, -1), (1, 0), (1, 1))
norm_eps = 1e-06
BF = jnp.bfloat16
F32 = jnp.float32


def one_hot(shape, pairs):
    table = np.zeros(shape, np.float32)
    for source, target in pairs:
        table[source, target] = 1.0
    return table.astype(ml_dtypes.bfloat16)


def side_target(side, row, col, width, stride):
    if side == 0:
        return row * stride + 3 + col
    if side == -1:
        return row * stride + col - (width - 3) if col >= width - 3 else None
    return row * stride + 3 + width + col if col < 3 else None


def halo_pairs(cells, width, stride, first_row, flipped):
    block = max(lane for lane, _ in cells) // 128 * 128 + 128
    pairs = []
    for place, side in enumerate((-1, 0, 1)):
        for lane, index in cells:
            row, col = index // width, index % width
            if flipped:
                row, col = 2 - row, width - 1 - col
            target = side_target(side, row + first_row, col, width, stride)
            if target is not None:
                pairs.append((place * block + lane, target))
    return pairs


def fine_tables():
    first = [(t, t) for t in range(128)] + [(128 + t, 128 + t) for t in range(16)]
    last = [(t, 16 + t) for t in range(128)] + [(128 + t, t) for t in range(16)]
    halo = np.stack(
        [
            one_hot((768, 256), halo_pairs(last, TILE, 64, 1, False)),
            one_hot((768, 256), halo_pairs(first, TILE, 64, 0, False)),
            one_hot((768, 256), halo_pairs(last, TILE, 64, 0, True)),
        ]
    )
    pack, expand, compact, pool = [], [], [], []
    for row in range(8):
        for j in range(3):
            pack.append((row * 48 + j, row * 3 + j))
            pack.append((row * 48 + 45 + j, 128 + row * 3 + j))
            expand.append((384 + row * 3 + j, row * 64 + j))
            expand.append((384 + 24 + row * 3 + j, row * 64 + 51 + j))
        for col in range(48):
            expand.append((row * 48 + col, row * 64 + 3 + col))
            compact.append((row * 64 + 3 + col, row * 48 + col))
            pool.append((row * 48 + col, (row // 2) * 32 + 3 + col // 2))
    return {
        "halo": halo,
        "pack": one_hot((384, 256), pack),
        "expand": one_hot((512, 512), expand),
        "compact": one_hot((512, 384), compact),
        "pool": one_hot((384, 128), pool),
        "unpool": np.ascontiguousarray(one_hot((384, 128), pool).T),
    }


def coarse_tables():
    strip = [(t, t) for t in range(72)]
    halo = np.stack(
        [
            one_hot((384, 128), halo_pairs(strip, HALF, 32, 1, False)),
            one_hot((384, 128), halo_pairs(strip, HALF, 32, 0, False)),
            one_hot((384, 128), halo_pairs(strip, HALF, 32, 0, True)),
        ]
    )
    pack, sides = [], []
    for row in range(3):
        for col in range(HALF):
            pack.append((row * 32 + 3 + col, row * 24 + col))
            pack.append(((21 + row) * 32 + 3 + col, 128 + row * 24 + col))
    for row in range(HALF):
        for j in range(3):
            index = row * 3 + j
            lane = 72 + index if row < 16 else index - 48
            pack.append((row * 32 + 3 + j, lane if row < 16 else 256 + lane))
            pack.append((row * 32 + 24 + j, 128 + lane if row < 16 else 256 + 64 + lane))
            sides.append((lane, row * 32 + j))
            sides.append((128 + lane, row * 32 + 27 + j))
    return {
        "halo": halo,
        "pack": one_hot((768, 384), pack),
        "sides": one_hot((256, 768), sides),
    }


FINE = fine_tables()
COARSE = coarse_tables()


def dot(left, right):
    return jnp.dot(left, right, preferred_element_type=F32)


def stacked(value, width):
    return jnp.concatenate([value[:, i * width : (i + 1) * width] for i in range(GROUPS)], axis=0)


def lane_ids(shape):
    return lax.broadcasted_iota(jnp.int32, shape, 1)


def columns(row):
    high = row.astype(BF)
    rest = row - high.astype(F32)
    middle = rest.astype(BF)
    low = (rest - middle.astype(F32)).astype(BF)
    n = row.shape[1]
    terms = jnp.concatenate([high, middle, low, jnp.zeros((13, n), BF)], axis=0)
    return lax.dot_general(terms, jnp.ones((16, 128), BF), (((0,), (0,)), ((), ())), preferred_element_type=F32)


def wide(block, lanes):
    return jnp.concatenate([block] * (lanes // 128), axis=1)


def scan_tiles(count, step, carry):
    if count <= 16:
        for k in range(count):
            carry = step(k, carry)
        return carry
    return lax.fori_loop(0, count, step, carry)


def make_prep(grid_x):
    def prep(slots_ref, dev_ref, x_ref, pack_ref, msg_ref, tab_ref, rows_ref, cols_ref, row_rest_ref, col_rest_ref):
        count = slots_ref.shape[0]
        me = lax.axis_index("tile")
        my_slot = scan_tiles(count, lambda k, c: c + jnp.where(dev_ref[k] == me, slots_ref[k], 0), jnp.int32(0))
        my_x = lax.rem(my_slot, grid_x)
        my_y = lax.div(my_slot, grid_x)
        wanted = []
        for up_by, right_by in BANDS:
            near_x = lax.rem(my_x + (right_by + grid_x), grid_x)
            near_y = my_y + up_by
            folded = near_y >= GRID_Y
            from_x = jnp.where(folded, grid_x - 1 - near_x, near_x)
            from_y = jnp.where(folded, GRID_Y - 1, near_y)
            wanted.append(from_y * grid_x + from_x)

        def find(k, found):
            slot, dev = slots_ref[k], dev_ref[k]
            return tuple(jnp.where(slot == want, dev, old) for want, old in zip(wanted, found))

        found = scan_tiles(count, find, tuple(jnp.int32(-1) for _ in BANDS))
        for band in range(8):
            tab_ref[band] = found[band]
        tab_ref[8] = jnp.where(my_y == GRID_Y - 1, 2, 1)

        x = x_ref[0]
        cols = dot(stacked(x, FINE_IN), pack_ref[...])
        lane = lane_ids((ROWS, 128))
        for side in range(2):
            part = cols[:, side * 128 : side * 128 + 128]
            main = part[0:ROWS]
            for i in range(1, 5):
                main = main + pltpu.roll(part[i * ROWS : (i + 1) * ROWS], 24 * i, 1)
            cols_ref[side] = main.astype(BF)
            rest = pltpu.roll(part[5 * ROWS : 6 * ROWS], 16, 1)
            col_rest_ref[side] = rest[0:16] + pltpu.roll(rest[16:32], 40, 1) + pltpu.roll(rest[32:48], 80, 1)
        rows_ref[0] = x[:, 0:128]
        rows_ref[1] = x[:, 2176:2304]
        ends = (x[:, 128:256].astype(F32), pltpu.roll(x[:, 2048:2176].astype(F32), 16, 1))
        for side in range(2):
            rest = jnp.where(lane < 16, ends[side], 0.0)
            row_rest_ref[side] = rest[0:16] + pltpu.roll(rest[16:32], 40, 1) + pltpu.roll(rest[32:48], 80, 1)

        def fill(k, carry):
            slot, dev = slots_ref[k], dev_ref[k]
            row_pick = jnp.where(lax.div(slot, grid_x) + 1 == my_y, 0, 1)
            col_pick = jnp.where(lax.rem(slot, grid_x) == lax.rem(my_x + (grid_x - 1), grid_x), 0, 1)
            for g in range(3):
                msg_ref[dev, :, 256 * g : 256 * g + 128] = rows_ref[row_pick, 16 * g : 16 * g + 16, :]
                msg_ref[dev, :, 256 * g + 128 : 256 * g + 256] = cols_ref[col_pick, 16 * g : 16 * g + 16, :]
            msg_ref[dev, :, 768:896] = (row_rest_ref[row_pick] + col_rest_ref[col_pick]).astype(BF)
            return carry

        scan_tiles(count, fill, jnp.int32(0))

    return prep


def band_source(tab_ref, band):
    source = tab_ref[band]
    return jnp.maximum(source, 0), jnp.where(source >= 0, 1.0, 0.0).astype(F32)


def lane_shifted(value, lanes):
    return pltpu.roll(value, value.shape[1] - lanes, 1)


def conv_fine(tab_ref, x_ref, recv_ref, halo_ref, expand_ref, compact_ref, weight_ref, bias_ref, out_ref, pad_ref, odd_ref, wide_ref, sum_ref):
    for tap in range(49):
        wide_ref[tap] = jnp.broadcast_to(weight_ref[0][:, tap : tap + 1], (ROWS, 128))
    lane = lane_ids((ROWS, 128))

    def rest_of(source, scale):
        rest = recv_ref[source, :, 768:896].astype(F32) * scale
        return jnp.concatenate([rest, pltpu.roll(rest, 128 - 40, 1), pltpu.roll(rest, 128 - 80, 1)], axis=0)

    def main_of(source, scale, offset):
        parts = [recv_ref[source, :, 256 * g + offset : 256 * g + offset + 128] for g in range(3)]
        return jnp.concatenate(parts, axis=0).astype(F32) * scale

    def row_strips(bands):
        pieces = []
        for band in bands:
            source, scale = band_source(tab_ref, band)
            pieces += [main_of(source, scale, 0).astype(BF), rest_of(source, scale).astype(BF)]
        return jnp.concatenate(pieces, axis=1)

    pad_ref[:, 0:256] = dot(row_strips((0, 1, 2)), halo_ref[0])
    pad_ref[:, 3328:3584] = dot(row_strips((5, 6, 7)), halo_ref[tab_ref[8]])
    sides = []
    for band in (3, 4):
        source, scale = band_source(tab_ref, band)
        main, rest = main_of(source, scale, 128), rest_of(source, scale)
        sides.append([pltpu.roll(main, (128 - 24 * i) % 128, 1) if i else main for i in range(5)] + [pltpu.roll(rest, 128 - 16, 1)])
    halos = []
    for i in range(GROUPS):
        both = jnp.where(lane < 24, sides[0][i], pltpu.roll(sides[1][i], 24, 1))
        halos.append(jnp.where(lane < 48, both, 0.0))
    x = x_ref[0]
    joined = jnp.concatenate([stacked(x, FINE_IN), jnp.concatenate(halos, axis=0).astype(BF)], axis=1)
    padded = dot(joined, expand_ref[...])
    for i in range(GROUPS):
        pad_ref[:, 256 + 512 * i : 768 + 512 * i] = padded[i * ROWS : (i + 1) * ROWS]
    odd_ref[...] = lane_shifted(pad_ref[...], 64)
    bias = columns(bias_ref[0:1, :])
    sum_ref[...] = wide(bias, 3072)

    def group(g, carry):
        rows = pl.ds(pl.multiple_of(g * 8, 8), 8)
        for chunk in range(6):
            base = chunk * 512
            taken = []
            for a in range(1, 8):
                ref = odd_ref if a % 2 else pad_ref
                start = base + (a // 2) * 128
                taken.append([ref[rows, start + 128 * j : start + 128 * j + 128] for j in range(4)])
            total = [sum_ref[rows, base + 128 * j : base + 128 * j + 128] for j in range(4)]
            for b in range(7):
                weights = [wide_ref[a * 7 + b, rows, :] for a in range(7)]
                for j in range(4):
                    partial = weights[0] * taken[0][j]
                    for a in range(1, 7):
                        partial = partial + weights[a] * taken[a][j]
                    total[j] = total[j] + (pltpu.roll(partial, (3 - b) % 128, 1) if b != 3 else partial)
            for j in range(4):
                sum_ref[rows, base + 128 * j : base + 128 * j + 128] = total[j]
        return carry

    lax.fori_loop(0, 6, group, 0)
    dense = dot(stacked(sum_ref[...].astype(BF), FINE_PAD), compact_ref[...]).astype(BF)
    for i in range(GROUPS):
        out_ref[:, i * FINE_IN : (i + 1) * FINE_IN] = dense[i * ROWS : (i + 1) * ROWS]


def conv_coarse(tab_ref, x_ref, recv_ref, halo_ref, sides_ref, weight_ref, bias_ref, out_ref, pad_ref, wide_ref, sum_ref):
    for tap in range(49):
        wide_ref[tap] = jnp.broadcast_to(weight_ref[1][:, tap : tap + 1], (ROWS, 128))
    lane = lane_ids((ROWS, 128))

    def main_of(source, scale):
        parts = [recv_ref[source, :, 128 * g : 128 * g + 128] for g in range(3)]
        return jnp.concatenate(parts, axis=0).astype(F32) * scale

    def row_strips(bands):
        pieces = []
        for band in bands:
            source, scale = band_source(tab_ref, band)
            pieces.append(main_of(source, scale).astype(BF))
        return jnp.concatenate(pieces, axis=1)

    pad_ref[0, :, 0:128] = dot(row_strips((0, 1, 2)), halo_ref[0])
    pad_ref[0, :, 896:1024] = dot(row_strips((5, 6, 7)), halo_ref[tab_ref[8]])
    pieces = []
    for band in (3, 4):
        source, scale = band_source(tab_ref, band)
        rest = recv_ref[source, :, 384:512].astype(F32) * scale
        rest = jnp.concatenate([rest, pltpu.roll(rest, 128 - 24, 1), pltpu.roll(rest, 128 - 48, 1)], axis=0)
        main = main_of(source, scale)
        pieces.append(jnp.where(lane < 24, rest, main).astype(BF))
    pad_ref[0, :, 128:896] = dot(jnp.concatenate(pieces, axis=1), sides_ref[...]) + x_ref[...].astype(F32)
    padded = pad_ref[0]
    for turn in range(1, 4):
        pad_ref[turn] = lane_shifted(padded, 32 * turn)
    bias = columns(bias_ref[1:2, :])
    sum_ref[...] = wide(bias, 768)

    def group(g, carry):
        rows = pl.ds(pl.multiple_of(g * 8, 8), 8)
        for chunk in range(2):
            base = chunk * 384
            taken = []
            for a in range(1, 8):
                start = base + (a // 4) * 128
                taken.append([pad_ref[a % 4, rows, start + 128 * j : start + 128 * j + 128] for j in range(3)])
            total = [sum_ref[rows, base + 128 * j : base + 128 * j + 128] for j in range(3)]
            for b in range(7):
                weights = [wide_ref[a * 7 + b, rows, :] for a in range(7)]
                for j in range(3):
                    partial = weights[0] * taken[0][j]
                    for a in range(1, 7):
                        partial = partial + weights[a] * taken[a][j]
                    total[j] = total[j] + (pltpu.roll(partial, (3 - b) % 128, 1) if b != 3 else partial)
            for j in range(3):
                sum_ref[rows, base + 128 * j : base + 128 * j + 128] = total[j]
        return carry

    lax.fori_loop(0, 6, group, 0)
    out_ref[...] = sum_ref[...].astype(BF)


def gather_rows(pieces, cat_ref):
    me = lax.axis_index("chan")
    for k, piece in enumerate(pieces):
        first = pl.multiple_of(lax.bitwise_xor(me, k) * ROWS, 16)
        cat_ref[pl.ds(first, ROWS), :] = piece[...]


def make_branch(level, cat_ref, gain_ref, shift_ref, up_ref, up_bias_ref, down_ref, down_bias_ref, block):
    me = lax.axis_index("chan")
    row = slice(level, level + 1)
    gain = wide(columns(gain_ref[row, :]), block)
    shift = wide(columns(shift_ref[row, :]), block)
    up_bias = columns(up_bias_ref[row, :])
    down_bias = columns(down_bias_ref[row, :])
    first = pl.multiple_of(me * ROWS, 16)
    bias_rows = jnp.zeros((ROWS, 128), F32)
    for k in range(down_bias.shape[0] // ROWS):
        bias_rows = jnp.where(me == k, down_bias[k * ROWS : (k + 1) * ROWS], bias_rows)
    bias_rows = wide(bias_rows, block)
    hidden_rows = up_ref.shape[1]

    def branch(start):
        values = cat_ref[:, pl.ds(start, block)].astype(F32)
        mean = jnp.mean(values, axis=0, keepdims=True)
        centred = values - mean
        spread = jnp.mean(centred * centred, axis=0, keepdims=True)
        normed = (centred * lax.rsqrt(spread + norm_eps) * gain + shift).astype(BF)
        out = bias_rows
        for part in range(0, hidden_rows, 256):
            hidden = dot(up_ref[level, part : part + 256, :], normed) + wide(up_bias[part : part + 256], block)
            hidden = 0.5 * hidden * (1.0 + lax.erf(hidden * np.float32(0.5**0.5)))
            out = out + dot(down_ref[level, pl.ds(first, ROWS), part : part + 256], hidden.astype(BF))
        return out

    return branch


def cell_weights(weight_ref):
    lane = lane_ids((ROWS, FINE_IN))
    odd_row = (lane // TILE) % 2
    odd_col = (lane % TILE) % 2
    kind = 2 * odd_row + odd_col
    result = jnp.zeros((ROWS, FINE_IN), F32)
    for k in range(4):
        result = jnp.where(kind == k, weight_ref[:, k : k + 1], result)
    return result


def make_mix_fine(grid_x):
    def mix_fine(
        slots_ref, dev_ref, own_ref, p1_ref, p2_ref, p3_ref, x_ref, mask_ref, gain_ref, shift_ref, up_ref, up_bias_ref,
        down_ref, down_bias_ref, scale_ref, pool_weight_ref, pool_ref, pack_ref,
        fine_ref, pooled_ref, small_mask_ref, msg_ref, cat_ref, mains_ref, rest_ref,
    ):
        gather_rows((own_ref, p1_ref, p2_ref, p3_ref), cat_ref)
        block = 256
        branch = make_branch(0, cat_ref, gain_ref, shift_ref, up_ref, up_bias_ref, down_ref, down_bias_ref, block)
        scale = wide(columns(scale_ref[0:1, :]), block)

        def one(step, carry):
            start = pl.multiple_of(step * block, block)
            here = pl.ds(start, block)
            value = x_ref[0, :, here].astype(F32) + scale * branch(start)
            fine_ref[:, here] = (mask_ref[:, here].astype(F32) * value).astype(BF)
            return carry

        lax.fori_loop(0, TILE * TILE // block, one, 0, unroll=3)

        weights = cell_weights(pool_weight_ref)
        highs, lows, masks = [], [], []
        for i in range(GROUPS):
            lanes = slice(i * FINE_IN, (i + 1) * FINE_IN)
            product = fine_ref[:, lanes].astype(F32) * weights
            high = product.astype(BF)
            highs.append(high)
            lows.append((product - high.astype(F32)).astype(BF))
            masks.append(jnp.broadcast_to(mask_ref[:, lanes].astype(F32), (8, FINE_IN)))
        pool_table = pool_ref[...]
        pooled = dot(jnp.concatenate(highs, axis=0), pool_table) + dot(jnp.concatenate(lows, axis=0), pool_table)
        pooled = pooled.astype(BF)
        for i in range(GROUPS):
            pooled_ref[:, i * 128 : (i + 1) * 128] = pooled[i * ROWS : (i + 1) * ROWS]
        counts = dot(jnp.concatenate(masks, axis=0).astype(BF), pool_table)
        small_mask_ref[...] = jnp.where(counts > 0.5, 1.0, 0.0)

        packed = dot(pooled_ref[...], pack_ref[...])
        lane = lane_ids((ROWS, 128))
        blocks = (packed[:, 0:128], packed[:, 128:256])
        for r in range(2):
            for c in range(2):
                mains_ref[2 * r + c] = jnp.where(lane < 72, blocks[r], blocks[c]).astype(BF)
        lane = lane_ids((16, 128))
        for c in range(2):
            rest = packed[:, 256:384]
            rest = pltpu.roll(rest, 64, 1) if c else rest
            parts = [rest[0:16], pltpu.roll(rest[16:32], 24, 1), pltpu.roll(rest[32:48], 48, 1)]
            joined = jnp.where(lane < 24, parts[0], jnp.where(lane < 48, parts[1], parts[2]))
            rest_ref[c] = jnp.where(lane < 72, joined, 0.0).astype(BF)

        count = slots_ref.shape[0]
        me = lax.axis_index("tile")
        my_slot = scan_tiles(count, lambda k, c: c + jnp.where(dev_ref[k] == me, slots_ref[k], 0), jnp.int32(0))
        my_x = lax.rem(my_slot, grid_x)
        my_y = lax.div(my_slot, grid_x)

        def fill(k, carry):
            slot, dev = slots_ref[k], dev_ref[k]
            row_pick = jnp.where(lax.div(slot, grid_x) + 1 == my_y, 0, 1)
            col_pick = jnp.where(lax.rem(slot, grid_x) == lax.rem(my_x + (grid_x - 1), grid_x), 0, 1)
            both = 2 * row_pick + col_pick
            for g in range(3):
                msg_ref[dev, :, 128 * g : 128 * g + 128] = mains_ref[both, 16 * g : 16 * g + 16, :]
            msg_ref[dev, :, 384:512] = rest_ref[col_pick]
            return carry

        scan_tiles(count, fill, jnp.int32(0))

    return mix_fine


def mix_coarse(
    own_ref, p1_ref, p2_ref, p3_ref, pooled_ref, small_mask_ref, fine_ref, mask_ref, gain_ref, shift_ref, up_ref, up_bias_ref,
    down_ref, down_bias_ref, scale_ref, spread_weight_ref, unpool_ref, out_ref, cat_ref,
):
    gather_rows((own_ref, p1_ref, p2_ref, p3_ref), cat_ref)
    block = 256
    branch = make_branch(1, cat_ref, gain_ref, shift_ref, up_ref, up_bias_ref, down_ref, down_bias_ref, block)
    scale = wide(columns(scale_ref[1:2, :]), block)
    parts = []
    for step in range(768 // block):
        value = pooled_ref[:, step * block : (step + 1) * block].astype(F32) + scale * branch(step * block)
        for half in range(2):
            i = 2 * step + half
            cells = small_mask_ref[8 * i : 8 * i + 1, :] * value[:, half * 128 : half * 128 + 128]
            parts.append(cells.astype(BF))
    spread = dot(jnp.concatenate(parts, axis=0), unpool_ref[...])
    weights = cell_weights(spread_weight_ref)
    for i in range(GROUPS):
        lanes = slice(i * FINE_IN, (i + 1) * FINE_IN)
        value = fine_ref[:, lanes].astype(F32) + weights * spread[i * ROWS : (i + 1) * ROWS]
        out_ref[0, :, lanes] = (mask_ref[:, lanes].astype(F32) * value).astype(BF)


VMEM = pl.BlockSpec(memory_space=pltpu.VMEM)
SMEM = pl.BlockSpec(memory_space=pltpu.SMEM)


def shaped(*shape, dtype=BF):
    return jax.ShapeDtypeStruct(shape, dtype)


PARAMS = pltpu.CompilerParams(vmem_limit_bytes=48 * 1024 * 1024)


def every_channel(own):
    pairs = lambda bit: [(i, i ^ bit) for i in range(4)]
    across = lax.ppermute(own, "chan", pairs(2))
    beside = lax.ppermute(own, "chan", pairs(1))
    diagonal = lax.ppermute(across, "chan", pairs(1))
    return own, beside, across, diagonal


def per_device(
    features, land_mask, wet_slots, device_of, depth_weight, depth_bias, norm_gain, norm_bias, up_weight, up_bias,
    down_weight, down_bias, layer_scale, pool_weight, spread_weight,
):
    count = wet_slots.shape[0]
    grid_x = 2 * count // GRID_Y
    cells = TILE * TILE
    messages, table = pl.pallas_call(
        make_prep(grid_x),
        in_specs=[SMEM, SMEM, VMEM, VMEM],
        out_specs=[VMEM, SMEM],
        out_shape=[shaped(count, 16, 896), shaped(16, dtype=jnp.int32)],
        scratch_shapes=[
            pltpu.VMEM((2, ROWS, 128), BF),
            pltpu.VMEM((2, ROWS, 128), BF),
            pltpu.VMEM((2, 16, 128), F32),
            pltpu.VMEM((2, 16, 128), F32),
        ],
        compiler_params=PARAMS,
        name="prep",
    )(wet_slots, device_of, features, jnp.asarray(FINE["pack"]))
    arrived = lax.all_to_all(messages, "tile", 0, 0, tiled=True)
    conv = pl.pallas_call(
        conv_fine,
        in_specs=[SMEM, VMEM, VMEM, VMEM, VMEM, VMEM, VMEM, VMEM],
        out_specs=VMEM,
        out_shape=shaped(ROWS, cells),
        scratch_shapes=[
            pltpu.VMEM((ROWS, 3584), F32),
            pltpu.VMEM((ROWS, 3584), F32),
            pltpu.VMEM((49, ROWS, 128), F32),
            pltpu.VMEM((ROWS, 3072), F32),
        ],
        compiler_params=PARAMS,
        name="conv_fine",
    )(
        table, features, arrived, jnp.asarray(FINE["halo"]), jnp.asarray(FINE["expand"]), jnp.asarray(FINE["compact"]),
        depth_weight, depth_bias,
    )
    fine, pooled, small_mask, messages = pl.pallas_call(
        make_mix_fine(grid_x),
        in_specs=[SMEM, SMEM] + [VMEM] * 8 + [VMEM] * 8,
        out_specs=[VMEM] * 4,
        out_shape=[shaped(ROWS, cells), shaped(ROWS, 768), shaped(48, 128, dtype=F32), shaped(count, 16, 512)],
        scratch_shapes=[
            pltpu.VMEM((4 * ROWS, cells), BF),
            pltpu.VMEM((4, ROWS, 128), BF),
            pltpu.VMEM((2, 16, 128), BF),
        ],
        compiler_params=PARAMS,
        name="mix_fine",
    )(
        wet_slots, device_of, *every_channel(conv), features, land_mask, norm_gain, norm_bias, up_weight, up_bias,
        down_weight, down_bias, layer_scale, pool_weight, jnp.asarray(FINE["pool"]), jnp.asarray(COARSE["pack"]),
    )
    arrived = lax.all_to_all(messages, "tile", 0, 0, tiled=True)
    conv = pl.pallas_call(
        conv_coarse,
        in_specs=[SMEM, VMEM, VMEM, VMEM, VMEM, VMEM, VMEM],
        out_specs=VMEM,
        out_shape=shaped(ROWS, 768),
        scratch_shapes=[
            pltpu.VMEM((4, ROWS, 1024), F32),
            pltpu.VMEM((49, ROWS, 128), F32),
            pltpu.VMEM((ROWS, 768), F32),
        ],
        compiler_params=PARAMS,
        name="conv_coarse",
    )(table, pooled, arrived, jnp.asarray(COARSE["halo"]), jnp.asarray(COARSE["sides"]), depth_weight, depth_bias)
    return pl.pallas_call(
        mix_coarse,
        in_specs=[VMEM] * 10 + [VMEM] * 7,
        out_specs=VMEM,
        out_shape=shaped(1, ROWS, cells),
        scratch_shapes=[pltpu.VMEM((4 * ROWS, 768), BF)],
        compiler_params=PARAMS,
        name="mix_coarse",
    )(
        *every_channel(conv), pooled, small_mask, fine, land_mask, norm_gain, norm_bias, up_weight, up_bias,
        down_weight, down_bias, layer_scale, spread_weight, jnp.asarray(FINE["unpool"]),
    )


def solution(mesh):
    placed = (
        P("tile", "chan", None),
        P("tile", None),
        P(),
        P(),
        P(None, "chan", None),
        P(None, "chan"),
        P(),
        P(),
        P(),
        P(),
        P(),
        P(),
        P(None, "chan"),
        P("chan", None),
        P("chan", None),
    )
    return jax.shard_map(
        per_device, mesh=mesh, in_specs=placed, out_specs=P("tile", "chan", None), check_vma=False
    )
```

```python
import jax
import jax.numpy as jnp
import ml_dtypes
import numpy as np
from jax import lax
from jax.experimental import pallas as pl
from jax.experimental.pallas import tpu as pltpu
from jax.sharding import PartitionSpec as P

TILE = 48
HALF = TILE // 2
GRID_Y = 4
GROUPS = 6
ROWS = 48
FINE_IN = 8 * TILE
FINE_PAD = 8 * 64
BANDS = ((-1, -1), (-1, 0), (-1, 1), (0, -1), (0, 1), (1, -1), (1, 0), (1, 1))
norm_eps = 1e-06
BF = jnp.bfloat16
F32 = jnp.float32


def one_hot(shape, pairs):
    table = np.zeros(shape, np.float32)
    for source, target in pairs:
        table[source, target] = 1.0
    return table.astype(ml_dtypes.bfloat16)


def side_target(side, row, col, width, stride):
    if side == 0:
        return row * stride + 3 + col
    if side == -1:
        return row * stride + col - (width - 3) if col >= width - 3 else None
    return row * stride + 3 + width + col if col < 3 else None


def halo_pairs(cells, width, stride, first_row, flipped):
    block = max(lane for lane, _ in cells) // 128 * 128 + 128
    pairs = []
    for place, side in enumerate((-1, 0, 1)):
        for lane, index in cells:
            row, col = index // width, index % width
            if flipped:
                row, col = 2 - row, width - 1 - col
            target = side_target(side, row + first_row, col, width, stride)
            if target is not None:
                pairs.append((place * block + lane, target))
    return pairs


def fine_tables():
    first = [(t, t) for t in range(128)] + [(128 + t, 128 + t) for t in range(16)]
    last = [(t, 16 + t) for t in range(128)] + [(128 + t, t) for t in range(16)]
    halo = np.stack(
        [
            one_hot((768, 256), halo_pairs(last, TILE, 64, 1, False)),
            one_hot((768, 256), halo_pairs(first, TILE, 64, 0, False)),
            one_hot((768, 256), halo_pairs(last, TILE, 64, 0, True)),
        ]
    )
    pack, expand, compact, pool = [], [], [], []
    for row in range(8):
        for j in range(3):
            pack.append((row * 48 + j, row * 3 + j))
            pack.append((row * 48 + 45 + j, 128 + row * 3 + j))
            expand.append((384 + row * 3 + j, row * 64 + j))
            expand.append((384 + 24 + row * 3 + j, row * 64 + 51 + j))
        for col in range(48):
            expand.append((row * 48 + col, row * 64 + 3 + col))
            compact.append((row * 64 + 3 + col, row * 48 + col))
            pool.append((row * 48 + col, (row // 2) * 32 + 3 + col // 2))
    return {
        "halo": halo,
        "pack": one_hot((384, 256), pack),
        "expand": one_hot((512, 512), expand),
        "compact": one_hot((512, 384), compact),
        "pool": one_hot((384, 128), pool),
        "unpool": np.ascontiguousarray(one_hot((384, 128), pool).T),
    }


def coarse_tables():
    strip = [(t, t) for t in range(72)]
    halo = np.stack(
        [
            one_hot((384, 128), halo_pairs(strip, HALF, 32, 1, False)),
            one_hot((384, 128), halo_pairs(strip, HALF, 32, 0, False)),
            one_hot((384, 128), halo_pairs(strip, HALF, 32, 0, True)),
        ]
    )
    pack, sides = [], []
    for row in range(3):
        for col in range(HALF):
            pack.append((row * 32 + 3 + col, row * 24 + col))
            pack.append(((21 + row) * 32 + 3 + col, 128 + row * 24 + col))
    for row in range(HALF):
        for j in range(3):
            index = row * 3 + j
            lane = 72 + index if row < 16 else index - 48
            pack.append((row * 32 + 3 + j, lane if row < 16 else 256 + lane))
            pack.append((row * 32 + 24 + j, 128 + lane if row < 16 else 256 + 64 + lane))
            sides.append((lane, row * 32 + j))
            sides.append((128 + lane, row * 32 + 27 + j))
    return {
        "halo": halo,
        "pack": one_hot((768, 384), pack),
        "sides": one_hot((256, 768), sides),
    }


FINE = fine_tables()
COARSE = coarse_tables()


def dot(left, right):
    return jnp.dot(left, right, preferred_element_type=F32)


def stacked(value, width):
    return jnp.concatenate([value[:, i * width : (i + 1) * width] for i in range(GROUPS)], axis=0)


def lane_ids(shape):
    return lax.broadcasted_iota(jnp.int32, shape, 1)


def columns(row):
    high = row.astype(BF)
    rest = row - high.astype(F32)
    middle = rest.astype(BF)
    low = (rest - middle.astype(F32)).astype(BF)
    n = row.shape[1]
    terms = jnp.concatenate([high, middle, low, jnp.zeros((13, n), BF)], axis=0)
    return lax.dot_general(terms, jnp.ones((16, 128), BF), (((0,), (0,)), ((), ())), preferred_element_type=F32)


def wide(block, lanes):
    return jnp.concatenate([block] * (lanes // 128), axis=1)


def scan_tiles(count, step, carry):
    if count <= 16:
        for k in range(count):
            carry = step(k, carry)
        return carry
    return lax.fori_loop(0, count, step, carry)


LOADED = ("x", "mask", "weight", "bias", "halo", "expand", "compact", "small_halo", "sides", "pool", "unpool", "small_pack")


def make_prep(grid_x):
    def prep(slots_hbm, dev_hbm, pack_hbm, *refs):
        size = len(LOADED)
        sources, (msg_ref, tab_ref), targets = refs[:size], refs[size : size + 2], refs[size + 2 : 2 * size + 2]
        slots_ref, dev_ref, pack_ref, rows_ref, cols_ref, row_rest_ref, col_rest_ref, sems = refs[2 * size + 2 :]
        pairs = [(slots_hbm, slots_ref), (dev_hbm, dev_ref), (sources[0], targets[0]), (pack_hbm, pack_ref)]
        pairs += list(zip(sources[1:], targets[1:]))
        loads = [pltpu.make_async_copy(source, target, sems.at[i]) for i, (source, target) in enumerate(pairs)]
        for load in loads:
            load.start()
        loads[0].wait()
        loads[1].wait()
        count = slots_ref.shape[0]
        me = lax.axis_index("tile")
        my_slot = scan_tiles(count, lambda k, c: c + jnp.where(dev_ref[k] == me, slots_ref[k], 0), jnp.int32(0))
        my_x = lax.rem(my_slot, grid_x)
        my_y = lax.div(my_slot, grid_x)
        wanted = []
        for up_by, right_by in BANDS:
            near_x = lax.rem(my_x + (right_by + grid_x), grid_x)
            near_y = my_y + up_by
            folded = near_y >= GRID_Y
            from_x = jnp.where(folded, grid_x - 1 - near_x, near_x)
            from_y = jnp.where(folded, GRID_Y - 1, near_y)
            wanted.append(from_y * grid_x + from_x)

        def find(k, found):
            slot, dev = slots_ref[k], dev_ref[k]
            row_pick = jnp.where(lax.div(slot, grid_x) + 1 == my_y, 0, 1)
            col_pick = jnp.where(lax.rem(slot, grid_x) == lax.rem(my_x + (grid_x - 1), grid_x), 0, 1)
            tab_ref[16 + dev] = 2 * row_pick + col_pick
            return tuple(jnp.where(slot == want, dev, old) for want, old in zip(wanted, found))

        found = scan_tiles(count, find, tuple(jnp.int32(-1) for _ in BANDS))
        for band in range(8):
            tab_ref[band] = found[band]
        tab_ref[8] = jnp.where(my_y == GRID_Y - 1, 2, 1)
        for spare in range(9, 16):
            tab_ref[spare] = 0

        loads[2].wait()
        loads[3].wait()
        x = targets[0][0]
        cols = dot(stacked(x, FINE_IN), pack_ref[...])
        lane = lane_ids((ROWS, 128))
        for side in range(2):
            part = cols[:, side * 128 : side * 128 + 128]
            main = part[0:ROWS]
            for i in range(1, 5):
                main = main + pltpu.roll(part[i * ROWS : (i + 1) * ROWS], 24 * i, 1)
            cols_ref[side] = main.astype(BF)
            rest = pltpu.roll(part[5 * ROWS : 6 * ROWS], 16, 1)
            col_rest_ref[side] = rest[0:16] + pltpu.roll(rest[16:32], 40, 1) + pltpu.roll(rest[32:48], 80, 1)
        rows_ref[0] = x[:, 0:128]
        rows_ref[1] = x[:, 2176:2304]
        ends = (x[:, 128:256].astype(F32), pltpu.roll(x[:, 2048:2176].astype(F32), 16, 1))
        for side in range(2):
            rest = jnp.where(lane < 16, ends[side], 0.0)
            row_rest_ref[side] = rest[0:16] + pltpu.roll(rest[16:32], 40, 1) + pltpu.roll(rest[32:48], 80, 1)

        def fill(dev, carry):
            row_pick = lax.div(tab_ref[16 + dev], 2)
            col_pick = lax.rem(tab_ref[16 + dev], 2)
            for g in range(3):
                msg_ref[dev, :, 256 * g : 256 * g + 128] = rows_ref[row_pick, 16 * g : 16 * g + 16, :]
                msg_ref[dev, :, 256 * g + 128 : 256 * g + 256] = cols_ref[col_pick, 16 * g : 16 * g + 16, :]
            msg_ref[dev, :, 768:896] = (row_rest_ref[row_pick] + col_rest_ref[col_pick]).astype(BF)
            return carry

        scan_tiles(count, fill, jnp.int32(0))
        for load in loads[4:]:
            load.wait()

    return prep


def band_source(tab_ref, band):
    source = tab_ref[band]
    return jnp.maximum(source, 0), jnp.where(source >= 0, 1.0, 0.0).astype(F32)


def lane_shifted(value, lanes):
    return pltpu.roll(value, value.shape[1] - lanes, 1)


def conv_fine(tab_ref, x_ref, recv_ref, halo_ref, expand_ref, compact_ref, weight_ref, bias_ref, out_ref, pad_ref, odd_ref, wide_ref, sum_ref):
    for tap in range(49):
        wide_ref[tap] = jnp.broadcast_to(weight_ref[0][:, tap : tap + 1], (ROWS, 128))
    lane = lane_ids((ROWS, 128))

    def rest_of(source, scale):
        rest = recv_ref[source, :, 768:896].astype(F32) * scale
        return jnp.concatenate([rest, pltpu.roll(rest, 128 - 40, 1), pltpu.roll(rest, 128 - 80, 1)], axis=0)

    def main_of(source, scale, offset):
        parts = [recv_ref[source, :, 256 * g + offset : 256 * g + offset + 128] for g in range(3)]
        return jnp.concatenate(parts, axis=0).astype(F32) * scale

    def row_strips(bands):
        pieces = []
        for band in bands:
            source, scale = band_source(tab_ref, band)
            pieces += [main_of(source, scale, 0).astype(BF), rest_of(source, scale).astype(BF)]
        return jnp.concatenate(pieces, axis=1)

    pad_ref[:, 0:256] = dot(row_strips((0, 1, 2)), halo_ref[0])
    pad_ref[:, 3328:3584] = dot(row_strips((5, 6, 7)), halo_ref[tab_ref[8]])
    sides = []
    for band in (3, 4):
        source, scale = band_source(tab_ref, band)
        main, rest = main_of(source, scale, 128), rest_of(source, scale)
        sides.append([pltpu.roll(main, (128 - 24 * i) % 128, 1) if i else main for i in range(5)] + [pltpu.roll(rest, 128 - 16, 1)])
    halos = []
    for i in range(GROUPS):
        both = jnp.where(lane < 24, sides[0][i], pltpu.roll(sides[1][i], 24, 1))
        halos.append(jnp.where(lane < 48, both, 0.0))
    x = x_ref[0]
    joined = jnp.concatenate([stacked(x, FINE_IN), jnp.concatenate(halos, axis=0).astype(BF)], axis=1)
    padded = dot(joined, expand_ref[...])
    for i in range(GROUPS):
        pad_ref[:, 256 + 512 * i : 768 + 512 * i] = padded[i * ROWS : (i + 1) * ROWS]
    odd_ref[...] = lane_shifted(pad_ref[...], 64)
    bias = columns(bias_ref[0:1, :])
    sum_ref[...] = wide(bias, 3072)

    def group(g, carry):
        rows = pl.ds(pl.multiple_of(g * 8, 8), 8)
        for chunk in range(6):
            base = chunk * 512
            taken = []
            for a in range(1, 8):
                ref = odd_ref if a % 2 else pad_ref
                start = base + (a // 2) * 128
                taken.append([ref[rows, start + 128 * j : start + 128 * j + 128] for j in range(4)])
            total = [sum_ref[rows, base + 128 * j : base + 128 * j + 128] for j in range(4)]
            for b in range(7):
                weights = [wide_ref[a * 7 + b, rows, :] for a in range(7)]
                for j in range(4):
                    partial = weights[0] * taken[0][j]
                    for a in range(1, 7):
                        partial = partial + weights[a] * taken[a][j]
                    total[j] = total[j] + (pltpu.roll(partial, (3 - b) % 128, 1) if b != 3 else partial)
            for j in range(4):
                sum_ref[rows, base + 128 * j : base + 128 * j + 128] = total[j]
        return carry

    lax.fori_loop(0, 6, group, 0)
    dense = dot(stacked(sum_ref[...].astype(BF), FINE_PAD), compact_ref[...]).astype(BF)
    for i in range(GROUPS):
        out_ref[:, i * FINE_IN : (i + 1) * FINE_IN] = dense[i * ROWS : (i + 1) * ROWS]


def conv_coarse(tab_ref, x_ref, recv_ref, halo_ref, sides_ref, weight_ref, bias_ref, out_ref, pad_ref, wide_ref, sum_ref):
    for tap in range(49):
        wide_ref[tap] = jnp.broadcast_to(weight_ref[1][:, tap : tap + 1], (ROWS, 128))
    lane = lane_ids((ROWS, 128))

    def main_of(source, scale):
        parts = [recv_ref[source, :, 128 * g : 128 * g + 128] for g in range(3)]
        return jnp.concatenate(parts, axis=0).astype(F32) * scale

    def row_strips(bands):
        pieces = []
        for band in bands:
            source, scale = band_source(tab_ref, band)
            pieces.append(main_of(source, scale).astype(BF))
        return jnp.concatenate(pieces, axis=1)

    pad_ref[0, :, 0:128] = dot(row_strips((0, 1, 2)), halo_ref[0])
    pad_ref[0, :, 896:1024] = dot(row_strips((5, 6, 7)), halo_ref[tab_ref[8]])
    pieces = []
    for band in (3, 4):
        source, scale = band_source(tab_ref, band)
        rest = recv_ref[source, :, 384:512].astype(F32) * scale
        rest = jnp.concatenate([rest, pltpu.roll(rest, 128 - 24, 1), pltpu.roll(rest, 128 - 48, 1)], axis=0)
        main = main_of(source, scale)
        pieces.append(jnp.where(lane < 24, rest, main).astype(BF))
    pad_ref[0, :, 128:896] = dot(jnp.concatenate(pieces, axis=1), sides_ref[...]) + x_ref[...].astype(F32)
    padded = pad_ref[0]
    for turn in range(1, 4):
        pad_ref[turn] = lane_shifted(padded, 32 * turn)
    bias = columns(bias_ref[1:2, :])
    sum_ref[...] = wide(bias, 768)

    def group(g, carry):
        rows = pl.ds(pl.multiple_of(g * 8, 8), 8)
        for chunk in range(2):
            base = chunk * 384
            taken = []
            for a in range(1, 8):
                start = base + (a // 4) * 128
                taken.append([pad_ref[a % 4, rows, start + 128 * j : start + 128 * j + 128] for j in range(3)])
            total = [sum_ref[rows, base + 128 * j : base + 128 * j + 128] for j in range(3)]
            for b in range(7):
                weights = [wide_ref[a * 7 + b, rows, :] for a in range(7)]
                for j in range(3):
                    partial = weights[0] * taken[0][j]
                    for a in range(1, 7):
                        partial = partial + weights[a] * taken[a][j]
                    total[j] = total[j] + (pltpu.roll(partial, (3 - b) % 128, 1) if b != 3 else partial)
            for j in range(3):
                sum_ref[rows, base + 128 * j : base + 128 * j + 128] = total[j]
        return carry

    lax.fori_loop(0, 6, group, 0)
    out_ref[...] = sum_ref[...].astype(BF)


def gather_rows(pieces, cat_ref):
    me = lax.axis_index("chan")
    for k, piece in enumerate(pieces):
        first = pl.multiple_of(lax.bitwise_xor(me, k) * ROWS, 16)
        cat_ref[pl.ds(first, ROWS), :] = piece[...]


def make_branch(level, cat_ref, gain_ref, shift_ref, up_ref, up_bias_ref, down_ref, down_bias_ref, block):
    me = lax.axis_index("chan")
    row = slice(level, level + 1)
    gain = wide(columns(gain_ref[row, :]), block)
    shift = wide(columns(shift_ref[row, :]), block)
    up_bias = columns(up_bias_ref[row, :])
    down_bias = columns(down_bias_ref[row, :])
    first = pl.multiple_of(me * ROWS, 16)
    bias_rows = jnp.zeros((ROWS, 128), F32)
    for k in range(down_bias.shape[0] // ROWS):
        bias_rows = jnp.where(me == k, down_bias[k * ROWS : (k + 1) * ROWS], bias_rows)
    bias_rows = wide(bias_rows, block)
    hidden_rows = up_ref.shape[1]

    def branch(start):
        values = cat_ref[:, pl.ds(start, block)].astype(F32)
        mean = jnp.mean(values, axis=0, keepdims=True)
        centred = values - mean
        spread = jnp.mean(centred * centred, axis=0, keepdims=True)
        normed = (centred * lax.rsqrt(spread + norm_eps) * gain + shift).astype(BF)
        out = bias_rows
        for part in range(0, hidden_rows, 256):
            hidden = dot(up_ref[level, part : part + 256, :], normed) + wide(up_bias[part : part + 256], block)
            hidden = 0.5 * hidden * (1.0 + lax.erf(hidden * np.float32(0.5**0.5)))
            out = out + dot(down_ref[level, pl.ds(first, ROWS), part : part + 256], hidden.astype(BF))
        return out

    return branch


def cell_weights(weight_ref):
    lane = lane_ids((ROWS, FINE_IN))
    odd_row = (lane // TILE) % 2
    odd_col = (lane % TILE) % 2
    kind = 2 * odd_row + odd_col
    result = jnp.zeros((ROWS, FINE_IN), F32)
    for k in range(4):
        result = jnp.where(kind == k, weight_ref[:, k : k + 1], result)
    return result


def make_mix_fine(count):
    def mix_fine(
        tab_ref, own_ref, p1_ref, p2_ref, p3_ref, x_ref, mask_ref, gain_ref, shift_ref, up_ref, up_bias_ref,
        down_ref, down_bias_ref, scale_ref, pool_weight_ref, pool_ref, pack_ref,
        fine_ref, pooled_ref, small_mask_ref, msg_ref, cat_ref, mains_ref, rest_ref,
    ):
        gather_rows((own_ref, p1_ref, p2_ref, p3_ref), cat_ref)
        block = 256
        branch = make_branch(0, cat_ref, gain_ref, shift_ref, up_ref, up_bias_ref, down_ref, down_bias_ref, block)
        scale = wide(columns(scale_ref[0:1, :]), block)

        def one(step, carry):
            start = pl.multiple_of(step * block, block)
            here = pl.ds(start, block)
            value = x_ref[0, :, here].astype(F32) + scale * branch(start)
            fine_ref[:, here] = (mask_ref[:, here].astype(F32) * value).astype(BF)
            return carry

        lax.fori_loop(0, TILE * TILE // block, one, 0, unroll=3)

        weights = cell_weights(pool_weight_ref)
        highs, lows, masks = [], [], []
        for i in range(GROUPS):
            lanes = slice(i * FINE_IN, (i + 1) * FINE_IN)
            product = fine_ref[:, lanes].astype(F32) * weights
            high = product.astype(BF)
            highs.append(high)
            lows.append((product - high.astype(F32)).astype(BF))
            masks.append(jnp.broadcast_to(mask_ref[:, lanes].astype(F32), (8, FINE_IN)))
        pool_table = pool_ref[...]
        pooled = dot(jnp.concatenate(highs, axis=0), pool_table) + dot(jnp.concatenate(lows, axis=0), pool_table)
        pooled = pooled.astype(BF)
        for i in range(GROUPS):
            pooled_ref[:, i * 128 : (i + 1) * 128] = pooled[i * ROWS : (i + 1) * ROWS]
        counts = dot(jnp.concatenate(masks, axis=0).astype(BF), pool_table)
        small_mask_ref[...] = jnp.where(counts > 0.5, 1.0, 0.0)

        packed = dot(pooled_ref[...], pack_ref[...])
        lane = lane_ids((ROWS, 128))
        blocks = (packed[:, 0:128], packed[:, 128:256])
        for r in range(2):
            for c in range(2):
                mains_ref[2 * r + c] = jnp.where(lane < 72, blocks[r], blocks[c]).astype(BF)
        lane = lane_ids((16, 128))
        for c in range(2):
            rest = packed[:, 256:384]
            rest = pltpu.roll(rest, 64, 1) if c else rest
            parts = [rest[0:16], pltpu.roll(rest[16:32], 24, 1), pltpu.roll(rest[32:48], 48, 1)]
            joined = jnp.where(lane < 24, parts[0], jnp.where(lane < 48, parts[1], parts[2]))
            rest_ref[c] = jnp.where(lane < 72, joined, 0.0).astype(BF)

        def fill(dev, carry):
            both = tab_ref[16 + dev]
            col_pick = lax.rem(both, 2)
            for g in range(3):
                msg_ref[dev, :, 128 * g : 128 * g + 128] = mains_ref[both, 16 * g : 16 * g + 16, :]
            msg_ref[dev, :, 384:512] = rest_ref[col_pick]
            return carry

        scan_tiles(count, fill, jnp.int32(0))

    return mix_fine


def mix_coarse(
    own_ref, p1_ref, p2_ref, p3_ref, pooled_ref, small_mask_ref, fine_ref, mask_ref, gain_ref, shift_ref, up_ref, up_bias_ref,
    down_ref, down_bias_ref, scale_ref, spread_weight_ref, unpool_ref, out_ref, cat_ref,
):
    gather_rows((own_ref, p1_ref, p2_ref, p3_ref), cat_ref)
    block = 256
    branch = make_branch(1, cat_ref, gain_ref, shift_ref, up_ref, up_bias_ref, down_ref, down_bias_ref, block)
    scale = wide(columns(scale_ref[1:2, :]), block)
    parts = []
    for step in range(768 // block):
        value = pooled_ref[:, step * block : (step + 1) * block].astype(F32) + scale * branch(step * block)
        for half in range(2):
            i = 2 * step + half
            cells = small_mask_ref[8 * i : 8 * i + 1, :] * value[:, half * 128 : half * 128 + 128]
            parts.append(cells.astype(BF))
    spread = dot(jnp.concatenate(parts, axis=0), unpool_ref[...])
    weights = cell_weights(spread_weight_ref)
    for i in range(GROUPS):
        lanes = slice(i * FINE_IN, (i + 1) * FINE_IN)
        value = fine_ref[:, lanes].astype(F32) + weights * spread[i * ROWS : (i + 1) * ROWS]
        out_ref[0, :, lanes] = (mask_ref[:, lanes].astype(F32) * value).astype(BF)


VMEM = pl.BlockSpec(memory_space=pltpu.VMEM)
SMEM = pl.BlockSpec(memory_space=pltpu.SMEM)
ANY = pl.BlockSpec(memory_space=pl.ANY)


def shaped(*shape, dtype=BF):
    return jax.ShapeDtypeStruct(shape, dtype)


PARAMS = pltpu.CompilerParams(vmem_limit_bytes=24 * 1024 * 1024)


def every_channel(own):
    pairs = lambda bit: [(i, i ^ bit) for i in range(4)]
    across = lax.ppermute(own, "chan", pairs(2))
    beside = lax.ppermute(own, "chan", pairs(1))
    diagonal = lax.ppermute(across, "chan", pairs(1))
    return own, beside, across, diagonal


def per_device(
    features, land_mask, wet_slots, device_of, depth_weight, depth_bias, norm_gain, norm_bias, up_weight, up_bias,
    down_weight, down_bias, layer_scale, pool_weight, spread_weight,
):
    count = wet_slots.shape[0]
    grid_x = 2 * count // GRID_Y
    cells = TILE * TILE
    given = {
        "x": features,
        "mask": land_mask,
        "weight": depth_weight,
        "bias": depth_bias,
        "halo": jnp.asarray(FINE["halo"]),
        "expand": jnp.asarray(FINE["expand"]),
        "compact": jnp.asarray(FINE["compact"]),
        "small_halo": jnp.asarray(COARSE["halo"]),
        "sides": jnp.asarray(COARSE["sides"]),
        "pool": jnp.asarray(FINE["pool"]),
        "unpool": jnp.asarray(FINE["unpool"]),
        "small_pack": jnp.asarray(COARSE["pack"]),
    }
    given = [given[name] for name in LOADED]
    pack = jnp.asarray(FINE["pack"])
    results = pl.pallas_call(
        make_prep(grid_x),
        in_specs=[ANY] * (3 + len(given)),
        out_specs=[VMEM, SMEM] + [VMEM] * len(given),
        out_shape=[shaped(count, 16, 896), shaped(16 + count, dtype=jnp.int32)]
        + [shaped(*array.shape, dtype=array.dtype) for array in given],
        scratch_shapes=[
            pltpu.SMEM((count,), jnp.int32),
            pltpu.SMEM((count,), jnp.int32),
            pltpu.VMEM(pack.shape, BF),
            pltpu.VMEM((2, ROWS, 128), BF),
            pltpu.VMEM((2, ROWS, 128), BF),
            pltpu.VMEM((2, 16, 128), F32),
            pltpu.VMEM((2, 16, 128), F32),
            pltpu.SemaphoreType.DMA((3 + len(given),)),
        ],
        compiler_params=PARAMS,
        name="prep",
    )(wet_slots, device_of, pack, *given)
    messages, table = results[:2]
    held = dict(zip(LOADED, results[2:]))
    arrived = lax.all_to_all(messages, "tile", 0, 0, tiled=True)
    conv = pl.pallas_call(
        conv_fine,
        in_specs=[SMEM] + [VMEM] * 7,
        out_specs=VMEM,
        out_shape=shaped(ROWS, cells),
        scratch_shapes=[
            pltpu.VMEM((ROWS, 3584), F32),
            pltpu.VMEM((ROWS, 3584), F32),
            pltpu.VMEM((49, ROWS, 128), F32),
            pltpu.VMEM((ROWS, 3072), F32),
        ],
        compiler_params=PARAMS,
        name="conv_fine",
    )(table, held["x"], arrived, held["halo"], held["expand"], held["compact"], held["weight"], held["bias"])
    fine, pooled, small_mask, messages = pl.pallas_call(
        make_mix_fine(count),
        in_specs=[SMEM] + [VMEM] * 16,
        out_specs=[VMEM] * 4,
        out_shape=[shaped(ROWS, cells), shaped(ROWS, 768), shaped(48, 128, dtype=F32), shaped(count, 16, 512)],
        scratch_shapes=[
            pltpu.VMEM((4 * ROWS, cells), BF),
            pltpu.VMEM((4, ROWS, 128), BF),
            pltpu.VMEM((2, 16, 128), BF),
        ],
        compiler_params=PARAMS,
        name="mix_fine",
    )(
        table, *every_channel(conv), held["x"], held["mask"], norm_gain, norm_bias, up_weight, up_bias,
        down_weight, down_bias, layer_scale, pool_weight, held["pool"], held["small_pack"],
    )
    arrived = lax.all_to_all(messages, "tile", 0, 0, tiled=True)
    conv = pl.pallas_call(
        conv_coarse,
        in_specs=[SMEM] + [VMEM] * 6,
        out_specs=VMEM,
        out_shape=shaped(ROWS, 768),
        scratch_shapes=[
            pltpu.VMEM((4, ROWS, 1024), F32),
            pltpu.VMEM((49, ROWS, 128), F32),
            pltpu.VMEM((ROWS, 768), F32),
        ],
        compiler_params=PARAMS,
        name="conv_coarse",
    )(table, pooled, arrived, held["small_halo"], held["sides"], held["weight"], held["bias"])
    return pl.pallas_call(
        mix_coarse,
        in_specs=[VMEM] * 17,
        out_specs=VMEM,
        out_shape=shaped(1, ROWS, cells),
        scratch_shapes=[pltpu.VMEM((4 * ROWS, 768), BF)],
        compiler_params=PARAMS,
        name="mix_coarse",
    )(
        *every_channel(conv), pooled, small_mask, fine, held["mask"], norm_gain, norm_bias, up_weight, up_bias,
        down_weight, down_bias, layer_scale, spread_weight, held["unpool"],
    )


def solution(mesh):
    placed = (
        P("tile", "chan", None),
        P("tile", None),
        P(),
        P(),
        P(None, "chan", None),
        P(None, "chan"),
        P(),
        P(),
        P(),
        P(),
        P(),
        P(),
        P(None, "chan"),
        P("chan", None),
        P("chan", None),
    )
    return jax.shard_map(
        per_device, mesh=mesh, in_specs=placed, out_specs=P("tile", "chan", None), check_vma=False
    )
```

```python
import jax
import jax.numpy as jnp
import ml_dtypes
import numpy as np
from jax import lax
from jax.experimental import pallas as pl
from jax.experimental.pallas import tpu as pltpu
from jax.sharding import PartitionSpec as P

TILE = 48
HALF = TILE // 2
GRID_Y = 4
GROUPS = 6
ROWS = 48
FINE_IN = 8 * TILE
FINE_PAD = 8 * 64
BANDS = ((-1, -1), (-1, 0), (-1, 1), (0, -1), (0, 1), (1, -1), (1, 0), (1, 1))
norm_eps = 1e-06
BF = jnp.bfloat16
F32 = jnp.float32


def one_hot(shape, pairs):
    table = np.zeros(shape, np.float32)
    for source, target in pairs:
        table[source, target] = 1.0
    return table.astype(ml_dtypes.bfloat16)


def side_target(side, row, col, width, stride):
    if side == 0:
        return row * stride + 3 + col
    if side == -1:
        return row * stride + col - (width - 3) if col >= width - 3 else None
    return row * stride + 3 + width + col if col < 3 else None


def halo_pairs(cells, width, stride, first_row, flipped):
    block = max(lane for lane, _ in cells) // 128 * 128 + 128
    pairs = []
    for place, side in enumerate((-1, 0, 1)):
        for lane, index in cells:
            row, col = index // width, index % width
            if flipped:
                row, col = 2 - row, width - 1 - col
            target = side_target(side, row + first_row, col, width, stride)
            if target is not None:
                pairs.append((place * block + lane, target))
    return pairs


def fine_tables():
    first = [(t, t) for t in range(128)] + [(128 + t, 128 + t) for t in range(16)]
    last = [(t, 16 + t) for t in range(128)] + [(128 + t, t) for t in range(16)]
    halo = np.stack(
        [
            one_hot((768, 256), halo_pairs(last, TILE, 64, 1, False)),
            one_hot((768, 256), halo_pairs(first, TILE, 64, 0, False)),
            one_hot((768, 256), halo_pairs(last, TILE, 64, 0, True)),
        ]
    )
    pack, expand, compact, pool = [], [], [], []
    for row in range(8):
        for j in range(3):
            pack.append((row * 48 + j, row * 3 + j))
            pack.append((row * 48 + 45 + j, 128 + row * 3 + j))
            expand.append((384 + row * 3 + j, row * 64 + j))
            expand.append((384 + 24 + row * 3 + j, row * 64 + 51 + j))
        for col in range(48):
            expand.append((row * 48 + col, row * 64 + 3 + col))
            compact.append((row * 64 + 3 + col, row * 48 + col))
            pool.append((row * 48 + col, (row // 2) * 32 + 3 + col // 2))
    return {
        "halo": halo,
        "pack": one_hot((384, 256), pack),
        "expand": one_hot((512, 512), expand),
        "compact": one_hot((512, 384), compact),
        "pool": one_hot((384, 128), pool),
        "unpool": np.ascontiguousarray(one_hot((384, 128), pool).T),
    }


def coarse_tables():
    strip = [(t, t) for t in range(72)]
    halo = np.stack(
        [
            one_hot((384, 128), halo_pairs(strip, HALF, 32, 1, False)),
            one_hot((384, 128), halo_pairs(strip, HALF, 32, 0, False)),
            one_hot((384, 128), halo_pairs(strip, HALF, 32, 0, True)),
        ]
    )
    pack, sides = [], []
    for row in range(3):
        for col in range(HALF):
            pack.append((row * 32 + 3 + col, row * 24 + col))
            pack.append(((21 + row) * 32 + 3 + col, 128 + row * 24 + col))
    for row in range(HALF):
        for j in range(3):
            index = row * 3 + j
            lane = 72 + index if row < 16 else index - 48
            pack.append((row * 32 + 3 + j, lane if row < 16 else 256 + lane))
            pack.append((row * 32 + 24 + j, 128 + lane if row < 16 else 256 + 64 + lane))
            sides.append((lane, row * 32 + j))
            sides.append((128 + lane, row * 32 + 27 + j))
    return {
        "halo": halo,
        "pack": one_hot((768, 384), pack),
        "sides": one_hot((256, 768), sides),
    }


FINE = fine_tables()
COARSE = coarse_tables()


def dot(left, right):
    return jnp.dot(left, right, preferred_element_type=F32)


def stacked(value, width):
    return jnp.concatenate([value[:, i * width : (i + 1) * width] for i in range(GROUPS)], axis=0)


def lane_ids(shape):
    return lax.broadcasted_iota(jnp.int32, shape, 1)


def columns(row):
    high = row.astype(BF)
    rest = row - high.astype(F32)
    middle = rest.astype(BF)
    low = (rest - middle.astype(F32)).astype(BF)
    n = row.shape[1]
    terms = jnp.concatenate([high, middle, low, jnp.zeros((13, n), BF)], axis=0)
    return lax.dot_general(terms, jnp.ones((16, 128), BF), (((0,), (0,)), ((), ())), preferred_element_type=F32)


def wide(block, lanes):
    return jnp.concatenate([block] * (lanes // 128), axis=1)


def scan_tiles(count, step, carry):
    if count <= 16:
        for k in range(count):
            carry = step(k, carry)
        return carry
    return lax.fori_loop(0, count, step, carry)


def strip_table(pack_ref):
    shape = (FINE_IN, 256)
    source = lax.broadcasted_iota(jnp.int32, shape, 0)
    lane = lane_ids(shape)
    within = lane % 128
    wanted = (within // 3) * TILE + within % 3 + jnp.where(lane >= 128, TILE - 3, 0)
    pack_ref[...] = jnp.where((within < 24) & (source == wanted), 1.0, 0.0).astype(BF)


def make_prep(grid_x):
    def prep(slots_ref, dev_ref, x_ref, pack_ref, msg_ref, tab_ref, rows_ref, cols_ref, row_rest_ref, col_rest_ref):
        count = slots_ref.shape[0]
        me = lax.axis_index("tile")
        my_slot = scan_tiles(count, lambda k, c: c + jnp.where(dev_ref[k] == me, slots_ref[k], 0), jnp.int32(0))
        my_x = lax.rem(my_slot, grid_x)
        my_y = lax.div(my_slot, grid_x)
        wanted = []
        for up_by, right_by in BANDS:
            near_x = lax.rem(my_x + (right_by + grid_x), grid_x)
            near_y = my_y + up_by
            folded = near_y >= GRID_Y
            from_x = jnp.where(folded, grid_x - 1 - near_x, near_x)
            from_y = jnp.where(folded, GRID_Y - 1, near_y)
            wanted.append(from_y * grid_x + from_x)

        def find(k, found):
            slot, dev = slots_ref[k], dev_ref[k]
            row_pick = jnp.where(lax.div(slot, grid_x) + 1 == my_y, 0, 1)
            col_pick = jnp.where(lax.rem(slot, grid_x) == lax.rem(my_x + (grid_x - 1), grid_x), 0, 1)
            tab_ref[16 + dev] = 2 * row_pick + col_pick
            return tuple(jnp.where(slot == want, dev, old) for want, old in zip(wanted, found))

        found = scan_tiles(count, find, tuple(jnp.int32(-1) for _ in BANDS))
        for band in range(8):
            tab_ref[band] = found[band]
        tab_ref[8] = jnp.where(my_y == GRID_Y - 1, 2, 1)
        for spare in range(9, 16):
            tab_ref[spare] = 0

        x = x_ref[0]
        cols = dot(stacked(x, FINE_IN), pack_ref[...])
        lane = lane_ids((ROWS, 128))
        for side in range(2):
            part = cols[:, side * 128 : side * 128 + 128]
            main = part[0:ROWS]
            for i in range(1, 5):
                main = main + pltpu.roll(part[i * ROWS : (i + 1) * ROWS], 24 * i, 1)
            cols_ref[side] = main.astype(BF)
            rest = pltpu.roll(part[5 * ROWS : 6 * ROWS], 16, 1)
            col_rest_ref[side] = rest[0:16] + pltpu.roll(rest[16:32], 40, 1) + pltpu.roll(rest[32:48], 80, 1)
        rows_ref[0] = x[:, 0:128]
        rows_ref[1] = x[:, 2176:2304]
        ends = (x[:, 128:256].astype(F32), pltpu.roll(x[:, 2048:2176].astype(F32), 16, 1))
        for side in range(2):
            rest = jnp.where(lane < 16, ends[side], 0.0)
            row_rest_ref[side] = rest[0:16] + pltpu.roll(rest[16:32], 40, 1) + pltpu.roll(rest[32:48], 80, 1)

        def fill(dev, carry):
            row_pick = lax.div(tab_ref[16 + dev], 2)
            col_pick = lax.rem(tab_ref[16 + dev], 2)
            for g in range(3):
                msg_ref[dev, :, 256 * g : 256 * g + 128] = rows_ref[row_pick, 16 * g : 16 * g + 16, :]
                msg_ref[dev, :, 256 * g + 128 : 256 * g + 256] = cols_ref[col_pick, 16 * g : 16 * g + 16, :]
            msg_ref[dev, :, 768:896] = (row_rest_ref[row_pick] + col_rest_ref[col_pick]).astype(BF)
            return carry

        scan_tiles(count, fill, jnp.int32(0))

    return prep


def band_source(tab_ref, band):
    source = tab_ref[band]
    return jnp.maximum(source, 0), jnp.where(source >= 0, 1.0, 0.0).astype(F32)


def lane_shifted(value, lanes):
    return pltpu.roll(value, value.shape[1] - lanes, 1)


def conv_fine(tab_ref, x_ref, recv_ref, halo_ref, expand_ref, compact_ref, weight_ref, bias_ref, out_ref, pad_ref, odd_ref, wide_ref, sum_ref):
    for tap in range(49):
        wide_ref[tap] = jnp.broadcast_to(weight_ref[0][:, tap : tap + 1], (ROWS, 128))
    lane = lane_ids((ROWS, 128))

    def rest_of(source, scale):
        rest = recv_ref[source, :, 768:896].astype(F32) * scale
        return jnp.concatenate([rest, pltpu.roll(rest, 128 - 40, 1), pltpu.roll(rest, 128 - 80, 1)], axis=0)

    def main_of(source, scale, offset):
        parts = [recv_ref[source, :, 256 * g + offset : 256 * g + offset + 128] for g in range(3)]
        return jnp.concatenate(parts, axis=0).astype(F32) * scale

    def row_strips(bands):
        pieces = []
        for band in bands:
            source, scale = band_source(tab_ref, band)
            pieces += [main_of(source, scale, 0).astype(BF), rest_of(source, scale).astype(BF)]
        return jnp.concatenate(pieces, axis=1)

    pad_ref[:, 0:256] = dot(row_strips((0, 1, 2)), halo_ref[0])
    pad_ref[:, 3328:3584] = dot(row_strips((5, 6, 7)), halo_ref[tab_ref[8]])
    sides = []
    for band in (3, 4):
        source, scale = band_source(tab_ref, band)
        main, rest = main_of(source, scale, 128), rest_of(source, scale)
        sides.append([pltpu.roll(main, (128 - 24 * i) % 128, 1) if i else main for i in range(5)] + [pltpu.roll(rest, 128 - 16, 1)])
    halos = []
    for i in range(GROUPS):
        both = jnp.where(lane < 24, sides[0][i], pltpu.roll(sides[1][i], 24, 1))
        halos.append(jnp.where(lane < 48, both, 0.0))
    x = x_ref[0]
    joined = jnp.concatenate([stacked(x, FINE_IN), jnp.concatenate(halos, axis=0).astype(BF)], axis=1)
    padded = dot(joined, expand_ref[...])
    for i in range(GROUPS):
        pad_ref[:, 256 + 512 * i : 768 + 512 * i] = padded[i * ROWS : (i + 1) * ROWS]
    odd_ref[...] = lane_shifted(pad_ref[...], 64)
    bias = columns(bias_ref[0:1, :])
    sum_ref[...] = wide(bias, 3072)

    def group(g, carry):
        rows = pl.ds(pl.multiple_of(g * 8, 8), 8)
        for chunk in range(6):
            base = chunk * 512
            taken = []
            for a in range(1, 8):
                ref = odd_ref if a % 2 else pad_ref
                start = base + (a // 2) * 128
                taken.append([ref[rows, start + 128 * j : start + 128 * j + 128] for j in range(4)])
            total = [sum_ref[rows, base + 128 * j : base + 128 * j + 128] for j in range(4)]
            for b in range(7):
                weights = [wide_ref[a * 7 + b, rows, :] for a in range(7)]
                for j in range(4):
                    partial = weights[0] * taken[0][j]
                    for a in range(1, 7):
                        partial = partial + weights[a] * taken[a][j]
                    total[j] = total[j] + (pltpu.roll(partial, (3 - b) % 128, 1) if b != 3 else partial)
            for j in range(4):
                sum_ref[rows, base + 128 * j : base + 128 * j + 128] = total[j]
        return carry

    lax.fori_loop(0, 6, group, 0)
    dense = dot(stacked(sum_ref[...].astype(BF), FINE_PAD), compact_ref[...]).astype(BF)
    for i in range(GROUPS):
        out_ref[:, i * FINE_IN : (i + 1) * FINE_IN] = dense[i * ROWS : (i + 1) * ROWS]


def conv_coarse(tab_ref, x_ref, recv_ref, halo_ref, sides_ref, weight_ref, bias_ref, out_ref, pad_ref, wide_ref, sum_ref):
    for tap in range(49):
        wide_ref[tap] = jnp.broadcast_to(weight_ref[1][:, tap : tap + 1], (ROWS, 128))
    lane = lane_ids((ROWS, 128))

    def main_of(source, scale):
        parts = [recv_ref[source, :, 128 * g : 128 * g + 128] for g in range(3)]
        return jnp.concatenate(parts, axis=0).astype(F32) * scale

    def row_strips(bands):
        pieces = []
        for band in bands:
            source, scale = band_source(tab_ref, band)
            pieces.append(main_of(source, scale).astype(BF))
        return jnp.concatenate(pieces, axis=1)

    pad_ref[0, :, 0:128] = dot(row_strips((0, 1, 2)), halo_ref[0])
    pad_ref[0, :, 896:1024] = dot(row_strips((5, 6, 7)), halo_ref[tab_ref[8]])
    pieces = []
    for band in (3, 4):
        source, scale = band_source(tab_ref, band)
        rest = recv_ref[source, :, 384:512].astype(F32) * scale
        rest = jnp.concatenate([rest, pltpu.roll(rest, 128 - 24, 1), pltpu.roll(rest, 128 - 48, 1)], axis=0)
        main = main_of(source, scale)
        pieces.append(jnp.where(lane < 24, rest, main).astype(BF))
    pad_ref[0, :, 128:896] = dot(jnp.concatenate(pieces, axis=1), sides_ref[...]) + x_ref[...].astype(F32)
    padded = pad_ref[0]
    for turn in range(1, 4):
        pad_ref[turn] = lane_shifted(padded, 32 * turn)
    bias = columns(bias_ref[1:2, :])
    sum_ref[...] = wide(bias, 768)

    def group(g, carry):
        rows = pl.ds(pl.multiple_of(g * 8, 8), 8)
        for chunk in range(2):
            base = chunk * 384
            taken = []
            for a in range(1, 8):
                start = base + (a // 4) * 128
                taken.append([pad_ref[a % 4, rows, start + 128 * j : start + 128 * j + 128] for j in range(3)])
            total = [sum_ref[rows, base + 128 * j : base + 128 * j + 128] for j in range(3)]
            for b in range(7):
                weights = [wide_ref[a * 7 + b, rows, :] for a in range(7)]
                for j in range(3):
                    partial = weights[0] * taken[0][j]
                    for a in range(1, 7):
                        partial = partial + weights[a] * taken[a][j]
                    total[j] = total[j] + (pltpu.roll(partial, (3 - b) % 128, 1) if b != 3 else partial)
            for j in range(3):
                sum_ref[rows, base + 128 * j : base + 128 * j + 128] = total[j]
        return carry

    lax.fori_loop(0, 6, group, 0)
    out_ref[...] = sum_ref[...].astype(BF)


def gather_rows(pieces, cat_ref):
    me = lax.axis_index("chan")
    for k, piece in enumerate(pieces):
        first = pl.multiple_of(lax.bitwise_xor(me, k) * ROWS, 16)
        cat_ref[pl.ds(first, ROWS), :] = piece[...]


def make_branch(level, cat_ref, gain_ref, shift_ref, up_ref, up_bias_ref, down_ref, down_bias_ref, block):
    me = lax.axis_index("chan")
    row = slice(level, level + 1)
    gain = wide(columns(gain_ref[row, :]), block)
    shift = wide(columns(shift_ref[row, :]), block)
    up_bias = columns(up_bias_ref[row, :])
    down_bias = columns(down_bias_ref[row, :])
    first = pl.multiple_of(me * ROWS, 16)
    bias_rows = jnp.zeros((ROWS, 128), F32)
    for k in range(down_bias.shape[0] // ROWS):
        bias_rows = jnp.where(me == k, down_bias[k * ROWS : (k + 1) * ROWS], bias_rows)
    bias_rows = wide(bias_rows, block)
    hidden_rows = up_ref.shape[1]

    def branch(start):
        values = cat_ref[:, pl.ds(start, block)].astype(F32)
        mean = jnp.mean(values, axis=0, keepdims=True)
        centred = values - mean
        spread = jnp.mean(centred * centred, axis=0, keepdims=True)
        normed = (centred * lax.rsqrt(spread + norm_eps) * gain + shift).astype(BF)
        out = bias_rows
        for part in range(0, hidden_rows, 256):
            hidden = dot(up_ref[level, part : part + 256, :], normed) + wide(up_bias[part : part + 256], block)
            hidden = 0.5 * hidden * (1.0 + lax.erf(hidden * np.float32(0.5**0.5)))
            out = out + dot(down_ref[level, pl.ds(first, ROWS), part : part + 256], hidden.astype(BF))
        return out

    return branch


def cell_weights(weight_ref):
    lane = lane_ids((ROWS, FINE_IN))
    odd_row = (lane // TILE) % 2
    odd_col = (lane % TILE) % 2
    kind = 2 * odd_row + odd_col
    result = jnp.zeros((ROWS, FINE_IN), F32)
    for k in range(4):
        result = jnp.where(kind == k, weight_ref[:, k : k + 1], result)
    return result


def make_mix_fine(count):
    def mix_fine(
        tab_ref, own_ref, p1_ref, p2_ref, p3_ref, x_ref, mask_ref, gain_ref, shift_ref, up_ref, up_bias_ref,
        down_ref, down_bias_ref, scale_ref, pool_weight_ref, pool_ref, pack_ref,
        fine_ref, pooled_ref, small_mask_ref, msg_ref, cat_ref, mains_ref, rest_ref,
    ):
        gather_rows((own_ref, p1_ref, p2_ref, p3_ref), cat_ref)
        block = 256
        branch = make_branch(0, cat_ref, gain_ref, shift_ref, up_ref, up_bias_ref, down_ref, down_bias_ref, block)
        scale = wide(columns(scale_ref[0:1, :]), block)

        def one(step, carry):
            start = pl.multiple_of(step * block, block)
            here = pl.ds(start, block)
            value = x_ref[0, :, here].astype(F32) + scale * branch(start)
            fine_ref[:, here] = (mask_ref[:, here].astype(F32) * value).astype(BF)
            return carry

        lax.fori_loop(0, TILE * TILE // block, one, 0, unroll=3)

        weights = cell_weights(pool_weight_ref)
        highs, lows, masks = [], [], []
        for i in range(GROUPS):
            lanes = slice(i * FINE_IN, (i + 1) * FINE_IN)
            product = fine_ref[:, lanes].astype(F32) * weights
            high = product.astype(BF)
            highs.append(high)
            lows.append((product - high.astype(F32)).astype(BF))
            masks.append(jnp.broadcast_to(mask_ref[:, lanes].astype(F32), (8, FINE_IN)))
        pool_table = pool_ref[...]
        pooled = dot(jnp.concatenate(highs, axis=0), pool_table) + dot(jnp.concatenate(lows, axis=0), pool_table)
        pooled = pooled.astype(BF)
        for i in range(GROUPS):
            pooled_ref[:, i * 128 : (i + 1) * 128] = pooled[i * ROWS : (i + 1) * ROWS]
        counts = dot(jnp.concatenate(masks, axis=0).astype(BF), pool_table)
        small_mask_ref[...] = jnp.where(counts > 0.5, 1.0, 0.0)

        packed = dot(pooled_ref[...], pack_ref[...])
        lane = lane_ids((ROWS, 128))
        blocks = (packed[:, 0:128], packed[:, 128:256])
        for r in range(2):
            for c in range(2):
                mains_ref[2 * r + c] = jnp.where(lane < 72, blocks[r], blocks[c]).astype(BF)
        lane = lane_ids((16, 128))
        for c in range(2):
            rest = packed[:, 256:384]
            rest = pltpu.roll(rest, 64, 1) if c else rest
            parts = [rest[0:16], pltpu.roll(rest[16:32], 24, 1), pltpu.roll(rest[32:48], 48, 1)]
            joined = jnp.where(lane < 24, parts[0], jnp.where(lane < 48, parts[1], parts[2]))
            rest_ref[c] = jnp.where(lane < 72, joined, 0.0).astype(BF)

        def fill(dev, carry):
            both = tab_ref[16 + dev]
            col_pick = lax.rem(both, 2)
            for g in range(3):
                msg_ref[dev, :, 128 * g : 128 * g + 128] = mains_ref[both, 16 * g : 16 * g + 16, :]
            msg_ref[dev, :, 384:512] = rest_ref[col_pick]
            return carry

        scan_tiles(count, fill, jnp.int32(0))

    return mix_fine


def mix_coarse(
    own_ref, p1_ref, p2_ref, p3_ref, pooled_ref, small_mask_ref, fine_ref, mask_ref, gain_ref, shift_ref, up_ref, up_bias_ref,
    down_ref, down_bias_ref, scale_ref, spread_weight_ref, unpool_ref, out_ref, cat_ref,
):
    gather_rows((own_ref, p1_ref, p2_ref, p3_ref), cat_ref)
    block = 256
    branch = make_branch(1, cat_ref, gain_ref, shift_ref, up_ref, up_bias_ref, down_ref, down_bias_ref, block)
    scale = wide(columns(scale_ref[1:2, :]), block)
    parts = []
    for step in range(768 // block):
        value = pooled_ref[:, step * block : (step + 1) * block].astype(F32) + scale * branch(step * block)
        for half in range(2):
            i = 2 * step + half
            cells = small_mask_ref[8 * i : 8 * i + 1, :] * value[:, half * 128 : half * 128 + 128]
            parts.append(cells.astype(BF))
    spread = dot(jnp.concatenate(parts, axis=0), unpool_ref[...])
    weights = cell_weights(spread_weight_ref)
    for i in range(GROUPS):
        lanes = slice(i * FINE_IN, (i + 1) * FINE_IN)
        value = fine_ref[:, lanes].astype(F32) + weights * spread[i * ROWS : (i + 1) * ROWS]
        out_ref[0, :, lanes] = (mask_ref[:, lanes].astype(F32) * value).astype(BF)


VMEM = pl.BlockSpec(memory_space=pltpu.VMEM)
SMEM = pl.BlockSpec(memory_space=pltpu.SMEM)

def takes(microseconds):
    return pl.CostEstimate(flops=microseconds * 1_000_000_000, bytes_accessed=0, transcendentals=0)


def shaped(*shape, dtype=BF):
    return jax.ShapeDtypeStruct(shape, dtype)


PARAMS = pltpu.CompilerParams(vmem_limit_bytes=24 * 1024 * 1024)


def every_channel(own):
    pairs = lambda bit: [(i, i ^ bit) for i in range(4)]
    across = lax.ppermute(own, "chan", pairs(2))
    beside = lax.ppermute(own, "chan", pairs(1))
    diagonal = lax.ppermute(across, "chan", pairs(1))
    return own, beside, across, diagonal


def per_device(
    features, land_mask, wet_slots, device_of, depth_weight, depth_bias, norm_gain, norm_bias, up_weight, up_bias,
    down_weight, down_bias, layer_scale, pool_weight, spread_weight,
):
    count = wet_slots.shape[0]
    grid_x = 2 * count // GRID_Y
    cells = TILE * TILE
    pack = pl.pallas_call(
        strip_table, out_specs=VMEM, out_shape=shaped(FINE_IN, 256), compiler_params=PARAMS, cost_estimate=takes(2), name="strip_table"
    )()
    messages, table = pl.pallas_call(
        make_prep(grid_x),
        in_specs=[SMEM, SMEM, VMEM, VMEM],
        out_specs=[VMEM, SMEM],
        out_shape=[shaped(count, 16, 896), shaped(16 + count, dtype=jnp.int32)],
        scratch_shapes=[
            pltpu.VMEM((2, ROWS, 128), BF),
            pltpu.VMEM((2, ROWS, 128), BF),
            pltpu.VMEM((2, 16, 128), F32),
            pltpu.VMEM((2, 16, 128), F32),
        ],
        compiler_params=PARAMS,
        cost_estimate=takes(10),
        name="prep",
    )(wet_slots, device_of, features, pack)
    held = {
        "x": features,
        "mask": land_mask,
        "weight": depth_weight,
        "bias": depth_bias,
        "halo": jnp.asarray(FINE["halo"]),
        "expand": jnp.asarray(FINE["expand"]),
        "compact": jnp.asarray(FINE["compact"]),
        "small_halo": jnp.asarray(COARSE["halo"]),
        "sides": jnp.asarray(COARSE["sides"]),
        "pool": jnp.asarray(FINE["pool"]),
        "unpool": jnp.asarray(FINE["unpool"]),
        "small_pack": jnp.asarray(COARSE["pack"]),
    }
    arrived = lax.all_to_all(messages, "tile", 0, 0, tiled=True)
    conv = pl.pallas_call(
        conv_fine,
        in_specs=[SMEM] + [VMEM] * 7,
        out_specs=VMEM,
        out_shape=shaped(ROWS, cells),
        scratch_shapes=[
            pltpu.VMEM((ROWS, 3584), F32),
            pltpu.VMEM((ROWS, 3584), F32),
            pltpu.VMEM((49, ROWS, 128), F32),
            pltpu.VMEM((ROWS, 3072), F32),
        ],
        compiler_params=PARAMS,
        cost_estimate=takes(4),
        name="conv_fine",
    )(table, held["x"], arrived, held["halo"], held["expand"], held["compact"], held["weight"], held["bias"])
    fine, pooled, small_mask, messages = pl.pallas_call(
        make_mix_fine(count),
        in_specs=[SMEM] + [VMEM] * 16,
        out_specs=[VMEM] * 4,
        out_shape=[shaped(ROWS, cells), shaped(ROWS, 768), shaped(48, 128, dtype=F32), shaped(count, 16, 512)],
        scratch_shapes=[
            pltpu.VMEM((4 * ROWS, cells), BF),
            pltpu.VMEM((4, ROWS, 128), BF),
            pltpu.VMEM((2, 16, 128), BF),
        ],
        compiler_params=PARAMS,
        cost_estimate=takes(6),
        name="mix_fine",
    )(
        table, *every_channel(conv), held["x"], held["mask"], norm_gain, norm_bias, up_weight, up_bias,
        down_weight, down_bias, layer_scale, pool_weight, held["pool"], held["small_pack"],
    )
    arrived = lax.all_to_all(messages, "tile", 0, 0, tiled=True)
    conv = pl.pallas_call(
        conv_coarse,
        in_specs=[SMEM] + [VMEM] * 6,
        out_specs=VMEM,
        out_shape=shaped(ROWS, 768),
        scratch_shapes=[
            pltpu.VMEM((4, ROWS, 1024), F32),
            pltpu.VMEM((49, ROWS, 128), F32),
            pltpu.VMEM((ROWS, 768), F32),
        ],
        compiler_params=PARAMS,
        cost_estimate=takes(2),
        name="conv_coarse",
    )(table, pooled, arrived, held["small_halo"], held["sides"], held["weight"], held["bias"])
    return pl.pallas_call(
        mix_coarse,
        in_specs=[VMEM] * 17,
        out_specs=VMEM,
        out_shape=shaped(1, ROWS, cells),
        scratch_shapes=[pltpu.VMEM((4 * ROWS, 768), BF)],
        compiler_params=PARAMS,
        cost_estimate=takes(3),
        name="mix_coarse",
    )(
        *every_channel(conv), pooled, small_mask, fine, held["mask"], norm_gain, norm_bias, up_weight, up_bias,
        down_weight, down_bias, layer_scale, spread_weight, held["unpool"],
    )


def solution(mesh):
    placed = (
        P("tile", "chan", None),
        P("tile", None),
        P(),
        P(),
        P(None, "chan", None),
        P(None, "chan"),
        P(),
        P(),
        P(),
        P(),
        P(),
        P(),
        P(None, "chan"),
        P("chan", None),
        P("chan", None),
    )
    return jax.shard_map(
        per_device, mesh=mesh, in_specs=placed, out_specs=P("tile", "chan", None), check_vma=False
    )
```

```python
import jax
import jax.numpy as jnp
import ml_dtypes
import numpy as np
from jax import lax
from jax.experimental import pallas as pl
from jax.experimental.pallas import tpu as pltpu
from jax.sharding import PartitionSpec as P

TILE = 48
HALF = TILE // 2
GRID_Y = 4
GROUPS = 6
ROWS = 48
FINE_IN = 8 * TILE
FINE_PAD = 8 * 64
BANDS = ((-1, -1), (-1, 0), (-1, 1), (0, -1), (0, 1), (1, -1), (1, 0), (1, 1))
norm_eps = 1e-06
BF = jnp.bfloat16
F32 = jnp.float32


def one_hot(shape, pairs):
    table = np.zeros(shape, np.float32)
    for source, target in pairs:
        table[source, target] = 1.0
    return table.astype(ml_dtypes.bfloat16)


def side_target(side, row, col, width, stride):
    if side == 0:
        return row * stride + 3 + col
    if side == -1:
        return row * stride + col - (width - 3) if col >= width - 3 else None
    return row * stride + 3 + width + col if col < 3 else None


def halo_pairs(cells, width, stride, first_row, flipped):
    block = max(lane for lane, _ in cells) // 128 * 128 + 128
    pairs = []
    for place, side in enumerate((-1, 0, 1)):
        for lane, index in cells:
            row, col = index // width, index % width
            if flipped:
                row, col = 2 - row, width - 1 - col
            target = side_target(side, row + first_row, col, width, stride)
            if target is not None:
                pairs.append((place * block + lane, target))
    return pairs


def fine_tables():
    first = [(t, t) for t in range(128)] + [(128 + t, 128 + t) for t in range(16)]
    last = [(t, 16 + t) for t in range(128)] + [(128 + t, t) for t in range(16)]
    halo = np.stack(
        [
            one_hot((768, 256), halo_pairs(last, TILE, 64, 1, False)),
            one_hot((768, 256), halo_pairs(first, TILE, 64, 0, False)),
            one_hot((768, 256), halo_pairs(last, TILE, 64, 0, True)),
        ]
    )
    expand, compact, pool = [], [], []
    for row in range(8):
        for j in range(3):
            expand.append((384 + row * 3 + j, row * 64 + j))
            expand.append((384 + 24 + row * 3 + j, row * 64 + 51 + j))
        for col in range(48):
            expand.append((row * 48 + col, row * 64 + 3 + col))
            compact.append((row * 64 + 3 + col, row * 48 + col))
            pool.append((row * 48 + col, (row // 2) * 32 + 3 + col // 2))
    return {
        "halo": halo,
        "expand": one_hot((512, 512), expand),
        "compact": one_hot((512, 384), compact),
        "pool": one_hot((384, 128), pool),
    }


def coarse_tables():
    strip = [(t, t) for t in range(72)]
    halo = np.stack(
        [
            one_hot((384, 128), halo_pairs(strip, HALF, 32, 1, False)),
            one_hot((384, 128), halo_pairs(strip, HALF, 32, 0, False)),
            one_hot((384, 128), halo_pairs(strip, HALF, 32, 0, True)),
        ]
    )
    pack, sides = [], []
    for row in range(3):
        for col in range(HALF):
            pack.append((row * 32 + 3 + col, row * 24 + col))
            pack.append(((21 + row) * 32 + 3 + col, 128 + row * 24 + col))
    for row in range(HALF):
        for j in range(3):
            index = row * 3 + j
            lane = 72 + index if row < 16 else index - 48
            pack.append((row * 32 + 3 + j, lane if row < 16 else 256 + lane))
            pack.append((row * 32 + 24 + j, 128 + lane if row < 16 else 256 + 64 + lane))
            sides.append((lane, row * 32 + j))
            sides.append((128 + lane, row * 32 + 27 + j))
    return {
        "halo": halo,
        "pack": one_hot((768, 384), pack),
        "sides": one_hot((256, 768), sides),
    }


FINE = fine_tables()
COARSE = coarse_tables()


def dot(left, right):
    return jnp.dot(left, right, preferred_element_type=F32)


def stacked(value, width):
    return jnp.concatenate([value[:, i * width : (i + 1) * width] for i in range(GROUPS)], axis=0)


def lane_ids(shape):
    return lax.broadcasted_iota(jnp.int32, shape, 1)


def columns(row):
    high = row.astype(BF)
    rest = row - high.astype(F32)
    middle = rest.astype(BF)
    low = (rest - middle.astype(F32)).astype(BF)
    n = row.shape[1]
    terms = jnp.concatenate([high, middle, low, jnp.zeros((13, n), BF)], axis=0)
    return lax.dot_general(terms, jnp.ones((16, 128), BF), (((0,), (0,)), ((), ())), preferred_element_type=F32)


def wide(block, lanes):
    return jnp.concatenate([block] * (lanes // 128), axis=1)


def scan_tiles(count, step, carry):
    if count <= 16:
        for k in range(count):
            carry = step(k, carry)
        return carry
    return lax.fori_loop(0, count, step, carry)


def strip_table(pack_ref):
    shape = (FINE_IN, 256)
    source = lax.broadcasted_iota(jnp.int32, shape, 0)
    lane = lane_ids(shape)
    within = lane % 128
    wanted = (within // 3) * TILE + within % 3 + jnp.where(lane >= 128, TILE - 3, 0)
    pack_ref[...] = jnp.where((within < 24) & (source == wanted), 1.0, 0.0).astype(BF)


def make_prep(grid_x):
    def prep(slots_ref, dev_ref, x_ref, pack_ref, msg_ref, tab_ref, rows_ref, cols_ref, row_rest_ref, col_rest_ref):
        count = slots_ref.shape[0]
        me = lax.axis_index("tile")
        my_slot = scan_tiles(count, lambda k, c: c + jnp.where(dev_ref[k] == me, slots_ref[k], 0), jnp.int32(0))
        my_x = lax.rem(my_slot, grid_x)
        my_y = lax.div(my_slot, grid_x)
        wanted = []
        for up_by, right_by in BANDS:
            near_x = lax.rem(my_x + (right_by + grid_x), grid_x)
            near_y = my_y + up_by
            folded = near_y >= GRID_Y
            from_x = jnp.where(folded, grid_x - 1 - near_x, near_x)
            from_y = jnp.where(folded, GRID_Y - 1, near_y)
            wanted.append(from_y * grid_x + from_x)

        def find(k, found):
            slot, dev = slots_ref[k], dev_ref[k]
            row_pick = jnp.where(lax.div(slot, grid_x) + 1 == my_y, 0, 1)
            col_pick = jnp.where(lax.rem(slot, grid_x) == lax.rem(my_x + (grid_x - 1), grid_x), 0, 1)
            tab_ref[16 + dev] = 2 * row_pick + col_pick
            return tuple(jnp.where(slot == want, dev, old) for want, old in zip(wanted, found))

        found = scan_tiles(count, find, tuple(jnp.int32(-1) for _ in BANDS))
        for band in range(8):
            tab_ref[band] = found[band]
        tab_ref[8] = jnp.where(my_y == GRID_Y - 1, 2, 1)
        for spare in range(9, 16):
            tab_ref[spare] = 0

        x = x_ref[0]
        cols = dot(stacked(x, FINE_IN), pack_ref[...])
        lane = lane_ids((ROWS, 128))
        for side in range(2):
            part = cols[:, side * 128 : side * 128 + 128]
            main = part[0:ROWS]
            for i in range(1, 5):
                main = main + pltpu.roll(part[i * ROWS : (i + 1) * ROWS], 24 * i, 1)
            cols_ref[side] = main.astype(BF)
            rest = pltpu.roll(part[5 * ROWS : 6 * ROWS], 16, 1)
            col_rest_ref[side] = rest[0:16] + pltpu.roll(rest[16:32], 40, 1) + pltpu.roll(rest[32:48], 80, 1)
        rows_ref[0] = x[:, 0:128]
        rows_ref[1] = x[:, 2176:2304]
        ends = (x[:, 128:256].astype(F32), pltpu.roll(x[:, 2048:2176].astype(F32), 16, 1))
        for side in range(2):
            rest = jnp.where(lane < 16, ends[side], 0.0)
            row_rest_ref[side] = rest[0:16] + pltpu.roll(rest[16:32], 40, 1) + pltpu.roll(rest[32:48], 80, 1)

        def fill(dev, carry):
            row_pick = lax.div(tab_ref[16 + dev], 2)
            col_pick = lax.rem(tab_ref[16 + dev], 2)
            for g in range(3):
                msg_ref[dev, :, 256 * g : 256 * g + 128] = rows_ref[row_pick, 16 * g : 16 * g + 16, :]
                msg_ref[dev, :, 256 * g + 128 : 256 * g + 256] = cols_ref[col_pick, 16 * g : 16 * g + 16, :]
            msg_ref[dev, :, 768:896] = (row_rest_ref[row_pick] + col_rest_ref[col_pick]).astype(BF)
            return carry

        scan_tiles(count, fill, jnp.int32(0))

    return prep


def band_source(tab_ref, band):
    source = tab_ref[band]
    return jnp.maximum(source, 0), jnp.where(source >= 0, 1.0, 0.0).astype(F32)


def lane_shifted(value, lanes):
    return pltpu.roll(value, value.shape[1] - lanes, 1)


def make_conv_fine(first, rows):
    def conv_fine(tab_ref, x_ref, recv_ref, halo_ref, expand_ref, compact_ref, weight_ref, bias_ref, out_ref, pad_ref, odd_ref, wide_ref, sum_ref):
        for tap in range(49):
            wide_ref[tap] = jnp.broadcast_to(weight_ref[0, first : first + rows, tap : tap + 1], (rows, 128))
        lane = lane_ids((rows, 128))
        parts = range(first // 16, (first + rows) // 16)

        def rest_of(source, scale):
            rest = recv_ref[source, :, 768:896].astype(F32) * scale
            return jnp.concatenate([pltpu.roll(rest, 128 - 40 * g, 1) if g else rest for g in parts], axis=0)

        def main_of(source, scale, offset):
            pieces = [recv_ref[source, :, 256 * g + offset : 256 * g + offset + 128] for g in parts]
            return jnp.concatenate(pieces, axis=0).astype(F32) * scale

        def row_strips(bands):
            pieces = []
            for band in bands:
                source, scale = band_source(tab_ref, band)
                pieces += [main_of(source, scale, 0).astype(BF), rest_of(source, scale).astype(BF)]
            return jnp.concatenate(pieces, axis=1)

        pad_ref[:, 0:256] = dot(row_strips((0, 1, 2)), halo_ref[0])
        pad_ref[:, 3328:3584] = dot(row_strips((5, 6, 7)), halo_ref[tab_ref[8]])
        sides = []
        for band in (3, 4):
            source, scale = band_source(tab_ref, band)
            main, rest = main_of(source, scale, 128), rest_of(source, scale)
            turned = [pltpu.roll(main, 128 - 24 * i, 1) if i else main for i in range(5)]
            sides.append(turned + [pltpu.roll(rest, 128 - 16, 1)])
        halos = []
        for i in range(GROUPS):
            both = jnp.where(lane < 24, sides[0][i], pltpu.roll(sides[1][i], 24, 1))
            halos.append(jnp.where(lane < 48, both, 0.0))
        x = x_ref[0, first : first + rows, :]
        joined = jnp.concatenate([stacked(x, FINE_IN), jnp.concatenate(halos, axis=0).astype(BF)], axis=1)
        padded = dot(joined, expand_ref[...])
        for i in range(GROUPS):
            pad_ref[:, 256 + 512 * i : 768 + 512 * i] = padded[i * rows : (i + 1) * rows]
        odd_ref[...] = lane_shifted(pad_ref[...], 64)
        sum_ref[...] = wide(columns(bias_ref[0:1, :])[first : first + rows], 3072)

        def group(g, carry):
            here = pl.ds(pl.multiple_of(g * 8, 8), 8)
            for chunk in range(6):
                base = chunk * 512
                taken = []
                for a in range(1, 8):
                    ref = odd_ref if a % 2 else pad_ref
                    start = base + (a // 2) * 128
                    taken.append([ref[here, start + 128 * j : start + 128 * j + 128] for j in range(4)])
                total = [sum_ref[here, base + 128 * j : base + 128 * j + 128] for j in range(4)]
                for b in range(7):
                    weights = [wide_ref[a * 7 + b, here, :] for a in range(7)]
                    for j in range(4):
                        partial = weights[0] * taken[0][j]
                        for a in range(1, 7):
                            partial = partial + weights[a] * taken[a][j]
                        total[j] = total[j] + (pltpu.roll(partial, (3 - b) % 128, 1) if b != 3 else partial)
                for j in range(4):
                    sum_ref[here, base + 128 * j : base + 128 * j + 128] = total[j]
            return carry

        lax.fori_loop(0, rows // 8, group, 0)
        dense = dot(stacked(sum_ref[...].astype(BF), FINE_PAD), compact_ref[...]).astype(BF)
        for i in range(GROUPS):
            out_ref[:, i * FINE_IN : (i + 1) * FINE_IN] = dense[i * rows : (i + 1) * rows]

    return conv_fine


def params(
    after_ref, weight_ref, bias_ref, gain_ref, shift_ref, up_bias_ref, down_bias_ref, scale_ref, pool_weight_ref, spread_weight_ref,
    taps_ref, conv_bias_ref, gains_ref, shifts_ref, up_biases_ref, down_biases_ref, scales_ref, pool_cells_ref, spread_cells_ref,
):
    for tap in range(49):
        taps_ref[tap] = jnp.broadcast_to(weight_ref[1, :, tap : tap + 1], (ROWS, 128))
    conv_bias_ref[...] = columns(bias_ref[1:2, :])
    me = lax.axis_index("chan")
    for level in range(2):
        row = slice(level, level + 1)
        gains_ref[level] = columns(gain_ref[row, :])
        shifts_ref[level] = columns(shift_ref[row, :])
        up_biases_ref[level] = columns(up_bias_ref[row, :])
        scales_ref[level] = columns(scale_ref[row, :])
        down_bias = columns(down_bias_ref[row, :])
        own = down_bias[0:ROWS]
        for k in range(1, down_bias.shape[0] // ROWS):
            own = jnp.where(me == k, down_bias[k * ROWS : (k + 1) * ROWS], own)
        down_biases_ref[level] = own
    pool_cells_ref[...] = cell_weights(pool_weight_ref)
    spread_cells_ref[...] = cell_weights(spread_weight_ref)


def conv_coarse(tab_ref, x_ref, recv_ref, halo_ref, sides_ref, wide_ref, bias_ref, out_ref, pad_ref, sum_ref):
    lane = lane_ids((ROWS, 128))

    def main_of(source, scale):
        parts = [recv_ref[source, :, 128 * g : 128 * g + 128] for g in range(3)]
        return jnp.concatenate(parts, axis=0).astype(F32) * scale

    def row_strips(bands):
        pieces = []
        for band in bands:
            source, scale = band_source(tab_ref, band)
            pieces.append(main_of(source, scale).astype(BF))
        return jnp.concatenate(pieces, axis=1)

    pad_ref[0, :, 0:128] = dot(row_strips((0, 1, 2)), halo_ref[0])
    pad_ref[0, :, 896:1024] = dot(row_strips((5, 6, 7)), halo_ref[tab_ref[8]])
    pieces = []
    for band in (3, 4):
        source, scale = band_source(tab_ref, band)
        rest = recv_ref[source, :, 384:512].astype(F32) * scale
        rest = jnp.concatenate([rest, pltpu.roll(rest, 128 - 24, 1), pltpu.roll(rest, 128 - 48, 1)], axis=0)
        main = main_of(source, scale)
        pieces.append(jnp.where(lane < 24, rest, main).astype(BF))
    pad_ref[0, :, 128:896] = dot(jnp.concatenate(pieces, axis=1), sides_ref[...]) + x_ref[...].astype(F32)
    padded = pad_ref[0]
    for turn in range(1, 4):
        pad_ref[turn] = lane_shifted(padded, 32 * turn)
    sum_ref[...] = wide(bias_ref[...], 768)

    def group(g, carry):
        rows = pl.ds(pl.multiple_of(g * 8, 8), 8)
        for chunk in range(2):
            base = chunk * 384
            taken = []
            for a in range(1, 8):
                start = base + (a // 4) * 128
                taken.append([pad_ref[a % 4, rows, start + 128 * j : start + 128 * j + 128] for j in range(3)])
            total = [sum_ref[rows, base + 128 * j : base + 128 * j + 128] for j in range(3)]
            for b in range(7):
                weights = [wide_ref[a * 7 + b, rows, :] for a in range(7)]
                for j in range(3):
                    partial = weights[0] * taken[0][j]
                    for a in range(1, 7):
                        partial = partial + weights[a] * taken[a][j]
                    total[j] = total[j] + (pltpu.roll(partial, (3 - b) % 128, 1) if b != 3 else partial)
            for j in range(3):
                sum_ref[rows, base + 128 * j : base + 128 * j + 128] = total[j]
        return carry

    lax.fori_loop(0, 6, group, 0)
    out_ref[...] = sum_ref[...].astype(BF)


def gather_rows(pieces, cat_ref):
    me = lax.axis_index("chan")
    for k, parts in enumerate(pieces):
        first = pl.multiple_of(lax.bitwise_xor(me, k) * ROWS, 16)
        for part in parts:
            rows = part.shape[0]
            cat_ref[pl.ds(first, rows), :] = part[...]
            first = pl.multiple_of(first + rows, 16)


def make_branch(level, cat_ref, gain_ref, shift_ref, up_ref, up_bias_ref, down_ref, down_bias_ref, block):
    first = pl.multiple_of(lax.axis_index("chan") * ROWS, 16)
    gain, shift = wide(gain_ref[level], block), wide(shift_ref[level], block)

    def branch(start):
        values = cat_ref[:, pl.ds(start, block)].astype(F32)
        mean = jnp.mean(values, axis=0, keepdims=True)
        centred = values - mean
        spread = jnp.mean(centred * centred, axis=0, keepdims=True)
        normed = (centred * lax.rsqrt(spread + norm_eps) * gain + shift).astype(BF)
        hidden = dot(up_ref[level], normed) + wide(up_bias_ref[level], block)
        hidden = 0.5 * hidden * (1.0 + lax.erf(hidden * np.float32(0.5**0.5)))
        return dot(down_ref[level, pl.ds(first, ROWS), :], hidden.astype(BF)) + wide(down_bias_ref[level], block)

    return branch


def cell_weights(weight_ref):
    lane = lane_ids((ROWS, FINE_IN))
    odd_row = (lane // TILE) % 2
    odd_col = (lane % TILE) % 2
    kind = 2 * odd_row + odd_col
    result = jnp.zeros((ROWS, FINE_IN), F32)
    for k in range(4):
        result = jnp.where(kind == k, weight_ref[:, k : k + 1], result)
    return result


def make_mix_fine(count):
    def mix_fine(
        tab_ref, own_a_ref, own_b_ref, p1_a_ref, p1_b_ref, p2_a_ref, p2_b_ref, p3_a_ref, p3_b_ref, x_ref, mask_ref,
        gain_ref, shift_ref, up_ref, up_bias_ref, down_ref, down_bias_ref, scale_ref, pool_cells_ref, pool_ref, pack_ref,
        fine_ref, pooled_ref, small_mask_ref, msg_ref, cat_ref, mains_ref, rest_ref,
    ):
        gather_rows(((own_a_ref, own_b_ref), (p1_a_ref, p1_b_ref), (p2_a_ref, p2_b_ref), (p3_a_ref, p3_b_ref)), cat_ref)
        block = 768
        branch = make_branch(0, cat_ref, gain_ref, shift_ref, up_ref, up_bias_ref, down_ref, down_bias_ref, block)
        scale = wide(scale_ref[0], block)

        for start in range(0, TILE * TILE, block):
            here = slice(start, start + block)
            value = x_ref[0, :, here].astype(F32) + scale * branch(start)
            fine_ref[:, here] = (mask_ref[:, here].astype(F32) * value).astype(BF)

        weights = pool_cells_ref[...]
        highs, lows, masks = [], [], []
        for i in range(GROUPS):
            lanes = slice(i * FINE_IN, (i + 1) * FINE_IN)
            product = fine_ref[:, lanes].astype(F32) * weights
            high = product.astype(BF)
            highs.append(high)
            lows.append((product - high.astype(F32)).astype(BF))
            masks.append(jnp.broadcast_to(mask_ref[:, lanes].astype(F32), (8, FINE_IN)))
        pool_table = pool_ref[...]
        pooled = dot(jnp.concatenate(highs, axis=0), pool_table) + dot(jnp.concatenate(lows, axis=0), pool_table)
        pooled = pooled.astype(BF)
        for i in range(GROUPS):
            pooled_ref[:, i * 128 : (i + 1) * 128] = pooled[i * ROWS : (i + 1) * ROWS]
        counts = dot(jnp.concatenate(masks, axis=0).astype(BF), pool_table)
        small_mask_ref[...] = jnp.where(counts > 0.5, 1.0, 0.0)

        packed = dot(pooled_ref[...], pack_ref[...])
        lane = lane_ids((ROWS, 128))
        blocks = (packed[:, 0:128], packed[:, 128:256])
        for r in range(2):
            for c in range(2):
                mains_ref[2 * r + c] = jnp.where(lane < 72, blocks[r], blocks[c]).astype(BF)
        lane = lane_ids((16, 128))
        for c in range(2):
            rest = packed[:, 256:384]
            rest = pltpu.roll(rest, 64, 1) if c else rest
            parts = [rest[0:16], pltpu.roll(rest[16:32], 24, 1), pltpu.roll(rest[32:48], 48, 1)]
            joined = jnp.where(lane < 24, parts[0], jnp.where(lane < 48, parts[1], parts[2]))
            rest_ref[c] = jnp.where(lane < 72, joined, 0.0).astype(BF)

        def fill(dev, carry):
            both = tab_ref[16 + dev]
            col_pick = lax.rem(both, 2)
            for g in range(3):
                msg_ref[dev, :, 128 * g : 128 * g + 128] = mains_ref[both, 16 * g : 16 * g + 16, :]
            msg_ref[dev, :, 384:512] = rest_ref[col_pick]
            return carry

        scan_tiles(count, fill, jnp.int32(0))

    return mix_fine


def mix_coarse(
    own_ref, p1_ref, p2_ref, p3_ref, pooled_ref, small_mask_ref, fine_ref, mask_ref, gain_ref, shift_ref, up_ref, up_bias_ref,
    down_ref, down_bias_ref, scale_ref, spread_cells_ref, pool_ref, out_ref, cat_ref,
):
    gather_rows(((own_ref,), (p1_ref,), (p2_ref,), (p3_ref,)), cat_ref)
    cells = cat_ref.shape[1]
    branch = make_branch(1, cat_ref, gain_ref, shift_ref, up_ref, up_bias_ref, down_ref, down_bias_ref, cells)
    value = pooled_ref[...].astype(F32) + wide(scale_ref[1], cells) * branch(0)
    parts = []
    for i in range(GROUPS):
        parts.append((small_mask_ref[8 * i : 8 * i + 1, :] * value[:, 128 * i : 128 * i + 128]).astype(BF))
    spread = lax.dot_general(
        jnp.concatenate(parts, axis=0), pool_ref[...], (((1,), (1,)), ((), ())), preferred_element_type=F32
    )
    weights = spread_cells_ref[...]
    for i in range(GROUPS):
        lanes = slice(i * FINE_IN, (i + 1) * FINE_IN)
        merged = fine_ref[:, lanes].astype(F32) + weights * spread[i * ROWS : (i + 1) * ROWS]
        out_ref[0, :, lanes] = (mask_ref[:, lanes].astype(F32) * merged).astype(BF)


VMEM = pl.BlockSpec(memory_space=pltpu.VMEM)
SMEM = pl.BlockSpec(memory_space=pltpu.SMEM)

def takes(microseconds):
    return pl.CostEstimate(flops=microseconds * 1_000_000_000, bytes_accessed=0, transcendentals=0)


def shaped(*shape, dtype=BF):
    return jax.ShapeDtypeStruct(shape, dtype)


PARAMS = pltpu.CompilerParams(vmem_limit_bytes=24 * 1024 * 1024)


def every_channel(own):
    pairs = lambda bit: [(i, i ^ bit) for i in range(4)]
    across = lax.ppermute(own, "chan", pairs(2))
    beside = lax.ppermute(own, "chan", pairs(1))
    diagonal = lax.ppermute(across, "chan", pairs(1))
    return own, beside, across, diagonal


def per_device(
    features, land_mask, wet_slots, device_of, depth_weight, depth_bias, norm_gain, norm_bias, up_weight, up_bias,
    down_weight, down_bias, layer_scale, pool_weight, spread_weight,
):
    count = wet_slots.shape[0]
    grid_x = 2 * count // GRID_Y
    cells = TILE * TILE
    pack = pl.pallas_call(
        strip_table, out_specs=VMEM, out_shape=shaped(FINE_IN, 256), compiler_params=PARAMS, cost_estimate=takes(2), name="strip_table"
    )()
    messages, table = pl.pallas_call(
        make_prep(grid_x),
        in_specs=[SMEM, SMEM, VMEM, VMEM],
        out_specs=[VMEM, SMEM],
        out_shape=[shaped(count, 16, 896), shaped(16 + count, dtype=jnp.int32)],
        scratch_shapes=[
            pltpu.VMEM((2, ROWS, 128), BF),
            pltpu.VMEM((2, ROWS, 128), BF),
            pltpu.VMEM((2, 16, 128), F32),
            pltpu.VMEM((2, 16, 128), F32),
        ],
        compiler_params=PARAMS,
        cost_estimate=takes(10),
        name="prep",
    )(wet_slots, device_of, features, pack)
    held = {
        "x": features,
        "mask": land_mask,
        "weight": depth_weight,
        "bias": depth_bias,
        "halo": jnp.asarray(FINE["halo"]),
        "expand": jnp.asarray(FINE["expand"]),
        "compact": jnp.asarray(FINE["compact"]),
        "small_halo": jnp.asarray(COARSE["halo"]),
        "sides": jnp.asarray(COARSE["sides"]),
        "pool": jnp.asarray(FINE["pool"]),
        "small_pack": jnp.asarray(COARSE["pack"]),
    }
    arrived = lax.all_to_all(messages, "tile", 0, 0, tiled=True)
    convs = []
    for first, rows in ((0, 32), (32, 16)):
        own = pl.pallas_call(
            make_conv_fine(first, rows),
            in_specs=[SMEM] + [VMEM] * 7,
            out_specs=VMEM,
            out_shape=shaped(rows, cells),
            scratch_shapes=[
                pltpu.VMEM((rows, 3584), F32),
                pltpu.VMEM((rows, 3584), F32),
                pltpu.VMEM((49, rows, 128), F32),
                pltpu.VMEM((rows, 3072), F32),
            ],
            compiler_params=PARAMS,
            cost_estimate=takes(2),
            name=f"conv_fine_{first}",
        )(table, held["x"], arrived, held["halo"], held["expand"], held["compact"], held["weight"], held["bias"])
        convs.append(every_channel(own))
    taps, conv_bias, gains, shifts, up_biases, down_biases, scales, pool_cells, spread_cells = pl.pallas_call(
        params,
        in_specs=[VMEM] * 10,
        out_specs=[VMEM] * 9,
        out_shape=[
            shaped(*shape, dtype=F32)
            for shape in (
                (49, ROWS, 128), (ROWS, 128), (2, 192, 128), (2, 192, 128), (2, 768, 128), (2, ROWS, 128), (2, ROWS, 128),
                (ROWS, FINE_IN), (ROWS, FINE_IN),
            )
        ],
        compiler_params=PARAMS,
        cost_estimate=takes(2),
        name="params",
    )(
        convs[0][0], depth_weight, depth_bias, norm_gain, norm_bias, up_bias, down_bias, layer_scale, pool_weight, spread_weight
    )
    fine, pooled, small_mask, messages = pl.pallas_call(
        make_mix_fine(count),
        in_specs=[SMEM] + [VMEM] * 20,
        out_specs=[VMEM] * 4,
        out_shape=[shaped(ROWS, cells), shaped(ROWS, 768), shaped(48, 128, dtype=F32), shaped(count, 16, 512)],
        scratch_shapes=[
            pltpu.VMEM((4 * ROWS, cells), BF),
            pltpu.VMEM((4, ROWS, 128), BF),
            pltpu.VMEM((2, 16, 128), BF),
        ],
        compiler_params=PARAMS,
        cost_estimate=takes(4),
        name="mix_fine",
    )(
        table, *(part for pair in zip(*convs) for part in pair), held["x"], held["mask"], gains, shifts, up_weight, up_biases,
        down_weight, down_biases, scales, pool_cells, held["pool"], held["small_pack"],
    )
    arrived = lax.all_to_all(messages, "tile", 0, 0, tiled=True)
    conv = pl.pallas_call(
        conv_coarse,
        in_specs=[SMEM] + [VMEM] * 6,
        out_specs=VMEM,
        out_shape=shaped(ROWS, 768),
        scratch_shapes=[pltpu.VMEM((4, ROWS, 1024), F32), pltpu.VMEM((ROWS, 768), F32)],
        compiler_params=PARAMS,
        cost_estimate=takes(2),
        name="conv_coarse",
    )(table, pooled, arrived, held["small_halo"], held["sides"], taps, conv_bias)
    return pl.pallas_call(
        mix_coarse,
        in_specs=[VMEM] * 17,
        out_specs=VMEM,
        out_shape=shaped(1, ROWS, cells),
        scratch_shapes=[pltpu.VMEM((4 * ROWS, 768), BF)],
        compiler_params=PARAMS,
        cost_estimate=takes(2),
        name="mix_coarse",
    )(
        *every_channel(conv), pooled, small_mask, fine, held["mask"], gains, shifts, up_weight, up_biases, down_weight, down_biases,
        scales, spread_cells, held["pool"],
    )


def solution(mesh):
    placed = (
        P("tile", "chan", None),
        P("tile", None),
        P(),
        P(),
        P(None, "chan", None),
        P(None, "chan"),
        P(),
        P(),
        P(),
        P(),
        P(),
        P(),
        P(None, "chan"),
        P("chan", None),
        P("chan", None),
    )
    return jax.shard_map(
        per_device, mesh=mesh, in_specs=placed, out_specs=P("tile", "chan", None), check_vma=False
    )
```

```python
import jax
import jax.numpy as jnp
import ml_dtypes
import numpy as np
from jax import lax
from jax.experimental import pallas as pl
from jax.experimental.pallas import tpu as pltpu
from jax.sharding import PartitionSpec as P

TILE = 48
HALF = TILE // 2
GRID_Y = 4
GROUPS = 6
ROWS = 48
FINE_IN = 8 * TILE
FINE_PAD = 8 * 64
BANDS = ((-1, -1), (-1, 0), (-1, 1), (0, -1), (0, 1), (1, -1), (1, 0), (1, 1))
norm_eps = 1e-06
BF = jnp.bfloat16
F32 = jnp.float32


def one_hot(shape, pairs):
    table = np.zeros(shape, np.float32)
    for source, target in pairs:
        table[source, target] = 1.0
    return table.astype(ml_dtypes.bfloat16)


def side_target(side, row, col, width, stride):
    if side == 0:
        return row * stride + 3 + col
    if side == -1:
        return row * stride + col - (width - 3) if col >= width - 3 else None
    return row * stride + 3 + width + col if col < 3 else None


def halo_pairs(cells, width, stride, first_row, flipped):
    block = max(lane for lane, _ in cells) // 128 * 128 + 128
    pairs = []
    for place, side in enumerate((-1, 0, 1)):
        for lane, index in cells:
            row, col = index // width, index % width
            if flipped:
                row, col = 2 - row, width - 1 - col
            target = side_target(side, row + first_row, col, width, stride)
            if target is not None:
                pairs.append((place * block + lane, target))
    return pairs


def fine_tables():
    first = [(t, t) for t in range(128)] + [(128 + t, 128 + t) for t in range(16)]
    last = [(t, 16 + t) for t in range(128)] + [(128 + t, t) for t in range(16)]
    halo = np.stack(
        [
            one_hot((768, 256), halo_pairs(last, TILE, 64, 1, False)),
            one_hot((768, 256), halo_pairs(first, TILE, 64, 0, False)),
            one_hot((768, 256), halo_pairs(last, TILE, 64, 0, True)),
        ]
    )
    expand, compact, pool, spread, sides = [], [], [], [], []
    for row in range(8):
        for col in range(48):
            expand.append((row * 48 + col, row * 64 + 3 + col))
            compact.append((row * 64 + 3 + col, row * 48 + col))
            pool.append((row * 48 + col, (row // 2) * 32 + 3 + col // 2))
        for q in range(3):
            spread.append((8 * q + row, row * 64 + 3 + q))
            spread.append((64 + 8 * q + row, row * 64 + 3 + 47 - q))
    for row in range(TILE):
        for j in range(3):
            lane = 3 * row + j if row < 40 else 128 + 16 + 3 * (row - 40) + j
            sides.append((lane, 128 * j + row))
            sides.append((256 + lane, 128 * (2 - j) + 64 + row))
    return {
        "halo": halo,
        "expand": one_hot((384, 512), expand),
        "compact": one_hot((512, 384), compact),
        "pool": one_hot((384, 128), pool),
        "spread": one_hot((128, 512), spread),
        "sides": one_hot((512, 384), sides),
    }


def coarse_tables():
    strip = [(t, t) for t in range(72)]
    halo = np.stack(
        [
            one_hot((384, 128), halo_pairs(strip, HALF, 32, 1, False)),
            one_hot((384, 128), halo_pairs(strip, HALF, 32, 0, False)),
            one_hot((384, 128), halo_pairs(strip, HALF, 32, 0, True)),
        ]
    )
    pack, sides = [], []
    for row in range(3):
        for col in range(HALF):
            pack.append((row * 32 + 3 + col, row * 24 + col))
            pack.append(((21 + row) * 32 + 3 + col, 128 + row * 24 + col))
    for row in range(HALF):
        for j in range(3):
            index = row * 3 + j
            lane = 72 + index if row < 16 else index - 48
            pack.append((row * 32 + 3 + j, lane if row < 16 else 256 + lane))
            pack.append((row * 32 + 24 + j, 128 + lane if row < 16 else 256 + 64 + lane))
            sides.append((lane, row * 32 + j))
            sides.append((128 + lane, row * 32 + 27 + j))
    return {
        "halo": halo,
        "pack": one_hot((768, 384), pack),
        "sides": one_hot((256, 768), sides),
    }


FINE = fine_tables()
COARSE = coarse_tables()


def dot(left, right):
    return jnp.dot(left, right, preferred_element_type=F32)


def stacked(value, width):
    return jnp.concatenate([value[:, i * width : (i + 1) * width] for i in range(GROUPS)], axis=0)


def lane_ids(shape):
    return lax.broadcasted_iota(jnp.int32, shape, 1)


def columns(row):
    high = row.astype(BF)
    rest = row - high.astype(F32)
    middle = rest.astype(BF)
    low = (rest - middle.astype(F32)).astype(BF)
    n = row.shape[1]
    terms = jnp.concatenate([high, middle, low, jnp.zeros((13, n), BF)], axis=0)
    return lax.dot_general(terms, jnp.ones((16, 128), BF), (((0,), (0,)), ((), ())), preferred_element_type=F32)


def wide(block, lanes):
    return jnp.concatenate([block] * (lanes // 128), axis=1)


def scan_tiles(count, step, carry):
    if count <= 16:
        for k in range(count):
            carry = step(k, carry)
        return carry
    return lax.fori_loop(0, count, step, carry)


def strip_table(pack_ref):
    shape = (FINE_IN, 256)
    source = lax.broadcasted_iota(jnp.int32, shape, 0)
    lane = lane_ids(shape)
    within = lane % 128
    wanted = (within // 3) * TILE + within % 3 + jnp.where(lane >= 128, TILE - 3, 0)
    pack_ref[...] = jnp.where((within < 24) & (source == wanted), 1.0, 0.0).astype(BF)


def quotient(value, divisor):
    if divisor & (divisor - 1) == 0:
        return lax.shift_right_logical(value, jnp.int32(divisor.bit_length() - 1))
    return lax.div(value, divisor)


def remainder(value, divisor):
    if divisor & (divisor - 1) == 0:
        return lax.bitwise_and(value, jnp.int32(divisor - 1))
    return lax.rem(value, divisor)


def make_prep(grid_x):
    def prep(slots_ref, dev_ref, x_ref, pack_ref, msg_ref, tab_ref, rows_ref, cols_ref, row_rest_ref, col_rest_ref):
        count = slots_ref.shape[0]
        me = lax.axis_index("tile")
        my_slot = scan_tiles(count, lambda k, c: c + jnp.where(dev_ref[k] == me, slots_ref[k], 0), jnp.int32(0))
        my_x = remainder(my_slot, grid_x)
        my_y = quotient(my_slot, grid_x)
        wanted = []
        for up_by, right_by in BANDS:
            near_x = remainder(my_x + (right_by + grid_x), grid_x)
            near_y = my_y + up_by
            folded = near_y >= GRID_Y
            from_x = jnp.where(folded, grid_x - 1 - near_x, near_x)
            from_y = jnp.where(folded, GRID_Y - 1, near_y)
            wanted.append(from_y * grid_x + from_x)

        def find(k, found):
            slot, dev = slots_ref[k], dev_ref[k]
            row_pick = jnp.where(quotient(slot, grid_x) + 1 == my_y, 0, 1)
            col_pick = jnp.where(remainder(slot, grid_x) == remainder(my_x + (grid_x - 1), grid_x), 0, 1)
            tab_ref[16 + dev] = 2 * row_pick + col_pick
            return tuple(jnp.where(slot == want, dev, old) for want, old in zip(wanted, found))

        found = scan_tiles(count, find, tuple(jnp.int32(-1) for _ in BANDS))
        for band in range(8):
            tab_ref[band] = found[band]
        tab_ref[8] = jnp.where(my_y == GRID_Y - 1, 2, 1)
        for spare in range(9, 16):
            tab_ref[spare] = 0

        x = x_ref[0]
        cols = dot(stacked(x, FINE_IN), pack_ref[...])
        lane = lane_ids((ROWS, 128))
        for side in range(2):
            part = cols[:, side * 128 : side * 128 + 128]
            main = part[0:ROWS]
            for i in range(1, 5):
                main = main + pltpu.roll(part[i * ROWS : (i + 1) * ROWS], 24 * i, 1)
            cols_ref[side] = main.astype(BF)
            rest = pltpu.roll(part[5 * ROWS : 6 * ROWS], 16, 1)
            col_rest_ref[side] = rest[0:16] + pltpu.roll(rest[16:32], 40, 1) + pltpu.roll(rest[32:48], 80, 1)
        rows_ref[0] = x[:, 0:128]
        rows_ref[1] = x[:, 2176:2304]
        ends = (x[:, 128:256].astype(F32), pltpu.roll(x[:, 2048:2176].astype(F32), 16, 1))
        for side in range(2):
            rest = jnp.where(lane < 16, ends[side], 0.0)
            row_rest_ref[side] = rest[0:16] + pltpu.roll(rest[16:32], 40, 1) + pltpu.roll(rest[32:48], 80, 1)

        def fill(dev, carry):
            row_pick = quotient(tab_ref[16 + dev], 2)
            col_pick = remainder(tab_ref[16 + dev], 2)
            for g in range(3):
                msg_ref[dev, :, 256 * g : 256 * g + 128] = rows_ref[row_pick, 16 * g : 16 * g + 16, :]
                msg_ref[dev, :, 256 * g + 128 : 256 * g + 256] = cols_ref[col_pick, 16 * g : 16 * g + 16, :]
            msg_ref[dev, :, 768:896] = (row_rest_ref[row_pick] + col_rest_ref[col_pick]).astype(BF)
            return carry

        scan_tiles(count, fill, jnp.int32(0))

    return prep


def band_source(tab_ref, band):
    source = tab_ref[band]
    return jnp.maximum(source, 0), jnp.where(source >= 0, 1.0, 0.0).astype(F32)


def lane_shifted(value, lanes):
    return pltpu.roll(value, value.shape[1] - lanes, 1)


def conv_inner(x_ref, expand_ref, weight_ref, bias_ref, sum_ref, wide_ref, pad_ref, odd_ref):
    for tap in range(49):
        wide_ref[tap] = jnp.broadcast_to(weight_ref[0, :, tap : tap + 1], (ROWS, 128))
    pad_ref[:, 0:256] = jnp.zeros((ROWS, 256), F32)
    pad_ref[:, 3328:3584] = jnp.zeros((ROWS, 256), F32)
    padded = dot(stacked(x_ref[0], FINE_IN), expand_ref[...])
    for i in range(GROUPS):
        pad_ref[:, 256 + 512 * i : 768 + 512 * i] = padded[i * ROWS : (i + 1) * ROWS]
    odd_ref[...] = lane_shifted(pad_ref[...], 64)
    sum_ref[...] = wide(columns(bias_ref[0:1, :]), 3072)

    def group(g, carry):
        here = pl.ds(pl.multiple_of(g * 8, 8), 8)
        for chunk in range(6):
            base = chunk * 512
            taken = []
            for a in range(1, 8):
                ref = odd_ref if a % 2 else pad_ref
                start = base + (a // 2) * 128
                taken.append([ref[here, start + 128 * j : start + 128 * j + 128] for j in range(4)])
            total = [sum_ref[here, base + 128 * j : base + 128 * j + 128] for j in range(4)]
            for b in range(7):
                weights = [wide_ref[a * 7 + b, here, :] for a in range(7)]
                for j in range(4):
                    partial = weights[0] * taken[0][j]
                    for a in range(1, 7):
                        partial = partial + weights[a] * taken[a][j]
                    total[j] = total[j] + (pltpu.roll(partial, (3 - b) % 128, 1) if b != 3 else partial)
            for j in range(4):
                sum_ref[here, base + 128 * j : base + 128 * j + 128] = total[j]
        return carry

    lax.fori_loop(0, ROWS // 8, group, 0)


def conv_border(tab_ref, recv_ref, sum_ref, wide_ref, halo_ref, sides_ref, spread_ref, compact_ref, out_ref):
    lane = lane_ids((ROWS, 128))
    low_half = lane < 64

    def rest_of(source, scale):
        rest = recv_ref[source, :, 768:896].astype(F32) * scale
        return jnp.concatenate([rest, pltpu.roll(rest, 128 - 40, 1), pltpu.roll(rest, 128 - 80, 1)], axis=0)

    def strips(bands, offset):
        pieces = []
        for band in bands:
            source, scale = band_source(tab_ref, band)
            main = jnp.concatenate([recv_ref[source, :, 256 * g + offset : 256 * g + offset + 128] for g in range(3)], axis=0)
            pieces += [(main.astype(F32) * scale).astype(BF), rest_of(source, scale).astype(BF)]
        return jnp.concatenate(pieces, axis=1)

    def tap(a, b):
        return wide_ref[a * 7 + b]

    def row_fix(uses):
        total = [jnp.zeros((ROWS, 128), F32)] * 2
        for b in range(7):
            partial = [None, None]
            for place, a, cells in uses:
                term = tap(a, b) * cells
                partial[place] = term if partial[place] is None else partial[place] + term
            for place in range(2):
                total[place] = total[place] + (pltpu.roll(partial[place], (3 - b) % 128, 1) if b != 3 else partial[place])
        return total

    below = dot(strips((0, 1, 2), 0), halo_ref[0])
    above = dot(strips((5, 6, 7), 0), halo_ref[tab_ref[8]])
    turned = [pltpu.roll(below[:, 128 * k : 128 * k + 128], 64, 1) for k in range(2)]
    last = jnp.where(low_half, turned[1], 0.0)
    first_fix = row_fix(((0, 0, jnp.where(low_half, turned[0], turned[1])), (0, 1, below[:, 128:256]), (0, 2, last), (1, 0, last)))
    turned = [pltpu.roll(above[:, 128 * k : 128 * k + 128], 64, 1) for k in range(2)]
    first = jnp.where(low_half, 0.0, turned[0])
    last_fix = row_fix(((0, 6, first), (1, 4, first), (1, 5, above[:, 0:128]), (1, 6, jnp.where(low_half, turned[0], turned[1]))))

    beside = dot(strips((3, 4), 128), sides_ref[...])
    beside = [beside[:, 128 * j : 128 * j + 128] for j in range(3)]
    column_fix = [jnp.zeros((ROWS, 128), F32)] * 3
    for a in range(7):
        weights = [jnp.where(low_half, tap(a, b), tap(a, 6 - b)) for b in range(3)]
        for q in range(3):
            partial = weights[0] * beside[q]
            for j in range(q + 1, 3):
                partial = partial + weights[j - q] * beside[j]
            column_fix[q] = column_fix[q] + (pltpu.roll(partial, (3 - a) % 128, 1) if a != 3 else partial)
    within = lane % 64
    highs, lows = [], []
    for i in range(GROUPS):
        parts = [pltpu.roll(column_fix[q], (8 * q - 8 * i) % 128, 1) if q != i else column_fix[q] for q in range(3)]
        value = jnp.where(within < 8, parts[0], jnp.where(within < 16, parts[1], jnp.where(within < 24, parts[2], 0.0)))
        high = value.astype(BF)
        highs.append(high)
        lows.append((value - high.astype(F32)).astype(BF))
    table = spread_ref[...]
    fixes = dot(jnp.concatenate(highs, axis=0), table) + dot(jnp.concatenate(lows, axis=0), table)
    sums = []
    for i in range(GROUPS):
        value = sum_ref[:, 512 * i : 512 * i + 512] + fixes[i * ROWS : (i + 1) * ROWS]
        if i == 0:
            value = jnp.concatenate([value[:, 0:128] + first_fix[0], value[:, 128:256] + first_fix[1], value[:, 256:512]], axis=1)
        if i == GROUPS - 1:
            value = jnp.concatenate([value[:, 0:256], value[:, 256:384] + last_fix[0], value[:, 384:512] + last_fix[1]], axis=1)
        sums.append(value.astype(BF))
    dense = dot(jnp.concatenate(sums, axis=0), compact_ref[...]).astype(BF)
    for i in range(GROUPS):
        out_ref[:, i * FINE_IN : (i + 1) * FINE_IN] = dense[i * ROWS : (i + 1) * ROWS]


def params(
    tab_ref, weight_ref, bias_ref, gain_ref, shift_ref, up_bias_ref, down_bias_ref, scale_ref, pool_weight_ref, spread_weight_ref,
    taps_ref, conv_bias_ref, gains_ref, shifts_ref, up_biases_ref, down_biases_ref, scales_ref, pool_cells_ref, spread_cells_ref,
):
    for tap in range(49):
        taps_ref[tap] = jnp.broadcast_to(weight_ref[1, :, tap : tap + 1], (ROWS, 128))
    conv_bias_ref[...] = columns(bias_ref[1:2, :])
    me = lax.axis_index("chan")
    for level in range(2):
        row = slice(level, level + 1)
        gains_ref[level] = columns(gain_ref[row, :])
        shifts_ref[level] = columns(shift_ref[row, :])
        up_biases_ref[level] = columns(up_bias_ref[row, :])
        scales_ref[level] = columns(scale_ref[row, :])
        down_bias = columns(down_bias_ref[row, :])
        own = down_bias[0:ROWS]
        for k in range(1, down_bias.shape[0] // ROWS):
            own = jnp.where(me == k, down_bias[k * ROWS : (k + 1) * ROWS], own)
        down_biases_ref[level] = own
    pool_cells_ref[...] = cell_weights(pool_weight_ref)
    spread_cells_ref[...] = cell_weights(spread_weight_ref)


def conv_coarse(tab_ref, x_ref, recv_ref, halo_ref, sides_ref, wide_ref, bias_ref, out_ref, pad_ref, sum_ref):
    lane = lane_ids((ROWS, 128))

    def main_of(source, scale):
        parts = [recv_ref[source, :, 128 * g : 128 * g + 128] for g in range(3)]
        return jnp.concatenate(parts, axis=0).astype(F32) * scale

    def row_strips(bands):
        pieces = []
        for band in bands:
            source, scale = band_source(tab_ref, band)
            pieces.append(main_of(source, scale).astype(BF))
        return jnp.concatenate(pieces, axis=1)

    pad_ref[0, :, 0:128] = dot(row_strips((0, 1, 2)), halo_ref[0])
    pad_ref[0, :, 896:1024] = dot(row_strips((5, 6, 7)), halo_ref[tab_ref[8]])
    pieces = []
    for band in (3, 4):
        source, scale = band_source(tab_ref, band)
        rest = recv_ref[source, :, 384:512].astype(F32) * scale
        rest = jnp.concatenate([rest, pltpu.roll(rest, 128 - 24, 1), pltpu.roll(rest, 128 - 48, 1)], axis=0)
        main = main_of(source, scale)
        pieces.append(jnp.where(lane < 24, rest, main).astype(BF))
    pad_ref[0, :, 128:896] = dot(jnp.concatenate(pieces, axis=1), sides_ref[...]) + x_ref[...].astype(F32)
    padded = pad_ref[0]
    for turn in range(1, 4):
        pad_ref[turn] = lane_shifted(padded, 32 * turn)
    sum_ref[...] = wide(bias_ref[...], 768)

    def group(g, carry):
        rows = pl.ds(pl.multiple_of(g * 8, 8), 8)
        for chunk in range(2):
            base = chunk * 384
            taken = []
            for a in range(1, 8):
                start = base + (a // 4) * 128
                taken.append([pad_ref[a % 4, rows, start + 128 * j : start + 128 * j + 128] for j in range(3)])
            total = [sum_ref[rows, base + 128 * j : base + 128 * j + 128] for j in range(3)]
            for b in range(7):
                weights = [wide_ref[a * 7 + b, rows, :] for a in range(7)]
                for j in range(3):
                    partial = weights[0] * taken[0][j]
                    for a in range(1, 7):
                        partial = partial + weights[a] * taken[a][j]
                    total[j] = total[j] + (pltpu.roll(partial, (3 - b) % 128, 1) if b != 3 else partial)
            for j in range(3):
                sum_ref[rows, base + 128 * j : base + 128 * j + 128] = total[j]
        return carry

    lax.fori_loop(0, 6, group, 0)
    out_ref[...] = sum_ref[...].astype(BF)


def gather_rows(pieces, cat_ref):
    me = lax.axis_index("chan")
    for k, piece in enumerate(pieces):
        first = pl.multiple_of(lax.bitwise_xor(me, k) * ROWS, 16)
        cat_ref[pl.ds(first, ROWS), :] = piece[...]


def make_branch(level, cat_ref, gain_ref, shift_ref, up_ref, up_bias_ref, down_ref, down_bias_ref, block):
    first = pl.multiple_of(lax.axis_index("chan") * ROWS, 16)
    gain, shift = wide(gain_ref[level], block), wide(shift_ref[level], block)

    def branch(start):
        values = cat_ref[:, pl.ds(start, block)].astype(F32)
        mean = jnp.mean(values, axis=0, keepdims=True)
        centred = values - mean
        spread = jnp.mean(centred * centred, axis=0, keepdims=True)
        normed = (centred * lax.rsqrt(spread + norm_eps) * gain + shift).astype(BF)
        hidden = dot(up_ref[level], normed) + wide(up_bias_ref[level], block)
        hidden = 0.5 * hidden * (1.0 + lax.erf(hidden * np.float32(0.5**0.5)))
        return dot(down_ref[level, pl.ds(first, ROWS), :], hidden.astype(BF)) + wide(down_bias_ref[level], block)

    return branch


def cell_weights(weight_ref):
    lane = lane_ids((ROWS, FINE_IN))
    odd_row = (lane // TILE) % 2
    odd_col = (lane % TILE) % 2
    kind = 2 * odd_row + odd_col
    result = jnp.zeros((ROWS, FINE_IN), F32)
    for k in range(4):
        result = jnp.where(kind == k, weight_ref[:, k : k + 1], result)
    return result


def make_mix_fine(count):
    def mix_fine(
        tab_ref, own_ref, p1_ref, p2_ref, p3_ref, x_ref, mask_ref,
        gain_ref, shift_ref, up_ref, up_bias_ref, down_ref, down_bias_ref, scale_ref, pool_cells_ref, pool_ref, pack_ref,
        fine_ref, pooled_ref, small_mask_ref, msg_ref, cat_ref, mains_ref, rest_ref,
    ):
        gather_rows((own_ref, p1_ref, p2_ref, p3_ref), cat_ref)
        block = 768
        branch = make_branch(0, cat_ref, gain_ref, shift_ref, up_ref, up_bias_ref, down_ref, down_bias_ref, block)
        scale = wide(scale_ref[0], block)

        for start in range(0, TILE * TILE, block):
            here = slice(start, start + block)
            value = x_ref[0, :, here].astype(F32) + scale * branch(start)
            fine_ref[:, here] = (mask_ref[:, here].astype(F32) * value).astype(BF)

        weights = pool_cells_ref[...]
        highs, lows, masks = [], [], []
        for i in range(GROUPS):
            lanes = slice(i * FINE_IN, (i + 1) * FINE_IN)
            product = fine_ref[:, lanes].astype(F32) * weights
            high = product.astype(BF)
            highs.append(high)
            lows.append((product - high.astype(F32)).astype(BF))
            masks.append(jnp.broadcast_to(mask_ref[:, lanes].astype(F32), (8, FINE_IN)))
        pool_table = pool_ref[...]
        pooled = dot(jnp.concatenate(highs, axis=0), pool_table) + dot(jnp.concatenate(lows, axis=0), pool_table)
        pooled = pooled.astype(BF)
        for i in range(GROUPS):
            pooled_ref[:, i * 128 : (i + 1) * 128] = pooled[i * ROWS : (i + 1) * ROWS]
        counts = dot(jnp.concatenate(masks, axis=0).astype(BF), pool_table)
        small_mask_ref[...] = jnp.where(counts > 0.5, 1.0, 0.0)

        packed = dot(pooled_ref[...], pack_ref[...])
        lane = lane_ids((ROWS, 128))
        blocks = (packed[:, 0:128], packed[:, 128:256])
        for r in range(2):
            for c in range(2):
                mains_ref[2 * r + c] = jnp.where(lane < 72, blocks[r], blocks[c]).astype(BF)
        lane = lane_ids((16, 128))
        for c in range(2):
            rest = packed[:, 256:384]
            rest = pltpu.roll(rest, 64, 1) if c else rest
            parts = [rest[0:16], pltpu.roll(rest[16:32], 24, 1), pltpu.roll(rest[32:48], 48, 1)]
            joined = jnp.where(lane < 24, parts[0], jnp.where(lane < 48, parts[1], parts[2]))
            rest_ref[c] = jnp.where(lane < 72, joined, 0.0).astype(BF)

        def fill(dev, carry):
            both = tab_ref[16 + dev]
            col_pick = lax.rem(both, 2)
            for g in range(3):
                msg_ref[dev, :, 128 * g : 128 * g + 128] = mains_ref[both, 16 * g : 16 * g + 16, :]
            msg_ref[dev, :, 384:512] = rest_ref[col_pick]
            return carry

        scan_tiles(count, fill, jnp.int32(0))

    return mix_fine


def mix_coarse(
    own_ref, p1_ref, p2_ref, p3_ref, pooled_ref, small_mask_ref, fine_ref, mask_ref, gain_ref, shift_ref, up_ref, up_bias_ref,
    down_ref, down_bias_ref, scale_ref, spread_cells_ref, pool_ref, out_ref, cat_ref,
):
    gather_rows((own_ref, p1_ref, p2_ref, p3_ref), cat_ref)
    cells = cat_ref.shape[1]
    branch = make_branch(1, cat_ref, gain_ref, shift_ref, up_ref, up_bias_ref, down_ref, down_bias_ref, cells)
    value = pooled_ref[...].astype(F32) + wide(scale_ref[1], cells) * branch(0)
    parts = []
    for i in range(GROUPS):
        parts.append((small_mask_ref[8 * i : 8 * i + 1, :] * value[:, 128 * i : 128 * i + 128]).astype(BF))
    spread = lax.dot_general(
        jnp.concatenate(parts, axis=0), pool_ref[...], (((1,), (1,)), ((), ())), preferred_element_type=F32
    )
    weights = spread_cells_ref[...]
    for i in range(GROUPS):
        lanes = slice(i * FINE_IN, (i + 1) * FINE_IN)
        merged = fine_ref[:, lanes].astype(F32) + weights * spread[i * ROWS : (i + 1) * ROWS]
        out_ref[0, :, lanes] = (mask_ref[:, lanes].astype(F32) * merged).astype(BF)


VMEM = pl.BlockSpec(memory_space=pltpu.VMEM)
SMEM = pl.BlockSpec(memory_space=pltpu.SMEM)

def takes(microseconds):
    return pl.CostEstimate(flops=microseconds * 1_000_000_000, bytes_accessed=0, transcendentals=0)


def shaped(*shape, dtype=BF):
    return jax.ShapeDtypeStruct(shape, dtype)


PARAMS = pltpu.CompilerParams(vmem_limit_bytes=24 * 1024 * 1024)


def every_channel(own):
    pairs = lambda bit: [(i, i ^ bit) for i in range(4)]
    across = lax.ppermute(own, "chan", pairs(2))
    beside = lax.ppermute(own, "chan", pairs(1))
    diagonal = lax.ppermute(across, "chan", pairs(1))
    return own, beside, across, diagonal


def per_device(
    features, land_mask, wet_slots, device_of, depth_weight, depth_bias, norm_gain, norm_bias, up_weight, up_bias,
    down_weight, down_bias, layer_scale, pool_weight, spread_weight,
):
    count = wet_slots.shape[0]
    grid_x = 2 * count // GRID_Y
    cells = TILE * TILE
    pack = pl.pallas_call(
        strip_table, out_specs=VMEM, out_shape=shaped(FINE_IN, 256), compiler_params=PARAMS, cost_estimate=takes(2), name="strip_table"
    )()
    messages, table = pl.pallas_call(
        make_prep(grid_x),
        in_specs=[SMEM, SMEM, VMEM, VMEM],
        out_specs=[VMEM, SMEM],
        out_shape=[shaped(count, 16, 896), shaped(16 + count, dtype=jnp.int32)],
        scratch_shapes=[
            pltpu.VMEM((2, ROWS, 128), BF),
            pltpu.VMEM((2, ROWS, 128), BF),
            pltpu.VMEM((2, 16, 128), F32),
            pltpu.VMEM((2, 16, 128), F32),
        ],
        compiler_params=PARAMS,
        cost_estimate=takes(10),
        name="prep",
    )(wet_slots, device_of, features, pack)
    held = {
        "x": features,
        "mask": land_mask,
        "weight": depth_weight,
        "bias": depth_bias,
        "halo": jnp.asarray(FINE["halo"]),
        "expand": jnp.asarray(FINE["expand"]),
        "compact": jnp.asarray(FINE["compact"]),
        "spread": jnp.asarray(FINE["spread"]),
        "fine_sides": jnp.asarray(FINE["sides"]),
        "small_halo": jnp.asarray(COARSE["halo"]),
        "sides": jnp.asarray(COARSE["sides"]),
        "pool": jnp.asarray(FINE["pool"]),
        "small_pack": jnp.asarray(COARSE["pack"]),
    }
    arrived = lax.all_to_all(messages, "tile", 0, 0, tiled=True)
    taps, conv_bias, gains, shifts, up_biases, down_biases, scales, pool_cells, spread_cells = pl.pallas_call(
        params,
        in_specs=[SMEM] + [VMEM] * 9,
        out_specs=[VMEM] * 9,
        out_shape=[
            shaped(*shape, dtype=F32)
            for shape in (
                (49, ROWS, 128), (ROWS, 128), (2, 192, 128), (2, 192, 128), (2, 768, 128), (2, ROWS, 128), (2, ROWS, 128),
                (ROWS, FINE_IN), (ROWS, FINE_IN),
            )
        ],
        compiler_params=PARAMS,
        cost_estimate=takes(1),
        name="params",
    )(table, depth_weight, depth_bias, norm_gain, norm_bias, up_bias, down_bias, layer_scale, pool_weight, spread_weight)
    inner, fine_taps = pl.pallas_call(
        lambda tab_ref, *refs: conv_inner(*refs),
        in_specs=[SMEM] + [VMEM] * 4,
        out_specs=[VMEM] * 2,
        out_shape=[shaped(ROWS, 3072, dtype=F32), shaped(49, ROWS, 128, dtype=F32)],
        scratch_shapes=[pltpu.VMEM((ROWS, 3584), F32), pltpu.VMEM((ROWS, 3584), F32)],
        compiler_params=PARAMS,
        cost_estimate=takes(4),
        name="conv_inner",
    )(table, held["x"], held["expand"], held["weight"], held["bias"])
    conv = pl.pallas_call(
        conv_border,
        in_specs=[SMEM] + [VMEM] * 7,
        out_specs=VMEM,
        out_shape=shaped(ROWS, cells),
        compiler_params=PARAMS,
        cost_estimate=takes(2),
        name="conv_border",
    )(table, arrived, inner, fine_taps, held["halo"], held["fine_sides"], held["spread"], held["compact"])
    fine, pooled, small_mask, messages = pl.pallas_call(
        make_mix_fine(count),
        in_specs=[SMEM] + [VMEM] * 16,
        out_specs=[VMEM] * 4,
        out_shape=[shaped(ROWS, cells), shaped(ROWS, 768), shaped(48, 128, dtype=F32), shaped(count, 16, 512)],
        scratch_shapes=[
            pltpu.VMEM((4 * ROWS, cells), BF),
            pltpu.VMEM((4, ROWS, 128), BF),
            pltpu.VMEM((2, 16, 128), BF),
        ],
        compiler_params=PARAMS,
        cost_estimate=takes(4),
        name="mix_fine",
    )(
        table, *every_channel(conv), held["x"], held["mask"], gains, shifts, up_weight, up_biases,
        down_weight, down_biases, scales, pool_cells, held["pool"], held["small_pack"],
    )
    arrived = lax.all_to_all(messages, "tile", 0, 0, tiled=True)
    conv = pl.pallas_call(
        conv_coarse,
        in_specs=[SMEM] + [VMEM] * 6,
        out_specs=VMEM,
        out_shape=shaped(ROWS, 768),
        scratch_shapes=[pltpu.VMEM((4, ROWS, 1024), F32), pltpu.VMEM((ROWS, 768), F32)],
        compiler_params=PARAMS,
        cost_estimate=takes(2),
        name="conv_coarse",
    )(table, pooled, arrived, held["small_halo"], held["sides"], taps, conv_bias)
    return pl.pallas_call(
        mix_coarse,
        in_specs=[VMEM] * 17,
        out_specs=VMEM,
        out_shape=shaped(1, ROWS, cells),
        scratch_shapes=[pltpu.VMEM((4 * ROWS, 768), BF)],
        compiler_params=PARAMS,
        cost_estimate=takes(2),
        name="mix_coarse",
    )(
        *every_channel(conv), pooled, small_mask, fine, held["mask"], gains, shifts, up_weight, up_biases, down_weight, down_biases,
        scales, spread_cells, held["pool"],
    )


def solution(mesh):
    placed = (
        P("tile", "chan", None),
        P("tile", None),
        P(),
        P(),
        P(None, "chan", None),
        P(None, "chan"),
        P(),
        P(),
        P(),
        P(),
        P(),
        P(),
        P(None, "chan"),
        P("chan", None),
        P("chan", None),
    )
    return jax.shard_map(
        per_device, mesh=mesh, in_specs=placed, out_specs=P("tile", "chan", None), check_vma=False
    )
```

```python
import jax
import jax.numpy as jnp
import ml_dtypes
import numpy as np
from jax import lax
from jax.experimental import pallas as pl
from jax.experimental.pallas import tpu as pltpu
from jax.sharding import PartitionSpec as P

TILE = 48
HALF = TILE // 2
GRID_Y = 4
GROUPS = 6
ROWS = 48
FINE_IN = 8 * TILE
FINE_PAD = 8 * 64
BANDS = ((-1, -1), (-1, 0), (-1, 1), (0, -1), (0, 1), (1, -1), (1, 0), (1, 1))
norm_eps = 1e-06
BF = jnp.bfloat16
F32 = jnp.float32


def one_hot(shape, pairs):
    table = np.zeros(shape, np.float32)
    for source, target in pairs:
        table[source, target] = 1.0
    return table.astype(ml_dtypes.bfloat16)


def side_target(side, row, col, width, stride):
    if side == 0:
        return row * stride + 3 + col
    if side == -1:
        return row * stride + col - (width - 3) if col >= width - 3 else None
    return row * stride + 3 + width + col if col < 3 else None


def halo_pairs(cells, width, stride, first_row, flipped):
    block = max(lane for lane, _ in cells) // 128 * 128 + 128
    pairs = []
    for place, side in enumerate((-1, 0, 1)):
        for lane, index in cells:
            row, col = index // width, index % width
            if flipped:
                row, col = 2 - row, width - 1 - col
            target = side_target(side, row + first_row, col, width, stride)
            if target is not None:
                pairs.append((place * block + lane, target))
    return pairs


def pool_table():
    pairs = [(row * 48 + col, (row // 2) * 32 + 3 + col // 2) for row in range(8) for col in range(48)]
    return one_hot((384, 128), pairs)


def coarse_tables():
    strip = [(t, t) for t in range(72)]
    halo = np.stack(
        [
            one_hot((384, 128), halo_pairs(strip, HALF, 32, 1, False)),
            one_hot((384, 128), halo_pairs(strip, HALF, 32, 0, False)),
            one_hot((384, 128), halo_pairs(strip, HALF, 32, 0, True)),
        ]
    )
    pack, sides = [], []
    for row in range(3):
        for col in range(HALF):
            pack.append((row * 32 + 3 + col, row * 24 + col))
            pack.append(((21 + row) * 32 + 3 + col, 128 + row * 24 + col))
    for row in range(HALF):
        for j in range(3):
            index = row * 3 + j
            lane = 72 + index if row < 16 else index - 48
            pack.append((row * 32 + 3 + j, lane if row < 16 else 256 + lane))
            pack.append((row * 32 + 24 + j, 128 + lane if row < 16 else 256 + 64 + lane))
            sides.append((lane, row * 32 + j))
            sides.append((128 + lane, row * 32 + 27 + j))
    return {
        "halo": halo,
        "pack": one_hot((768, 384), pack),
        "sides": one_hot((256, 768), sides),
    }


POOL = pool_table()
COARSE = coarse_tables()


def dot(left, right):
    return jnp.dot(left, right, preferred_element_type=F32)


def stacked(value, width):
    return jnp.concatenate([value[:, i * width : (i + 1) * width] for i in range(GROUPS)], axis=0)


def lane_ids(shape):
    return lax.broadcasted_iota(jnp.int32, shape, 1)


def columns(row):
    high = row.astype(BF)
    rest = row - high.astype(F32)
    middle = rest.astype(BF)
    low = (rest - middle.astype(F32)).astype(BF)
    n = row.shape[1]
    terms = jnp.concatenate([high, middle, low, jnp.zeros((13, n), BF)], axis=0)
    return lax.dot_general(terms, jnp.ones((16, 128), BF), (((0,), (0,)), ((), ())), preferred_element_type=F32)


def wide(block, lanes):
    return jnp.concatenate([block] * (lanes // 128), axis=1)


def scan_tiles(count, step, carry):
    if count <= 16:
        for k in range(count):
            carry = step(k, carry)
        return carry
    return lax.fori_loop(0, count, step, carry)


def strip_table(pack_ref):
    shape = (FINE_IN, 256)
    source = lax.broadcasted_iota(jnp.int32, shape, 0)
    lane = lane_ids(shape)
    within = lane % 128
    wanted = (within // 3) * TILE + within % 3 + jnp.where(lane >= 128, TILE - 3, 0)
    pack_ref[...] = jnp.where((within < 24) & (source == wanted), 1.0, 0.0).astype(BF)


def quotient(value, divisor):
    if divisor & (divisor - 1) == 0:
        return lax.shift_right_logical(value, jnp.int32(divisor.bit_length() - 1))
    return lax.div(value, divisor)


def remainder(value, divisor):
    if divisor & (divisor - 1) == 0:
        return lax.bitwise_and(value, jnp.int32(divisor - 1))
    return lax.rem(value, divisor)


def make_prep(grid_x):
    def prep(slots_ref, dev_ref, x_ref, pack_ref, msg_ref, tab_ref, rows_ref, cols_ref, row_rest_ref, col_rest_ref):
        count = slots_ref.shape[0]
        me = lax.axis_index("tile")
        my_slot = scan_tiles(count, lambda k, c: c + jnp.where(dev_ref[k] == me, slots_ref[k], 0), jnp.int32(0))
        my_x = remainder(my_slot, grid_x)
        my_y = quotient(my_slot, grid_x)
        wanted = []
        for up_by, right_by in BANDS:
            near_x = remainder(my_x + (right_by + grid_x), grid_x)
            near_y = my_y + up_by
            folded = near_y >= GRID_Y
            from_x = jnp.where(folded, grid_x - 1 - near_x, near_x)
            from_y = jnp.where(folded, GRID_Y - 1, near_y)
            wanted.append(from_y * grid_x + from_x)

        def find(k, found):
            slot, dev = slots_ref[k], dev_ref[k]
            row_pick = jnp.where(quotient(slot, grid_x) + 1 == my_y, 0, 1)
            col_pick = jnp.where(remainder(slot, grid_x) == remainder(my_x + (grid_x - 1), grid_x), 0, 1)
            tab_ref[16 + dev] = 2 * row_pick + col_pick
            return tuple(jnp.where(slot == want, dev, old) for want, old in zip(wanted, found))

        found = scan_tiles(count, find, tuple(jnp.int32(-1) for _ in BANDS))
        for band in range(8):
            tab_ref[band] = found[band]
        tab_ref[8] = jnp.where(my_y == GRID_Y - 1, 2, 1)
        for spare in range(9, 16):
            tab_ref[spare] = 0

        x = x_ref[0]
        cols = dot(stacked(x, FINE_IN), pack_ref[...])
        lane = lane_ids((ROWS, 128))
        for side in range(2):
            part = cols[:, side * 128 : side * 128 + 128]
            main = part[0:ROWS]
            for i in range(1, 5):
                main = main + pltpu.roll(part[i * ROWS : (i + 1) * ROWS], 24 * i, 1)
            cols_ref[side] = main.astype(BF)
            rest = pltpu.roll(part[5 * ROWS : 6 * ROWS], 16, 1)
            col_rest_ref[side] = rest[0:16] + pltpu.roll(rest[16:32], 40, 1) + pltpu.roll(rest[32:48], 80, 1)
        rows_ref[0] = x[:, 0:128]
        rows_ref[1] = x[:, 2176:2304]
        ends = (x[:, 128:256].astype(F32), pltpu.roll(x[:, 2048:2176].astype(F32), 16, 1))
        for side in range(2):
            rest = jnp.where(lane < 16, ends[side], 0.0)
            row_rest_ref[side] = rest[0:16] + pltpu.roll(rest[16:32], 40, 1) + pltpu.roll(rest[32:48], 80, 1)

        def fill(dev, carry):
            row_pick = quotient(tab_ref[16 + dev], 2)
            col_pick = remainder(tab_ref[16 + dev], 2)
            for g in range(3):
                msg_ref[dev, :, 256 * g : 256 * g + 128] = rows_ref[row_pick, 16 * g : 16 * g + 16, :]
                msg_ref[dev, :, 256 * g + 128 : 256 * g + 256] = cols_ref[col_pick, 16 * g : 16 * g + 16, :]
            msg_ref[dev, :, 768:896] = (row_rest_ref[row_pick] + col_rest_ref[col_pick]).astype(BF)
            return carry

        scan_tiles(count, fill, jnp.int32(0))

    return prep


def band_source(tab_ref, band):
    source = tab_ref[band]
    return jnp.maximum(source, 0), jnp.where(source >= 0, 1.0, 0.0).astype(F32)


def lane_shifted(value, lanes):
    return pltpu.roll(value, value.shape[1] - lanes, 1)


def tall(row_block):
    return jnp.concatenate([row_block] * (ROWS // 8), axis=0)


def lanes_from(value, index):
    return jnp.take_along_axis(value, index, axis=1)


def conv_inner(x_ref, weight_ref, bias_ref, sum_ref, pad_ref, odd_ref, wide_ref, total_ref):
    for tap in range(49):
        wide_ref[tap] = jnp.broadcast_to(weight_ref[0, :, tap : tap + 1], (ROWS, 128))
    pad_ref[:, 0:256] = jnp.zeros((ROWS, 256), F32)
    pad_ref[:, 3328:3584] = jnp.zeros((ROWS, 256), F32)
    lane = lane_ids((8, 128))
    half, within = lane // 64, lane % 64
    valid = tall((within >= 3) & (within < 51))
    col = jnp.clip(within - 3, 0, 47)
    cells = [96 * k + 48 * half + col for k in range(4)]
    indices = [tall(cell % 128) for cell in cells]
    for i in range(GROUPS):
        tiles = [x_ref[0, :, 384 * i + 128 * m : 384 * i + 128 * m + 128].astype(F32) for m in range(3)]
        for k in range(4):
            first, final = (96 * k) // 128, (96 * k + 95) // 128
            value = lanes_from(tiles[first], indices[k])
            if final != first:
                value = jnp.where(tall(cells[k] < 128 * final), value, lanes_from(tiles[final], indices[k]))
            start = 256 + 512 * i + 128 * k
            pad_ref[:, start : start + 128] = jnp.where(valid, value, 0.0)
    odd_ref[...] = lane_shifted(pad_ref[...], 64)
    total_ref[...] = wide(columns(bias_ref[0:1, :]), 3072)

    def group(g, carry):
        here = pl.ds(pl.multiple_of(g * 8, 8), 8)
        for chunk in range(6):
            base = chunk * 512
            taken = []
            for a in range(1, 8):
                ref = odd_ref if a % 2 else pad_ref
                start = base + (a // 2) * 128
                taken.append([ref[here, start + 128 * j : start + 128 * j + 128] for j in range(4)])
            total = [total_ref[here, base + 128 * j : base + 128 * j + 128] for j in range(4)]
            for b in range(7):
                weights = [wide_ref[a * 7 + b, here, :] for a in range(7)]
                for j in range(4):
                    partial = weights[0] * taken[0][j]
                    for a in range(1, 7):
                        partial = partial + weights[a] * taken[a][j]
                    total[j] = total[j] + (pltpu.roll(partial, (3 - b) % 128, 1) if b != 3 else partial)
            for j in range(4):
                total_ref[here, base + 128 * j : base + 128 * j + 128] = total[j]
        return carry

    lax.fori_loop(0, ROWS // 8, group, 0)
    cells = [128 * m + lane for m in range(3)]
    indices = [tall((cell // 48) % 2 * 64 + 3 + cell % 48) for cell in cells]
    for i in range(GROUPS):
        tiles = [total_ref[:, 512 * i + 128 * k : 512 * i + 128 * k + 128] for k in range(4)]
        for m in range(3):
            value = jnp.where(
                tall(cells[m] < 96 * (m + 1)), lanes_from(tiles[m], indices[m]), lanes_from(tiles[m + 1], indices[m])
            )
            sum_ref[:, 384 * i + 128 * m : 384 * i + 128 * m + 128] = value


def conv_border(tab_ref, recv_ref, sum_ref, weight_ref, out_ref, taps_ref):
    lane = lane_ids((8, 128))
    half, within = lane // 64, lane % 64
    low_half = tall(lane < 64)
    taps_ref[...] = jnp.zeros((ROWS, 128), F32)
    taps_ref[:, 0:49] = weight_ref[0]
    taps = taps_ref[...]

    def band_cells(band, offset):
        source, scale = band_source(tab_ref, band)
        main = jnp.concatenate([recv_ref[source, :, 256 * g + offset : 256 * g + offset + 128] for g in range(3)], axis=0)
        rest = recv_ref[source, :, 768:896].astype(F32) * scale
        rest = jnp.concatenate([rest, pltpu.roll(rest, 128 - 40, 1), pltpu.roll(rest, 128 - 80, 1)], axis=0)
        return main.astype(F32) * scale, rest

    def halo_rows(bands, folded, last):
        left, middle, right = [band_cells(band, 0) for band in bands]
        tiles = []
        for first_row in (0, 2):
            row = first_row + half
            col = jnp.where(within < 3, 45 + within, jnp.where(within < 51, within - 3, within - 51))
            index = row * 48 + col
            index = jnp.where(folded, 143 - index, index)
            in_main = index - jnp.where(last, 16, 0)
            rest = (in_main < 0) | (in_main > 127)
            in_rest = jnp.where(in_main < 0, in_main + 16, in_main - 128)
            main_index, rest_index = tall(in_main & 127), tall(in_rest & 127)
            picked = [jnp.where(tall(rest), lanes_from(r, rest_index), lanes_from(m, main_index)) for m, r in (left, middle, right)]
            value = jnp.where(tall(within < 3), picked[0], jnp.where(tall(within < 51), picked[1], picked[2]))
            tiles.append(jnp.where(tall((within < 54) & (row < 3)), value, 0.0))
        return tiles

    def row_fix(uses):
        total = [jnp.zeros((ROWS, 128), F32)] * 2
        for b in range(7):
            partial = [None, None]
            weights = {}
            for place, a, cells in uses:
                if a not in weights:
                    weights[a] = jnp.broadcast_to(taps[:, a * 7 + b : a * 7 + b + 1], (ROWS, 128))
                term = weights[a] * cells
                partial[place] = term if partial[place] is None else partial[place] + term
            for place in range(2):
                total[place] = total[place] + (pltpu.roll(partial[place], (3 - b) % 128, 1) if b != 3 else partial[place])
        return total

    def joined(first, second):
        return jnp.where(low_half, pltpu.roll(first, 64, 1), pltpu.roll(second, 64, 1))

    zeros = jnp.zeros((ROWS, 128), F32)
    below = halo_rows((0, 1, 2), False, True)
    first_fix = row_fix(((0, 0, below[0]), (0, 1, joined(below[0], below[1])), (0, 2, below[1]), (1, 0, below[1])))
    folded = tab_ref[8] == 2
    above = halo_rows((5, 6, 7), folded, folded)
    edge = joined(zeros, above[0])
    last_fix = row_fix(((0, 6, edge), (1, 4, edge), (1, 5, above[0]), (1, 6, joined(above[0], above[1]))))

    left, right = band_cells(3, 128), band_cells(4, 128)
    beside = []
    for j in range(3):
        which = jnp.where(half == 0, j, 2 - j)
        in_main = jnp.minimum(3 * within + which, 127)
        main_index, rest_index = tall(in_main), tall(jnp.clip(3 * (within - 40) + 16 + which, 0, 127))
        picked = [
            jnp.where(tall(within < 40), lanes_from(main, main_index), lanes_from(rest, rest_index)) for main, rest in (left, right)
        ]
        beside.append(jnp.where(tall(within < 48), jnp.where(low_half, picked[0], picked[1]), 0.0))
    column_fix = [zeros] * 3
    for a in range(7):
        weights = [lanes_from(taps, tall(jnp.where(half == 0, a * 7 + b, a * 7 + 6 - b))) for b in range(3)]
        for q in range(3):
            partial = weights[0] * beside[q]
            for j in range(q + 1, 3):
                partial = partial + weights[j - q] * beside[j]
            column_fix[q] = column_fix[q] + (pltpu.roll(partial, (3 - a) % 128, 1) if a != 3 else partial)

    for m in range(TILE * TILE // 128):
        cell = 128 * m + lane
        row, col = cell // 48, cell % 48
        index = tall(jnp.where(col < 24, row, 64 + row))
        value = sum_ref[:, 128 * m : 128 * m + 128]
        fix = zeros
        for q in range(3):
            fix = jnp.where(tall((col == q) | (col == 47 - q)), lanes_from(column_fix[q], index), fix)
        value = value + fix
        row_index = tall(row % 2 * 64 + 3 + col)
        for pair, tile in ((0, first_fix[0]), (1, first_fix[1]), (22, last_fix[0]), (23, last_fix[1])):
            if 96 * pair < 128 * m + 128 and 96 * pair + 96 > 128 * m:
                value = value + jnp.where(tall(row // 2 == pair), lanes_from(tile, row_index), 0.0)
        out_ref[:, 128 * m : 128 * m + 128] = value.astype(BF)


def params(
    after_ref, weight_ref, bias_ref, gain_ref, shift_ref, up_ref, up_bias_ref, down_bias_ref, scale_ref, pool_weight_ref, spread_weight_ref,
    taps_ref, conv_bias_ref, gains_ref, shifts_ref, ups_ref, up_biases_ref, down_biases_ref, scales_ref, pool_cells_ref, spread_cells_ref,
):
    for tap in range(49):
        taps_ref[tap] = jnp.broadcast_to(weight_ref[1, :, tap : tap + 1], (ROWS, 128))
    conv_bias_ref[...] = columns(bias_ref[1:2, :])
    me = lax.axis_index("chan")
    for level in range(2):
        row = slice(level, level + 1)
        ups_ref[level] = jnp.transpose(up_ref[level], (1, 0))
        gains_ref[level] = columns(gain_ref[row, :])
        shifts_ref[level] = columns(shift_ref[row, :])
        up_biases_ref[level] = columns(up_bias_ref[row, :])
        scales_ref[level] = columns(scale_ref[row, :])
        down_bias = columns(down_bias_ref[row, :])
        own = down_bias[0:ROWS]
        for k in range(1, down_bias.shape[0] // ROWS):
            own = jnp.where(me == k, down_bias[k * ROWS : (k + 1) * ROWS], own)
        down_biases_ref[level] = own
    pool_cells_ref[...] = cell_weights(pool_weight_ref)
    spread_cells_ref[...] = cell_weights(spread_weight_ref)


def conv_coarse(tab_ref, x_ref, recv_ref, halo_ref, sides_ref, wide_ref, bias_ref, out_ref, pad_ref, sum_ref):
    lane = lane_ids((ROWS, 128))

    def main_of(source, scale):
        parts = [recv_ref[source, :, 128 * g : 128 * g + 128] for g in range(3)]
        return jnp.concatenate(parts, axis=0).astype(F32) * scale

    def row_strips(bands):
        pieces = []
        for band in bands:
            source, scale = band_source(tab_ref, band)
            pieces.append(main_of(source, scale).astype(BF))
        return jnp.concatenate(pieces, axis=1)

    pad_ref[0, :, 0:128] = dot(row_strips((0, 1, 2)), halo_ref[0])
    pad_ref[0, :, 896:1024] = dot(row_strips((5, 6, 7)), halo_ref[tab_ref[8]])
    pieces = []
    for band in (3, 4):
        source, scale = band_source(tab_ref, band)
        rest = recv_ref[source, :, 384:512].astype(F32) * scale
        rest = jnp.concatenate([rest, pltpu.roll(rest, 128 - 24, 1), pltpu.roll(rest, 128 - 48, 1)], axis=0)
        main = main_of(source, scale)
        pieces.append(jnp.where(lane < 24, rest, main).astype(BF))
    pad_ref[0, :, 128:896] = dot(jnp.concatenate(pieces, axis=1), sides_ref[...]) + x_ref[...].astype(F32)
    padded = pad_ref[0]
    for turn in range(1, 4):
        pad_ref[turn] = lane_shifted(padded, 32 * turn)
    sum_ref[...] = wide(bias_ref[...], 768)

    def group(g, carry):
        rows = pl.ds(pl.multiple_of(g * 8, 8), 8)
        for chunk in range(2):
            base = chunk * 384
            taken = []
            for a in range(1, 8):
                start = base + (a // 4) * 128
                taken.append([pad_ref[a % 4, rows, start + 128 * j : start + 128 * j + 128] for j in range(3)])
            total = [sum_ref[rows, base + 128 * j : base + 128 * j + 128] for j in range(3)]
            for b in range(7):
                weights = [wide_ref[a * 7 + b, rows, :] for a in range(7)]
                for j in range(3):
                    partial = weights[0] * taken[0][j]
                    for a in range(1, 7):
                        partial = partial + weights[a] * taken[a][j]
                    total[j] = total[j] + (pltpu.roll(partial, (3 - b) % 128, 1) if b != 3 else partial)
            for j in range(3):
                sum_ref[rows, base + 128 * j : base + 128 * j + 128] = total[j]
        return carry

    lax.fori_loop(0, 6, group, 0)
    out_ref[...] = sum_ref[...].astype(BF)


def gather_rows(pieces, cat_ref):
    me = lax.axis_index("chan")
    for k, piece in enumerate(pieces):
        first = pl.multiple_of(lax.bitwise_xor(me, k) * ROWS, 16)
        cat_ref[pl.ds(first, ROWS), :] = piece[...]


def make_branch(level, cat_ref, gain_ref, shift_ref, up_ref, up_bias_ref, down_ref, down_bias_ref, block):
    first = pl.multiple_of(lax.axis_index("chan") * ROWS, 16)
    gain, shift = wide(gain_ref[level], block), wide(shift_ref[level], block)

    def branch(start):
        values = cat_ref[:, pl.ds(start, block)].astype(F32)
        mean = jnp.mean(values, axis=0, keepdims=True)
        centred = values - mean
        spread = jnp.mean(centred * centred, axis=0, keepdims=True)
        normed = (centred * lax.rsqrt(spread + norm_eps) * gain + shift).astype(BF)
        hidden = dot(up_ref[level], normed) + wide(up_bias_ref[level], block)
        hidden = 0.5 * hidden * (1.0 + lax.erf(hidden * np.float32(0.5**0.5)))
        return dot(down_ref[level, pl.ds(first, ROWS), :], hidden.astype(BF)) + wide(down_bias_ref[level], block)

    return branch


def cell_weights(weight_ref):
    lane = lane_ids((ROWS, FINE_IN))
    odd_row = (lane // TILE) % 2
    odd_col = (lane % TILE) % 2
    kind = 2 * odd_row + odd_col
    result = jnp.zeros((ROWS, FINE_IN), F32)
    for k in range(4):
        result = jnp.where(kind == k, weight_ref[:, k : k + 1], result)
    return result


def make_mix_fine(count):
    def mix_fine(
        tab_ref, own_ref, p1_ref, p2_ref, p3_ref, x_ref, mask_ref,
        gain_ref, shift_ref, up_ref, up_bias_ref, down_ref, down_bias_ref, scale_ref, pool_cells_ref, pool_ref, pack_ref,
        fine_ref, pooled_ref, small_mask_ref, msg_ref, cat_ref, mains_ref, rest_ref,
    ):
        gather_rows((own_ref, p1_ref, p2_ref, p3_ref), cat_ref)
        block = 768
        branch = make_branch(0, cat_ref, gain_ref, shift_ref, up_ref, up_bias_ref, down_ref, down_bias_ref, block)
        scale = wide(scale_ref[0], block)

        for start in range(0, TILE * TILE, block):
            here = slice(start, start + block)
            value = x_ref[0, :, here].astype(F32) + scale * branch(start)
            fine_ref[:, here] = (mask_ref[:, here].astype(F32) * value).astype(BF)

        weights = pool_cells_ref[...]
        highs, lows, masks = [], [], []
        for i in range(GROUPS):
            lanes = slice(i * FINE_IN, (i + 1) * FINE_IN)
            product = fine_ref[:, lanes].astype(F32) * weights
            high = product.astype(BF)
            highs.append(high)
            lows.append((product - high.astype(F32)).astype(BF))
            masks.append(jnp.broadcast_to(mask_ref[:, lanes].astype(F32), (8, FINE_IN)))
        pool_table = pool_ref[...]
        pooled = dot(jnp.concatenate(highs, axis=0), pool_table) + dot(jnp.concatenate(lows, axis=0), pool_table)
        pooled = pooled.astype(BF)
        for i in range(GROUPS):
            pooled_ref[:, i * 128 : (i + 1) * 128] = pooled[i * ROWS : (i + 1) * ROWS]
        counts = dot(jnp.concatenate(masks, axis=0).astype(BF), pool_table)
        small_mask_ref[...] = jnp.where(counts > 0.5, 1.0, 0.0)

        packed = dot(pooled_ref[...], pack_ref[...])
        lane = lane_ids((ROWS, 128))
        blocks = (packed[:, 0:128], packed[:, 128:256])
        for r in range(2):
            for c in range(2):
                mains_ref[2 * r + c] = jnp.where(lane < 72, blocks[r], blocks[c]).astype(BF)
        lane = lane_ids((16, 128))
        for c in range(2):
            rest = packed[:, 256:384]
            rest = pltpu.roll(rest, 64, 1) if c else rest
            parts = [rest[0:16], pltpu.roll(rest[16:32], 24, 1), pltpu.roll(rest[32:48], 48, 1)]
            joined = jnp.where(lane < 24, parts[0], jnp.where(lane < 48, parts[1], parts[2]))
            rest_ref[c] = jnp.where(lane < 72, joined, 0.0).astype(BF)

        def fill(dev, carry):
            both = tab_ref[16 + dev]
            col_pick = lax.rem(both, 2)
            for g in range(3):
                msg_ref[dev, :, 128 * g : 128 * g + 128] = mains_ref[both, 16 * g : 16 * g + 16, :]
            msg_ref[dev, :, 384:512] = rest_ref[col_pick]
            return carry

        scan_tiles(count, fill, jnp.int32(0))

    return mix_fine


def mix_coarse(
    own_ref, p1_ref, p2_ref, p3_ref, pooled_ref, small_mask_ref, fine_ref, mask_ref, gain_ref, shift_ref, up_ref, up_bias_ref,
    down_ref, down_bias_ref, scale_ref, spread_cells_ref, pool_ref, out_ref, cat_ref,
):
    gather_rows((own_ref, p1_ref, p2_ref, p3_ref), cat_ref)
    cells = cat_ref.shape[1]
    branch = make_branch(1, cat_ref, gain_ref, shift_ref, up_ref, up_bias_ref, down_ref, down_bias_ref, cells)
    value = pooled_ref[...].astype(F32) + wide(scale_ref[1], cells) * branch(0)
    parts = []
    for i in range(GROUPS):
        parts.append((small_mask_ref[8 * i : 8 * i + 1, :] * value[:, 128 * i : 128 * i + 128]).astype(BF))
    spread = lax.dot_general(
        jnp.concatenate(parts, axis=0), pool_ref[...], (((1,), (1,)), ((), ())), preferred_element_type=F32
    )
    weights = spread_cells_ref[...]
    for i in range(GROUPS):
        lanes = slice(i * FINE_IN, (i + 1) * FINE_IN)
        merged = fine_ref[:, lanes].astype(F32) + weights * spread[i * ROWS : (i + 1) * ROWS]
        out_ref[0, :, lanes] = (mask_ref[:, lanes].astype(F32) * merged).astype(BF)


VMEM = pl.BlockSpec(memory_space=pltpu.VMEM)
SMEM = pl.BlockSpec(memory_space=pltpu.SMEM)

def takes(microseconds):
    return pl.CostEstimate(flops=microseconds * 1_000_000_000, bytes_accessed=0, transcendentals=0)


def shaped(*shape, dtype=BF):
    return jax.ShapeDtypeStruct(shape, dtype)


PARAMS = pltpu.CompilerParams(vmem_limit_bytes=24 * 1024 * 1024)


def every_channel(own, beside_work=lambda own: ()):
    pairs = lambda bit: [(i, i ^ bit) for i in range(4)]
    across = lax.ppermute(own, "chan", pairs(2))
    beside = lax.ppermute(own, "chan", pairs(1))
    across, *results = lax.optimization_barrier((across, *beside_work(own)))
    diagonal = lax.ppermute(across, "chan", pairs(1))
    return (own, beside, across, diagonal), results


def per_device(
    features, land_mask, wet_slots, device_of, depth_weight, depth_bias, norm_gain, norm_bias, up_weight, up_bias,
    down_weight, down_bias, layer_scale, pool_weight, spread_weight,
):
    count = wet_slots.shape[0]
    grid_x = 2 * count // GRID_Y
    cells = TILE * TILE
    pack = pl.pallas_call(
        strip_table, out_specs=VMEM, out_shape=shaped(FINE_IN, 256), compiler_params=PARAMS, cost_estimate=takes(2), name="strip_table"
    )()
    messages, table = pl.pallas_call(
        make_prep(grid_x),
        in_specs=[SMEM, SMEM, VMEM, VMEM],
        out_specs=[VMEM, SMEM],
        out_shape=[shaped(count, 16, 896), shaped(16 + count, dtype=jnp.int32)],
        scratch_shapes=[
            pltpu.VMEM((2, ROWS, 128), BF),
            pltpu.VMEM((2, ROWS, 128), BF),
            pltpu.VMEM((2, 16, 128), F32),
            pltpu.VMEM((2, 16, 128), F32),
        ],
        compiler_params=PARAMS,
        cost_estimate=takes(10),
        name="prep",
    )(wet_slots, device_of, features, pack)
    held = {
        "x": features,
        "mask": land_mask,
        "weight": depth_weight,
        "bias": depth_bias,
        "small_halo": jnp.asarray(COARSE["halo"]),
        "sides": jnp.asarray(COARSE["sides"]),
        "pool": jnp.asarray(POOL),
        "small_pack": jnp.asarray(COARSE["pack"]),
    }
    arrived = lax.all_to_all(messages, "tile", 0, 0, tiled=True)
    inner = pl.pallas_call(
        lambda tab_ref, *refs: conv_inner(*refs),
        in_specs=[SMEM] + [VMEM] * 3,
        out_specs=VMEM,
        out_shape=shaped(ROWS, cells, dtype=F32),
        scratch_shapes=[
            pltpu.VMEM((ROWS, 3584), F32),
            pltpu.VMEM((ROWS, 3584), F32),
            pltpu.VMEM((49, ROWS, 128), F32),
            pltpu.VMEM((ROWS, 3072), F32),
        ],
        compiler_params=PARAMS,
        cost_estimate=takes(4),
        name="conv_inner",
    )(table, held["x"], held["weight"], held["bias"])
    conv = pl.pallas_call(
        conv_border,
        in_specs=[SMEM] + [VMEM] * 3,
        out_specs=VMEM,
        out_shape=shaped(ROWS, cells),
        scratch_shapes=[pltpu.VMEM((ROWS, 128), F32)],
        compiler_params=PARAMS,
        cost_estimate=takes(2),
        name="conv_border",
    )(table, arrived, inner, held["weight"])

    def spread_params(own):
        return pl.pallas_call(
            params,
            in_specs=[VMEM] * 11,
            out_specs=[VMEM] * 10,
            out_shape=[
                shaped(*shape, dtype=dtype)
                for shape, dtype in (
                    ((49, ROWS, 128), F32), ((ROWS, 128), F32), ((2, 192, 128), F32), ((2, 192, 128), F32), (up_weight.shape, BF),
                    ((2, 768, 128), F32), ((2, ROWS, 128), F32), ((2, ROWS, 128), F32), ((ROWS, FINE_IN), F32), ((ROWS, FINE_IN), F32),
                )
            ],
            compiler_params=PARAMS,
            cost_estimate=takes(2),
            name="params",
        )(
            own, depth_weight, depth_bias, norm_gain, norm_bias, jnp.swapaxes(up_weight, 1, 2), up_bias, down_bias, layer_scale,
            pool_weight, spread_weight,
        )

    pieces, results = every_channel(conv, spread_params)
    taps, conv_bias, gains, shifts, ups, up_biases, down_biases, scales, pool_cells, spread_cells = results
    fine, pooled, small_mask, messages = pl.pallas_call(
        make_mix_fine(count),
        in_specs=[SMEM] + [VMEM] * 16,
        out_specs=[VMEM] * 4,
        out_shape=[shaped(ROWS, cells), shaped(ROWS, 768), shaped(48, 128, dtype=F32), shaped(count, 16, 512)],
        scratch_shapes=[
            pltpu.VMEM((4 * ROWS, cells), BF),
            pltpu.VMEM((4, ROWS, 128), BF),
            pltpu.VMEM((2, 16, 128), BF),
        ],
        compiler_params=PARAMS,
        cost_estimate=takes(4),
        name="mix_fine",
    )(
        table, *pieces, held["x"], held["mask"], gains, shifts, ups, up_biases,
        down_weight, down_biases, scales, pool_cells, held["pool"], held["small_pack"],
    )
    arrived = lax.all_to_all(messages, "tile", 0, 0, tiled=True)
    conv = pl.pallas_call(
        conv_coarse,
        in_specs=[SMEM] + [VMEM] * 6,
        out_specs=VMEM,
        out_shape=shaped(ROWS, 768),
        scratch_shapes=[pltpu.VMEM((4, ROWS, 1024), F32), pltpu.VMEM((ROWS, 768), F32)],
        compiler_params=PARAMS,
        cost_estimate=takes(2),
        name="conv_coarse",
    )(table, pooled, arrived, held["small_halo"], held["sides"], taps, conv_bias)
    pieces, _ = every_channel(conv)
    return pl.pallas_call(
        mix_coarse,
        in_specs=[VMEM] * 17,
        out_specs=VMEM,
        out_shape=shaped(1, ROWS, cells),
        scratch_shapes=[pltpu.VMEM((4 * ROWS, 768), BF)],
        compiler_params=PARAMS,
        cost_estimate=takes(2),
        name="mix_coarse",
    )(
        *pieces, pooled, small_mask, fine, held["mask"], gains, shifts, ups, up_biases, down_weight, down_biases,
        scales, spread_cells, held["pool"],
    )


def solution(mesh):
    placed = (
        P("tile", "chan", None),
        P("tile", None),
        P(),
        P(),
        P(None, "chan", None),
        P(None, "chan"),
        P(),
        P(),
        P(),
        P(),
        P(),
        P(),
        P(None, "chan"),
        P("chan", None),
        P("chan", None),
    )
    return jax.shard_map(
        per_device, mesh=mesh, in_specs=placed, out_specs=P("tile", "chan", None), check_vma=False
    )
```

```python
import jax
import jax.numpy as jnp
import ml_dtypes
import numpy as np
from jax import lax
from jax.experimental import pallas as pl
from jax.experimental.pallas import tpu as pltpu
from jax.sharding import PartitionSpec as P

TILE = 48
HALF = TILE // 2
GRID_Y = 4
GROUPS = 6
ROWS = 48
FINE_IN = 8 * TILE
FINE_PAD = 8 * 64
BANDS = ((-1, -1), (-1, 0), (-1, 1), (0, -1), (0, 1), (1, -1), (1, 0), (1, 1))
norm_eps = 1e-06
BF = jnp.bfloat16
F32 = jnp.float32


def one_hot(shape, pairs):
    table = np.zeros(shape, np.float32)
    for source, target in pairs:
        table[source, target] = 1.0
    return table.astype(ml_dtypes.bfloat16)


def side_target(side, row, col, width, stride):
    if side == 0:
        return row * stride + 3 + col
    if side == -1:
        return row * stride + col - (width - 3) if col >= width - 3 else None
    return row * stride + 3 + width + col if col < 3 else None


def halo_pairs(cells, width, stride, first_row, flipped):
    block = max(lane for lane, _ in cells) // 128 * 128 + 128
    pairs = []
    for place, side in enumerate((-1, 0, 1)):
        for lane, index in cells:
            row, col = index // width, index % width
            if flipped:
                row, col = 2 - row, width - 1 - col
            target = side_target(side, row + first_row, col, width, stride)
            if target is not None:
                pairs.append((place * block + lane, target))
    return pairs


def pool_table():
    pairs = [(row * 48 + col, (row // 2) * 32 + 3 + col // 2) for row in range(8) for col in range(48)]
    return one_hot((384, 128), pairs)


def coarse_tables():
    strip = [(t, t) for t in range(72)]
    halo = np.stack(
        [
            one_hot((384, 128), halo_pairs(strip, HALF, 32, 1, False)),
            one_hot((384, 128), halo_pairs(strip, HALF, 32, 0, False)),
            one_hot((384, 128), halo_pairs(strip, HALF, 32, 0, True)),
        ]
    )
    pack, sides = [], []
    for row in range(3):
        for col in range(HALF):
            pack.append((row * 32 + 3 + col, row * 24 + col))
            pack.append(((21 + row) * 32 + 3 + col, 128 + row * 24 + col))
    for row in range(HALF):
        for j in range(3):
            index = row * 3 + j
            lane = 72 + index if row < 16 else index - 48
            pack.append((row * 32 + 3 + j, lane if row < 16 else 256 + lane))
            pack.append((row * 32 + 24 + j, 128 + lane if row < 16 else 256 + 64 + lane))
            sides.append((lane, row * 32 + j))
            sides.append((128 + lane, row * 32 + 27 + j))
    return {
        "halo": halo,
        "pack": one_hot((768, 384), pack),
        "sides": one_hot((256, 768), sides),
    }


POOL = pool_table()
COARSE = coarse_tables()


def dot(left, right):
    return jnp.dot(left, right, preferred_element_type=F32)


def stacked(value, width):
    return jnp.concatenate([value[:, i * width : (i + 1) * width] for i in range(GROUPS)], axis=0)


def lane_ids(shape):
    return lax.broadcasted_iota(jnp.int32, shape, 1)


def three_terms(row):
    high = row.astype(BF)
    rest = row - high.astype(F32)
    middle = rest.astype(BF)
    low = (rest - middle.astype(F32)).astype(BF)
    return jnp.concatenate([high, middle, low, jnp.zeros((13, row.shape[1]), BF)], axis=0)


def columns(row):
    return lax.dot_general(
        three_terms(row), jnp.ones((16, 128), BF), (((0,), (0,)), ((), ())), preferred_element_type=F32
    )


def wide(block, lanes):
    return jnp.concatenate([block] * (lanes // 128), axis=1)


def scan_tiles(count, step, carry):
    if count <= 16:
        for k in range(count):
            carry = step(k, carry)
        return carry
    return lax.fori_loop(0, count, step, carry)


def strip_table(pack_ref):
    shape = (FINE_IN, 256)
    source = lax.broadcasted_iota(jnp.int32, shape, 0)
    lane = lane_ids(shape)
    within = lane % 128
    wanted = (within // 3) * TILE + within % 3 + jnp.where(lane >= 128, TILE - 3, 0)
    pack_ref[...] = jnp.where((within < 24) & (source == wanted), 1.0, 0.0).astype(BF)


def quotient(value, divisor):
    if divisor & (divisor - 1) == 0:
        return lax.shift_right_logical(value, jnp.int32(divisor.bit_length() - 1))
    return lax.div(value, divisor)


def remainder(value, divisor):
    if divisor & (divisor - 1) == 0:
        return lax.bitwise_and(value, jnp.int32(divisor - 1))
    return lax.rem(value, divisor)


def make_prep(grid_x):
    def prep(slots_ref, dev_ref, x_ref, pack_ref, msg_ref, tab_ref, rows_ref, cols_ref, row_rest_ref, col_rest_ref):
        count = slots_ref.shape[0]
        me = lax.axis_index("tile")
        my_slot = scan_tiles(count, lambda k, c: c + jnp.where(dev_ref[k] == me, slots_ref[k], 0), jnp.int32(0))
        my_x = remainder(my_slot, grid_x)
        my_y = quotient(my_slot, grid_x)
        wanted = []
        for up_by, right_by in BANDS:
            near_x = remainder(my_x + (right_by + grid_x), grid_x)
            near_y = my_y + up_by
            folded = near_y >= GRID_Y
            from_x = jnp.where(folded, grid_x - 1 - near_x, near_x)
            from_y = jnp.where(folded, GRID_Y - 1, near_y)
            wanted.append(from_y * grid_x + from_x)

        def find(k, found):
            slot, dev = slots_ref[k], dev_ref[k]
            row_pick = jnp.where(quotient(slot, grid_x) + 1 == my_y, 0, 1)
            col_pick = jnp.where(remainder(slot, grid_x) == remainder(my_x + (grid_x - 1), grid_x), 0, 1)
            tab_ref[16 + dev] = 2 * row_pick + col_pick
            return tuple(jnp.where(slot == want, dev, old) for want, old in zip(wanted, found))

        found = scan_tiles(count, find, tuple(jnp.int32(-1) for _ in BANDS))
        for band in range(8):
            tab_ref[band] = found[band]
        tab_ref[8] = jnp.where(my_y == GRID_Y - 1, 2, 1)
        for spare in range(9, 16):
            tab_ref[spare] = 0

        x = x_ref[0]
        cols = dot(stacked(x, FINE_IN), pack_ref[...])
        lane = lane_ids((ROWS, 128))
        for side in range(2):
            part = cols[:, side * 128 : side * 128 + 128]
            main = part[0:ROWS]
            for i in range(1, 5):
                main = main + pltpu.roll(part[i * ROWS : (i + 1) * ROWS], 24 * i, 1)
            cols_ref[side] = main.astype(BF)
            rest = pltpu.roll(part[5 * ROWS : 6 * ROWS], 16, 1)
            col_rest_ref[side] = rest[0:16] + pltpu.roll(rest[16:32], 40, 1) + pltpu.roll(rest[32:48], 80, 1)
        rows_ref[0] = x[:, 0:128]
        rows_ref[1] = x[:, 2176:2304]
        ends = (x[:, 128:256].astype(F32), pltpu.roll(x[:, 2048:2176].astype(F32), 16, 1))
        for side in range(2):
            rest = jnp.where(lane < 16, ends[side], 0.0)
            row_rest_ref[side] = rest[0:16] + pltpu.roll(rest[16:32], 40, 1) + pltpu.roll(rest[32:48], 80, 1)

        def fill(dev, carry):
            row_pick = quotient(tab_ref[16 + dev], 2)
            col_pick = remainder(tab_ref[16 + dev], 2)
            for g in range(3):
                msg_ref[dev, :, 256 * g : 256 * g + 128] = rows_ref[row_pick, 16 * g : 16 * g + 16, :]
                msg_ref[dev, :, 256 * g + 128 : 256 * g + 256] = cols_ref[col_pick, 16 * g : 16 * g + 16, :]
            msg_ref[dev, :, 768:896] = (row_rest_ref[row_pick] + col_rest_ref[col_pick]).astype(BF)
            return carry

        scan_tiles(count, fill, jnp.int32(0))

    return prep


def band_source(tab_ref, band):
    source = tab_ref[band]
    return jnp.maximum(source, 0), jnp.where(source >= 0, 1.0, 0.0).astype(F32)


def lane_shifted(value, lanes):
    return pltpu.roll(value, value.shape[1] - lanes, 1)


def tall(row_block):
    return jnp.concatenate([row_block] * (ROWS // 8), axis=0)


def lanes_from(value, index):
    return jnp.take_along_axis(value, index, axis=1)


def conv_inner(x_ref, weight_ref, bias_ref, sum_ref, wide_ref, pad_ref, odd_ref, total_ref):
    for tap in range(49):
        wide_ref[tap] = jnp.broadcast_to(weight_ref[0, :, tap : tap + 1], (ROWS, 128))
    pad_ref[:, 0:256] = jnp.zeros((ROWS, 256), F32)
    pad_ref[:, 3328:3584] = jnp.zeros((ROWS, 256), F32)
    lane = lane_ids((8, 128))
    half, within = lane // 64, lane % 64
    valid = tall((within >= 3) & (within < 51))
    col = jnp.clip(within - 3, 0, 47)
    cells = [96 * k + 48 * half + col for k in range(4)]
    indices = [tall(cell % 128) for cell in cells]
    for i in range(GROUPS):
        tiles = [x_ref[0, :, 384 * i + 128 * m : 384 * i + 128 * m + 128].astype(F32) for m in range(3)]
        for k in range(4):
            first, final = (96 * k) // 128, (96 * k + 95) // 128
            value = lanes_from(tiles[first], indices[k])
            if final != first:
                value = jnp.where(tall(cells[k] < 128 * final), value, lanes_from(tiles[final], indices[k]))
            start = 256 + 512 * i + 128 * k
            pad_ref[:, start : start + 128] = jnp.where(valid, value, 0.0)
    odd_ref[...] = lane_shifted(pad_ref[...], 64)
    total_ref[...] = wide(columns(bias_ref[0:1, :]), 3072)

    def group(g, carry):
        here = pl.ds(pl.multiple_of(g * 8, 8), 8)
        for chunk in range(6):
            base = chunk * 512
            taken = []
            for a in range(1, 8):
                ref = odd_ref if a % 2 else pad_ref
                start = base + (a // 2) * 128
                taken.append([ref[here, start + 128 * j : start + 128 * j + 128] for j in range(4)])
            total = [total_ref[here, base + 128 * j : base + 128 * j + 128] for j in range(4)]
            for b in range(7):
                weights = [wide_ref[a * 7 + b, here, :] for a in range(7)]
                for j in range(4):
                    partial = weights[0] * taken[0][j]
                    for a in range(1, 7):
                        partial = partial + weights[a] * taken[a][j]
                    total[j] = total[j] + (pltpu.roll(partial, (3 - b) % 128, 1) if b != 3 else partial)
            for j in range(4):
                total_ref[here, base + 128 * j : base + 128 * j + 128] = total[j]
        return carry

    lax.fori_loop(0, ROWS // 8, group, 0)
    cells = [128 * m + lane for m in range(3)]
    indices = [tall((cell // 48) % 2 * 64 + 3 + cell % 48) for cell in cells]
    for i in range(GROUPS):
        tiles = [total_ref[:, 512 * i + 128 * k : 512 * i + 128 * k + 128] for k in range(4)]
        for m in range(3):
            value = jnp.where(
                tall(cells[m] < 96 * (m + 1)), lanes_from(tiles[m], indices[m]), lanes_from(tiles[m + 1], indices[m])
            )
            sum_ref[:, 384 * i + 128 * m : 384 * i + 128 * m + 128] = value


def conv_border(tab_ref, recv_ref, sum_ref, wide_ref, out_ref):
    lane = lane_ids((8, 128))
    half, within = lane // 64, lane % 64
    low_half = tall(lane < 64)

    def tap(a, b):
        return wide_ref[a * 7 + b]

    def band_cells(band, offset):
        source, scale = band_source(tab_ref, band)
        main = jnp.concatenate([recv_ref[source, :, 256 * g + offset : 256 * g + offset + 128] for g in range(3)], axis=0)
        rest = recv_ref[source, :, 768:896].astype(F32) * scale
        rest = jnp.concatenate([rest, pltpu.roll(rest, 128 - 40, 1), pltpu.roll(rest, 128 - 80, 1)], axis=0)
        return main.astype(F32) * scale, rest

    def halo_rows(bands, folded, last):
        left, middle, right = [band_cells(band, 0) for band in bands]
        tiles = []
        for first_row in (0, 2):
            row = first_row + half
            col = jnp.where(within < 3, 45 + within, jnp.where(within < 51, within - 3, within - 51))
            index = row * 48 + col
            index = jnp.where(folded, 143 - index, index)
            in_main = index - jnp.where(last, 16, 0)
            rest = (in_main < 0) | (in_main > 127)
            in_rest = jnp.where(in_main < 0, in_main + 16, in_main - 128)
            main_index, rest_index = tall(in_main & 127), tall(in_rest & 127)
            picked = [jnp.where(tall(rest), lanes_from(r, rest_index), lanes_from(m, main_index)) for m, r in (left, middle, right)]
            value = jnp.where(tall(within < 3), picked[0], jnp.where(tall(within < 51), picked[1], picked[2]))
            tiles.append(jnp.where(tall((within < 54) & (row < 3)), value, 0.0))
        return tiles

    def row_fix(uses):
        total = [jnp.zeros((ROWS, 128), F32)] * 2
        for b in range(7):
            partial = [None, None]
            for place, a, cells in uses:
                term = tap(a, b) * cells
                partial[place] = term if partial[place] is None else partial[place] + term
            for place in range(2):
                total[place] = total[place] + (pltpu.roll(partial[place], (3 - b) % 128, 1) if b != 3 else partial[place])
        return total

    def joined(first, second):
        return jnp.where(low_half, pltpu.roll(first, 64, 1), pltpu.roll(second, 64, 1))

    zeros = jnp.zeros((ROWS, 128), F32)
    below = halo_rows((0, 1, 2), False, True)
    first_fix = row_fix(((0, 0, below[0]), (0, 1, joined(below[0], below[1])), (0, 2, below[1]), (1, 0, below[1])))
    folded = tab_ref[8] == 2
    above = halo_rows((5, 6, 7), folded, folded)
    edge = joined(zeros, above[0])
    last_fix = row_fix(((0, 6, edge), (1, 4, edge), (1, 5, above[0]), (1, 6, joined(above[0], above[1]))))

    left, right = band_cells(3, 128), band_cells(4, 128)
    beside = []
    for j in range(3):
        which = jnp.where(half == 0, j, 2 - j)
        in_main = jnp.minimum(3 * within + which, 127)
        main_index, rest_index = tall(in_main), tall(jnp.clip(3 * (within - 40) + 16 + which, 0, 127))
        picked = [
            jnp.where(tall(within < 40), lanes_from(main, main_index), lanes_from(rest, rest_index)) for main, rest in (left, right)
        ]
        beside.append(jnp.where(tall(within < 48), jnp.where(low_half, picked[0], picked[1]), 0.0))
    column_fix = [zeros] * 3
    for a in range(7):
        weights = [jnp.where(low_half, tap(a, b), tap(a, 6 - b)) for b in range(3)]
        for q in range(3):
            partial = weights[0] * beside[q]
            for j in range(q + 1, 3):
                partial = partial + weights[j - q] * beside[j]
            column_fix[q] = column_fix[q] + (pltpu.roll(partial, (3 - a) % 128, 1) if a != 3 else partial)

    for m in range(TILE * TILE // 128):
        cell = 128 * m + lane
        row, col = cell // 48, cell % 48
        index = tall(jnp.where(col < 24, row, 64 + row))
        value = sum_ref[:, 128 * m : 128 * m + 128]
        fix = zeros
        for q in range(3):
            fix = jnp.where(tall((col == q) | (col == 47 - q)), lanes_from(column_fix[q], index), fix)
        value = value + fix
        row_index = tall(row % 2 * 64 + 3 + col)
        for pair, tile in ((0, first_fix[0]), (1, first_fix[1]), (22, last_fix[0]), (23, last_fix[1])):
            if 96 * pair < 128 * m + 128 and 96 * pair + 96 > 128 * m:
                value = value + jnp.where(tall(row // 2 == pair), lanes_from(tile, row_index), 0.0)
        out_ref[:, 128 * m : 128 * m + 128] = value.astype(BF)


def params(
    after_ref, weight_ref, bias_ref, gain_ref, shift_ref, up_ref, up_bias_ref, down_bias_ref, scale_ref, pool_weight_ref, spread_weight_ref,
    taps_ref, conv_bias_ref, gains_ref, shifts_ref, ups_ref, down_biases_ref, scales_ref, pool_cells_ref, spread_cells_ref,
):
    for tap in range(49):
        taps_ref[tap] = jnp.broadcast_to(weight_ref[1, :, tap : tap + 1], (ROWS, 128))
    conv_bias_ref[...] = columns(bias_ref[1:2, :])
    me = lax.axis_index("chan")
    for level in range(2):
        row = slice(level, level + 1)
        ups_ref[level] = jnp.transpose(jnp.concatenate([up_ref[level], three_terms(up_bias_ref[row, :])], axis=0), (1, 0))
        gains_ref[level] = columns(gain_ref[row, :])
        shifts_ref[level] = columns(shift_ref[row, :])
        scales_ref[level] = columns(scale_ref[row, :])
        down_bias = columns(down_bias_ref[row, :])
        own = down_bias[0:ROWS]
        for k in range(1, down_bias.shape[0] // ROWS):
            own = jnp.where(me == k, down_bias[k * ROWS : (k + 1) * ROWS], own)
        down_biases_ref[level] = own
    pool_cells_ref[...] = cell_weights(pool_weight_ref)
    spread_cells_ref[...] = cell_weights(spread_weight_ref)


def conv_coarse(tab_ref, x_ref, recv_ref, halo_ref, sides_ref, wide_ref, bias_ref, out_ref, pad_ref, sum_ref):
    lane = lane_ids((ROWS, 128))

    def main_of(source, scale):
        parts = [recv_ref[source, :, 128 * g : 128 * g + 128] for g in range(3)]
        return jnp.concatenate(parts, axis=0).astype(F32) * scale

    def row_strips(bands):
        pieces = []
        for band in bands:
            source, scale = band_source(tab_ref, band)
            pieces.append(main_of(source, scale).astype(BF))
        return jnp.concatenate(pieces, axis=1)

    pad_ref[0, :, 0:128] = dot(row_strips((0, 1, 2)), halo_ref[0])
    pad_ref[0, :, 896:1024] = dot(row_strips((5, 6, 7)), halo_ref[tab_ref[8]])
    pieces = []
    for band in (3, 4):
        source, scale = band_source(tab_ref, band)
        rest = recv_ref[source, :, 384:512].astype(F32) * scale
        rest = jnp.concatenate([rest, pltpu.roll(rest, 128 - 24, 1), pltpu.roll(rest, 128 - 48, 1)], axis=0)
        main = main_of(source, scale)
        pieces.append(jnp.where(lane < 24, rest, main).astype(BF))
    pad_ref[0, :, 128:896] = dot(jnp.concatenate(pieces, axis=1), sides_ref[...]) + x_ref[...].astype(F32)
    padded = pad_ref[0]
    for turn in range(1, 4):
        pad_ref[turn] = lane_shifted(padded, 32 * turn)
    sum_ref[...] = wide(bias_ref[...], 768)

    def group(g, carry):
        rows = pl.ds(pl.multiple_of(g * 8, 8), 8)
        for chunk in range(2):
            base = chunk * 384
            taken = []
            for a in range(1, 8):
                start = base + (a // 4) * 128
                taken.append([pad_ref[a % 4, rows, start + 128 * j : start + 128 * j + 128] for j in range(3)])
            total = [sum_ref[rows, base + 128 * j : base + 128 * j + 128] for j in range(3)]
            for b in range(7):
                weights = [wide_ref[a * 7 + b, rows, :] for a in range(7)]
                for j in range(3):
                    partial = weights[0] * taken[0][j]
                    for a in range(1, 7):
                        partial = partial + weights[a] * taken[a][j]
                    total[j] = total[j] + (pltpu.roll(partial, (3 - b) % 128, 1) if b != 3 else partial)
            for j in range(3):
                sum_ref[rows, base + 128 * j : base + 128 * j + 128] = total[j]
        return carry

    lax.fori_loop(0, 6, group, 0)
    out_ref[...] = sum_ref[...].astype(BF)


def gather_rows(pieces, cat_ref):
    me = lax.axis_index("chan")
    for k, piece in enumerate(pieces):
        first = pl.multiple_of(lax.bitwise_xor(me, k) * ROWS, 16)
        cat_ref[pl.ds(first, ROWS), :] = piece[...]


def make_branch(level, cat_ref, gain_ref, shift_ref, up_ref, down_ref, down_bias_ref, block):
    first = pl.multiple_of(lax.axis_index("chan") * ROWS, 16)
    gain, shift = wide(gain_ref[level], block), wide(shift_ref[level], block)

    def branch(start):
        values = cat_ref[:, pl.ds(start, block)].astype(F32)
        mean = jnp.mean(values, axis=0, keepdims=True)
        centred = values - mean
        spread = jnp.mean(centred * centred, axis=0, keepdims=True)
        normed = (centred * lax.rsqrt(spread + norm_eps) * gain + shift).astype(BF)
        hidden = dot(up_ref[level], jnp.concatenate([normed, jnp.ones((16, block), BF)], axis=0))
        hidden = 0.5 * hidden * (1.0 + lax.erf(hidden * np.float32(0.5**0.5)))
        return dot(down_ref[level, pl.ds(first, ROWS), :], hidden.astype(BF)) + wide(down_bias_ref[level], block)

    return branch


def cell_weights(weight_ref):
    lane = lane_ids((ROWS, FINE_IN))
    odd_row = (lane // TILE) % 2
    odd_col = (lane % TILE) % 2
    kind = 2 * odd_row + odd_col
    result = jnp.zeros((ROWS, FINE_IN), F32)
    for k in range(4):
        result = jnp.where(kind == k, weight_ref[:, k : k + 1], result)
    return result


def make_mix_fine(count):
    def mix_fine(
        tab_ref, own_ref, p1_ref, p2_ref, p3_ref, x_ref, mask_ref,
        gain_ref, shift_ref, up_ref, down_ref, down_bias_ref, scale_ref, pool_cells_ref, pool_ref, pack_ref,
        fine_ref, pooled_ref, small_mask_ref, msg_ref, cat_ref, mains_ref, rest_ref,
    ):
        gather_rows((own_ref, p1_ref, p2_ref, p3_ref), cat_ref)
        block = 768
        branch = make_branch(0, cat_ref, gain_ref, shift_ref, up_ref, down_ref, down_bias_ref, block)
        scale = wide(scale_ref[0], block)

        for start in range(0, TILE * TILE, block):
            here = slice(start, start + block)
            value = x_ref[0, :, here].astype(F32) + scale * branch(start)
            fine_ref[:, here] = (mask_ref[:, here].astype(F32) * value).astype(BF)

        weights = pool_cells_ref[...]
        highs, lows, masks = [], [], []
        for i in range(GROUPS):
            lanes = slice(i * FINE_IN, (i + 1) * FINE_IN)
            product = fine_ref[:, lanes].astype(F32) * weights
            high = product.astype(BF)
            highs.append(high)
            lows.append((product - high.astype(F32)).astype(BF))
            masks.append(jnp.broadcast_to(mask_ref[:, lanes].astype(F32), (8, FINE_IN)))
        pool_table = pool_ref[...]
        pooled = dot(jnp.concatenate(highs, axis=0), pool_table) + dot(jnp.concatenate(lows, axis=0), pool_table)
        pooled = pooled.astype(BF)
        for i in range(GROUPS):
            pooled_ref[:, i * 128 : (i + 1) * 128] = pooled[i * ROWS : (i + 1) * ROWS]
        counts = dot(jnp.concatenate(masks, axis=0).astype(BF), pool_table)
        small_mask_ref[...] = jnp.where(counts > 0.5, 1.0, 0.0)

        packed = dot(pooled_ref[...], pack_ref[...])
        lane = lane_ids((ROWS, 128))
        blocks = (packed[:, 0:128], packed[:, 128:256])
        for r in range(2):
            for c in range(2):
                mains_ref[2 * r + c] = jnp.where(lane < 72, blocks[r], blocks[c]).astype(BF)
        lane = lane_ids((16, 128))
        for c in range(2):
            rest = packed[:, 256:384]
            rest = pltpu.roll(rest, 64, 1) if c else rest
            parts = [rest[0:16], pltpu.roll(rest[16:32], 24, 1), pltpu.roll(rest[32:48], 48, 1)]
            joined = jnp.where(lane < 24, parts[0], jnp.where(lane < 48, parts[1], parts[2]))
            rest_ref[c] = jnp.where(lane < 72, joined, 0.0).astype(BF)

        def fill(dev, carry):
            both = tab_ref[16 + dev]
            col_pick = lax.rem(both, 2)
            for g in range(3):
                msg_ref[dev, :, 128 * g : 128 * g + 128] = mains_ref[both, 16 * g : 16 * g + 16, :]
            msg_ref[dev, :, 384:512] = rest_ref[col_pick]
            return carry

        scan_tiles(count, fill, jnp.int32(0))

    return mix_fine


def mix_coarse(
    own_ref, p1_ref, p2_ref, p3_ref, pooled_ref, small_mask_ref, fine_ref, mask_ref, gain_ref, shift_ref, up_ref,
    down_ref, down_bias_ref, scale_ref, spread_cells_ref, pool_ref, out_ref, cat_ref,
):
    gather_rows((own_ref, p1_ref, p2_ref, p3_ref), cat_ref)
    cells = cat_ref.shape[1]
    branch = make_branch(1, cat_ref, gain_ref, shift_ref, up_ref, down_ref, down_bias_ref, cells)
    value = pooled_ref[...].astype(F32) + wide(scale_ref[1], cells) * branch(0)
    parts = []
    for i in range(GROUPS):
        parts.append((small_mask_ref[8 * i : 8 * i + 1, :] * value[:, 128 * i : 128 * i + 128]).astype(BF))
    spread = lax.dot_general(
        jnp.concatenate(parts, axis=0), pool_ref[...], (((1,), (1,)), ((), ())), preferred_element_type=F32
    )
    weights = spread_cells_ref[...]
    for i in range(GROUPS):
        lanes = slice(i * FINE_IN, (i + 1) * FINE_IN)
        merged = fine_ref[:, lanes].astype(F32) + weights * spread[i * ROWS : (i + 1) * ROWS]
        out_ref[0, :, lanes] = (mask_ref[:, lanes].astype(F32) * merged).astype(BF)


VMEM = pl.BlockSpec(memory_space=pltpu.VMEM)
SMEM = pl.BlockSpec(memory_space=pltpu.SMEM)

def takes(microseconds):
    return pl.CostEstimate(flops=microseconds * 1_000_000_000, bytes_accessed=0, transcendentals=0)


def shaped(*shape, dtype=BF):
    return jax.ShapeDtypeStruct(shape, dtype)


PARAMS = pltpu.CompilerParams(vmem_limit_bytes=24 * 1024 * 1024)


def every_channel(own, beside_work=lambda own: ()):
    pairs = lambda bit: [(i, i ^ bit) for i in range(4)]
    across = lax.ppermute(own, "chan", pairs(2))
    beside = lax.ppermute(own, "chan", pairs(1))
    across, *results = lax.optimization_barrier((across, *beside_work(own)))
    diagonal = lax.ppermute(across, "chan", pairs(1))
    return (own, beside, across, diagonal), results


def per_device(
    features, land_mask, wet_slots, device_of, depth_weight, depth_bias, norm_gain, norm_bias, up_weight, up_bias,
    down_weight, down_bias, layer_scale, pool_weight, spread_weight,
):
    count = wet_slots.shape[0]
    grid_x = 2 * count // GRID_Y
    cells = TILE * TILE
    pack = pl.pallas_call(
        strip_table, out_specs=VMEM, out_shape=shaped(FINE_IN, 256), compiler_params=PARAMS, cost_estimate=takes(2), name="strip_table"
    )()
    messages, table = pl.pallas_call(
        make_prep(grid_x),
        in_specs=[SMEM, SMEM, VMEM, VMEM],
        out_specs=[VMEM, SMEM],
        out_shape=[shaped(count, 16, 896), shaped(16 + count, dtype=jnp.int32)],
        scratch_shapes=[
            pltpu.VMEM((2, ROWS, 128), BF),
            pltpu.VMEM((2, ROWS, 128), BF),
            pltpu.VMEM((2, 16, 128), F32),
            pltpu.VMEM((2, 16, 128), F32),
        ],
        compiler_params=PARAMS,
        cost_estimate=takes(10),
        name="prep",
    )(wet_slots, device_of, features, pack)
    held = {
        "x": features,
        "mask": land_mask,
        "weight": depth_weight,
        "bias": depth_bias,
        "small_halo": jnp.asarray(COARSE["halo"]),
        "sides": jnp.asarray(COARSE["sides"]),
        "pool": jnp.asarray(POOL),
        "small_pack": jnp.asarray(COARSE["pack"]),
    }
    arrived = lax.all_to_all(messages, "tile", 0, 0, tiled=True)
    inner, fine_taps = pl.pallas_call(
        lambda tab_ref, *refs: conv_inner(*refs),
        in_specs=[SMEM] + [VMEM] * 3,
        out_specs=[VMEM] * 2,
        out_shape=[shaped(ROWS, cells, dtype=F32), shaped(49, ROWS, 128, dtype=F32)],
        scratch_shapes=[
            pltpu.VMEM((ROWS, 3584), F32),
            pltpu.VMEM((ROWS, 3584), F32),
            pltpu.VMEM((ROWS, 3072), F32),
        ],
        compiler_params=PARAMS,
        cost_estimate=takes(4),
        name="conv_inner",
    )(table, held["x"], held["weight"], held["bias"])
    conv = pl.pallas_call(
        conv_border,
        in_specs=[SMEM] + [VMEM] * 3,
        out_specs=VMEM,
        out_shape=shaped(ROWS, cells),
        compiler_params=PARAMS,
        cost_estimate=takes(2),
        name="conv_border",
    )(table, arrived, inner, fine_taps)

    def spread_params(own):
        return pl.pallas_call(
            params,
            in_specs=[VMEM] * 11,
            out_specs=[VMEM] * 9,
            out_shape=[
                shaped(*shape, dtype=dtype)
                for shape, dtype in (
                    ((49, ROWS, 128), F32), ((ROWS, 128), F32), ((2, 192, 128), F32), ((2, 192, 128), F32), ((2, up_weight.shape[1], up_weight.shape[2] + 16), BF),
                    ((2, ROWS, 128), F32), ((2, ROWS, 128), F32), ((ROWS, FINE_IN), F32), ((ROWS, FINE_IN), F32),
                )
            ],
            compiler_params=PARAMS,
            cost_estimate=takes(2),
            name="params",
        )(
            own, depth_weight, depth_bias, norm_gain, norm_bias, jnp.swapaxes(up_weight, 1, 2), up_bias, down_bias, layer_scale,
            pool_weight, spread_weight,
        )

    pieces, results = every_channel(conv, spread_params)
    taps, conv_bias, gains, shifts, ups, down_biases, scales, pool_cells, spread_cells = results
    fine, pooled, small_mask, messages = pl.pallas_call(
        make_mix_fine(count),
        in_specs=[SMEM] + [VMEM] * 15,
        out_specs=[VMEM] * 4,
        out_shape=[shaped(ROWS, cells), shaped(ROWS, 768), shaped(48, 128, dtype=F32), shaped(count, 16, 512)],
        scratch_shapes=[
            pltpu.VMEM((4 * ROWS, cells), BF),
            pltpu.VMEM((4, ROWS, 128), BF),
            pltpu.VMEM((2, 16, 128), BF),
        ],
        compiler_params=PARAMS,
        cost_estimate=takes(4),
        name="mix_fine",
    )(
        table, *pieces, held["x"], held["mask"], gains, shifts, ups,
        down_weight, down_biases, scales, pool_cells, held["pool"], held["small_pack"],
    )
    arrived = lax.all_to_all(messages, "tile", 0, 0, tiled=True)
    conv = pl.pallas_call(
        conv_coarse,
        in_specs=[SMEM] + [VMEM] * 6,
        out_specs=VMEM,
        out_shape=shaped(ROWS, 768),
        scratch_shapes=[pltpu.VMEM((4, ROWS, 1024), F32), pltpu.VMEM((ROWS, 768), F32)],
        compiler_params=PARAMS,
        cost_estimate=takes(2),
        name="conv_coarse",
    )(table, pooled, arrived, held["small_halo"], held["sides"], taps, conv_bias)
    pieces, _ = every_channel(conv)
    return pl.pallas_call(
        mix_coarse,
        in_specs=[VMEM] * 16,
        out_specs=VMEM,
        out_shape=shaped(1, ROWS, cells),
        scratch_shapes=[pltpu.VMEM((4 * ROWS, 768), BF)],
        compiler_params=PARAMS,
        cost_estimate=takes(2),
        name="mix_coarse",
    )(
        *pieces, pooled, small_mask, fine, held["mask"], gains, shifts, ups, down_weight, down_biases,
        scales, spread_cells, held["pool"],
    )


def solution(mesh):
    placed = (
        P("tile", "chan", None),
        P("tile", None),
        P(),
        P(),
        P(None, "chan", None),
        P(None, "chan"),
        P(),
        P(),
        P(),
        P(),
        P(),
        P(),
        P(None, "chan"),
        P("chan", None),
        P("chan", None),
    )
    return jax.shard_map(
        per_device, mesh=mesh, in_specs=placed, out_specs=P("tile", "chan", None), check_vma=False
    )
```

```python
import jax
import jax.numpy as jnp
import ml_dtypes
import numpy as np
from jax import lax
from jax.experimental import pallas as pl
from jax.experimental.pallas import tpu as pltpu
from jax.sharding import PartitionSpec as P

TILE = 48
HALF = TILE // 2
GRID_Y = 4
GROUPS = 6
ROWS = 48
FINE_IN = 8 * TILE
RIM = 1280
MIDDLE = 1024
BANDS = ((-1, -1), (-1, 0), (-1, 1), (0, -1), (0, 1), (1, -1), (1, 0), (1, 1))
norm_eps = 1e-06
BF = jnp.bfloat16
F32 = jnp.float32


def one_hot(shape, pairs):
    table = np.zeros(shape, np.float32)
    for source, target in pairs:
        table[source, target] = 1.0
    return table.astype(ml_dtypes.bfloat16)


def pool_tables():
    dense, rim, middle = [], [], []
    for row in range(8):
        for col in range(48):
            target = (row // 2) * 32 + 3 + col // 2
            dense.append((row * 48 + col, target))
            if 8 <= col < 40:
                middle.append((row * 32 + col - 8, target))
            else:
                rim.append((row * 16 + (col if col < 8 else col - 32), target))
    return one_hot((384, 128), dense), one_hot((128, 128), rim), one_hot((256, 128), middle)


def strip_pairs():
    pack = []
    for row in range(3):
        for col in range(HALF):
            pack.append((row * 32 + 3 + col, row * 24 + col))
            pack.append(((21 + row) * 32 + 3 + col, 128 + row * 24 + col))
    for row in range(HALF):
        for j in range(3):
            index = row * 3 + j
            lane = 72 + index if row < 16 else index - 48
            pack.append((row * 32 + 3 + j, lane if row < 16 else 256 + lane))
            pack.append((row * 32 + 24 + j, 128 + lane if row < 16 else 256 + 64 + lane))
    return pack


POOL, RIM_POOL, MIDDLE_POOL = pool_tables()
SMALL_PACK = one_hot((768, 384), strip_pairs())


def dot(left, right):
    return jnp.dot(left, right, preferred_element_type=F32)


def stacked(value, width):
    return jnp.concatenate([value[:, i * width : (i + 1) * width] for i in range(GROUPS)], axis=0)


def lane_ids(shape):
    return lax.broadcasted_iota(jnp.int32, shape, 1)


def three_terms(row):
    high = row.astype(BF)
    rest = row - high.astype(F32)
    middle = rest.astype(BF)
    low = (rest - middle.astype(F32)).astype(BF)
    return jnp.concatenate([high, middle, low, jnp.zeros((13, row.shape[1]), BF)], axis=0)


def columns(row):
    return lax.dot_general(
        three_terms(row), jnp.ones((16, 128), BF), (((0,), (0,)), ((), ())), preferred_element_type=F32
    )


def wide(block, lanes):
    return jnp.concatenate([block] * (lanes // 128), axis=1)


def scan_tiles(count, step, carry):
    if count <= 16:
        for k in range(count):
            carry = step(k, carry)
        return carry
    return lax.fori_loop(0, count, step, carry)


def strip_table(pack_ref):
    shape = (FINE_IN, 256)
    source = lax.broadcasted_iota(jnp.int32, shape, 0)
    lane = lane_ids(shape)
    within = lane % 128
    wanted = (within // 3) * TILE + within % 3 + jnp.where(lane >= 128, TILE - 3, 0)
    pack_ref[...] = jnp.where((within < 24) & (source == wanted), 1.0, 0.0).astype(BF)


def quotient(value, divisor):
    if divisor & (divisor - 1) == 0:
        return lax.shift_right_logical(value, jnp.int32(divisor.bit_length() - 1))
    return lax.div(value, divisor)


def remainder(value, divisor):
    if divisor & (divisor - 1) == 0:
        return lax.bitwise_and(value, jnp.int32(divisor - 1))
    return lax.rem(value, divisor)


def make_prep(grid_x):
    def prep(slots_ref, dev_ref, x_ref, pack_ref, msg_ref, tab_ref, rows_ref, cols_ref, row_rest_ref, col_rest_ref):
        count = slots_ref.shape[0]
        me = lax.axis_index("tile")
        my_slot = scan_tiles(count, lambda k, c: c + jnp.where(dev_ref[k] == me, slots_ref[k], 0), jnp.int32(0))
        my_x = remainder(my_slot, grid_x)
        my_y = quotient(my_slot, grid_x)
        wanted = []
        for up_by, right_by in BANDS:
            near_x = remainder(my_x + (right_by + grid_x), grid_x)
            near_y = my_y + up_by
            folded = near_y >= GRID_Y
            from_x = jnp.where(folded, grid_x - 1 - near_x, near_x)
            from_y = jnp.where(folded, GRID_Y - 1, near_y)
            wanted.append(from_y * grid_x + from_x)

        def find(k, found):
            slot, dev = slots_ref[k], dev_ref[k]
            row_pick = jnp.where(quotient(slot, grid_x) + 1 == my_y, 0, 1)
            col_pick = jnp.where(remainder(slot, grid_x) == remainder(my_x + (grid_x - 1), grid_x), 0, 1)
            tab_ref[16 + dev] = 2 * row_pick + col_pick
            return tuple(jnp.where(slot == want, dev, old) for want, old in zip(wanted, found))

        found = scan_tiles(count, find, tuple(jnp.int32(-1) for _ in BANDS))
        for band in range(8):
            tab_ref[band] = found[band]
        tab_ref[8] = jnp.where(my_y == GRID_Y - 1, 2, 1)
        for spare in range(9, 16):
            tab_ref[spare] = 0

        x = x_ref[0]
        cols = dot(stacked(x, FINE_IN), pack_ref[...])
        lane = lane_ids((ROWS, 128))
        for side in range(2):
            part = cols[:, side * 128 : side * 128 + 128]
            main = part[0:ROWS]
            for i in range(1, 5):
                main = main + pltpu.roll(part[i * ROWS : (i + 1) * ROWS], 24 * i, 1)
            cols_ref[side] = main.astype(BF)
            rest = pltpu.roll(part[5 * ROWS : 6 * ROWS], 16, 1)
            col_rest_ref[side] = rest[0:16] + pltpu.roll(rest[16:32], 40, 1) + pltpu.roll(rest[32:48], 80, 1)
        rows_ref[0] = x[:, 0:128]
        rows_ref[1] = x[:, 2176:2304]
        ends = (x[:, 128:256].astype(F32), pltpu.roll(x[:, 2048:2176].astype(F32), 16, 1))
        for side in range(2):
            rest = jnp.where(lane < 16, ends[side], 0.0)
            row_rest_ref[side] = rest[0:16] + pltpu.roll(rest[16:32], 40, 1) + pltpu.roll(rest[32:48], 80, 1)

        def fill(dev, carry):
            row_pick = quotient(tab_ref[16 + dev], 2)
            col_pick = remainder(tab_ref[16 + dev], 2)
            for g in range(3):
                msg_ref[dev, :, 256 * g : 256 * g + 128] = rows_ref[row_pick, 16 * g : 16 * g + 16, :]
                msg_ref[dev, :, 256 * g + 128 : 256 * g + 256] = cols_ref[col_pick, 16 * g : 16 * g + 16, :]
            msg_ref[dev, :, 768:896] = (row_rest_ref[row_pick] + col_rest_ref[col_pick]).astype(BF)
            return carry

        scan_tiles(count, fill, jnp.int32(0))

    return prep


def band_source(tab_ref, band):
    source = tab_ref[band]
    return jnp.maximum(source, 0), jnp.where(source >= 0, 1.0, 0.0).astype(F32)


def lane_shifted(value, lanes):
    return pltpu.roll(value, value.shape[1] - lanes, 1)


def tall(row_block):
    return jnp.concatenate([row_block] * (ROWS // 8), axis=0)


def lanes_from(value, index):
    return jnp.take_along_axis(value, index, axis=1)


def conv_inner(x_ref, weight_ref, bias_ref, sum_ref, wide_ref, pad_ref, odd_ref, total_ref):
    for tap in range(49):
        wide_ref[tap] = jnp.broadcast_to(weight_ref[0, :, tap : tap + 1], (ROWS, 128))
    pad_ref[:, 0:256] = jnp.zeros((ROWS, 256), F32)
    pad_ref[:, 3328:3584] = jnp.zeros((ROWS, 256), F32)
    lane = lane_ids((8, 128))
    half, within = lane // 64, lane % 64
    valid = tall((within >= 3) & (within < 51))
    col = jnp.clip(within - 3, 0, 47)
    cells = [96 * k + 48 * half + col for k in range(4)]
    indices = [tall(cell % 128) for cell in cells]
    for i in range(GROUPS):
        tiles = [x_ref[0, :, 384 * i + 128 * m : 384 * i + 128 * m + 128].astype(F32) for m in range(3)]
        for k in range(4):
            first, final = (96 * k) // 128, (96 * k + 95) // 128
            value = lanes_from(tiles[first], indices[k])
            if final != first:
                value = jnp.where(tall(cells[k] < 128 * final), value, lanes_from(tiles[final], indices[k]))
            start = 256 + 512 * i + 128 * k
            pad_ref[:, start : start + 128] = jnp.where(valid, value, 0.0)
    odd_ref[...] = lane_shifted(pad_ref[...], 64)
    total_ref[...] = wide(columns(bias_ref[0:1, :]), 3072)

    def group(g, carry):
        here = pl.ds(pl.multiple_of(g * 8, 8), 8)
        for chunk in range(6):
            base = chunk * 512
            taken = []
            for a in range(1, 8):
                ref = odd_ref if a % 2 else pad_ref
                start = base + (a // 2) * 128
                taken.append([ref[here, start + 128 * j : start + 128 * j + 128] for j in range(4)])
            total = [total_ref[here, base + 128 * j : base + 128 * j + 128] for j in range(4)]
            for b in range(7):
                weights = [wide_ref[a * 7 + b, here, :] for a in range(7)]
                for j in range(4):
                    partial = weights[0] * taken[0][j]
                    for a in range(1, 7):
                        partial = partial + weights[a] * taken[a][j]
                    total[j] = total[j] + (pltpu.roll(partial, (3 - b) % 128, 1) if b != 3 else partial)
            for j in range(4):
                total_ref[here, base + 128 * j : base + 128 * j + 128] = total[j]
        return carry

    lax.fori_loop(0, ROWS // 8, group, 0)
    for m in range((RIM + MIDDLE) // 128):
        row, col = place_of(m)
        index = tall(row % 2 * 64 + 3 + col)
        value = None
        for pair in pairs_of(m):
            picked = lanes_from(total_ref[:, 128 * pair : 128 * pair + 128], index)
            value = picked if value is None else jnp.where(tall(row // 2 == pair), picked, value)
        sum_ref[:, 128 * m : 128 * m + 128] = value


def place_of(m):
    lane = lane_ids((8, 128))
    if m < 6:
        cell = 128 * (m % 3) + lane
        return cell // 48 + (40 if m >= 3 else 0), cell % 48
    if m < 10:
        col = lane % 16
        return 8 * (m - 5) + lane // 16, jnp.where(col < 8, col, col + 32)
    return 8 + 4 * (m - 10) + lane // 32, 8 + lane % 32


def pairs_of(m):
    if m < 6:
        first = 128 * (m % 3)
        start = 20 if m >= 3 else 0
        return range(start + first // 96, start + (first + 127) // 96 + 1)
    if m < 10:
        return range(4 * (m - 5), 4 * (m - 5) + 4)
    return range(4 + 2 * (m - 10), 6 + 2 * (m - 10))


def column_sums(beside, tap):
    low_half = tall(lane_ids((8, 128)) < 64)
    total = [jnp.zeros((ROWS, 128), F32)] * 3
    for a in range(7):
        weights = [jnp.where(low_half, tap(a, b), tap(a, 6 - b)) for b in range(3)]
        for q in range(3):
            partial = weights[0] * beside[q]
            for j in range(q + 1, 3):
                partial = partial + weights[j - q] * beside[j]
            total[q] = total[q] + (pltpu.roll(partial, (3 - a) % 128, 1) if a != 3 else partial)
    return total


def row_sums(uses, tap):
    places = 1 + max(place for place, _, _ in uses)
    total = [jnp.zeros((ROWS, 128), F32)] * places
    for b in range(7):
        partial = [None] * places
        for place, a, cells in uses:
            term = tap(a, b) * cells
            partial[place] = term if partial[place] is None else partial[place] + term
        for place in range(places):
            total[place] = total[place] + (pltpu.roll(partial[place], (3 - b) % 128, 1) if b != 3 else partial[place])
    return total


def conv_border(tab_ref, recv_ref, sum_ref, wide_ref, out_ref):
    lane = lane_ids((8, 128))
    half, within = lane // 64, lane % 64
    low_half = tall(lane < 64)

    def tap(a, b):
        return wide_ref[a * 7 + b]

    def band_cells(band, offset):
        source, scale = band_source(tab_ref, band)
        main = jnp.concatenate([recv_ref[source, :, 256 * g + offset : 256 * g + offset + 128] for g in range(3)], axis=0)
        rest = recv_ref[source, :, 768:896].astype(F32) * scale
        rest = jnp.concatenate([rest, pltpu.roll(rest, 128 - 40, 1), pltpu.roll(rest, 128 - 80, 1)], axis=0)
        return main.astype(F32) * scale, rest

    def halo_rows(bands, folded, last):
        left, middle, right = [band_cells(band, 0) for band in bands]
        tiles = []
        for first_row in (0, 2):
            row = first_row + half
            col = jnp.where(within < 3, 45 + within, jnp.where(within < 51, within - 3, within - 51))
            index = row * 48 + col
            index = jnp.where(folded, 143 - index, index)
            in_main = index - jnp.where(last, 16, 0)
            rest = (in_main < 0) | (in_main > 127)
            in_rest = jnp.where(in_main < 0, in_main + 16, in_main - 128)
            main_index, rest_index = tall(in_main & 127), tall(in_rest & 127)
            picked = [jnp.where(tall(rest), lanes_from(r, rest_index), lanes_from(m, main_index)) for m, r in (left, middle, right)]
            value = jnp.where(tall(within < 3), picked[0], jnp.where(tall(within < 51), picked[1], picked[2]))
            tiles.append(jnp.where(tall((within < 54) & (row < 3)), value, 0.0))
        return tiles

    def joined(first, second):
        return jnp.where(low_half, pltpu.roll(first, 64, 1), pltpu.roll(second, 64, 1))

    zeros = jnp.zeros((ROWS, 128), F32)
    below = halo_rows((0, 1, 2), False, True)
    first_fix = row_sums(((0, 0, below[0]), (0, 1, joined(below[0], below[1])), (0, 2, below[1]), (1, 0, below[1])), tap)
    folded = tab_ref[8] == 2
    above = halo_rows((5, 6, 7), folded, folded)
    edge = joined(zeros, above[0])
    last_fix = row_sums(((0, 6, edge), (1, 4, edge), (1, 5, above[0]), (1, 6, joined(above[0], above[1]))), tap)

    left, right = band_cells(3, 128), band_cells(4, 128)
    beside = []
    for j in range(3):
        which = jnp.where(half == 0, j, 2 - j)
        in_main = jnp.minimum(3 * within + which, 127)
        main_index, rest_index = tall(in_main), tall(jnp.clip(3 * (within - 40) + 16 + which, 0, 127))
        picked = [
            jnp.where(tall(within < 40), lanes_from(main, main_index), lanes_from(rest, rest_index)) for main, rest in (left, right)
        ]
        beside.append(jnp.where(tall(within < 48), jnp.where(low_half, picked[0], picked[1]), 0.0))
    column_fix = column_sums(beside, tap)
    fixes = {0: first_fix[0], 1: first_fix[1], 22: last_fix[0], 23: last_fix[1]}
    for m in range((RIM + MIDDLE) // 128):
        value = sum_ref[:, 128 * m : 128 * m + 128]
        if m < RIM // 128:
            row, col = place_of(m)
            index = tall(jnp.where(col < 24, row, 64 + row))
            fix = zeros
            for q in range(3):
                fix = jnp.where(tall((col == q) | (col == 47 - q)), lanes_from(column_fix[q], index), fix)
            value = value + fix
            row_index = tall(row % 2 * 64 + 3 + col)
            for pair in pairs_of(m):
                if pair in fixes:
                    value = value + jnp.where(tall(row // 2 == pair), lanes_from(fixes[pair], row_index), 0.0)
        out_ref[:, 128 * m : 128 * m + 128] = value.astype(BF)


def params(
    after_ref, x_ref, mask_ref, gain_ref, shift_ref, up_ref, up_bias_ref, down_bias_ref, scale_ref, pool_weight_ref, spread_weight_ref, pool_ref,
    cells_ref, cell_mask_ref, small_mask_ref, gains_ref, shifts_ref, ups_ref, down_biases_ref, scales_ref, pool_cells_ref, spread_cells_ref,
):
    me = lax.axis_index("chan")
    for level in range(2):
        row = slice(level, level + 1)
        ups_ref[level] = jnp.transpose(jnp.concatenate([up_ref[level], three_terms(up_bias_ref[row, :])], axis=0), (1, 0))
        gains_ref[level] = columns(gain_ref[row, :])
        shifts_ref[level] = columns(shift_ref[row, :])
        scales_ref[level] = columns(scale_ref[row, :])
        down_bias = columns(down_bias_ref[row, :])
        own = down_bias[0:ROWS]
        for k in range(1, down_bias.shape[0] // ROWS):
            own = jnp.where(me == k, down_bias[k * ROWS : (k + 1) * ROWS], own)
        down_biases_ref[level] = own
    lane = lane_ids((ROWS, FINE_IN))
    pool_cells_ref[:, 0:384] = cell_weights(pool_weight_ref, lane // 48, lane % 48)
    lane = lane_ids((ROWS, 128))
    pool_cells_ref[:, 384:512] = cell_weights(pool_weight_ref, lane // 16, lane)
    pool_cells_ref[:, 512:640] = cell_weights(pool_weight_ref, lane // 32, lane)
    lane = lane_ids((ROWS, FINE_IN))
    spread_cells_ref[...] = cell_weights(spread_weight_ref, lane // 48, lane % 48)

    masks = []
    for i in range(GROUPS):
        masks.append(jnp.broadcast_to(mask_ref[:, i * FINE_IN : (i + 1) * FINE_IN].astype(F32), (8, FINE_IN)))
    counts = dot(jnp.concatenate(masks, axis=0).astype(BF), pool_ref[...])
    small_mask_ref[...] = jnp.where(counts > 0.5, 1.0, 0.0)
    for m in range((RIM + MIDDLE) // 128):
        here = slice(128 * m, 128 * m + 128)
        if m < 6:
            source = 128 * (m if m < 3 else m + 12)
            cells_ref[:, here] = x_ref[0, :, source : source + 128]
            cell_mask_ref[:, here] = jnp.broadcast_to(mask_ref[:, source : source + 128].astype(F32), (8, 128))
            continue
        row, col = place_of(m)
        cell = row * 48 + col
        first, final = (8 * (m - 5) * 48, 8 * (m - 4) * 48 - 1) if m < 10 else ((4 * m - 32) * 48 + 8, (4 * m - 29) * 48 + 39)
        index, value, mask = cell % 128, None, None
        for tile in range(first // 128, final // 128 + 1):
            lanes = slice(128 * tile, 128 * tile + 128)
            part = lanes_from(x_ref[0, :, lanes].astype(F32), tall(index))
            mask_part = lanes_from(jnp.broadcast_to(mask_ref[:, lanes].astype(F32), (8, 128)), index)
            value = part if value is None else jnp.where(tall(cell // 128 == tile), part, value)
            mask = mask_part if mask is None else jnp.where(cell // 128 == tile, mask_part, mask)
        cells_ref[:, here] = value.astype(BF)
        cell_mask_ref[:, here] = mask


def in_rows(rim_ref, middle_ref, out_ref):
    out_ref[:, 0:FINE_IN] = rim_ref[:, 0:FINE_IN]
    out_ref[:, 5 * FINE_IN :] = rim_ref[:, FINE_IN : 2 * FINE_IN]
    for i in range(1, 5):
        rim = rim_ref[:, 768 + 128 * (i - 1) : 768 + 128 * i].astype(F32)
        middle = [middle_ref[:, 256 * (i - 1) + 128 * h : 256 * (i - 1) + 128 * h + 128].astype(F32) for h in range(2)]
        for m in range(3):
            cell = 128 * m + lane_ids((8, 128))
            row, col = cell // 48, cell % 48
            value = lanes_from(rim, tall((row * 16 + jnp.where(col < 8, col, col - 32)) & 127))
            in_middle = (col >= 8) & (col < 40)
            index = tall((row % 4 * 32 + col - 8) & 127)
            for h in range(2):
                if 192 * h < 128 * m + 128 and 192 * h + 192 > 128 * m:
                    value = jnp.where(tall(in_middle & (row // 4 == h)), lanes_from(middle[h], index), value)
            out_ref[:, i * FINE_IN + 128 * m : i * FINE_IN + 128 * m + 128] = value.astype(BF)


def conv_coarse(x_ref, weight_ref, bias_ref, sum_ref, wide_ref, pad_ref):
    for tap in range(49):
        wide_ref[tap] = jnp.broadcast_to(weight_ref[1, :, tap : tap + 1], (ROWS, 128))
    pad_ref[0, :, 0:128] = jnp.zeros((ROWS, 128), F32)
    pad_ref[0, :, 896:1024] = jnp.zeros((ROWS, 128), F32)
    pad_ref[0, :, 128:896] = x_ref[...].astype(F32)
    padded = pad_ref[0]
    for turn in range(1, 4):
        pad_ref[turn] = lane_shifted(padded, 32 * turn)
    sum_ref[...] = wide(columns(bias_ref[1:2, :]), 768)

    def group(g, carry):
        rows = pl.ds(pl.multiple_of(g * 8, 8), 8)
        for chunk in range(2):
            base = chunk * 384
            taken = []
            for a in range(1, 8):
                start = base + (a // 4) * 128
                taken.append([pad_ref[a % 4, rows, start + 128 * j : start + 128 * j + 128] for j in range(3)])
            total = [sum_ref[rows, base + 128 * j : base + 128 * j + 128] for j in range(3)]
            for b in range(7):
                weights = [wide_ref[a * 7 + b, rows, :] for a in range(7)]
                for j in range(3):
                    partial = weights[0] * taken[0][j]
                    for a in range(1, 7):
                        partial = partial + weights[a] * taken[a][j]
                    total[j] = total[j] + (pltpu.roll(partial, (3 - b) % 128, 1) if b != 3 else partial)
            for j in range(3):
                sum_ref[rows, base + 128 * j : base + 128 * j + 128] = total[j]
        return carry

    lax.fori_loop(0, 6, group, 0)


def border_coarse(tab_ref, recv_ref, sum_ref, wide_ref, out_ref):
    lane = lane_ids((8, 128))
    half, within, segment, inside = lane // 64, lane % 64, lane // 32, lane % 32

    def tap(a, b):
        return wide_ref[a * 7 + b]

    def band_main(band):
        source, scale = band_source(tab_ref, band)
        return jnp.concatenate([recv_ref[source, :, 128 * g : 128 * g + 128] for g in range(3)], axis=0).astype(F32) * scale

    def band_rest(band):
        source, scale = band_source(tab_ref, band)
        rest = recv_ref[source, :, 384:512].astype(F32) * scale
        return jnp.concatenate([rest, pltpu.roll(rest, 128 - 24, 1), pltpu.roll(rest, 128 - 48, 1)], axis=0)

    def halo_rows(bands, folded):
        col = jnp.where(inside < 3, 21 + inside, jnp.where(inside < 27, inside - 3, inside - 27))
        index = segment * 24 + col
        index = tall(jnp.where(folded, 71 - index, index) & 127)
        picked = [lanes_from(band_main(band), index) for band in bands]
        value = jnp.where(tall(inside < 3), picked[0], jnp.where(tall(inside < 27), picked[1], picked[2]))
        return jnp.where(tall((inside < 30) & (segment < 3)), value, 0.0)

    def turned(cells, lanes, kept):
        return jnp.where(tall(kept), pltpu.roll(cells, lanes, 1), 0.0)

    below = halo_rows((0, 1, 2), False)
    first_fix = row_sums(((0, 0, below), (0, 1, turned(below, 96, lane < 64)), (0, 2, turned(below, 64, lane < 32))), tap)[0]
    above = halo_rows((5, 6, 7), tab_ref[8] == 2)
    last_fix = row_sums(
        ((0, 6, turned(above, 32, lane >= 32)), (0, 5, turned(above, 64, lane >= 64)), (0, 4, turned(above, 96, lane >= 96))), tap
    )[0]
    sides = [(band_main(band), band_rest(band)) for band in (3, 4)]
    beside = []
    for j in range(3):
        which = jnp.where(half == 0, j, 2 - j)
        main_index = tall(jnp.minimum(72 + 3 * within + which, 127))
        rest_index = tall(jnp.clip(3 * (within - 16) + which, 0, 127))
        picked = [
            jnp.where(tall(within < 16), lanes_from(main, main_index), lanes_from(rest, rest_index)) for main, rest in sides
        ]
        beside.append(jnp.where(tall(within < HALF), jnp.where(tall(half == 0), picked[0], picked[1]), 0.0))
    column_fix = column_sums(beside, tap)
    for m in range(GROUPS):
        row, col = 4 * m + segment, inside - 3
        index = tall(jnp.where(col < 12, row, 64 + row))
        value = sum_ref[:, 128 * m : 128 * m + 128]
        fix = jnp.zeros((ROWS, 128), F32)
        for q in range(3):
            fix = jnp.where(tall((col == q) | (col == 23 - q)), lanes_from(column_fix[q], index), fix)
        value = value + fix
        if m == 0:
            value = value + first_fix
        if m == GROUPS - 1:
            value = value + last_fix
        out_ref[:, 128 * m : 128 * m + 128] = value.astype(BF)


def gather_rows(pieces, cat_ref):
    me = lax.axis_index("chan")
    for k, piece in enumerate(pieces):
        first = pl.multiple_of(lax.bitwise_xor(me, k) * ROWS, 16)
        cat_ref[pl.ds(first, ROWS), :] = piece[...]


def make_branch(level, cat_ref, gain_ref, shift_ref, up_ref, down_ref, down_bias_ref, block):
    first = pl.multiple_of(lax.axis_index("chan") * ROWS, 16)
    gain, shift = wide(gain_ref[level], block), wide(shift_ref[level], block)

    def branch(start):
        values = cat_ref[:, pl.ds(start, block)].astype(F32)
        mean = jnp.mean(values, axis=0, keepdims=True)
        centred = values - mean
        spread = jnp.mean(centred * centred, axis=0, keepdims=True)
        normed = (centred * lax.rsqrt(spread + norm_eps) * gain + shift).astype(BF)
        hidden = dot(up_ref[level], jnp.concatenate([normed, jnp.ones((16, block), BF)], axis=0))
        hidden = 0.5 * hidden * (1.0 + lax.erf(hidden * np.float32(0.5**0.5)))
        return dot(down_ref[level, pl.ds(first, ROWS), :], hidden.astype(BF)) + wide(down_bias_ref[level], block)

    return branch


def cell_weights(weight_ref, row, col):
    kind = 2 * (row % 2) + col % 2
    result = jnp.zeros(row.shape, F32)
    for k in range(4):
        result = jnp.where(kind == k, weight_ref[:, k : k + 1], result)
    return result


def pooled_cells(products, table):
    highs = [product.astype(BF) for product in products]
    lows = [(product - high.astype(F32)).astype(BF) for product, high in zip(products, highs)]
    return dot(jnp.concatenate(highs, axis=0), table) + dot(jnp.concatenate(lows, axis=0), table)


def make_mix_rim(count):
    def mix_rim(
        tab_ref, own_ref, p1_ref, p2_ref, p3_ref, x_ref, mask_ref, gain_ref, shift_ref, up_ref, down_ref, down_bias_ref, scale_ref,
        pool_cells_ref, pool_ref, rim_pool_ref, pack_ref,
        fine_ref, pooled_ref, msg_ref, middle_ref, cat_ref, mains_ref, rest_ref,
    ):
        me = lax.axis_index("chan")
        for k, piece in enumerate((own_ref, p1_ref, p2_ref, p3_ref)):
            here = pl.ds(pl.multiple_of(lax.bitwise_xor(me, k) * ROWS, 16), ROWS)
            cat_ref[here, :] = piece[:, 0:RIM]
            middle_ref[here, :] = piece[:, RIM:]
        block = RIM // 2
        branch = make_branch(0, cat_ref, gain_ref, shift_ref, up_ref, down_ref, down_bias_ref, block)
        scale = wide(scale_ref[0], block)
        for start in range(0, RIM, block):
            here = slice(start, start + block)
            value = x_ref[:, here].astype(F32) + scale * branch(start)
            fine_ref[:, here] = (mask_ref[0:1, here] * value).astype(BF)

        weights = pool_cells_ref[:, 0:384]
        whole = pooled_cells([fine_ref[:, start : start + 384].astype(F32) * weights for start in (0, 384)], pool_ref[...])
        weights = pool_cells_ref[:, 384:512]
        rim = pooled_cells([fine_ref[:, 768 + 128 * i : 896 + 128 * i].astype(F32) * weights for i in range(4)], rim_pool_ref[...])
        pooled_ref[:, 0:128] = whole[0:ROWS].astype(BF)
        pooled_ref[:, 640:768] = whole[ROWS : 2 * ROWS].astype(BF)
        for i in range(4):
            pooled_ref[:, 128 * i + 128 : 128 * i + 256] = rim[i * ROWS : (i + 1) * ROWS].astype(BF)

        packed = dot(pooled_ref[...], pack_ref[...])
        lane = lane_ids((ROWS, 128))
        blocks = (packed[:, 0:128], packed[:, 128:256])
        for r in range(2):
            for c in range(2):
                mains_ref[2 * r + c] = jnp.where(lane < 72, blocks[r], blocks[c]).astype(BF)
        lane = lane_ids((16, 128))
        for c in range(2):
            rest = packed[:, 256:384]
            rest = pltpu.roll(rest, 64, 1) if c else rest
            parts = [rest[0:16], pltpu.roll(rest[16:32], 24, 1), pltpu.roll(rest[32:48], 48, 1)]
            joined = jnp.where(lane < 24, parts[0], jnp.where(lane < 48, parts[1], parts[2]))
            rest_ref[c] = jnp.where(lane < 72, joined, 0.0).astype(BF)

        def fill(dev, carry):
            both = tab_ref[16 + dev]
            for g in range(3):
                msg_ref[dev, :, 128 * g : 128 * g + 128] = mains_ref[both, 16 * g : 16 * g + 16, :]
            msg_ref[dev, :, 384:512] = rest_ref[lax.bitwise_and(both, 1)]
            return carry

        scan_tiles(count, fill, jnp.int32(0))

    return mix_rim


def mix_middle(
    cat_ref, x_ref, mask_ref, gain_ref, shift_ref, up_ref, down_ref, down_bias_ref, scale_ref, pool_cells_ref, middle_pool_ref, rim_ref,
    fine_ref, pooled_ref,
):
    block = MIDDLE // 2
    branch = make_branch(0, cat_ref, gain_ref, shift_ref, up_ref, down_ref, down_bias_ref, block)
    scale = wide(scale_ref[0], block)
    for start in range(0, MIDDLE, block):
        here, there = slice(start, start + block), slice(RIM + start, RIM + start + block)
        value = x_ref[:, there].astype(F32) + scale * branch(start)
        fine_ref[:, here] = (mask_ref[0:1, there] * value).astype(BF)
    weights = wide(pool_cells_ref[:, 512:640], 256)
    middle = pooled_cells([fine_ref[:, 256 * i : 256 * i + 256].astype(F32) * weights for i in range(4)], middle_pool_ref[...])
    pooled_ref[...] = rim_ref[...]
    for i in range(4):
        here = slice(128 * i + 128, 128 * i + 256)
        pooled_ref[:, here] = (rim_ref[:, here].astype(F32) + middle[i * ROWS : (i + 1) * ROWS].astype(BF).astype(F32)).astype(BF)


def mix_coarse(
    own_ref, p1_ref, p2_ref, p3_ref, pooled_ref, small_mask_ref, fine_ref, mask_ref, gain_ref, shift_ref, up_ref,
    down_ref, down_bias_ref, scale_ref, spread_cells_ref, pool_ref, out_ref, cat_ref,
):
    gather_rows((own_ref, p1_ref, p2_ref, p3_ref), cat_ref)
    cells = cat_ref.shape[1]
    branch = make_branch(1, cat_ref, gain_ref, shift_ref, up_ref, down_ref, down_bias_ref, cells)
    value = pooled_ref[...].astype(F32) + wide(scale_ref[1], cells) * branch(0)
    parts = []
    for i in range(GROUPS):
        parts.append((small_mask_ref[8 * i : 8 * i + 1, :] * value[:, 128 * i : 128 * i + 128]).astype(BF))
    spread = lax.dot_general(
        jnp.concatenate(parts, axis=0), pool_ref[...], (((1,), (1,)), ((), ())), preferred_element_type=F32
    )
    weights = spread_cells_ref[...]
    for i in range(GROUPS):
        lanes = slice(i * FINE_IN, (i + 1) * FINE_IN)
        merged = fine_ref[:, lanes].astype(F32) + weights * spread[i * ROWS : (i + 1) * ROWS]
        out_ref[0, :, lanes] = (mask_ref[:, lanes].astype(F32) * merged).astype(BF)


VMEM = pl.BlockSpec(memory_space=pltpu.VMEM)
SMEM = pl.BlockSpec(memory_space=pltpu.SMEM)

def takes(microseconds):
    return pl.CostEstimate(flops=microseconds * 1_000_000_000, bytes_accessed=0, transcendentals=0)


def shaped(*shape, dtype=BF):
    return jax.ShapeDtypeStruct(shape, dtype)


PARAMS = pltpu.CompilerParams(vmem_limit_bytes=24 * 1024 * 1024)


def every_channel(own, beside_work=lambda own: ()):
    pairs = lambda bit: [(i, i ^ bit) for i in range(4)]
    across = lax.ppermute(own, "chan", pairs(2))
    beside = lax.ppermute(own, "chan", pairs(1))
    across, *results = lax.optimization_barrier((across, *beside_work(own)))
    diagonal = lax.ppermute(across, "chan", pairs(1))
    return (own, beside, across, diagonal), results


def per_device(
    features, land_mask, wet_slots, device_of, depth_weight, depth_bias, norm_gain, norm_bias, up_weight, up_bias,
    down_weight, down_bias, layer_scale, pool_weight, spread_weight,
):
    count = wet_slots.shape[0]
    grid_x = 2 * count // GRID_Y
    cells = TILE * TILE
    pack = pl.pallas_call(
        strip_table, out_specs=VMEM, out_shape=shaped(FINE_IN, 256), compiler_params=PARAMS, cost_estimate=takes(2), name="strip_table"
    )()
    messages, table = pl.pallas_call(
        make_prep(grid_x),
        in_specs=[SMEM, SMEM, VMEM, VMEM],
        out_specs=[VMEM, SMEM],
        out_shape=[shaped(count, 16, 896), shaped(16 + count, dtype=jnp.int32)],
        scratch_shapes=[
            pltpu.VMEM((2, ROWS, 128), BF),
            pltpu.VMEM((2, ROWS, 128), BF),
            pltpu.VMEM((2, 16, 128), F32),
            pltpu.VMEM((2, 16, 128), F32),
        ],
        compiler_params=PARAMS,
        cost_estimate=takes(10),
        name="prep",
    )(wet_slots, device_of, features, pack)
    pool = jnp.asarray(POOL)
    arrived = lax.all_to_all(messages, "tile", 0, 0, tiled=True)
    inner, fine_taps = pl.pallas_call(
        lambda tab_ref, *refs: conv_inner(*refs),
        in_specs=[SMEM] + [VMEM] * 3,
        out_specs=[VMEM] * 2,
        out_shape=[shaped(ROWS, cells, dtype=F32), shaped(49, ROWS, 128, dtype=F32)],
        scratch_shapes=[
            pltpu.VMEM((ROWS, 3584), F32),
            pltpu.VMEM((ROWS, 3584), F32),
            pltpu.VMEM((ROWS, 3072), F32),
        ],
        compiler_params=PARAMS,
        cost_estimate=takes(4),
        name="conv_inner",
    )(table, features, depth_weight, depth_bias)
    conv = pl.pallas_call(
        conv_border,
        in_specs=[SMEM] + [VMEM] * 3,
        out_specs=VMEM,
        out_shape=shaped(ROWS, cells),
        compiler_params=PARAMS,
        cost_estimate=takes(2),
        name="conv_border",
    )(table, arrived, inner, fine_taps)

    def spread_params(own):
        return pl.pallas_call(
            params,
            in_specs=[VMEM] * 12,
            out_specs=[VMEM] * 10,
            out_shape=[
                shaped(*shape, dtype=dtype)
                for shape, dtype in (
                    ((ROWS, cells), BF), ((8, cells), F32), ((48, 128), F32), ((2, 192, 128), F32), ((2, 192, 128), F32),
                    ((2, up_weight.shape[1], up_weight.shape[2] + 16), BF), ((2, ROWS, 128), F32), ((2, ROWS, 128), F32),
                    ((ROWS, 640), F32), ((ROWS, FINE_IN), F32),
                )
            ],
            compiler_params=PARAMS,
            cost_estimate=takes(2),
            name="params",
        )(
            own, features, land_mask, norm_gain, norm_bias, jnp.swapaxes(up_weight, 1, 2), up_bias, down_bias, layer_scale,
            pool_weight, spread_weight, pool,
        )

    pieces, results = every_channel(conv, spread_params)
    own_cells, own_mask, small_mask, gains, shifts, ups, down_biases, scales, pool_cells, spread_cells = results
    rim, rim_pooled, messages, middle = pl.pallas_call(
        make_mix_rim(count),
        in_specs=[SMEM] + [VMEM] * 16,
        out_specs=[VMEM] * 4,
        out_shape=[shaped(ROWS, RIM), shaped(ROWS, 768), shaped(count, 16, 512), shaped(4 * ROWS, MIDDLE)],
        scratch_shapes=[
            pltpu.VMEM((4 * ROWS, RIM), BF),
            pltpu.VMEM((4, ROWS, 128), BF),
            pltpu.VMEM((2, 16, 128), BF),
        ],
        compiler_params=PARAMS,
        cost_estimate=takes(3),
        name="mix_rim",
    )(
        table, *pieces, own_cells, own_mask, gains, shifts, ups, down_weight, down_biases, scales, pool_cells, pool,
        jnp.asarray(RIM_POOL), jnp.asarray(SMALL_PACK),
    )
    arrived = lax.all_to_all(messages, "tile", 0, 0, tiled=True)
    middle, pooled = pl.pallas_call(
        mix_middle,
        in_specs=[VMEM] * 12,
        out_specs=[VMEM] * 2,
        out_shape=[shaped(ROWS, MIDDLE), shaped(ROWS, 768)],
        compiler_params=PARAMS,
        cost_estimate=takes(2),
        name="mix_middle",
    )(
        middle, own_cells, own_mask, gains, shifts, ups, down_weight, down_biases, scales, pool_cells, jnp.asarray(MIDDLE_POOL), rim_pooled
    )
    inner, taps = pl.pallas_call(
        conv_coarse,
        in_specs=[VMEM] * 3,
        out_specs=[VMEM] * 2,
        out_shape=[shaped(ROWS, 768, dtype=F32), shaped(49, ROWS, 128, dtype=F32)],
        scratch_shapes=[pltpu.VMEM((4, ROWS, 1024), F32)],
        compiler_params=PARAMS,
        cost_estimate=takes(2),
        name="conv_coarse",
    )(pooled, depth_weight, depth_bias)
    conv = pl.pallas_call(
        border_coarse,
        in_specs=[SMEM] + [VMEM] * 3,
        out_specs=VMEM,
        out_shape=shaped(ROWS, 768),
        compiler_params=PARAMS,
        cost_estimate=takes(1),
        name="border_coarse",
    )(table, arrived, inner, taps)

    def back_in_rows(own):
        return pl.pallas_call(
            lambda after_ref, *refs: in_rows(*refs),
            in_specs=[VMEM] * 3,
            out_specs=[VMEM],
            out_shape=[shaped(ROWS, cells)],
            compiler_params=PARAMS,
            cost_estimate=takes(1),
            name="in_rows",
        )(own, rim, middle)

    pieces, (fine,) = every_channel(conv, back_in_rows)
    return pl.pallas_call(
        mix_coarse,
        in_specs=[VMEM] * 16,
        out_specs=VMEM,
        out_shape=shaped(1, ROWS, cells),
        scratch_shapes=[pltpu.VMEM((4 * ROWS, 768), BF)],
        compiler_params=PARAMS,
        cost_estimate=takes(2),
        name="mix_coarse",
    )(
        *pieces, pooled, small_mask, fine, land_mask, gains, shifts, ups, down_weight, down_biases, scales, spread_cells, pool
    )


def solution(mesh):
    placed = (
        P("tile", "chan", None),
        P("tile", None),
        P(),
        P(),
        P(None, "chan", None),
        P(None, "chan"),
        P(),
        P(),
        P(),
        P(),
        P(),
        P(),
        P(None, "chan"),
        P("chan", None),
        P("chan", None),
    )
    return jax.shard_map(
        per_device, mesh=mesh, in_specs=placed, out_specs=P("tile", "chan", None), check_vma=False
    )
```

```python
import jax
import jax.numpy as jnp
import ml_dtypes
import numpy as np
from jax import lax
from jax.experimental import pallas as pl
from jax.experimental.pallas import tpu as pltpu
from jax.sharding import PartitionSpec as P

TILE = 48
HALF = TILE // 2
GRID_Y = 4
GROUPS = 6
ROWS = 48
FINE_IN = 8 * TILE
RIM = 1280
MIDDLE = 1024
BANDS = ((-1, -1), (-1, 0), (-1, 1), (0, -1), (0, 1), (1, -1), (1, 0), (1, 1))
norm_eps = 1e-06
BF = jnp.bfloat16
F32 = jnp.float32


def one_hot(shape, pairs):
    table = np.zeros(shape, np.float32)
    for source, target in pairs:
        table[source, target] = 1.0
    return table.astype(ml_dtypes.bfloat16)


def pool_tables():
    dense, rim, middle = [], [], []
    for row in range(8):
        for col in range(48):
            target = (row // 2) * 32 + 3 + col // 2
            dense.append((row * 48 + col, target))
            if 8 <= col < 40:
                middle.append((row * 32 + col - 8, target))
            else:
                rim.append((row * 16 + (col if col < 8 else col - 32), target))
    return one_hot((384, 128), dense), one_hot((128, 128), rim), one_hot((256, 128), middle)


def strip_pairs():
    pack = []
    for row in range(3):
        for col in range(HALF):
            pack.append((row * 32 + 3 + col, row * 24 + col))
            pack.append(((21 + row) * 32 + 3 + col, 128 + row * 24 + col))
    for row in range(HALF):
        for j in range(3):
            index = row * 3 + j
            lane = 72 + index if row < 16 else index - 48
            pack.append((row * 32 + 3 + j, lane if row < 16 else 256 + lane))
            pack.append((row * 32 + 24 + j, 128 + lane if row < 16 else 256 + 64 + lane))
    return pack


POOL, RIM_POOL, MIDDLE_POOL = pool_tables()
SMALL_PACK = one_hot((768, 384), strip_pairs())


def dot(left, right):
    return jnp.dot(left, right, preferred_element_type=F32)


def stacked(value, width):
    return jnp.concatenate([value[:, i * width : (i + 1) * width] for i in range(GROUPS)], axis=0)


def lane_ids(shape):
    return lax.broadcasted_iota(jnp.int32, shape, 1)


def three_terms(row):
    high = row.astype(BF)
    rest = row - high.astype(F32)
    middle = rest.astype(BF)
    low = (rest - middle.astype(F32)).astype(BF)
    return jnp.concatenate([high, middle, low, jnp.zeros((13, row.shape[1]), BF)], axis=0)


def columns(row):
    return lax.dot_general(
        three_terms(row), jnp.ones((16, 128), BF), (((0,), (0,)), ((), ())), preferred_element_type=F32
    )


def wide(block, lanes):
    return jnp.concatenate([block] * (lanes // 128), axis=1)


def scan_tiles(count, step, carry):
    if count <= 16:
        for k in range(count):
            carry = step(k, carry)
        return carry
    return lax.fori_loop(0, count, step, carry)


def strip_table(pack_ref):
    shape = (FINE_IN, 256)
    source = lax.broadcasted_iota(jnp.int32, shape, 0)
    lane = lane_ids(shape)
    within = lane % 128
    wanted = (within // 3) * TILE + within % 3 + jnp.where(lane >= 128, TILE - 3, 0)
    pack_ref[...] = jnp.where((within < 24) & (source == wanted), 1.0, 0.0).astype(BF)


def quotient(value, divisor):
    if divisor & (divisor - 1) == 0:
        return lax.shift_right_logical(value, jnp.int32(divisor.bit_length() - 1))
    return lax.div(value, divisor)


def remainder(value, divisor):
    if divisor & (divisor - 1) == 0:
        return lax.bitwise_and(value, jnp.int32(divisor - 1))
    return lax.rem(value, divisor)


def make_prep(grid_x):
    def prep(slots_ref, dev_ref, x_ref, pack_ref, msg_ref, tab_ref, rows_ref, cols_ref, row_rest_ref, col_rest_ref):
        count = slots_ref.shape[0]
        me = lax.axis_index("tile")
        my_slot = scan_tiles(count, lambda k, c: c + jnp.where(dev_ref[k] == me, slots_ref[k], 0), jnp.int32(0))
        my_x = remainder(my_slot, grid_x)
        my_y = quotient(my_slot, grid_x)
        wanted = []
        for up_by, right_by in BANDS:
            near_x = remainder(my_x + (right_by + grid_x), grid_x)
            near_y = my_y + up_by
            folded = near_y >= GRID_Y
            from_x = jnp.where(folded, grid_x - 1 - near_x, near_x)
            from_y = jnp.where(folded, GRID_Y - 1, near_y)
            wanted.append(from_y * grid_x + from_x)

        def find(k, found):
            slot, dev = slots_ref[k], dev_ref[k]
            row_pick = jnp.where(quotient(slot, grid_x) + 1 == my_y, 0, 1)
            col_pick = jnp.where(remainder(slot, grid_x) == remainder(my_x + (grid_x - 1), grid_x), 0, 1)
            tab_ref[16 + dev] = 2 * row_pick + col_pick
            return tuple(jnp.where(slot == want, dev, old) for want, old in zip(wanted, found))

        found = scan_tiles(count, find, tuple(jnp.int32(-1) for _ in BANDS))
        for band in range(8):
            tab_ref[band] = found[band]
        tab_ref[8] = jnp.where(my_y == GRID_Y - 1, 2, 1)
        for spare in range(9, 16):
            tab_ref[spare] = 0

        x = x_ref[0]
        cols = dot(stacked(x, FINE_IN), pack_ref[...])
        lane = lane_ids((ROWS, 128))
        for side in range(2):
            part = cols[:, side * 128 : side * 128 + 128]
            main = part[0:ROWS]
            for i in range(1, 5):
                main = main + pltpu.roll(part[i * ROWS : (i + 1) * ROWS], 24 * i, 1)
            cols_ref[side] = main.astype(BF)
            rest = pltpu.roll(part[5 * ROWS : 6 * ROWS], 16, 1)
            col_rest_ref[side] = rest[0:16] + pltpu.roll(rest[16:32], 40, 1) + pltpu.roll(rest[32:48], 80, 1)
        rows_ref[0] = x[:, 0:128]
        rows_ref[1] = x[:, 2176:2304]
        ends = (x[:, 128:256].astype(F32), pltpu.roll(x[:, 2048:2176].astype(F32), 16, 1))
        for side in range(2):
            rest = jnp.where(lane < 16, ends[side], 0.0)
            row_rest_ref[side] = rest[0:16] + pltpu.roll(rest[16:32], 40, 1) + pltpu.roll(rest[32:48], 80, 1)

        def fill(dev, carry):
            row_pick = quotient(tab_ref[16 + dev], 2)
            col_pick = remainder(tab_ref[16 + dev], 2)
            for g in range(3):
                msg_ref[dev, :, 256 * g : 256 * g + 128] = rows_ref[row_pick, 16 * g : 16 * g + 16, :]
                msg_ref[dev, :, 256 * g + 128 : 256 * g + 256] = cols_ref[col_pick, 16 * g : 16 * g + 16, :]
            msg_ref[dev, :, 768:896] = (row_rest_ref[row_pick] + col_rest_ref[col_pick]).astype(BF)
            return carry

        scan_tiles(count, fill, jnp.int32(0))

    return prep


def band_source(tab_ref, band):
    source = tab_ref[band]
    return jnp.maximum(source, 0), jnp.where(source >= 0, 1.0, 0.0).astype(F32)


def lane_shifted(value, lanes):
    return pltpu.roll(value, value.shape[1] - lanes, 1)


def tall(row_block):
    return jnp.concatenate([row_block] * (ROWS // 8), axis=0)


def lanes_from(value, index):
    return jnp.take_along_axis(value, index, axis=1)


def conv_inner(x_ref, weight_ref, bias_ref, sum_ref, middle_ref, mirror_ref, wide_ref, pad_ref, odd_ref, total_ref):
    for tap in range(49):
        wide_ref[tap] = jnp.broadcast_to(weight_ref[0, :, tap : tap + 1], (ROWS, 128))
    mirrored_taps(wide_ref, mirror_ref)
    pad_ref[:, 0:256] = jnp.zeros((ROWS, 256), F32)
    pad_ref[:, 3328:3584] = jnp.zeros((ROWS, 256), F32)
    lane = lane_ids((8, 128))
    half, within = lane // 64, lane % 64
    valid = tall((within >= 3) & (within < 51))
    col = jnp.clip(within - 3, 0, 47)
    cells = [96 * k + 48 * half + col for k in range(4)]
    indices = [tall(cell % 128) for cell in cells]
    for i in range(GROUPS):
        tiles = [x_ref[0, :, 384 * i + 128 * m : 384 * i + 128 * m + 128].astype(F32) for m in range(3)]
        for k in range(4):
            first, final = (96 * k) // 128, (96 * k + 95) // 128
            value = lanes_from(tiles[first], indices[k])
            if final != first:
                value = jnp.where(tall(cells[k] < 128 * final), value, lanes_from(tiles[final], indices[k]))
            start = 256 + 512 * i + 128 * k
            pad_ref[:, start : start + 128] = jnp.where(valid, value, 0.0)
    odd_ref[...] = lane_shifted(pad_ref[...], 64)
    total_ref[...] = wide(columns(bias_ref[0:1, :]), 3072)

    def group(g, carry):
        here = pl.ds(pl.multiple_of(g * 8, 8), 8)
        for chunk in range(6):
            base = chunk * 512
            taken = []
            for a in range(1, 8):
                ref = odd_ref if a % 2 else pad_ref
                start = base + (a // 2) * 128
                taken.append([ref[here, start + 128 * j : start + 128 * j + 128] for j in range(4)])
            total = [total_ref[here, base + 128 * j : base + 128 * j + 128] for j in range(4)]
            for b in range(7):
                weights = [wide_ref[a * 7 + b, here, :] for a in range(7)]
                for j in range(4):
                    partial = weights[0] * taken[0][j]
                    for a in range(1, 7):
                        partial = partial + weights[a] * taken[a][j]
                    total[j] = total[j] + (pltpu.roll(partial, (3 - b) % 128, 1) if b != 3 else partial)
            for j in range(4):
                total_ref[here, base + 128 * j : base + 128 * j + 128] = total[j]
        return carry

    lax.fori_loop(0, ROWS // 8, group, 0)
    for m in range((RIM + MIDDLE) // 128):
        row, col = place_of(m)
        index = tall(row % 2 * 64 + 3 + col)
        value = None
        for pair in pairs_of(m):
            picked = lanes_from(total_ref[:, 128 * pair : 128 * pair + 128], index)
            value = picked if value is None else jnp.where(tall(row // 2 == pair), picked, value)
        if m < RIM // 128:
            sum_ref[:, 128 * m : 128 * m + 128] = value
        else:
            middle_ref[:, 128 * m - RIM : 128 * m - RIM + 128] = value.astype(BF)


def place_of(m):
    lane = lane_ids((8, 128))
    if m < 6:
        cell = 128 * (m % 3) + lane
        return cell // 48 + (40 if m >= 3 else 0), cell % 48
    if m < 10:
        col = lane % 16
        return 8 * (m - 5) + lane // 16, jnp.where(col < 8, col, col + 32)
    return 8 + 4 * (m - 10) + lane // 32, 8 + lane % 32


def pairs_of(m):
    if m < 6:
        first = 128 * (m % 3)
        start = 20 if m >= 3 else 0
        return range(start + first // 96, start + (first + 127) // 96 + 1)
    if m < 10:
        return range(4 * (m - 5), 4 * (m - 5) + 4)
    return range(4 + 2 * (m - 10), 6 + 2 * (m - 10))


def column_sums(beside, mirror_ref):
    total = [jnp.zeros((ROWS, 128), F32)] * 3
    for a in range(7):
        if mirror_ref.shape[0] == 49:
            low_half = tall(lane_ids((8, 128)) < 64)
            weights = [jnp.where(low_half, mirror_ref[7 * a + b], mirror_ref[7 * a + 6 - b]) for b in range(3)]
        else:
            weights = [mirror_ref[4 * a + b] for b in range(3)]
        for q in range(3):
            partial = weights[0] * beside[q]
            for j in range(q + 1, 3):
                partial = partial + weights[j - q] * beside[j]
            total[q] = total[q] + (pltpu.roll(partial, (3 - a) % 128, 1) if a != 3 else partial)
    return total


def row_sums(uses, mirror_ref):
    places = 1 + max(place for place, _, _ in uses)
    taps = {a: whole_row(mirror_ref, a) for _, a, _ in uses}
    total = [jnp.zeros((ROWS, 128), F32)] * places
    for b in range(7):
        partial = [None] * places
        for place, a, cells in uses:
            term = taps[a][b] * cells
            partial[place] = term if partial[place] is None else partial[place] + term
        for place in range(places):
            total[place] = total[place] + (pltpu.roll(partial[place], (3 - b) % 128, 1) if b != 3 else partial[place])
    return total


def mirrored_taps(wide_ref, mirror_ref):
    low_half = tall(lane_ids((8, 128)) < 64)
    for a in range(7):
        for b in range(3):
            mirror_ref[4 * a + b] = jnp.where(low_half, wide_ref[a * 7 + b], wide_ref[a * 7 + 6 - b])
        mirror_ref[4 * a + 3] = wide_ref[a * 7 + 3]


def whole_row(mirror_ref, a):
    if mirror_ref.shape[0] == 49:
        return [mirror_ref[7 * a + b] for b in range(7)]
    low_half = tall(lane_ids((8, 128)) < 64)
    ends = [(mirror_ref[4 * a + b], pltpu.roll(mirror_ref[4 * a + b], 64, 1)) for b in range(3)]
    first = [jnp.where(low_half, plain, turned) for plain, turned in ends]
    last = [jnp.where(low_half, turned, plain) for plain, turned in ends]
    return first + [mirror_ref[4 * a + 3]] + last[::-1]


def conv_border(tab_ref, recv_ref, sum_ref, mirror_ref, out_ref):
    lane = lane_ids((8, 128))
    half, within = lane // 64, lane % 64
    low_half = tall(lane < 64)

    def band_cells(band, offset):
        source, scale = band_source(tab_ref, band)
        main = jnp.concatenate([recv_ref[source, :, 256 * g + offset : 256 * g + offset + 128] for g in range(3)], axis=0)
        rest = recv_ref[source, :, 768:896].astype(F32) * scale
        rest = jnp.concatenate([rest, pltpu.roll(rest, 128 - 40, 1), pltpu.roll(rest, 128 - 80, 1)], axis=0)
        return main.astype(F32) * scale, rest

    def halo_rows(bands, folded, last):
        left, middle, right = [band_cells(band, 0) for band in bands]
        tiles = []
        for first_row in (0, 2):
            row = first_row + half
            col = jnp.where(within < 3, 45 + within, jnp.where(within < 51, within - 3, within - 51))
            index = row * 48 + col
            index = jnp.where(folded, 143 - index, index)
            in_main = index - jnp.where(last, 16, 0)
            rest = (in_main < 0) | (in_main > 127)
            in_rest = jnp.where(in_main < 0, in_main + 16, in_main - 128)
            main_index, rest_index = tall(in_main & 127), tall(in_rest & 127)
            picked = [jnp.where(tall(rest), lanes_from(r, rest_index), lanes_from(m, main_index)) for m, r in (left, middle, right)]
            value = jnp.where(tall(within < 3), picked[0], jnp.where(tall(within < 51), picked[1], picked[2]))
            tiles.append(jnp.where(tall((within < 54) & (row < 3)), value, 0.0))
        return tiles

    def joined(first, second):
        return jnp.where(low_half, pltpu.roll(first, 64, 1), pltpu.roll(second, 64, 1))

    zeros = jnp.zeros((ROWS, 128), F32)
    below = halo_rows((0, 1, 2), False, True)
    first_fix = row_sums(((0, 0, below[0]), (0, 1, joined(below[0], below[1])), (0, 2, below[1]), (1, 0, below[1])), mirror_ref)
    folded = tab_ref[8] == 2
    above = halo_rows((5, 6, 7), folded, folded)
    edge = joined(zeros, above[0])
    last_fix = row_sums(((0, 6, edge), (1, 4, edge), (1, 5, above[0]), (1, 6, joined(above[0], above[1]))), mirror_ref)

    left, right = band_cells(3, 128), band_cells(4, 128)
    beside = []
    for j in range(3):
        which = jnp.where(half == 0, j, 2 - j)
        in_main = jnp.minimum(3 * within + which, 127)
        main_index, rest_index = tall(in_main), tall(jnp.clip(3 * (within - 40) + 16 + which, 0, 127))
        picked = [
            jnp.where(tall(within < 40), lanes_from(main, main_index), lanes_from(rest, rest_index)) for main, rest in (left, right)
        ]
        beside.append(jnp.where(tall(within < 48), jnp.where(low_half, picked[0], picked[1]), 0.0))
    column_fix = column_sums(beside, mirror_ref)
    fixes = {0: first_fix[0], 1: first_fix[1], 22: last_fix[0], 23: last_fix[1]}
    for m in range(RIM // 128):
        row, col = place_of(m)
        index = tall(jnp.where(col < 24, row, 64 + row))
        value = sum_ref[:, 128 * m : 128 * m + 128]
        fix = zeros
        for q in range(3):
            fix = jnp.where(tall((col == q) | (col == 47 - q)), lanes_from(column_fix[q], index), fix)
        value = value + fix
        row_index = tall(row % 2 * 64 + 3 + col)
        for pair in pairs_of(m):
            if pair in fixes:
                value = value + jnp.where(tall(row // 2 == pair), lanes_from(fixes[pair], row_index), 0.0)
        out_ref[:, 128 * m : 128 * m + 128] = value.astype(BF)


def params(
    after_ref, x_ref, mask_ref, gain_ref, shift_ref, up_ref, up_bias_ref, down_ref, down_bias_ref, scale_ref, pool_weight_ref, spread_weight_ref,
    pool_ref, rim_cells_ref, middle_cells_ref, rim_mask_ref, rim_weights_ref, *level_refs,
):
    me = lax.axis_index("chan")
    lane = lane_ids((192, 128))
    for level in range(2):
        weights_ref, values_ref = level_refs[2 * level : 2 * level + 2]
        row = slice(level, level + 1)
        spare = jnp.zeros((48, up_ref.shape[2]), BF)
        turned = jnp.concatenate([up_ref[level], three_terms(up_bias_ref[row, :]), spare], axis=0)
        weights_ref[0:768, :] = jnp.transpose(turned, (1, 0))
        own = down_ref[level, pl.ds(pl.multiple_of(me * ROWS, 16), ROWS), :]
        for j in range(3):
            weights_ref[768 + ROWS * j : 768 + ROWS * (j + 1), :] = own[:, 256 * j : 256 * j + 256]
        down_bias = columns(down_bias_ref[row, :])
        own = down_bias[0:ROWS]
        for k in range(1, down_bias.shape[0] // ROWS):
            own = jnp.where(me == k, down_bias[k * ROWS : (k + 1) * ROWS], own)
        rest = jnp.zeros((192 - ROWS, 128), F32)
        own, scale = [jnp.concatenate([value, rest], axis=0) for value in (own, columns(scale_ref[row, :]))]
        norm = jnp.where(lane == 0, columns(gain_ref[row, :]), columns(shift_ref[row, :]))
        values_ref[0:192, :] = jnp.where(lane < 2, norm, jnp.where(lane == 2, own, scale))
    fine_values_ref, coarse_values_ref = level_refs[1], level_refs[3]
    lane = lane_ids((ROWS, FINE_IN))
    rim_weights_ref[:, 0:384] = cell_weights(pool_weight_ref, lane // 48, lane % 48)
    spread = cell_weights(spread_weight_ref, lane // 48, lane % 48)
    for j in range(3):
        coarse_values_ref[240 + ROWS * j : 240 + ROWS * (j + 1), :] = spread[:, 128 * j : 128 * j + 128]
    lane = lane_ids((ROWS, 128))
    rim_weights_ref[:, 384:512] = cell_weights(pool_weight_ref, lane // 16, lane)
    fine_values_ref[192:240, :] = cell_weights(pool_weight_ref, lane // 32, lane)

    masks = []
    for i in range(GROUPS):
        masks.append(jnp.broadcast_to(mask_ref[:, i * FINE_IN : (i + 1) * FINE_IN].astype(F32), (8, FINE_IN)))
    counts = dot(jnp.concatenate(masks, axis=0).astype(BF), pool_ref[...])
    coarse_values_ref[192:240, :] = jnp.where(counts > 0.5, 1.0, 0.0)
    for m in range((RIM + MIDDLE) // 128):
        if m < 6:
            here = slice(128 * m, 128 * m + 128)
            source = 128 * (m if m < 3 else m + 12)
            rim_cells_ref[:, here] = x_ref[0, :, source : source + 128]
            rim_mask_ref[:, here] = jnp.broadcast_to(mask_ref[:, source : source + 128].astype(F32), (8, 128))
            continue
        row, col = place_of(m)
        cell = row * 48 + col
        first, final = (8 * (m - 5) * 48, 8 * (m - 4) * 48 - 1) if m < 10 else ((4 * m - 32) * 48 + 8, (4 * m - 29) * 48 + 39)
        index, value, mask = cell % 128, None, None
        for tile in range(first // 128, final // 128 + 1):
            lanes = slice(128 * tile, 128 * tile + 128)
            part = lanes_from(x_ref[0, :, lanes].astype(F32), tall(index))
            mask_part = lanes_from(jnp.broadcast_to(mask_ref[:, lanes].astype(F32), (8, 128)), index)
            value = part if value is None else jnp.where(tall(cell // 128 == tile), part, value)
            mask = mask_part if mask is None else jnp.where(cell // 128 == tile, mask_part, mask)
        if m < 10:
            rim_cells_ref[:, 128 * m : 128 * m + 128] = value.astype(BF)
            rim_mask_ref[:, 128 * m : 128 * m + 128] = mask
        else:
            middle_cells_ref[:, 128 * m - RIM : 128 * m - RIM + 128] = value.astype(BF)
            fine_values_ref[240 + 8 * (m - 10) : 248 + 8 * (m - 10), :] = mask


def in_rows(rim_ref, middle_ref, out_ref):
    out_ref[:, 0:FINE_IN] = rim_ref[:, 0:FINE_IN]
    out_ref[:, 5 * FINE_IN :] = rim_ref[:, FINE_IN : 2 * FINE_IN]
    for i in range(1, 5):
        rim = rim_ref[:, 768 + 128 * (i - 1) : 768 + 128 * i].astype(F32)
        middle = [middle_ref[:, 256 * (i - 1) + 128 * h : 256 * (i - 1) + 128 * h + 128].astype(F32) for h in range(2)]
        for m in range(3):
            cell = 128 * m + lane_ids((8, 128))
            row, col = cell // 48, cell % 48
            value = lanes_from(rim, tall((row * 16 + jnp.where(col < 8, col, col - 32)) & 127))
            in_middle = (col >= 8) & (col < 40)
            index = tall((row % 4 * 32 + col - 8) & 127)
            for h in range(2):
                if 192 * h < 128 * m + 128 and 192 * h + 192 > 128 * m:
                    value = jnp.where(tall(in_middle & (row // 4 == h)), lanes_from(middle[h], index), value)
            out_ref[:, i * FINE_IN + 128 * m : i * FINE_IN + 128 * m + 128] = value.astype(BF)


def conv_coarse(x_ref, weight_ref, bias_ref, sum_ref, wide_ref, pad_ref):
    for tap in range(49):
        wide_ref[tap] = jnp.broadcast_to(weight_ref[1, :, tap : tap + 1], (ROWS, 128))
    pad_ref[0, :, 0:128] = jnp.zeros((ROWS, 128), F32)
    pad_ref[0, :, 896:1024] = jnp.zeros((ROWS, 128), F32)
    pad_ref[0, :, 128:896] = x_ref[...].astype(F32)
    padded = pad_ref[0]
    for turn in range(1, 4):
        pad_ref[turn] = lane_shifted(padded, 32 * turn)
    sum_ref[...] = wide(columns(bias_ref[1:2, :]), 768)

    def group(g, carry):
        rows = pl.ds(pl.multiple_of(g * 8, 8), 8)
        for chunk in range(2):
            base = chunk * 384
            taken = []
            for a in range(1, 8):
                start = base + (a // 4) * 128
                taken.append([pad_ref[a % 4, rows, start + 128 * j : start + 128 * j + 128] for j in range(3)])
            total = [sum_ref[rows, base + 128 * j : base + 128 * j + 128] for j in range(3)]
            for b in range(7):
                weights = [wide_ref[a * 7 + b, rows, :] for a in range(7)]
                for j in range(3):
                    partial = weights[0] * taken[0][j]
                    for a in range(1, 7):
                        partial = partial + weights[a] * taken[a][j]
                    total[j] = total[j] + (pltpu.roll(partial, (3 - b) % 128, 1) if b != 3 else partial)
            for j in range(3):
                sum_ref[rows, base + 128 * j : base + 128 * j + 128] = total[j]
        return carry

    lax.fori_loop(0, 6, group, 0)


def border_coarse(tab_ref, recv_ref, sum_ref, mirror_ref, out_ref):
    lane = lane_ids((8, 128))
    half, within, segment, inside = lane // 64, lane % 64, lane // 32, lane % 32

    def band_main(band):
        source, scale = band_source(tab_ref, band)
        return jnp.concatenate([recv_ref[source, :, 128 * g : 128 * g + 128] for g in range(3)], axis=0).astype(F32) * scale

    def band_rest(band):
        source, scale = band_source(tab_ref, band)
        rest = recv_ref[source, :, 384:512].astype(F32) * scale
        return jnp.concatenate([rest, pltpu.roll(rest, 128 - 24, 1), pltpu.roll(rest, 128 - 48, 1)], axis=0)

    def halo_rows(bands, folded):
        col = jnp.where(inside < 3, 21 + inside, jnp.where(inside < 27, inside - 3, inside - 27))
        index = segment * 24 + col
        index = tall(jnp.where(folded, 71 - index, index) & 127)
        picked = [lanes_from(band_main(band), index) for band in bands]
        value = jnp.where(tall(inside < 3), picked[0], jnp.where(tall(inside < 27), picked[1], picked[2]))
        return jnp.where(tall((inside < 30) & (segment < 3)), value, 0.0)

    def turned(cells, lanes, kept):
        return jnp.where(tall(kept), pltpu.roll(cells, lanes, 1), 0.0)

    below = halo_rows((0, 1, 2), False)
    first_fix = row_sums(((0, 0, below), (0, 1, turned(below, 96, lane < 64)), (0, 2, turned(below, 64, lane < 32))), mirror_ref)[0]
    above = halo_rows((5, 6, 7), tab_ref[8] == 2)
    last_fix = row_sums(
        ((0, 6, turned(above, 32, lane >= 32)), (0, 5, turned(above, 64, lane >= 64)), (0, 4, turned(above, 96, lane >= 96))), mirror_ref
    )[0]
    sides = [(band_main(band), band_rest(band)) for band in (3, 4)]
    beside = []
    for j in range(3):
        which = jnp.where(half == 0, j, 2 - j)
        main_index = tall(jnp.minimum(72 + 3 * within + which, 127))
        rest_index = tall(jnp.clip(3 * (within - 16) + which, 0, 127))
        picked = [
            jnp.where(tall(within < 16), lanes_from(main, main_index), lanes_from(rest, rest_index)) for main, rest in sides
        ]
        beside.append(jnp.where(tall(within < HALF), jnp.where(tall(half == 0), picked[0], picked[1]), 0.0))
    column_fix = column_sums(beside, mirror_ref)
    for m in range(GROUPS):
        row, col = 4 * m + segment, inside - 3
        index = tall(jnp.where(col < 12, row, 64 + row))
        value = sum_ref[:, 128 * m : 128 * m + 128]
        fix = jnp.zeros((ROWS, 128), F32)
        for q in range(3):
            fix = jnp.where(tall((col == q) | (col == 23 - q)), lanes_from(column_fix[q], index), fix)
        value = value + fix
        if m == 0:
            value = value + first_fix
        if m == GROUPS - 1:
            value = value + last_fix
        out_ref[:, 128 * m : 128 * m + 128] = value.astype(BF)


def gather_rows(pieces, cat_ref):
    me = lax.axis_index("chan")
    for k, piece in enumerate(pieces):
        first = pl.multiple_of(lax.bitwise_xor(me, k) * ROWS, 16)
        cat_ref[pl.ds(first, ROWS), :] = piece[...]


def make_branch(cat_ref, weights_ref, values_ref, block):
    def spread_lane(rows, lane):
        return wide(jnp.broadcast_to(values_ref[0:rows, lane : lane + 1], (rows, 128)), block)

    gain, shift, down_bias, scale = spread_lane(192, 0), spread_lane(192, 1), spread_lane(ROWS, 2), spread_lane(ROWS, 3)
    down = jnp.concatenate([weights_ref[768 + ROWS * j : 768 + ROWS * (j + 1), :] for j in range(3)], axis=1)
    inputs = 4 * ROWS

    def branch(start):
        values = cat_ref[0:inputs, start : start + block].astype(F32)
        mean = jnp.mean(values, axis=0, keepdims=True)
        centred = values - mean
        spread = jnp.mean(centred * centred, axis=0, keepdims=True)
        normed = (centred * lax.rsqrt(spread + norm_eps) * gain + shift).astype(BF)
        hidden = dot(weights_ref[0:768, 0 : inputs + 16], jnp.concatenate([normed, jnp.ones((16, block), BF)], axis=0))
        hidden = 0.5 * hidden * (1.0 + lax.erf(hidden * np.float32(0.5**0.5)))
        return scale * (dot(down, hidden.astype(BF)) + down_bias)

    return branch


def cell_weights(weight_ref, row, col):
    kind = 2 * (row % 2) + col % 2
    result = jnp.zeros(row.shape, F32)
    for k in range(4):
        result = jnp.where(kind == k, weight_ref[:, k : k + 1], result)
    return result


def pooled_cells(products, table):
    highs = [product.astype(BF) for product in products]
    lows = [(product - high.astype(F32)).astype(BF) for product, high in zip(products, highs)]
    return dot(jnp.concatenate(highs, axis=0), table) + dot(jnp.concatenate(lows, axis=0), table)


def make_mix_rim(count):
    def mix_rim(
        tab_ref, own_ref, p1_ref, p2_ref, p3_ref, x_ref, mask_ref, pool_cells_ref, weights_ref, values_ref, pool_ref, rim_pool_ref,
        pack_ref, middle_pooled_ref, fine_ref, msg_ref, all_pooled_ref, cat_ref, pooled_ref, mains_ref, rest_ref,
    ):
        gather_rows((own_ref, p1_ref, p2_ref, p3_ref), cat_ref)
        block = RIM // 2
        branch = make_branch(cat_ref, weights_ref, values_ref, block)
        for start in range(0, RIM, block):
            here = slice(start, start + block)
            value = x_ref[:, here].astype(F32) + branch(start)
            fine_ref[:, here] = (mask_ref[0:1, here] * value).astype(BF)

        weights = pool_cells_ref[:, 0:384]
        whole = pooled_cells([fine_ref[:, start : start + 384].astype(F32) * weights for start in (0, 384)], pool_ref[...])
        weights = pool_cells_ref[:, 384:512]
        rim = pooled_cells([fine_ref[:, 768 + 128 * i : 896 + 128 * i].astype(F32) * weights for i in range(4)], rim_pool_ref[...])
        pooled_ref[:, 0:128] = whole[0:ROWS].astype(BF)
        pooled_ref[:, 640:768] = whole[ROWS : 2 * ROWS].astype(BF)
        for i in range(4):
            pooled_ref[:, 128 * i + 128 : 128 * i + 256] = rim[i * ROWS : (i + 1) * ROWS].astype(BF)

        packed = dot(pooled_ref[...], pack_ref[...])
        lane = lane_ids((ROWS, 128))
        blocks = (packed[:, 0:128], packed[:, 128:256])
        for r in range(2):
            for c in range(2):
                mains_ref[2 * r + c] = jnp.where(lane < 72, blocks[r], blocks[c]).astype(BF)
        lane = lane_ids((16, 128))
        for c in range(2):
            rest = packed[:, 256:384]
            rest = pltpu.roll(rest, 64, 1) if c else rest
            parts = [rest[0:16], pltpu.roll(rest[16:32], 24, 1), pltpu.roll(rest[32:48], 48, 1)]
            joined = jnp.where(lane < 24, parts[0], jnp.where(lane < 48, parts[1], parts[2]))
            rest_ref[c] = jnp.where(lane < 72, joined, 0.0).astype(BF)

        def fill(dev, carry):
            both = tab_ref[16 + dev]
            for g in range(3):
                msg_ref[dev, :, 128 * g : 128 * g + 128] = mains_ref[both, 16 * g : 16 * g + 16, :]
            msg_ref[dev, :, 384:512] = rest_ref[lax.bitwise_and(both, 1)]
            return carry

        scan_tiles(count, fill, jnp.int32(0))
        all_pooled_ref[...] = pooled_ref[...]
        for i in range(4):
            here = slice(128 * i + 128, 128 * i + 256)
            all_pooled_ref[:, here] = (pooled_ref[:, here].astype(F32) + middle_pooled_ref[:, 128 * i : 128 * i + 128].astype(F32)).astype(BF)

    return mix_rim


def mix_middle(
    own_ref, p1_ref, p2_ref, p3_ref, x_ref, weights_ref, values_ref, middle_pool_ref, fine_ref, pooled_ref, cat_ref
):
    gather_rows((own_ref, p1_ref, p2_ref, p3_ref), cat_ref)
    block = MIDDLE // 2
    branch = make_branch(cat_ref, weights_ref, values_ref, block)
    for start in range(0, MIDDLE, block):
        here = slice(start, start + block)
        value = x_ref[:, here].astype(F32) + branch(start)
        tiles = range(start // 128, (start + block) // 128)
        mask = jnp.concatenate([values_ref[240 + 8 * t : 241 + 8 * t, :] for t in tiles], axis=1)
        fine_ref[:, here] = (mask * value).astype(BF)
    weights = wide(values_ref[192:240, :], 256)
    middle = pooled_cells([fine_ref[:, 256 * i : 256 * i + 256].astype(F32) * weights for i in range(4)], middle_pool_ref[...])
    for i in range(4):
        pooled_ref[:, 128 * i : 128 * i + 128] = middle[i * ROWS : (i + 1) * ROWS].astype(BF)


def mix_coarse(
    own_ref, p1_ref, p2_ref, p3_ref, pooled_ref, fine_ref, mask_ref, weights_ref, values_ref, pool_ref, out_ref, cat_ref,
):
    gather_rows((own_ref, p1_ref, p2_ref, p3_ref), cat_ref)
    cells = cat_ref.shape[1]
    value = pooled_ref[...].astype(F32) + make_branch(cat_ref, weights_ref, values_ref, cells)(0)
    parts = []
    for i in range(GROUPS):
        parts.append((values_ref[192 + 8 * i : 193 + 8 * i, :] * value[:, 128 * i : 128 * i + 128]).astype(BF))
    spread = lax.dot_general(
        jnp.concatenate(parts, axis=0), pool_ref[...], (((1,), (1,)), ((), ())), preferred_element_type=F32
    )
    weights = jnp.concatenate([values_ref[240 + ROWS * j : 240 + ROWS * (j + 1), :] for j in range(3)], axis=1)
    for i in range(GROUPS):
        lanes = slice(i * FINE_IN, (i + 1) * FINE_IN)
        merged = fine_ref[:, lanes].astype(F32) + weights * spread[i * ROWS : (i + 1) * ROWS]
        out_ref[0, :, lanes] = (mask_ref[:, lanes].astype(F32) * merged).astype(BF)


VMEM = pl.BlockSpec(memory_space=pltpu.VMEM)
SMEM = pl.BlockSpec(memory_space=pltpu.SMEM)

def takes(microseconds):
    return pl.CostEstimate(flops=microseconds * 1_000_000_000, bytes_accessed=0, transcendentals=0)


def shaped(*shape, dtype=BF):
    return jax.ShapeDtypeStruct(shape, dtype)


PARAMS = pltpu.CompilerParams(vmem_limit_bytes=24 * 1024 * 1024)


def every_channel(own, beside_work=lambda own: ()):
    pairs = lambda bit: [(i, i ^ bit) for i in range(4)]
    across = lax.ppermute(own, "chan", pairs(2))
    beside = lax.ppermute(own, "chan", pairs(1))
    across, *results = lax.optimization_barrier((across, *beside_work(own)))
    diagonal = lax.ppermute(across, "chan", pairs(1))
    return (own, beside, across, diagonal), results


def per_device(
    features, land_mask, wet_slots, device_of, depth_weight, depth_bias, norm_gain, norm_bias, up_weight, up_bias,
    down_weight, down_bias, layer_scale, pool_weight, spread_weight,
):
    count = wet_slots.shape[0]
    grid_x = 2 * count // GRID_Y
    cells = TILE * TILE
    pack = pl.pallas_call(
        strip_table, out_specs=VMEM, out_shape=shaped(FINE_IN, 256), compiler_params=PARAMS, cost_estimate=takes(2), name="strip_table"
    )()
    messages, table = pl.pallas_call(
        make_prep(grid_x),
        in_specs=[SMEM, SMEM, VMEM, VMEM],
        out_specs=[VMEM, SMEM],
        out_shape=[shaped(count, 16, 896), shaped(16 + count, dtype=jnp.int32)],
        scratch_shapes=[
            pltpu.VMEM((2, ROWS, 128), BF),
            pltpu.VMEM((2, ROWS, 128), BF),
            pltpu.VMEM((2, 16, 128), F32),
            pltpu.VMEM((2, 16, 128), F32),
        ],
        compiler_params=PARAMS,
        cost_estimate=takes(10),
        name="prep",
    )(wet_slots, device_of, features, pack)
    pool = jnp.asarray(POOL)
    arrived = lax.all_to_all(messages, "tile", 0, 0, tiled=True)
    inner, inner_middle, fine_taps = pl.pallas_call(
        lambda tab_ref, *refs: conv_inner(*refs),
        in_specs=[SMEM] + [VMEM] * 3,
        out_specs=[VMEM] * 3,
        out_shape=[shaped(ROWS, RIM, dtype=F32), shaped(ROWS, MIDDLE), shaped(28, ROWS, 128, dtype=F32)],
        scratch_shapes=[
            pltpu.VMEM((49, ROWS, 128), F32),
            pltpu.VMEM((ROWS, 3584), F32),
            pltpu.VMEM((ROWS, 3584), F32),
            pltpu.VMEM((ROWS, 3072), F32),
        ],
        compiler_params=PARAMS,
        cost_estimate=takes(4),
        name="conv_inner",
    )(table, features, depth_weight, depth_bias)
    conv = pl.pallas_call(
        conv_border,
        in_specs=[SMEM] + [VMEM] * 3,
        out_specs=VMEM,
        out_shape=shaped(ROWS, RIM),
        compiler_params=PARAMS,
        cost_estimate=takes(2),
        name="conv_border",
    )(table, arrived, inner, fine_taps)

    pairs = lambda bit: [(i, i ^ bit) for i in range(4)]
    middle_across = lax.ppermute(inner_middle, "chan", pairs(2))
    middle_beside = lax.ppermute(inner_middle, "chan", pairs(1))
    middle_across, _ = lax.optimization_barrier((middle_across, conv))
    middle_pieces = (inner_middle, middle_beside, middle_across, lax.ppermute(middle_across, "chan", pairs(1)))

    def beside_gather(own):
        results = spread_params(own)
        return *results, *pl.pallas_call(
            mix_middle,
            in_specs=[VMEM] * 8,
            out_specs=[VMEM] * 2,
            out_shape=[shaped(ROWS, MIDDLE), shaped(ROWS, 512)],
            scratch_shapes=[pltpu.VMEM((4 * ROWS, MIDDLE), BF)],
            compiler_params=PARAMS,
            cost_estimate=takes(1),
            name="mix_middle",
        )(*middle_pieces, results[1], results[4], results[5], jnp.asarray(MIDDLE_POOL))

    def spread_params(own):
        shapes = [
            ((ROWS, RIM), BF), ((ROWS, MIDDLE), BF), ((8, RIM), F32), ((ROWS, 512), F32),
            ((912, 256), BF), ((304, 128), F32), ((912, 256), BF), ((384, 128), F32),
        ]
        return pl.pallas_call(
            params,
            in_specs=[VMEM] * 13,
            out_specs=[VMEM] * len(shapes),
            out_shape=[shaped(*shape, dtype=dtype) for shape, dtype in shapes],
            compiler_params=PARAMS,
            cost_estimate=takes(2),
            name="params",
        )(
            own, features, land_mask, norm_gain, norm_bias, jnp.swapaxes(up_weight, 1, 2), up_bias, down_weight, down_bias, layer_scale,
            pool_weight, spread_weight, pool,
        )

    pieces, results = every_channel(conv, beside_gather)
    rim_cells, _, rim_mask, rim_weights, fine_weights, fine_values, coarse_weights, coarse_values, middle, middle_pooled = results
    rim, messages, pooled = pl.pallas_call(
        make_mix_rim(count),
        in_specs=[SMEM] + [VMEM] * 13,
        out_specs=[VMEM] * 3,
        out_shape=[shaped(ROWS, RIM), shaped(count, 16, 512), shaped(ROWS, 768)],
        scratch_shapes=[
            pltpu.VMEM((4 * ROWS, RIM), BF),
            pltpu.VMEM((ROWS, 768), BF),
            pltpu.VMEM((4, ROWS, 128), BF),
            pltpu.VMEM((2, 16, 128), BF),
        ],
        compiler_params=PARAMS,
        cost_estimate=takes(3),
        name="mix_rim",
    )(
        table, *pieces, rim_cells, rim_mask, rim_weights, fine_weights, fine_values, pool, jnp.asarray(RIM_POOL),
        jnp.asarray(SMALL_PACK), middle_pooled,
    )
    arrived = lax.all_to_all(messages, "tile", 0, 0, tiled=True)
    inner, taps = pl.pallas_call(
        conv_coarse,
        in_specs=[VMEM] * 3,
        out_specs=[VMEM] * 2,
        out_shape=[shaped(ROWS, 768, dtype=F32), shaped(49, ROWS, 128, dtype=F32)],
        scratch_shapes=[pltpu.VMEM((4, ROWS, 1024), F32)],
        compiler_params=PARAMS,
        cost_estimate=takes(2),
        name="conv_coarse",
    )(pooled, depth_weight, depth_bias)
    conv = pl.pallas_call(
        border_coarse,
        in_specs=[SMEM] + [VMEM] * 3,
        out_specs=VMEM,
        out_shape=shaped(ROWS, 768),
        compiler_params=PARAMS,
        cost_estimate=takes(1),
        name="border_coarse",
    )(table, arrived, inner, taps)

    def back_in_rows(own):
        return pl.pallas_call(
            lambda after_ref, *refs: in_rows(*refs),
            in_specs=[VMEM] * 3,
            out_specs=[VMEM],
            out_shape=[shaped(ROWS, cells)],
            compiler_params=PARAMS,
            cost_estimate=takes(1),
            name="in_rows",
        )(own, rim, middle)

    pieces, (fine,) = every_channel(conv, back_in_rows)
    return pl.pallas_call(
        mix_coarse,
        in_specs=[VMEM] * 10,
        out_specs=VMEM,
        out_shape=shaped(1, ROWS, cells),
        scratch_shapes=[pltpu.VMEM((4 * ROWS, 768), BF)],
        compiler_params=PARAMS,
        cost_estimate=takes(2),
        name="mix_coarse",
    )(*pieces, pooled, fine, land_mask, coarse_weights, coarse_values, pool)


def solution(mesh):
    placed = (
        P("tile", "chan", None),
        P("tile", None),
        P(),
        P(),
        P(None, "chan", None),
        P(None, "chan"),
        P(),
        P(),
        P(),
        P(),
        P(),
        P(),
        P(None, "chan"),
        P("chan", None),
        P("chan", None),
    )
    return jax.shard_map(
        per_device, mesh=mesh, in_specs=placed, out_specs=P("tile", "chan", None), check_vma=False
    )
```

```python
import jax
import jax.numpy as jnp
import ml_dtypes
import numpy as np
from jax import lax
from jax.experimental import pallas as pl
from jax.experimental.pallas import tpu as pltpu
from jax.sharding import PartitionSpec as P

TILE = 48
HALF = TILE // 2
GRID_Y = 4
GROUPS = 6
ROWS = 48
FINE_IN = 8 * TILE
RIM = 1280
MIDDLE = 1024
BANDS = ((-1, -1), (-1, 0), (-1, 1), (0, -1), (0, 1), (1, -1), (1, 0), (1, 1))
norm_eps = 1e-06
BF = jnp.bfloat16
F32 = jnp.float32


def one_hot(shape, pairs):
    table = np.zeros(shape, np.float32)
    for source, target in pairs:
        table[source, target] = 1.0
    return table.astype(ml_dtypes.bfloat16)


def pool_tables():
    dense, rim, middle = [], [], []
    for row in range(8):
        for col in range(48):
            target = (row // 2) * 32 + 3 + col // 2
            dense.append((row * 48 + col, target))
            if 8 <= col < 40:
                middle.append((row * 32 + col - 8, target))
            else:
                rim.append((row * 16 + (col if col < 8 else col - 32), target))
    return one_hot((384, 128), dense), one_hot((128, 128), rim), one_hot((256, 128), middle)


POOL, RIM_POOL, MIDDLE_POOL = pool_tables()


def dot(left, right):
    return jnp.dot(left, right, preferred_element_type=F32)


def stacked(value, width):
    return jnp.concatenate([value[:, i * width : (i + 1) * width] for i in range(GROUPS)], axis=0)


def lane_ids(shape):
    return lax.broadcasted_iota(jnp.int32, shape, 1)


def three_terms(row):
    high = row.astype(BF)
    rest = row - high.astype(F32)
    middle = rest.astype(BF)
    low = (rest - middle.astype(F32)).astype(BF)
    return jnp.concatenate([high, middle, low, jnp.zeros((13, row.shape[1]), BF)], axis=0)


def columns(row):
    return lax.dot_general(
        three_terms(row), jnp.ones((16, 128), BF), (((0,), (0,)), ((), ())), preferred_element_type=F32
    )


def wide(block, lanes):
    return jnp.concatenate([block] * (lanes // 128), axis=1)


def scan_tiles(count, step, carry):
    if count <= 16:
        for k in range(count):
            carry = step(k, carry)
        return carry
    return lax.fori_loop(0, count, step, carry)


def strip_table(pack_ref):
    shape = (FINE_IN, 256)
    source = lax.broadcasted_iota(jnp.int32, shape, 0)
    lane = lane_ids(shape)
    within = lane % 128
    wanted = (within // 3) * TILE + within % 3 + jnp.where(lane >= 128, TILE - 3, 0)
    pack_ref[...] = jnp.where((within < 24) & (source == wanted), 1.0, 0.0).astype(BF)


def quotient(value, divisor):
    if divisor & (divisor - 1) == 0:
        return lax.shift_right_logical(value, jnp.int32(divisor.bit_length() - 1))
    return lax.div(value, divisor)


def remainder(value, divisor):
    if divisor & (divisor - 1) == 0:
        return lax.bitwise_and(value, jnp.int32(divisor - 1))
    return lax.rem(value, divisor)


def make_prep(grid_x):
    def prep(slots_ref, dev_ref, x_ref, pack_ref, msg_ref, tab_ref, rows_ref, cols_ref, row_rest_ref, col_rest_ref):
        count = slots_ref.shape[0]
        me = lax.axis_index("tile")
        my_slot = scan_tiles(count, lambda k, c: c + jnp.where(dev_ref[k] == me, slots_ref[k], 0), jnp.int32(0))
        my_x = remainder(my_slot, grid_x)
        my_y = quotient(my_slot, grid_x)
        wanted = []
        for up_by, right_by in BANDS:
            near_x = remainder(my_x + (right_by + grid_x), grid_x)
            near_y = my_y + up_by
            folded = near_y >= GRID_Y
            from_x = jnp.where(folded, grid_x - 1 - near_x, near_x)
            from_y = jnp.where(folded, GRID_Y - 1, near_y)
            wanted.append(from_y * grid_x + from_x)

        def find(k, found):
            slot, dev = slots_ref[k], dev_ref[k]
            row_pick = jnp.where(quotient(slot, grid_x) + 1 == my_y, 0, 1)
            col_pick = jnp.where(remainder(slot, grid_x) == remainder(my_x + (grid_x - 1), grid_x), 0, 1)
            tab_ref[16 + dev] = 2 * row_pick + col_pick
            return tuple(jnp.where(slot == want, dev, old) for want, old in zip(wanted, found))

        found = scan_tiles(count, find, tuple(jnp.int32(-1) for _ in BANDS))
        for band in range(8):
            tab_ref[band] = found[band]
        tab_ref[8] = jnp.where(my_y == GRID_Y - 1, 2, 1)
        for spare in range(9, 16):
            tab_ref[spare] = 0

        x = x_ref[0]
        cols = dot(stacked(x, FINE_IN), pack_ref[...])
        lane = lane_ids((ROWS, 128))
        for side in range(2):
            part = cols[:, side * 128 : side * 128 + 128]
            main = part[0:ROWS]
            for i in range(1, 5):
                main = main + pltpu.roll(part[i * ROWS : (i + 1) * ROWS], 24 * i, 1)
            cols_ref[side] = main.astype(BF)
            rest = pltpu.roll(part[5 * ROWS : 6 * ROWS], 16, 1)
            col_rest_ref[side] = rest[0:16] + pltpu.roll(rest[16:32], 40, 1) + pltpu.roll(rest[32:48], 80, 1)
        rows_ref[0] = x[:, 0:128]
        rows_ref[1] = x[:, 2176:2304]
        ends = (x[:, 128:256].astype(F32), pltpu.roll(x[:, 2048:2176].astype(F32), 16, 1))
        for side in range(2):
            rest = jnp.where(lane < 16, ends[side], 0.0)
            row_rest_ref[side] = rest[0:16] + pltpu.roll(rest[16:32], 40, 1) + pltpu.roll(rest[32:48], 80, 1)

        def fill(dev, carry):
            row_pick = quotient(tab_ref[16 + dev], 2)
            col_pick = remainder(tab_ref[16 + dev], 2)
            for g in range(3):
                msg_ref[dev, :, 256 * g : 256 * g + 128] = rows_ref[row_pick, 16 * g : 16 * g + 16, :]
                msg_ref[dev, :, 256 * g + 128 : 256 * g + 256] = cols_ref[col_pick, 16 * g : 16 * g + 16, :]
            msg_ref[dev, :, 768:896] = (row_rest_ref[row_pick] + col_rest_ref[col_pick]).astype(BF)
            return carry

        scan_tiles(count, fill, jnp.int32(0))

    return prep


def band_source(tab_ref, band):
    source = tab_ref[band]
    return jnp.maximum(source, 0), jnp.where(source >= 0, 1.0, 0.0).astype(F32)


def lane_shifted(value, lanes):
    return pltpu.roll(value, value.shape[1] - lanes, 1)


def tall(row_block):
    return jnp.concatenate([row_block] * (ROWS // 8), axis=0)


def lanes_from(value, index):
    return jnp.take_along_axis(value, index, axis=1)


def conv_inner(x_ref, weight_ref, bias_ref, sum_ref, middle_ref, mirror_ref, wide_ref, pad_ref, odd_ref, total_ref):
    for tap in range(49):
        wide_ref[tap] = jnp.broadcast_to(weight_ref[0, :, tap : tap + 1], (ROWS, 128))
    mirrored_taps(wide_ref, mirror_ref)
    pad_ref[:, 0:256] = jnp.zeros((ROWS, 256), F32)
    pad_ref[:, 3328:3584] = jnp.zeros((ROWS, 256), F32)
    lane = lane_ids((8, 128))
    half, within = lane // 64, lane % 64
    valid = tall((within >= 3) & (within < 51))
    col = jnp.clip(within - 3, 0, 47)
    cells = [96 * k + 48 * half + col for k in range(4)]
    indices = [tall(cell % 128) for cell in cells]
    for i in range(GROUPS):
        tiles = [x_ref[0, :, 384 * i + 128 * m : 384 * i + 128 * m + 128].astype(F32) for m in range(3)]
        for k in range(4):
            first, final = (96 * k) // 128, (96 * k + 95) // 128
            value = lanes_from(tiles[first], indices[k])
            if final != first:
                value = jnp.where(tall(cells[k] < 128 * final), value, lanes_from(tiles[final], indices[k]))
            start = 256 + 512 * i + 128 * k
            pad_ref[:, start : start + 128] = jnp.where(valid, value, 0.0)
    odd_ref[...] = lane_shifted(pad_ref[...], 64)
    total_ref[...] = wide(columns(bias_ref[0:1, :]), 3072)

    def group(g, carry):
        here = pl.ds(pl.multiple_of(g * 8, 8), 8)
        for chunk in range(6):
            base = chunk * 512
            taken = []
            for a in range(1, 8):
                ref = odd_ref if a % 2 else pad_ref
                start = base + (a // 2) * 128
                taken.append([ref[here, start + 128 * j : start + 128 * j + 128] for j in range(4)])
            total = [total_ref[here, base + 128 * j : base + 128 * j + 128] for j in range(4)]
            for b in range(7):
                weights = [wide_ref[a * 7 + b, here, :] for a in range(7)]
                for j in range(4):
                    partial = weights[0] * taken[0][j]
                    for a in range(1, 7):
                        partial = partial + weights[a] * taken[a][j]
                    total[j] = total[j] + (pltpu.roll(partial, (3 - b) % 128, 1) if b != 3 else partial)
            for j in range(4):
                total_ref[here, base + 128 * j : base + 128 * j + 128] = total[j]
        return carry

    lax.fori_loop(0, ROWS // 8, group, 0)
    for m in range((RIM + MIDDLE) // 128):
        row, col = place_of(m)
        index = tall(row % 2 * 64 + 3 + col)
        value = None
        for pair in pairs_of(m):
            picked = lanes_from(total_ref[:, 128 * pair : 128 * pair + 128], index)
            value = picked if value is None else jnp.where(tall(row // 2 == pair), picked, value)
        if m < RIM // 128:
            sum_ref[:, 128 * m : 128 * m + 128] = value
        else:
            middle_ref[:, 128 * m - RIM : 128 * m - RIM + 128] = value.astype(BF)


def place_of(m):
    lane = lane_ids((8, 128))
    if m < 6:
        cell = 128 * (m % 3) + lane
        return cell // 48 + (40 if m >= 3 else 0), cell % 48
    if m < 10:
        col = lane % 16
        return 8 * (m - 5) + lane // 16, jnp.where(col < 8, col, col + 32)
    return 8 + 4 * (m - 10) + lane // 32, 8 + lane % 32


def pairs_of(m):
    if m < 6:
        first = 128 * (m % 3)
        start = 20 if m >= 3 else 0
        return range(start + first // 96, start + (first + 127) // 96 + 1)
    if m < 10:
        return range(4 * (m - 5), 4 * (m - 5) + 4)
    return range(4 + 2 * (m - 10), 6 + 2 * (m - 10))


def column_sums(beside, mirror_ref):
    total = [jnp.zeros((ROWS, 128), F32)] * 3
    for a in range(7):
        if mirror_ref.shape[0] == 49:
            low_half = tall(lane_ids((8, 128)) < 64)
            weights = [jnp.where(low_half, mirror_ref[7 * a + b], mirror_ref[7 * a + 6 - b]) for b in range(3)]
        else:
            weights = [mirror_ref[4 * a + b] for b in range(3)]
        for q in range(3):
            partial = weights[0] * beside[q]
            for j in range(q + 1, 3):
                partial = partial + weights[j - q] * beside[j]
            total[q] = total[q] + (pltpu.roll(partial, (3 - a) % 128, 1) if a != 3 else partial)
    return total


def row_sums(uses, mirror_ref):
    places = 1 + max(place for place, _, _ in uses)
    taps = {a: whole_row(mirror_ref, a) for _, a, _ in uses}
    total = [jnp.zeros((ROWS, 128), F32)] * places
    for b in range(7):
        partial = [None] * places
        for place, a, cells in uses:
            term = taps[a][b] * cells
            partial[place] = term if partial[place] is None else partial[place] + term
        for place in range(places):
            total[place] = total[place] + (pltpu.roll(partial[place], (3 - b) % 128, 1) if b != 3 else partial[place])
    return total


def mirrored_taps(wide_ref, mirror_ref):
    low_half = tall(lane_ids((8, 128)) < 64)
    for a in range(7):
        for b in range(3):
            mirror_ref[4 * a + b] = jnp.where(low_half, wide_ref[a * 7 + b], wide_ref[a * 7 + 6 - b])
        mirror_ref[4 * a + 3] = wide_ref[a * 7 + 3]


def whole_row(mirror_ref, a):
    if mirror_ref.shape[0] == 49:
        return [mirror_ref[7 * a + b] for b in range(7)]
    low_half = tall(lane_ids((8, 128)) < 64)
    ends = [(mirror_ref[4 * a + b], pltpu.roll(mirror_ref[4 * a + b], 64, 1)) for b in range(3)]
    first = [jnp.where(low_half, plain, turned) for plain, turned in ends]
    last = [jnp.where(low_half, turned, plain) for plain, turned in ends]
    return first + [mirror_ref[4 * a + 3]] + last[::-1]


def conv_border(tab_ref, recv_ref, sum_ref, mirror_ref, out_ref):
    lane = lane_ids((8, 128))
    half, within = lane // 64, lane % 64
    low_half = tall(lane < 64)

    group = lax.broadcasted_iota(jnp.int32, (ROWS, 128), 0) // 16

    def band_cells(band, offset):
        source, scale = band_source(tab_ref, band)
        main = jnp.concatenate([recv_ref[source, :, 256 * g + offset : 256 * g + offset + 128] for g in range(3)], axis=0)
        return main.astype(F32) * scale, recv_ref[source, :, 768:896].astype(F32) * scale

    def halo_rows(bands, folded, last, rest_side):
        sides = [band_cells(band, 0) for band in bands]
        first_columns = jnp.where((lane + jnp.where(last, 16, 0)) % 48 < 24, 1, 0)
        ends = jnp.where(tall(first_columns + jnp.where(folded, 1, 0) == 1), sides[2][0], sides[0][0])
        rest_lane = lane_ids((16, 128)) % 40
        rests = jnp.where(rest_lane < 20, sides[1][1], pltpu.roll(sides[rest_side][1], 20, 1))
        rests = jnp.concatenate([rests] * 3, axis=0)
        tiles = []
        for first_row in (0, 2):
            row = first_row + half
            inner = (within >= 3) & (within < 51)
            col = jnp.where(within < 3, 45 + within, jnp.where(within < 51, within - 3, within - 51))
            index = row * 48 + col
            index = jnp.where(folded, 143 - index, index)
            in_main = index - jnp.where(last, 16, 0)
            rest = (in_main < 0) | (in_main > 127)
            in_rest = jnp.where(in_main < 0, in_main + 16, in_main - 128) + jnp.where(inner, 0, 20)
            main_index, rest_index = tall(in_main & 127), (tall(in_rest) + 40 * group) & 127
            value = jnp.where(tall(inner), lanes_from(sides[1][0], main_index), lanes_from(ends, main_index))
            value = jnp.where(tall(rest), lanes_from(rests, rest_index), value)
            tiles.append(jnp.where(tall((within < 54) & (row < 3)), value, 0.0))
        return tiles

    def joined(first, second):
        return jnp.where(low_half, pltpu.roll(first, 64, 1), pltpu.roll(second, 64, 1))

    zeros = jnp.zeros((ROWS, 128), F32)
    below = halo_rows((0, 1, 2), False, True, 2)
    first_fix = row_sums(((0, 0, below[0]), (0, 1, joined(below[0], below[1])), (0, 2, below[1]), (1, 0, below[1])), mirror_ref)
    folded = tab_ref[8] == 2
    above = halo_rows((5, 6, 7), folded, folded, 0)
    edge = joined(zeros, above[0])
    last_fix = row_sums(((0, 6, edge), (1, 4, edge), (1, 5, above[0]), (1, 6, joined(above[0], above[1]))), mirror_ref)

    left, right = [(main, jnp.concatenate([rest] * 3, axis=0)) for main, rest in (band_cells(3, 128), band_cells(4, 128))]
    beside = []
    for j in range(3):
        which = jnp.where(half == 0, j, 2 - j)
        in_main = jnp.minimum(3 * within + which, 127)
        main_index, rest_index = tall(in_main), tall(jnp.clip(3 * (within - 40) + 16 + which, 0, 39)) + 40 * group
        picked = [
            jnp.where(tall(within < 40), lanes_from(main, main_index), lanes_from(rest, rest_index)) for main, rest in (left, right)
        ]
        beside.append(jnp.where(tall(within < 48), jnp.where(low_half, picked[0], picked[1]), 0.0))
    column_fix = column_sums(beside, mirror_ref)
    fixes = {0: first_fix[0], 1: first_fix[1], 22: last_fix[0], 23: last_fix[1]}
    for m in range(RIM // 128):
        row, col = place_of(m)
        index = tall(jnp.where(col < 24, row, 64 + row))
        value = sum_ref[:, 128 * m : 128 * m + 128]
        fix = zeros
        for q in range(3):
            fix = jnp.where(tall((col == q) | (col == 47 - q)), lanes_from(column_fix[q], index), fix)
        value = value + fix
        row_index = tall(row % 2 * 64 + 3 + col)
        for pair in pairs_of(m):
            if pair in fixes:
                value = value + jnp.where(tall(row // 2 == pair), lanes_from(fixes[pair], row_index), 0.0)
        out_ref[:, 128 * m : 128 * m + 128] = value.astype(BF)


def params(
    after_ref, x_ref, mask_ref, gain_ref, shift_ref, up_ref, up_bias_ref, down_ref, down_bias_ref, scale_ref, pool_weight_ref, spread_weight_ref,
    pool_ref, rim_cells_ref, middle_cells_ref, rim_mask_ref, rim_weights_ref, *level_refs,
):
    me = lax.axis_index("chan")
    lane = lane_ids((192, 128))
    for level in range(2):
        weights_ref, values_ref = level_refs[2 * level : 2 * level + 2]
        row = slice(level, level + 1)
        spare = jnp.zeros((48, up_ref.shape[2]), BF)
        turned = jnp.concatenate([up_ref[level], three_terms(up_bias_ref[row, :]), spare], axis=0)
        weights_ref[0:768, :] = jnp.transpose(turned, (1, 0))
        own = down_ref[level, pl.ds(pl.multiple_of(me * ROWS, 16), ROWS), :]
        for j in range(3):
            weights_ref[768 + ROWS * j : 768 + ROWS * (j + 1), :] = own[:, 256 * j : 256 * j + 256]
        down_bias = columns(down_bias_ref[row, :])
        own = down_bias[0:ROWS]
        for k in range(1, down_bias.shape[0] // ROWS):
            own = jnp.where(me == k, down_bias[k * ROWS : (k + 1) * ROWS], own)
        rest = jnp.zeros((192 - ROWS, 128), F32)
        own, scale = [jnp.concatenate([value, rest], axis=0) for value in (own, columns(scale_ref[row, :]))]
        norm = jnp.where(lane == 0, columns(gain_ref[row, :]), columns(shift_ref[row, :]))
        values_ref[0:192, :] = jnp.where(lane < 2, norm, jnp.where(lane == 2, own, scale))
    fine_values_ref, coarse_values_ref = level_refs[1], level_refs[3]
    lane = lane_ids((ROWS, FINE_IN))
    rim_weights_ref[:, 0:384] = cell_weights(pool_weight_ref, lane // 48, lane % 48)
    spread = cell_weights(spread_weight_ref, lane // 48, lane % 48)
    for j in range(3):
        coarse_values_ref[240 + ROWS * j : 240 + ROWS * (j + 1), :] = spread[:, 128 * j : 128 * j + 128]
    lane = lane_ids((ROWS, 128))
    rim_weights_ref[:, 384:512] = cell_weights(pool_weight_ref, lane // 16, lane)
    fine_values_ref[192:240, :] = cell_weights(pool_weight_ref, lane // 32, lane)

    masks = []
    for i in range(GROUPS):
        masks.append(jnp.broadcast_to(mask_ref[:, i * FINE_IN : (i + 1) * FINE_IN].astype(F32), (8, FINE_IN)))
    counts = dot(jnp.concatenate(masks, axis=0).astype(BF), pool_ref[...])
    coarse_values_ref[192:240, :] = jnp.where(counts > 0.5, 1.0, 0.0)
    for m in range((RIM + MIDDLE) // 128):
        if m < 6:
            here = slice(128 * m, 128 * m + 128)
            source = 128 * (m if m < 3 else m + 12)
            rim_cells_ref[:, here] = x_ref[0, :, source : source + 128]
            rim_mask_ref[:, here] = jnp.broadcast_to(mask_ref[:, source : source + 128].astype(F32), (8, 128))
            continue
        row, col = place_of(m)
        cell = row * 48 + col
        first, final = (8 * (m - 5) * 48, 8 * (m - 4) * 48 - 1) if m < 10 else ((4 * m - 32) * 48 + 8, (4 * m - 29) * 48 + 39)
        index, value, mask = cell % 128, None, None
        for tile in range(first // 128, final // 128 + 1):
            lanes = slice(128 * tile, 128 * tile + 128)
            part = lanes_from(x_ref[0, :, lanes].astype(F32), tall(index))
            mask_part = lanes_from(jnp.broadcast_to(mask_ref[:, lanes].astype(F32), (8, 128)), index)
            value = part if value is None else jnp.where(tall(cell // 128 == tile), part, value)
            mask = mask_part if mask is None else jnp.where(cell // 128 == tile, mask_part, mask)
        if m < 10:
            rim_cells_ref[:, 128 * m : 128 * m + 128] = value.astype(BF)
            rim_mask_ref[:, 128 * m : 128 * m + 128] = mask
        else:
            middle_cells_ref[:, 128 * m - RIM : 128 * m - RIM + 128] = value.astype(BF)
            fine_values_ref[240 + 8 * (m - 10) : 248 + 8 * (m - 10), :] = mask


def in_rows(rim_ref, middle_ref, out_ref):
    out_ref[:, 0:FINE_IN] = rim_ref[:, 0:FINE_IN]
    out_ref[:, 5 * FINE_IN :] = rim_ref[:, FINE_IN : 2 * FINE_IN]
    for i in range(1, 5):
        rim = rim_ref[:, 768 + 128 * (i - 1) : 768 + 128 * i].astype(F32)
        middle = [middle_ref[:, 256 * (i - 1) + 128 * h : 256 * (i - 1) + 128 * h + 128].astype(F32) for h in range(2)]
        for m in range(3):
            cell = 128 * m + lane_ids((8, 128))
            row, col = cell // 48, cell % 48
            value = lanes_from(rim, tall((row * 16 + jnp.where(col < 8, col, col - 32)) & 127))
            in_middle = (col >= 8) & (col < 40)
            index = tall((row % 4 * 32 + col - 8) & 127)
            for h in range(2):
                if 192 * h < 128 * m + 128 and 192 * h + 192 > 128 * m:
                    value = jnp.where(tall(in_middle & (row // 4 == h)), lanes_from(middle[h], index), value)
            out_ref[:, i * FINE_IN + 128 * m : i * FINE_IN + 128 * m + 128] = value.astype(BF)


def conv_coarse(x_ref, weight_ref, bias_ref, sum_ref, wide_ref, pad_ref):
    for tap in range(49):
        wide_ref[tap] = jnp.broadcast_to(weight_ref[1, :, tap : tap + 1], (ROWS, 128))
    pad_ref[0, :, 0:128] = jnp.zeros((ROWS, 128), F32)
    pad_ref[0, :, 896:1024] = jnp.zeros((ROWS, 128), F32)
    pad_ref[0, :, 128:896] = x_ref[...].astype(F32)
    padded = pad_ref[0]
    for turn in range(1, 4):
        pad_ref[turn] = lane_shifted(padded, 32 * turn)
    sum_ref[...] = wide(columns(bias_ref[1:2, :]), 768)

    def group(g, carry):
        rows = pl.ds(pl.multiple_of(g * 8, 8), 8)
        for chunk in range(2):
            base = chunk * 384
            taken = []
            for a in range(1, 8):
                start = base + (a // 4) * 128
                taken.append([pad_ref[a % 4, rows, start + 128 * j : start + 128 * j + 128] for j in range(3)])
            total = [sum_ref[rows, base + 128 * j : base + 128 * j + 128] for j in range(3)]
            for b in range(7):
                weights = [wide_ref[a * 7 + b, rows, :] for a in range(7)]
                for j in range(3):
                    partial = weights[0] * taken[0][j]
                    for a in range(1, 7):
                        partial = partial + weights[a] * taken[a][j]
                    total[j] = total[j] + (pltpu.roll(partial, (3 - b) % 128, 1) if b != 3 else partial)
            for j in range(3):
                sum_ref[rows, base + 128 * j : base + 128 * j + 128] = total[j]
        return carry

    lax.fori_loop(0, 6, group, 0)


def border_coarse(tab_ref, recv_ref, sum_ref, mirror_ref, out_ref):
    lane = lane_ids((8, 128))
    half, within, segment, inside = lane // 64, lane % 64, lane // 32, lane % 32
    group = lax.broadcasted_iota(jnp.int32, (ROWS, 128), 0) // 16

    def band_main(band):
        source, scale = band_source(tab_ref, band)
        return jnp.concatenate([recv_ref[source, :, 128 * g : 128 * g + 128] for g in range(3)], axis=0).astype(F32) * scale

    def band_rest(band):
        source, scale = band_source(tab_ref, band)
        return jnp.concatenate([recv_ref[source, :, 384:512].astype(F32) * scale] * 3, axis=0)

    def halo_rows(bands, folded):
        col = jnp.where(inside < 3, 21 + inside, jnp.where(inside < 27, inside - 3, inside - 27))
        index = segment * 24 + col
        index = tall(jnp.where(folded, 71 - index, index) & 127)
        picked = [lanes_from(band_main(band), index) for band in bands]
        value = jnp.where(tall(inside < 3), picked[0], jnp.where(tall(inside < 27), picked[1], picked[2]))
        return jnp.where(tall((inside < 30) & (segment < 3)), value, 0.0)

    def turned(cells, lanes, kept):
        return jnp.where(tall(kept), pltpu.roll(cells, lanes, 1), 0.0)

    below = halo_rows((0, 1, 2), False)
    first_fix = row_sums(((0, 0, below), (0, 1, turned(below, 96, lane < 64)), (0, 2, turned(below, 64, lane < 32))), mirror_ref)[0]
    above = halo_rows((5, 6, 7), tab_ref[8] == 2)
    last_fix = row_sums(
        ((0, 6, turned(above, 32, lane >= 32)), (0, 5, turned(above, 64, lane >= 64)), (0, 4, turned(above, 96, lane >= 96))), mirror_ref
    )[0]
    sides = [(band_main(band), band_rest(band)) for band in (3, 4)]
    beside = []
    for j in range(3):
        which = jnp.where(half == 0, j, 2 - j)
        main_index = tall(jnp.minimum(72 + 3 * within + which, 127))
        rest_index = tall(jnp.clip(3 * (within - 16) + which, 0, 23)) + 24 * group
        picked = [
            jnp.where(tall(within < 16), lanes_from(main, main_index), lanes_from(rest, rest_index)) for main, rest in sides
        ]
        beside.append(jnp.where(tall(within < HALF), jnp.where(tall(half == 0), picked[0], picked[1]), 0.0))
    column_fix = column_sums(beside, mirror_ref)
    for m in range(GROUPS):
        row, col = 4 * m + segment, inside - 3
        index = tall(jnp.where(col < 12, row, 64 + row))
        value = sum_ref[:, 128 * m : 128 * m + 128]
        fix = jnp.zeros((ROWS, 128), F32)
        for q in range(3):
            fix = jnp.where(tall((col == q) | (col == 23 - q)), lanes_from(column_fix[q], index), fix)
        value = value + fix
        if m == 0:
            value = value + first_fix
        if m == GROUPS - 1:
            value = value + last_fix
        out_ref[:, 128 * m : 128 * m + 128] = value.astype(BF)


def gather_rows(pieces, cat_ref):
    me = lax.axis_index("chan")
    for k, piece in enumerate(pieces):
        first = pl.multiple_of(lax.bitwise_xor(me, k) * ROWS, 16)
        cat_ref[pl.ds(first, ROWS), :] = piece[...]


def make_branch(cat_ref, weights_ref, values_ref, block):
    def spread_lane(rows, lane):
        return wide(jnp.broadcast_to(values_ref[0:rows, lane : lane + 1], (rows, 128)), block)

    gain, shift, down_bias, scale = spread_lane(192, 0), spread_lane(192, 1), spread_lane(ROWS, 2), spread_lane(ROWS, 3)
    down = jnp.concatenate([weights_ref[768 + ROWS * j : 768 + ROWS * (j + 1), :] for j in range(3)], axis=1)
    inputs = 4 * ROWS

    def branch(start):
        values = cat_ref[0:inputs, start : start + block].astype(F32)
        mean = jnp.mean(values, axis=0, keepdims=True)
        centred = values - mean
        spread = jnp.mean(centred * centred, axis=0, keepdims=True)
        normed = (centred * lax.rsqrt(spread + norm_eps) * gain + shift).astype(BF)
        hidden = dot(weights_ref[0:768, 0 : inputs + 16], jnp.concatenate([normed, jnp.ones((16, block), BF)], axis=0))
        hidden = 0.5 * hidden * (1.0 + lax.erf(hidden * np.float32(0.5**0.5)))
        return scale * (dot(down, hidden.astype(BF)) + down_bias)

    return branch


def cell_weights(weight_ref, row, col):
    kind = 2 * (row % 2) + col % 2
    result = jnp.zeros(row.shape, F32)
    for k in range(4):
        result = jnp.where(kind == k, weight_ref[:, k : k + 1], result)
    return result


def pooled_cells(products, table):
    highs = [product.astype(BF) for product in products]
    lows = [(product - high.astype(F32)).astype(BF) for product, high in zip(products, highs)]
    return dot(jnp.concatenate(highs, axis=0), table) + dot(jnp.concatenate(lows, axis=0), table)


def make_mix_rim(count):
    def mix_rim(
        tab_ref, own_ref, p1_ref, p2_ref, p3_ref, x_ref, mask_ref, pool_cells_ref, weights_ref, values_ref, pool_ref, rim_pool_ref,
        middle_pooled_ref, fine_ref, msg_ref, all_pooled_ref, cat_ref, pooled_ref, mains_ref, rest_ref,
    ):
        gather_rows((own_ref, p1_ref, p2_ref, p3_ref), cat_ref)
        block = RIM // 2
        branch = make_branch(cat_ref, weights_ref, values_ref, block)
        for start in range(0, RIM, block):
            here = slice(start, start + block)
            value = x_ref[:, here].astype(F32) + branch(start)
            fine_ref[:, here] = (mask_ref[0:1, here] * value).astype(BF)

        weights = pool_cells_ref[:, 0:384]
        whole = pooled_cells([fine_ref[:, start : start + 384].astype(F32) * weights for start in (0, 384)], pool_ref[...])
        weights = pool_cells_ref[:, 384:512]
        rim = pooled_cells([fine_ref[:, 768 + 128 * i : 896 + 128 * i].astype(F32) * weights for i in range(4)], rim_pool_ref[...])
        pooled_ref[:, 0:128] = whole[0:ROWS].astype(BF)
        pooled_ref[:, 640:768] = whole[ROWS : 2 * ROWS].astype(BF)
        for i in range(4):
            pooled_ref[:, 128 * i + 128 : 128 * i + 256] = rim[i * ROWS : (i + 1) * ROWS].astype(BF)

        groups = [pooled_ref[:, 128 * i : 128 * i + 128].astype(F32) for i in range(GROUPS)]
        lane = lane_ids((8, 128))
        index = lane // 24 * 32 + 3 + lane % 24
        rows = [lanes_from(groups[0], tall(index & 127)), lanes_from(groups[5], tall((index + 32) & 127))]
        cell = jnp.clip(lane - 72, 0, 47)
        rest_cell = lane_ids((ROWS, 128)) - lax.broadcasted_iota(jnp.int32, (ROWS, 128), 0) // 16 * 24
        rest_valid = (rest_cell >= 0) & (rest_cell < 24)
        rest_cell = jnp.clip(rest_cell, 0, 23)
        for c in range(2):
            first = 24 if c else 3
            index = tall(cell // 3 % 4 * 32 + first + cell % 3)
            column = lanes_from(groups[0], index)
            for i in range(1, 4):
                column = jnp.where(tall(cell // 12 == i), lanes_from(groups[i], index), column)
            for r in range(2):
                mains_ref[2 * r + c] = jnp.where(tall(lane < 72), rows[r], column).astype(BF)
            index = rest_cell // 3 % 4 * 32 + first + rest_cell % 3
            rest = jnp.where(rest_cell < 12, lanes_from(groups[4], index), lanes_from(groups[5], index))
            rest = jnp.where(rest_valid, rest, 0.0)
            rest_ref[c] = (rest[0:16] + rest[16:32] + rest[32:48]).astype(BF)

        def fill(dev, carry):
            both = tab_ref[16 + dev]
            for g in range(3):
                msg_ref[dev, :, 128 * g : 128 * g + 128] = mains_ref[both, 16 * g : 16 * g + 16, :]
            msg_ref[dev, :, 384:512] = rest_ref[lax.bitwise_and(both, 1)]
            return carry

        scan_tiles(count, fill, jnp.int32(0))
        all_pooled_ref[...] = pooled_ref[...]
        for i in range(4):
            here = slice(128 * i + 128, 128 * i + 256)
            all_pooled_ref[:, here] = (pooled_ref[:, here].astype(F32) + middle_pooled_ref[:, 128 * i : 128 * i + 128].astype(F32)).astype(BF)

    return mix_rim


def mix_middle(
    own_ref, p1_ref, p2_ref, p3_ref, x_ref, weights_ref, values_ref, middle_pool_ref, fine_ref, pooled_ref, cat_ref
):
    gather_rows((own_ref, p1_ref, p2_ref, p3_ref), cat_ref)
    block = MIDDLE // 2
    branch = make_branch(cat_ref, weights_ref, values_ref, block)
    for start in range(0, MIDDLE, block):
        here = slice(start, start + block)
        value = x_ref[:, here].astype(F32) + branch(start)
        tiles = range(start // 128, (start + block) // 128)
        mask = jnp.concatenate([values_ref[240 + 8 * t : 241 + 8 * t, :] for t in tiles], axis=1)
        fine_ref[:, here] = (mask * value).astype(BF)
    weights = wide(values_ref[192:240, :], 256)
    middle = pooled_cells([fine_ref[:, 256 * i : 256 * i + 256].astype(F32) * weights for i in range(4)], middle_pool_ref[...])
    for i in range(4):
        pooled_ref[:, 128 * i : 128 * i + 128] = middle[i * ROWS : (i + 1) * ROWS].astype(BF)


def mix_coarse(
    own_ref, p1_ref, p2_ref, p3_ref, pooled_ref, fine_ref, mask_ref, weights_ref, values_ref, pool_ref, out_ref, cat_ref,
):
    gather_rows((own_ref, p1_ref, p2_ref, p3_ref), cat_ref)
    cells = cat_ref.shape[1]
    value = pooled_ref[...].astype(F32) + make_branch(cat_ref, weights_ref, values_ref, cells)(0)
    parts = []
    for i in range(GROUPS):
        parts.append((values_ref[192 + 8 * i : 193 + 8 * i, :] * value[:, 128 * i : 128 * i + 128]).astype(BF))
    spread = lax.dot_general(
        jnp.concatenate(parts, axis=0), pool_ref[...], (((1,), (1,)), ((), ())), preferred_element_type=F32
    )
    weights = jnp.concatenate([values_ref[240 + ROWS * j : 240 + ROWS * (j + 1), :] for j in range(3)], axis=1)
    for i in range(GROUPS):
        lanes = slice(i * FINE_IN, (i + 1) * FINE_IN)
        merged = fine_ref[:, lanes].astype(F32) + weights * spread[i * ROWS : (i + 1) * ROWS]
        out_ref[0, :, lanes] = (mask_ref[:, lanes].astype(F32) * merged).astype(BF)


VMEM = pl.BlockSpec(memory_space=pltpu.VMEM)
SMEM = pl.BlockSpec(memory_space=pltpu.SMEM)

def takes(microseconds):
    return pl.CostEstimate(flops=microseconds * 1_000_000_000, bytes_accessed=0, transcendentals=0)


def shaped(*shape, dtype=BF):
    return jax.ShapeDtypeStruct(shape, dtype)


PARAMS = pltpu.CompilerParams(vmem_limit_bytes=24 * 1024 * 1024)


def every_channel(own, first_work, later_work=lambda *results: ()):
    pairs = lambda bit: [(i, i ^ bit) for i in range(4)]
    across = lax.ppermute(own, "chan", pairs(2))
    near, *results = lax.optimization_barrier((own, *first_work(own)))
    beside = lax.ppermute(near, "chan", pairs(1))
    across, *results = lax.optimization_barrier((across, *results, *later_work(*results)))
    diagonal = lax.ppermute(across, "chan", pairs(1))
    return (own, beside, across, diagonal), results


def per_device(
    features, land_mask, wet_slots, device_of, depth_weight, depth_bias, norm_gain, norm_bias, up_weight, up_bias,
    down_weight, down_bias, layer_scale, pool_weight, spread_weight,
):
    count = wet_slots.shape[0]
    grid_x = 2 * count // GRID_Y
    cells = TILE * TILE
    pack = pl.pallas_call(
        strip_table, out_specs=VMEM, out_shape=shaped(FINE_IN, 256), compiler_params=PARAMS, cost_estimate=takes(2), name="strip_table"
    )()
    messages, table = pl.pallas_call(
        make_prep(grid_x),
        in_specs=[SMEM, SMEM, VMEM, VMEM],
        out_specs=[VMEM, SMEM],
        out_shape=[shaped(count, 16, 896), shaped(16 + count, dtype=jnp.int32)],
        scratch_shapes=[
            pltpu.VMEM((2, ROWS, 128), BF),
            pltpu.VMEM((2, ROWS, 128), BF),
            pltpu.VMEM((2, 16, 128), F32),
            pltpu.VMEM((2, 16, 128), F32),
        ],
        compiler_params=PARAMS,
        cost_estimate=takes(10),
        name="prep",
    )(wet_slots, device_of, features, pack)
    pool = jnp.asarray(POOL)
    arrived = lax.all_to_all(messages, "tile", 0, 0, tiled=True)
    inner, inner_middle, fine_taps = pl.pallas_call(
        lambda tab_ref, *refs: conv_inner(*refs),
        in_specs=[SMEM] + [VMEM] * 3,
        out_specs=[VMEM] * 3,
        out_shape=[shaped(ROWS, RIM, dtype=F32), shaped(ROWS, MIDDLE), shaped(28, ROWS, 128, dtype=F32)],
        scratch_shapes=[
            pltpu.VMEM((49, ROWS, 128), F32),
            pltpu.VMEM((ROWS, 3584), F32),
            pltpu.VMEM((ROWS, 3584), F32),
            pltpu.VMEM((ROWS, 3072), F32),
        ],
        compiler_params=PARAMS,
        cost_estimate=takes(4),
        name="conv_inner",
    )(table, features, depth_weight, depth_bias)
    conv = pl.pallas_call(
        conv_border,
        in_specs=[SMEM] + [VMEM] * 3,
        out_specs=VMEM,
        out_shape=shaped(ROWS, RIM),
        compiler_params=PARAMS,
        cost_estimate=takes(2),
        name="conv_border",
    )(table, arrived, inner, fine_taps)

    pairs = lambda bit: [(i, i ^ bit) for i in range(4)]
    middle_across = lax.ppermute(inner_middle, "chan", pairs(2))
    middle_beside = lax.ppermute(inner_middle, "chan", pairs(1))
    middle_across, _ = lax.optimization_barrier((middle_across, conv))
    middle_pieces = (inner_middle, middle_beside, middle_across, lax.ppermute(middle_across, "chan", pairs(1)))

    def mix_middle_cells(*results):
        return pl.pallas_call(
            mix_middle,
            in_specs=[VMEM] * 8,
            out_specs=[VMEM] * 2,
            out_shape=[shaped(ROWS, MIDDLE), shaped(ROWS, 512)],
            scratch_shapes=[pltpu.VMEM((4 * ROWS, MIDDLE), BF)],
            compiler_params=PARAMS,
            cost_estimate=takes(1),
            name="mix_middle",
        )(*middle_pieces, results[1], results[4], results[5], jnp.asarray(MIDDLE_POOL))

    def spread_params(own):
        shapes = [
            ((ROWS, RIM), BF), ((ROWS, MIDDLE), BF), ((8, RIM), F32), ((ROWS, 512), F32),
            ((912, 256), BF), ((304, 128), F32), ((912, 256), BF), ((384, 128), F32),
        ]
        return pl.pallas_call(
            params,
            in_specs=[VMEM] * 13,
            out_specs=[VMEM] * len(shapes),
            out_shape=[shaped(*shape, dtype=dtype) for shape, dtype in shapes],
            compiler_params=PARAMS,
            cost_estimate=takes(2),
            name="params",
        )(
            own, features, land_mask, norm_gain, norm_bias, jnp.swapaxes(up_weight, 1, 2), up_bias, down_weight, down_bias, layer_scale,
            pool_weight, spread_weight, pool,
        )

    pieces, results = every_channel(conv, spread_params, mix_middle_cells)
    rim_cells, _, rim_mask, rim_weights, fine_weights, fine_values, coarse_weights, coarse_values, middle, middle_pooled = results
    rim, messages, pooled = pl.pallas_call(
        make_mix_rim(count),
        in_specs=[SMEM] + [VMEM] * 12,
        out_specs=[VMEM] * 3,
        out_shape=[shaped(ROWS, RIM), shaped(count, 16, 512), shaped(ROWS, 768)],
        scratch_shapes=[
            pltpu.VMEM((4 * ROWS, RIM), BF),
            pltpu.VMEM((ROWS, 768), BF),
            pltpu.VMEM((4, ROWS, 128), BF),
            pltpu.VMEM((2, 16, 128), BF),
        ],
        compiler_params=PARAMS,
        cost_estimate=takes(3),
        name="mix_rim",
    )(
        table, *pieces, rim_cells, rim_mask, rim_weights, fine_weights, fine_values, pool, jnp.asarray(RIM_POOL),
        middle_pooled,
    )
    arrived = lax.all_to_all(messages, "tile", 0, 0, tiled=True)
    inner, taps = pl.pallas_call(
        conv_coarse,
        in_specs=[VMEM] * 3,
        out_specs=[VMEM] * 2,
        out_shape=[shaped(ROWS, 768, dtype=F32), shaped(49, ROWS, 128, dtype=F32)],
        scratch_shapes=[pltpu.VMEM((4, ROWS, 1024), F32)],
        compiler_params=PARAMS,
        cost_estimate=takes(2),
        name="conv_coarse",
    )(pooled, depth_weight, depth_bias)
    conv = pl.pallas_call(
        border_coarse,
        in_specs=[SMEM] + [VMEM] * 3,
        out_specs=VMEM,
        out_shape=shaped(ROWS, 768),
        compiler_params=PARAMS,
        cost_estimate=takes(1),
        name="border_coarse",
    )(table, arrived, inner, taps)

    def back_in_rows(own):
        return pl.pallas_call(
            lambda after_ref, *refs: in_rows(*refs),
            in_specs=[VMEM] * 3,
            out_specs=[VMEM],
            out_shape=[shaped(ROWS, cells)],
            compiler_params=PARAMS,
            cost_estimate=takes(1),
            name="in_rows",
        )(own, rim, middle)

    pieces, (fine,) = every_channel(conv, back_in_rows)
    return pl.pallas_call(
        mix_coarse,
        in_specs=[VMEM] * 10,
        out_specs=VMEM,
        out_shape=shaped(1, ROWS, cells),
        scratch_shapes=[pltpu.VMEM((4 * ROWS, 768), BF)],
        compiler_params=PARAMS,
        cost_estimate=takes(2),
        name="mix_coarse",
    )(*pieces, pooled, fine, land_mask, coarse_weights, coarse_values, pool)


def solution(mesh):
    placed = (
        P("tile", "chan", None),
        P("tile", None),
        P(),
        P(),
        P(None, "chan", None),
        P(None, "chan"),
        P(),
        P(),
        P(),
        P(),
        P(),
        P(),
        P(None, "chan"),
        P("chan", None),
        P("chan", None),
    )
    return jax.shard_map(
        per_device, mesh=mesh, in_specs=placed, out_specs=P("tile", "chan", None), check_vma=False
    )
```

```python
import jax
import jax.numpy as jnp
import ml_dtypes
import numpy as np
from jax import lax
from jax.experimental import pallas as pl
from jax.experimental.pallas import tpu as pltpu
from jax.sharding import PartitionSpec as P

TILE = 48
HALF = TILE // 2
GRID_Y = 4
GROUPS = 6
ROWS = 48
FINE_IN = 8 * TILE
RIM = 1280
MIDDLE = 1024
BANDS = ((-1, -1), (-1, 0), (-1, 1), (0, -1), (0, 1), (1, -1), (1, 0), (1, 1))
norm_eps = 1e-06
BF = jnp.bfloat16
F32 = jnp.float32


def one_hot(shape, pairs):
    table = np.zeros(shape, np.float32)
    for source, target in pairs:
        table[source, target] = 1.0
    return table.astype(ml_dtypes.bfloat16)


def pool_tables():
    dense, rim, middle = [], [], []
    for row in range(8):
        for col in range(48):
            target = (row // 2) * 32 + 3 + col // 2
            dense.append((row * 48 + col, target))
            if 8 <= col < 40:
                middle.append((row * 32 + col - 8, target))
            else:
                rim.append((row * 16 + (col if col < 8 else col - 32), target))
    return one_hot((384, 128), dense), one_hot((128, 128), rim), one_hot((256, 128), middle)


def coarse_spread_table():
    pairs = []
    for row in range(4):
        for col in range(HALF):
            if 4 <= col < 20:
                lane = 32 + row * 16 + col - 4
            else:
                lane = row * 8 + (col if col < 4 else col - 16)
            pairs += [(lane, (2 * row + u) * 48 + 2 * col + v) for u in range(2) for v in range(2)]
    return one_hot((128, 384), pairs)


POOL, RIM_POOL, MIDDLE_POOL = pool_tables()
COARSE_SPREAD = coarse_spread_table()


def dot(left, right):
    return jnp.dot(left, right, preferred_element_type=F32)


def stacked(value, width):
    return jnp.concatenate([value[:, i * width : (i + 1) * width] for i in range(GROUPS)], axis=0)


def lane_ids(shape):
    return lax.broadcasted_iota(jnp.int32, shape, 1)


def three_terms(row):
    high = row.astype(BF)
    rest = row - high.astype(F32)
    middle = rest.astype(BF)
    low = (rest - middle.astype(F32)).astype(BF)
    return jnp.concatenate([high, middle, low, jnp.zeros((13, row.shape[1]), BF)], axis=0)


def columns(row):
    return lax.dot_general(
        three_terms(row), jnp.ones((16, 128), BF), (((0,), (0,)), ((), ())), preferred_element_type=F32
    )


def wide(block, lanes):
    return jnp.concatenate([block] * (lanes // 128), axis=1)


def scan_tiles(count, step, carry):
    if count <= 16:
        for k in range(count):
            carry = step(k, carry)
        return carry
    return lax.fori_loop(0, count, step, carry)


def strip_table(pack_ref):
    shape = (FINE_IN, 256)
    source = lax.broadcasted_iota(jnp.int32, shape, 0)
    lane = lane_ids(shape)
    within = lane % 128
    wanted = (within // 3) * TILE + within % 3 + jnp.where(lane >= 128, TILE - 3, 0)
    pack_ref[...] = jnp.where((within < 24) & (source == wanted), 1.0, 0.0).astype(BF)


def quotient(value, divisor):
    if divisor & (divisor - 1) == 0:
        return lax.shift_right_logical(value, jnp.int32(divisor.bit_length() - 1))
    return lax.div(value, divisor)


def remainder(value, divisor):
    if divisor & (divisor - 1) == 0:
        return lax.bitwise_and(value, jnp.int32(divisor - 1))
    return lax.rem(value, divisor)


def make_prep(grid_x):
    def prep(slots_ref, dev_ref, x_ref, pack_ref, msg_ref, tab_ref, rows_ref, cols_ref, row_rest_ref, col_rest_ref):
        count = slots_ref.shape[0]
        me = lax.axis_index("tile")
        my_slot = scan_tiles(count, lambda k, c: c + jnp.where(dev_ref[k] == me, slots_ref[k], 0), jnp.int32(0))
        my_x = remainder(my_slot, grid_x)
        my_y = quotient(my_slot, grid_x)
        wanted = []
        for up_by, right_by in BANDS:
            near_x = remainder(my_x + (right_by + grid_x), grid_x)
            near_y = my_y + up_by
            folded = near_y >= GRID_Y
            from_x = jnp.where(folded, grid_x - 1 - near_x, near_x)
            from_y = jnp.where(folded, GRID_Y - 1, near_y)
            wanted.append(from_y * grid_x + from_x)

        def find(k, found):
            slot, dev = slots_ref[k], dev_ref[k]
            row_pick = jnp.where(quotient(slot, grid_x) + 1 == my_y, 0, 1)
            col_pick = jnp.where(remainder(slot, grid_x) == remainder(my_x + (grid_x - 1), grid_x), 0, 1)
            tab_ref[16 + dev] = 2 * row_pick + col_pick
            return tuple(jnp.where(slot == want, dev, old) for want, old in zip(wanted, found))

        found = scan_tiles(count, find, tuple(jnp.int32(-1) for _ in BANDS))
        for band in range(8):
            tab_ref[band] = found[band]
        tab_ref[8] = jnp.where(my_y == GRID_Y - 1, 2, 1)
        for spare in range(9, 16):
            tab_ref[spare] = 0

        x = x_ref[0]
        cols = dot(stacked(x, FINE_IN), pack_ref[...])
        lane = lane_ids((ROWS, 128))
        for side in range(2):
            part = cols[:, side * 128 : side * 128 + 128]
            main = part[0:ROWS]
            for i in range(1, 5):
                main = main + pltpu.roll(part[i * ROWS : (i + 1) * ROWS], 24 * i, 1)
            cols_ref[side] = main.astype(BF)
            rest = pltpu.roll(part[5 * ROWS : 6 * ROWS], 16, 1)
            col_rest_ref[side] = rest[0:16] + pltpu.roll(rest[16:32], 40, 1) + pltpu.roll(rest[32:48], 80, 1)
        rows_ref[0] = x[:, 0:128]
        rows_ref[1] = x[:, 2176:2304]
        ends = (x[:, 128:256].astype(F32), pltpu.roll(x[:, 2048:2176].astype(F32), 16, 1))
        for side in range(2):
            rest = jnp.where(lane < 16, ends[side], 0.0)
            row_rest_ref[side] = rest[0:16] + pltpu.roll(rest[16:32], 40, 1) + pltpu.roll(rest[32:48], 80, 1)

        def fill(dev, carry):
            row_pick = quotient(tab_ref[16 + dev], 2)
            col_pick = remainder(tab_ref[16 + dev], 2)
            for g in range(3):
                msg_ref[dev, :, 256 * g : 256 * g + 128] = rows_ref[row_pick, 16 * g : 16 * g + 16, :]
                msg_ref[dev, :, 256 * g + 128 : 256 * g + 256] = cols_ref[col_pick, 16 * g : 16 * g + 16, :]
            msg_ref[dev, :, 768:896] = (row_rest_ref[row_pick] + col_rest_ref[col_pick]).astype(BF)
            return carry

        scan_tiles(count, fill, jnp.int32(0))

    return prep


def band_source(tab_ref, band):
    source = tab_ref[band]
    return jnp.maximum(source, 0), jnp.where(source >= 0, 1.0, 0.0).astype(F32)


def lane_shifted(value, lanes):
    return pltpu.roll(value, value.shape[1] - lanes, 1)


def tall(row_block):
    return jnp.concatenate([row_block] * (ROWS // 8), axis=0)


def lanes_from(value, index):
    return jnp.take_along_axis(value, index, axis=1)


def conv_inner(x_ref, weight_ref, bias_ref, sum_ref, middle_ref, mirror_ref, wide_ref, pad_ref, odd_ref, total_ref):
    for tap in range(49):
        wide_ref[tap] = jnp.broadcast_to(weight_ref[0, :, tap : tap + 1], (ROWS, 128))
    mirrored_taps(wide_ref, mirror_ref)
    pad_ref[:, 0:256] = jnp.zeros((ROWS, 256), F32)
    pad_ref[:, 3328:3584] = jnp.zeros((ROWS, 256), F32)
    lane = lane_ids((8, 128))
    half, within = lane // 64, lane % 64
    valid = tall((within >= 3) & (within < 51))
    col = jnp.clip(within - 3, 0, 47)
    cells = [96 * k + 48 * half + col for k in range(4)]
    indices = [tall(cell % 128) for cell in cells]
    for i in range(GROUPS):
        tiles = [x_ref[0, :, 384 * i + 128 * m : 384 * i + 128 * m + 128].astype(F32) for m in range(3)]
        for k in range(4):
            first, final = (96 * k) // 128, (96 * k + 95) // 128
            value = lanes_from(tiles[first], indices[k])
            if final != first:
                value = jnp.where(tall(cells[k] < 128 * final), value, lanes_from(tiles[final], indices[k]))
            start = 256 + 512 * i + 128 * k
            pad_ref[:, start : start + 128] = jnp.where(valid, value, 0.0)
    odd_ref[...] = lane_shifted(pad_ref[...], 64)
    total_ref[...] = wide(columns(bias_ref[0:1, :]), 3072)

    def group(g, carry):
        here = pl.ds(pl.multiple_of(g * 8, 8), 8)
        for chunk in range(6):
            base = chunk * 512
            taken = []
            for a in range(1, 8):
                ref = odd_ref if a % 2 else pad_ref
                start = base + (a // 2) * 128
                taken.append([ref[here, start + 128 * j : start + 128 * j + 128] for j in range(4)])
            total = [total_ref[here, base + 128 * j : base + 128 * j + 128] for j in range(4)]
            for b in range(7):
                weights = [wide_ref[a * 7 + b, here, :] for a in range(7)]
                for j in range(4):
                    partial = weights[0] * taken[0][j]
                    for a in range(1, 7):
                        partial = partial + weights[a] * taken[a][j]
                    total[j] = total[j] + (pltpu.roll(partial, (3 - b) % 128, 1) if b != 3 else partial)
            for j in range(4):
                total_ref[here, base + 128 * j : base + 128 * j + 128] = total[j]
        return carry

    lax.fori_loop(0, ROWS // 8, group, 0)
    for m in range((RIM + MIDDLE) // 128):
        row, col = place_of(m)
        index = tall(row % 2 * 64 + 3 + col)
        value = None
        for pair in pairs_of(m):
            picked = lanes_from(total_ref[:, 128 * pair : 128 * pair + 128], index)
            value = picked if value is None else jnp.where(tall(row // 2 == pair), picked, value)
        if m < RIM // 128:
            sum_ref[:, 128 * m : 128 * m + 128] = value
        else:
            middle_ref[:, 128 * m - RIM : 128 * m - RIM + 128] = value.astype(BF)


def place_of(m):
    lane = lane_ids((8, 128))
    if m < 6:
        cell = 128 * (m % 3) + lane
        return cell // 48 + (40 if m >= 3 else 0), cell % 48
    if m < 10:
        col = lane % 16
        return 8 * (m - 5) + lane // 16, jnp.where(col < 8, col, col + 32)
    return 8 + 4 * (m - 10) + lane // 32, 8 + lane % 32


def pairs_of(m):
    if m < 6:
        first = 128 * (m % 3)
        start = 20 if m >= 3 else 0
        return range(start + first // 96, start + (first + 127) // 96 + 1)
    if m < 10:
        return range(4 * (m - 5), 4 * (m - 5) + 4)
    return range(4 + 2 * (m - 10), 6 + 2 * (m - 10))


def column_sums(beside, mirror_ref):
    total = [jnp.zeros((ROWS, 128), F32)] * 3
    for a in range(7):
        if mirror_ref.shape[0] == 49:
            low_half = tall(lane_ids((8, 128)) < 64)
            weights = [jnp.where(low_half, mirror_ref[7 * a + b], mirror_ref[7 * a + 6 - b]) for b in range(3)]
        else:
            weights = [mirror_ref[4 * a + b] for b in range(3)]
        for q in range(3):
            partial = weights[0] * beside[q]
            for j in range(q + 1, 3):
                partial = partial + weights[j - q] * beside[j]
            total[q] = total[q] + (pltpu.roll(partial, (3 - a) % 128, 1) if a != 3 else partial)
    return total


def row_sums(uses, mirror_ref):
    places = 1 + max(place for place, _, _ in uses)
    taps = {a: whole_row(mirror_ref, a) for _, a, _ in uses}
    total = [jnp.zeros((ROWS, 128), F32)] * places
    for b in range(7):
        partial = [None] * places
        for place, a, cells in uses:
            term = taps[a][b] * cells
            partial[place] = term if partial[place] is None else partial[place] + term
        for place in range(places):
            total[place] = total[place] + (pltpu.roll(partial[place], (3 - b) % 128, 1) if b != 3 else partial[place])
    return total


def mirrored_taps(wide_ref, mirror_ref):
    low_half = tall(lane_ids((8, 128)) < 64)
    for a in range(7):
        for b in range(3):
            mirror_ref[4 * a + b] = jnp.where(low_half, wide_ref[a * 7 + b], wide_ref[a * 7 + 6 - b])
        mirror_ref[4 * a + 3] = wide_ref[a * 7 + 3]


def whole_row(mirror_ref, a):
    if mirror_ref.shape[0] == 49:
        return [mirror_ref[7 * a + b] for b in range(7)]
    low_half = tall(lane_ids((8, 128)) < 64)
    ends = [(mirror_ref[4 * a + b], pltpu.roll(mirror_ref[4 * a + b], 64, 1)) for b in range(3)]
    first = [jnp.where(low_half, plain, turned) for plain, turned in ends]
    last = [jnp.where(low_half, turned, plain) for plain, turned in ends]
    return first + [mirror_ref[4 * a + 3]] + last[::-1]


def conv_border(tab_ref, recv_ref, sum_ref, mirror_ref, out_ref):
    lane = lane_ids((8, 128))
    half, within = lane // 64, lane % 64
    low_half = tall(lane < 64)

    group = lax.broadcasted_iota(jnp.int32, (ROWS, 128), 0) // 16

    def band_cells(band, offset):
        source, scale = band_source(tab_ref, band)
        main = jnp.concatenate([recv_ref[source, :, 256 * g + offset : 256 * g + offset + 128] for g in range(3)], axis=0)
        return main.astype(F32) * scale, recv_ref[source, :, 768:896].astype(F32) * scale

    def halo_rows(bands, folded, last, rest_side):
        sides = [band_cells(band, 0) for band in bands]
        first_columns = jnp.where((lane + jnp.where(last, 16, 0)) % 48 < 24, 1, 0)
        ends = jnp.where(tall(first_columns + jnp.where(folded, 1, 0) == 1), sides[2][0], sides[0][0])
        rest_lane = lane_ids((16, 128)) % 40
        rests = jnp.where(rest_lane < 20, sides[1][1], pltpu.roll(sides[rest_side][1], 20, 1))
        rests = jnp.concatenate([rests] * 3, axis=0)
        tiles = []
        for first_row in (0, 2):
            row = first_row + half
            inner = (within >= 3) & (within < 51)
            col = jnp.where(within < 3, 45 + within, jnp.where(within < 51, within - 3, within - 51))
            index = row * 48 + col
            index = jnp.where(folded, 143 - index, index)
            in_main = index - jnp.where(last, 16, 0)
            rest = (in_main < 0) | (in_main > 127)
            in_rest = jnp.where(in_main < 0, in_main + 16, in_main - 128) + jnp.where(inner, 0, 20)
            main_index, rest_index = tall(in_main & 127), (tall(in_rest) + 40 * group) & 127
            value = jnp.where(tall(inner), lanes_from(sides[1][0], main_index), lanes_from(ends, main_index))
            value = jnp.where(tall(rest), lanes_from(rests, rest_index), value)
            tiles.append(jnp.where(tall((within < 54) & (row < 3)), value, 0.0))
        return tiles

    def joined(first, second):
        return jnp.where(low_half, pltpu.roll(first, 64, 1), pltpu.roll(second, 64, 1))

    zeros = jnp.zeros((ROWS, 128), F32)
    below = halo_rows((0, 1, 2), False, True, 2)
    first_fix = row_sums(((0, 0, below[0]), (0, 1, joined(below[0], below[1])), (0, 2, below[1]), (1, 0, below[1])), mirror_ref)
    folded = tab_ref[8] == 2
    above = halo_rows((5, 6, 7), folded, folded, 0)
    edge = joined(zeros, above[0])
    last_fix = row_sums(((0, 6, edge), (1, 4, edge), (1, 5, above[0]), (1, 6, joined(above[0], above[1]))), mirror_ref)

    left, right = [(main, jnp.concatenate([rest] * 3, axis=0)) for main, rest in (band_cells(3, 128), band_cells(4, 128))]
    beside = []
    for j in range(3):
        which = jnp.where(half == 0, j, 2 - j)
        in_main = jnp.minimum(3 * within + which, 127)
        main_index, rest_index = tall(in_main), tall(jnp.clip(3 * (within - 40) + 16 + which, 0, 39)) + 40 * group
        picked = [
            jnp.where(tall(within < 40), lanes_from(main, main_index), lanes_from(rest, rest_index)) for main, rest in (left, right)
        ]
        beside.append(jnp.where(tall(within < 48), jnp.where(low_half, picked[0], picked[1]), 0.0))
    column_fix = column_sums(beside, mirror_ref)
    fixes = {0: first_fix[0], 1: first_fix[1], 22: last_fix[0], 23: last_fix[1]}
    for m in range(RIM // 128):
        row, col = place_of(m)
        index = tall(jnp.where(col < 24, row, 64 + row))
        value = sum_ref[:, 128 * m : 128 * m + 128]
        fix = zeros
        for q in range(3):
            fix = jnp.where(tall((col == q) | (col == 47 - q)), lanes_from(column_fix[q], index), fix)
        value = value + fix
        row_index = tall(row % 2 * 64 + 3 + col)
        for pair in pairs_of(m):
            if pair in fixes:
                value = value + jnp.where(tall(row // 2 == pair), lanes_from(fixes[pair], row_index), 0.0)
        out_ref[:, 128 * m : 128 * m + 128] = value.astype(BF)


def params(
    after_ref, x_ref, mask_ref, gain_ref, shift_ref, up_ref, up_bias_ref, down_ref, down_bias_ref, scale_ref, pool_weight_ref, spread_weight_ref,
    pool_ref, rim_cells_ref, middle_cells_ref, rim_mask_ref, rim_weights_ref, *level_refs,
):
    me = lax.axis_index("chan")
    lane = lane_ids((192, 128))
    for level in range(2):
        weights_ref, values_ref = level_refs[2 * level : 2 * level + 2]
        row = slice(level, level + 1)
        spare = jnp.zeros((48, up_ref.shape[2]), BF)
        turned = jnp.concatenate([up_ref[level], three_terms(up_bias_ref[row, :]), spare], axis=0)
        weights_ref[0:768, :] = jnp.transpose(turned, (1, 0))
        own = down_ref[level, pl.ds(pl.multiple_of(me * ROWS, 16), ROWS), :]
        for j in range(3):
            weights_ref[768 + ROWS * j : 768 + ROWS * (j + 1), :] = own[:, 256 * j : 256 * j + 256]
        down_bias = columns(down_bias_ref[row, :])
        own = down_bias[0:ROWS]
        for k in range(1, down_bias.shape[0] // ROWS):
            own = jnp.where(me == k, down_bias[k * ROWS : (k + 1) * ROWS], own)
        rest = jnp.zeros((192 - ROWS, 128), F32)
        own, scale = [jnp.concatenate([value, rest], axis=0) for value in (own, columns(scale_ref[row, :]))]
        norm = jnp.where(lane == 0, columns(gain_ref[row, :]), columns(shift_ref[row, :]))
        values_ref[0:192, :] = jnp.where(lane < 2, norm, jnp.where(lane == 2, own, scale))
    fine_values_ref, coarse_values_ref = level_refs[1], level_refs[3]
    lane = lane_ids((ROWS, FINE_IN))
    rim_weights_ref[:, 0:384] = cell_weights(pool_weight_ref, lane // 48, lane % 48)
    spread = cell_weights(spread_weight_ref, lane // 48, lane % 48)
    for j in range(3):
        coarse_values_ref[240 + ROWS * j : 240 + ROWS * (j + 1), :] = spread[:, 128 * j : 128 * j + 128]
    lane = lane_ids((ROWS, 128))
    rim_weights_ref[:, 384:512] = cell_weights(pool_weight_ref, lane // 16, lane)
    fine_values_ref[192:240, :] = cell_weights(pool_weight_ref, lane // 32, lane)

    masks = []
    for i in range(GROUPS):
        masks.append(jnp.broadcast_to(mask_ref[:, i * FINE_IN : (i + 1) * FINE_IN].astype(F32), (8, FINE_IN)))
    counts = dot(jnp.concatenate(masks, axis=0).astype(BF), pool_ref[...])
    small_mask = jnp.where(counts > 0.5, 1.0, 0.0)
    for m in range(5):
        coarse_values_ref[192 + 8 * m : 200 + 8 * m, :] = coarse_tile(m, lambda i: small_mask[8 * i : 8 * i + 8], lambda value: value)
    coarse_values_ref[232:240, :] = jnp.zeros((8, 128), F32)
    for m in range((RIM + MIDDLE) // 128):
        if m < 6:
            here = slice(128 * m, 128 * m + 128)
            source = 128 * (m if m < 3 else m + 12)
            rim_cells_ref[:, here] = x_ref[0, :, source : source + 128]
            rim_mask_ref[:, here] = jnp.broadcast_to(mask_ref[:, source : source + 128].astype(F32), (8, 128))
            continue
        row, col = place_of(m)
        cell = row * 48 + col
        first, final = (8 * (m - 5) * 48, 8 * (m - 4) * 48 - 1) if m < 10 else ((4 * m - 32) * 48 + 8, (4 * m - 29) * 48 + 39)
        index, value, mask = cell % 128, None, None
        for tile in range(first // 128, final // 128 + 1):
            lanes = slice(128 * tile, 128 * tile + 128)
            part = lanes_from(x_ref[0, :, lanes].astype(F32), tall(index))
            mask_part = lanes_from(jnp.broadcast_to(mask_ref[:, lanes].astype(F32), (8, 128)), index)
            value = part if value is None else jnp.where(tall(cell // 128 == tile), part, value)
            mask = mask_part if mask is None else jnp.where(cell // 128 == tile, mask_part, mask)
        if m < 10:
            rim_cells_ref[:, 128 * m : 128 * m + 128] = value.astype(BF)
            rim_mask_ref[:, 128 * m : 128 * m + 128] = mask
        else:
            middle_cells_ref[:, 128 * m - RIM : 128 * m - RIM + 128] = value.astype(BF)
            fine_values_ref[240 + 8 * (m - 10) : 248 + 8 * (m - 10), :] = mask


def in_rows(rim_ref, middle_ref, out_ref):
    out_ref[:, 0:FINE_IN] = rim_ref[:, 0:FINE_IN]
    out_ref[:, 5 * FINE_IN :] = rim_ref[:, FINE_IN : 2 * FINE_IN]
    for i in range(1, 5):
        rim = rim_ref[:, 768 + 128 * (i - 1) : 768 + 128 * i].astype(F32)
        middle = [middle_ref[:, 256 * (i - 1) + 128 * h : 256 * (i - 1) + 128 * h + 128].astype(F32) for h in range(2)]
        for m in range(3):
            cell = 128 * m + lane_ids((8, 128))
            row, col = cell // 48, cell % 48
            value = lanes_from(rim, tall((row * 16 + jnp.where(col < 8, col, col - 32)) & 127))
            in_middle = (col >= 8) & (col < 40)
            index = tall((row % 4 * 32 + col - 8) & 127)
            for h in range(2):
                if 192 * h < 128 * m + 128 and 192 * h + 192 > 128 * m:
                    value = jnp.where(tall(in_middle & (row // 4 == h)), lanes_from(middle[h], index), value)
            out_ref[:, i * FINE_IN + 128 * m : i * FINE_IN + 128 * m + 128] = value.astype(BF)


def conv_coarse(x_ref, weight_ref, bias_ref, rim_ref, middle_ref, cells_ref, wide_ref, pad_ref, sum_ref):
    for tap in range(49):
        wide_ref[tap] = jnp.broadcast_to(weight_ref[1, :, tap : tap + 1], (ROWS, 128))
    pad_ref[0, :, 0:128] = jnp.zeros((ROWS, 128), F32)
    pad_ref[0, :, 896:1024] = jnp.zeros((ROWS, 128), F32)
    pad_ref[0, :, 128:896] = x_ref[...].astype(F32)
    padded = pad_ref[0]
    for turn in range(1, 4):
        pad_ref[turn] = lane_shifted(padded, 32 * turn)
    sum_ref[...] = wide(columns(bias_ref[1:2, :]), 768)

    def group(g, carry):
        rows = pl.ds(pl.multiple_of(g * 8, 8), 8)
        for chunk in range(2):
            base = chunk * 384
            taken = []
            for a in range(1, 8):
                start = base + (a // 4) * 128
                taken.append([pad_ref[a % 4, rows, start + 128 * j : start + 128 * j + 128] for j in range(3)])
            total = [sum_ref[rows, base + 128 * j : base + 128 * j + 128] for j in range(3)]
            for b in range(7):
                weights = [wide_ref[a * 7 + b, rows, :] for a in range(7)]
                for j in range(3):
                    partial = weights[0] * taken[0][j]
                    for a in range(1, 7):
                        partial = partial + weights[a] * taken[a][j]
                    total[j] = total[j] + (pltpu.roll(partial, (3 - b) % 128, 1) if b != 3 else partial)
            for j in range(3):
                sum_ref[rows, base + 128 * j : base + 128 * j + 128] = total[j]
        return carry

    lax.fori_loop(0, 6, group, 0)
    for m in range(5):
        here = slice(128 * m, 128 * m + 128)
        cells_ref[:, here] = coarse_tile(m, lambda i: x_ref[:, 128 * i : 128 * i + 128].astype(F32)).astype(BF)
        value = coarse_tile(m, lambda i: sum_ref[:, 128 * i : 128 * i + 128])
        if m < 3:
            rim_ref[:, here] = value
        else:
            middle_ref[:, 128 * m - 384 : 128 * m - 256] = value.astype(BF)


def coarse_place(m):
    lane = lane_ids((8, 128))
    if m < 2:
        return 20 * m + lane // 32, lane % 32 - 3
    if m == 2:
        col = lane % 8
        return 4 + lane // 8, jnp.where(col < 4, col, col + 16)
    return 4 + 8 * (m - 3) + lane // 16, 4 + lane % 16


def coarse_tile(m, group, spread=tall):
    if m < 2:
        return group(5 * m)
    row, col = coarse_place(m)
    index, value = spread(row % 4 * 32 + 3 + col), None
    for i in range(1, 5) if m == 2 else range(2 * m - 5, 2 * m - 3):
        picked = lanes_from(group(i), index)
        value = picked if value is None else jnp.where(spread(row // 4 == i), picked, value)
    return value


def border_coarse(tab_ref, recv_ref, sum_ref, mirror_ref, out_ref):
    lane = lane_ids((8, 128))
    half, within, segment, inside = lane // 64, lane % 64, lane // 32, lane % 32
    group = lax.broadcasted_iota(jnp.int32, (ROWS, 128), 0) // 16

    def band_main(band):
        source, scale = band_source(tab_ref, band)
        return jnp.concatenate([recv_ref[source, :, 128 * g : 128 * g + 128] for g in range(3)], axis=0).astype(F32) * scale

    def band_rest(band):
        source, scale = band_source(tab_ref, band)
        return jnp.concatenate([recv_ref[source, :, 384:512].astype(F32) * scale] * 3, axis=0)

    def halo_rows(bands, folded):
        col = jnp.where(inside < 3, 21 + inside, jnp.where(inside < 27, inside - 3, inside - 27))
        index = segment * 24 + col
        index = tall(jnp.where(folded, 71 - index, index) & 127)
        picked = [lanes_from(band_main(band), index) for band in bands]
        value = jnp.where(tall(inside < 3), picked[0], jnp.where(tall(inside < 27), picked[1], picked[2]))
        return jnp.where(tall((inside < 30) & (segment < 3)), value, 0.0)

    def turned(cells, lanes, kept):
        return jnp.where(tall(kept), pltpu.roll(cells, lanes, 1), 0.0)

    below = halo_rows((0, 1, 2), False)
    first_fix = row_sums(((0, 0, below), (0, 1, turned(below, 96, lane < 64)), (0, 2, turned(below, 64, lane < 32))), mirror_ref)[0]
    above = halo_rows((5, 6, 7), tab_ref[8] == 2)
    last_fix = row_sums(
        ((0, 6, turned(above, 32, lane >= 32)), (0, 5, turned(above, 64, lane >= 64)), (0, 4, turned(above, 96, lane >= 96))), mirror_ref
    )[0]
    sides = [(band_main(band), band_rest(band)) for band in (3, 4)]
    beside = []
    for j in range(3):
        which = jnp.where(half == 0, j, 2 - j)
        main_index = tall(jnp.minimum(72 + 3 * within + which, 127))
        rest_index = tall(jnp.clip(3 * (within - 16) + which, 0, 23)) + 24 * group
        picked = [
            jnp.where(tall(within < 16), lanes_from(main, main_index), lanes_from(rest, rest_index)) for main, rest in sides
        ]
        beside.append(jnp.where(tall(within < HALF), jnp.where(tall(half == 0), picked[0], picked[1]), 0.0))
    column_fix = column_sums(beside, mirror_ref)
    for m in range(3):
        row, col = coarse_place(m)
        index = tall(jnp.where(col < 12, row, 64 + row))
        value = sum_ref[:, 128 * m : 128 * m + 128]
        fix = jnp.zeros((ROWS, 128), F32)
        for q in range(3):
            fix = jnp.where(tall((col == q) | (col == 23 - q)), lanes_from(column_fix[q], index), fix)
        value = value + fix
        if m < 2:
            value = value + (first_fix, last_fix)[m]
        out_ref[:, 128 * m : 128 * m + 128] = value.astype(BF)


def gather_rows(pieces, cat_ref):
    me = lax.axis_index("chan")
    for k, piece in enumerate(pieces):
        first = pl.multiple_of(lax.bitwise_xor(me, k) * ROWS, 16)
        cat_ref[pl.ds(first, ROWS), :] = piece[...]


def make_branch(cat_ref, weights_ref, values_ref, block):
    def spread_lane(rows, lane):
        return wide(jnp.broadcast_to(values_ref[0:rows, lane : lane + 1], (rows, 128)), block)

    gain, shift, down_bias, scale = spread_lane(192, 0), spread_lane(192, 1), spread_lane(ROWS, 2), spread_lane(ROWS, 3)
    down = jnp.concatenate([weights_ref[768 + ROWS * j : 768 + ROWS * (j + 1), :] for j in range(3)], axis=1)
    inputs = 4 * ROWS

    def branch(start):
        values = cat_ref[0:inputs, start : start + block].astype(F32)
        mean = jnp.mean(values, axis=0, keepdims=True)
        centred = values - mean
        spread = jnp.mean(centred * centred, axis=0, keepdims=True)
        normed = (centred * lax.rsqrt(spread + norm_eps) * gain + shift).astype(BF)
        hidden = dot(weights_ref[0:768, 0 : inputs + 16], jnp.concatenate([normed, jnp.ones((16, block), BF)], axis=0))
        hidden = 0.5 * hidden * (1.0 + lax.erf(hidden * np.float32(0.5**0.5)))
        return scale * (dot(down, hidden.astype(BF)) + down_bias)

    return branch


def cell_weights(weight_ref, row, col):
    kind = 2 * (row % 2) + col % 2
    result = jnp.zeros(row.shape, F32)
    for k in range(4):
        result = jnp.where(kind == k, weight_ref[:, k : k + 1], result)
    return result


def pooled_cells(products, table):
    highs = [product.astype(BF) for product in products]
    lows = [(product - high.astype(F32)).astype(BF) for product, high in zip(products, highs)]
    return dot(jnp.concatenate(highs, axis=0), table) + dot(jnp.concatenate(lows, axis=0), table)


def make_mix_rim(count):
    def mix_rim(
        tab_ref, own_ref, p1_ref, p2_ref, p3_ref, x_ref, mask_ref, pool_cells_ref, weights_ref, values_ref, pool_ref, rim_pool_ref,
        middle_pooled_ref, fine_ref, msg_ref, all_pooled_ref, cat_ref, pooled_ref, mains_ref, rest_ref,
    ):
        gather_rows((own_ref, p1_ref, p2_ref, p3_ref), cat_ref)
        block = RIM // 2
        branch = make_branch(cat_ref, weights_ref, values_ref, block)
        for start in range(0, RIM, block):
            here = slice(start, start + block)
            value = x_ref[:, here].astype(F32) + branch(start)
            fine_ref[:, here] = (mask_ref[0:1, here] * value).astype(BF)

        weights = pool_cells_ref[:, 0:384]
        whole = pooled_cells([fine_ref[:, start : start + 384].astype(F32) * weights for start in (0, 384)], pool_ref[...])
        weights = pool_cells_ref[:, 384:512]
        rim = pooled_cells([fine_ref[:, 768 + 128 * i : 896 + 128 * i].astype(F32) * weights for i in range(4)], rim_pool_ref[...])
        pooled_ref[:, 0:128] = whole[0:ROWS].astype(BF)
        pooled_ref[:, 640:768] = whole[ROWS : 2 * ROWS].astype(BF)
        for i in range(4):
            pooled_ref[:, 128 * i + 128 : 128 * i + 256] = rim[i * ROWS : (i + 1) * ROWS].astype(BF)

        groups = [pooled_ref[:, 128 * i : 128 * i + 128].astype(F32) for i in range(GROUPS)]
        lane = lane_ids((8, 128))
        index = lane // 24 * 32 + 3 + lane % 24
        rows = [lanes_from(groups[0], tall(index & 127)), lanes_from(groups[5], tall((index + 32) & 127))]
        cell = jnp.clip(lane - 72, 0, 47)
        rest_cell = lane_ids((ROWS, 128)) - lax.broadcasted_iota(jnp.int32, (ROWS, 128), 0) // 16 * 24
        rest_valid = (rest_cell >= 0) & (rest_cell < 24)
        rest_cell = jnp.clip(rest_cell, 0, 23)
        for c in range(2):
            first = 24 if c else 3
            index = tall(cell // 3 % 4 * 32 + first + cell % 3)
            column = lanes_from(groups[0], index)
            for i in range(1, 4):
                column = jnp.where(tall(cell // 12 == i), lanes_from(groups[i], index), column)
            for r in range(2):
                mains_ref[2 * r + c] = jnp.where(tall(lane < 72), rows[r], column).astype(BF)
            index = rest_cell // 3 % 4 * 32 + first + rest_cell % 3
            rest = jnp.where(rest_cell < 12, lanes_from(groups[4], index), lanes_from(groups[5], index))
            rest = jnp.where(rest_valid, rest, 0.0)
            rest_ref[c] = (rest[0:16] + rest[16:32] + rest[32:48]).astype(BF)

        def fill(dev, carry):
            both = tab_ref[16 + dev]
            for g in range(3):
                msg_ref[dev, :, 128 * g : 128 * g + 128] = mains_ref[both, 16 * g : 16 * g + 16, :]
            msg_ref[dev, :, 384:512] = rest_ref[lax.bitwise_and(both, 1)]
            return carry

        scan_tiles(count, fill, jnp.int32(0))
        all_pooled_ref[...] = pooled_ref[...]
        for i in range(4):
            here = slice(128 * i + 128, 128 * i + 256)
            all_pooled_ref[:, here] = (pooled_ref[:, here].astype(F32) + middle_pooled_ref[:, 128 * i : 128 * i + 128].astype(F32)).astype(BF)

    return mix_rim


def mix_middle(
    own_ref, p1_ref, p2_ref, p3_ref, x_ref, weights_ref, values_ref, middle_pool_ref, fine_ref, pooled_ref, cat_ref
):
    gather_rows((own_ref, p1_ref, p2_ref, p3_ref), cat_ref)
    block = MIDDLE // 2
    branch = make_branch(cat_ref, weights_ref, values_ref, block)
    for start in range(0, MIDDLE, block):
        here = slice(start, start + block)
        value = x_ref[:, here].astype(F32) + branch(start)
        tiles = range(start // 128, (start + block) // 128)
        mask = jnp.concatenate([values_ref[240 + 8 * t : 241 + 8 * t, :] for t in tiles], axis=1)
        fine_ref[:, here] = (mask * value).astype(BF)
    weights = wide(values_ref[192:240, :], 256)
    middle = pooled_cells([fine_ref[:, 256 * i : 256 * i + 256].astype(F32) * weights for i in range(4)], middle_pool_ref[...])
    for i in range(4):
        pooled_ref[:, 128 * i : 128 * i + 128] = middle[i * ROWS : (i + 1) * ROWS].astype(BF)


def coarse_cells(pieces, first, pooled_ref, weights_ref, values_ref, cat_ref):
    gather_rows(pieces, cat_ref)
    lanes = cat_ref.shape[1]
    value = pooled_ref[:, 128 * first : 128 * first + lanes].astype(F32) + make_branch(cat_ref, weights_ref, values_ref, lanes)(0)
    tiles = range(first, first + lanes // 128)
    return jnp.concatenate([values_ref[192 + 8 * m : 193 + 8 * m, :] for m in tiles], axis=1) * value


def mix_coarse_middle(own_ref, p1_ref, p2_ref, p3_ref, pooled_ref, weights_ref, values_ref, out_ref, cat_ref):
    out_ref[...] = coarse_cells((own_ref, p1_ref, p2_ref, p3_ref), 3, pooled_ref, weights_ref, values_ref, cat_ref).astype(BF)


def mix_coarse(
    own_ref, p1_ref, p2_ref, p3_ref, pooled_ref, middle_ref, fine_ref, mask_ref, weights_ref, values_ref, pool_ref, spread_ref, out_ref, cat_ref,
):
    rim = coarse_cells((own_ref, p1_ref, p2_ref, p3_ref), 0, pooled_ref, weights_ref, values_ref, cat_ref)
    ends = jnp.concatenate([rim[:, 0:128], rim[:, 128:256]], axis=0).astype(BF)
    ends = lax.dot_general(ends, pool_ref[...], (((1,), (1,)), ((), ())), preferred_element_type=F32)
    sides, lane = rim[:, 256:384], lane_ids((ROWS, 128))
    parts = []
    for i in range(4):
        middle = middle_ref[:, 128 * (i // 2) : 128 * (i // 2) + 128].astype(F32)
        side = pltpu.roll(sides, 128 - 32 * i, 1) if i else sides
        parts.append(jnp.where(lane < 32, side, pltpu.roll(middle, 96 if i % 2 else 32, 1)).astype(BF))
    inner = dot(jnp.concatenate(parts, axis=0), spread_ref[...])
    weights = jnp.concatenate([values_ref[240 + ROWS * j : 240 + ROWS * (j + 1), :] for j in range(3)], axis=1)
    for i in range(GROUPS):
        lanes = slice(i * FINE_IN, (i + 1) * FINE_IN)
        if i % 5 == 0:
            spread = ends[i // 5 * ROWS : (i // 5 + 1) * ROWS]
        else:
            spread = inner[(i - 1) * ROWS : i * ROWS]
        merged = fine_ref[:, lanes].astype(F32) + weights * spread
        out_ref[0, :, lanes] = (mask_ref[:, lanes].astype(F32) * merged).astype(BF)


VMEM = pl.BlockSpec(memory_space=pltpu.VMEM)
SMEM = pl.BlockSpec(memory_space=pltpu.SMEM)

def takes(microseconds):
    return pl.CostEstimate(flops=microseconds * 1_000_000_000, bytes_accessed=0, transcendentals=0)


def shaped(*shape, dtype=BF):
    return jax.ShapeDtypeStruct(shape, dtype)


PARAMS = pltpu.CompilerParams(vmem_limit_bytes=24 * 1024 * 1024)


def every_channel(own, first_work, later_work=lambda *results: ()):
    pairs = lambda bit: [(i, i ^ bit) for i in range(4)]
    across = lax.ppermute(own, "chan", pairs(2))
    near, *results = lax.optimization_barrier((own, *first_work(own)))
    beside = lax.ppermute(near, "chan", pairs(1))
    across, *results = lax.optimization_barrier((across, *results, *later_work(*results)))
    diagonal = lax.ppermute(across, "chan", pairs(1))
    return (own, beside, across, diagonal), results


def per_device(
    features, land_mask, wet_slots, device_of, depth_weight, depth_bias, norm_gain, norm_bias, up_weight, up_bias,
    down_weight, down_bias, layer_scale, pool_weight, spread_weight,
):
    count = wet_slots.shape[0]
    grid_x = 2 * count // GRID_Y
    cells = TILE * TILE
    pack = pl.pallas_call(
        strip_table, out_specs=VMEM, out_shape=shaped(FINE_IN, 256), compiler_params=PARAMS, cost_estimate=takes(2), name="strip_table"
    )()
    messages, table = pl.pallas_call(
        make_prep(grid_x),
        in_specs=[SMEM, SMEM, VMEM, VMEM],
        out_specs=[VMEM, SMEM],
        out_shape=[shaped(count, 16, 896), shaped(16 + count, dtype=jnp.int32)],
        scratch_shapes=[
            pltpu.VMEM((2, ROWS, 128), BF),
            pltpu.VMEM((2, ROWS, 128), BF),
            pltpu.VMEM((2, 16, 128), F32),
            pltpu.VMEM((2, 16, 128), F32),
        ],
        compiler_params=PARAMS,
        cost_estimate=takes(10),
        name="prep",
    )(wet_slots, device_of, features, pack)
    pool = jnp.asarray(POOL)
    arrived = lax.all_to_all(messages, "tile", 0, 0, tiled=True)
    inner, inner_middle, fine_taps = pl.pallas_call(
        lambda tab_ref, *refs: conv_inner(*refs),
        in_specs=[SMEM] + [VMEM] * 3,
        out_specs=[VMEM] * 3,
        out_shape=[shaped(ROWS, RIM, dtype=F32), shaped(ROWS, MIDDLE), shaped(28, ROWS, 128, dtype=F32)],
        scratch_shapes=[
            pltpu.VMEM((49, ROWS, 128), F32),
            pltpu.VMEM((ROWS, 3584), F32),
            pltpu.VMEM((ROWS, 3584), F32),
            pltpu.VMEM((ROWS, 3072), F32),
        ],
        compiler_params=PARAMS,
        cost_estimate=takes(4),
        name="conv_inner",
    )(table, features, depth_weight, depth_bias)
    conv = pl.pallas_call(
        conv_border,
        in_specs=[SMEM] + [VMEM] * 3,
        out_specs=VMEM,
        out_shape=shaped(ROWS, RIM),
        compiler_params=PARAMS,
        cost_estimate=takes(2),
        name="conv_border",
    )(table, arrived, inner, fine_taps)

    pairs = lambda bit: [(i, i ^ bit) for i in range(4)]
    middle_across = lax.ppermute(inner_middle, "chan", pairs(2))
    middle_beside = lax.ppermute(inner_middle, "chan", pairs(1))
    middle_across, _ = lax.optimization_barrier((middle_across, conv))
    middle_pieces = (inner_middle, middle_beside, middle_across, lax.ppermute(middle_across, "chan", pairs(1)))

    def mix_middle_cells(*results):
        return pl.pallas_call(
            mix_middle,
            in_specs=[VMEM] * 8,
            out_specs=[VMEM] * 2,
            out_shape=[shaped(ROWS, MIDDLE), shaped(ROWS, 512)],
            scratch_shapes=[pltpu.VMEM((4 * ROWS, MIDDLE), BF)],
            compiler_params=PARAMS,
            cost_estimate=takes(1),
            name="mix_middle",
        )(*middle_pieces, results[1], results[4], results[5], jnp.asarray(MIDDLE_POOL))

    def spread_params(own):
        shapes = [
            ((ROWS, RIM), BF), ((ROWS, MIDDLE), BF), ((8, RIM), F32), ((ROWS, 512), F32),
            ((912, 256), BF), ((304, 128), F32), ((912, 256), BF), ((384, 128), F32),
        ]
        return pl.pallas_call(
            params,
            in_specs=[VMEM] * 13,
            out_specs=[VMEM] * len(shapes),
            out_shape=[shaped(*shape, dtype=dtype) for shape, dtype in shapes],
            compiler_params=PARAMS,
            cost_estimate=takes(2),
            name="params",
        )(
            own, features, land_mask, norm_gain, norm_bias, jnp.swapaxes(up_weight, 1, 2), up_bias, down_weight, down_bias, layer_scale,
            pool_weight, spread_weight, pool,
        )

    pieces, results = every_channel(conv, spread_params, mix_middle_cells)
    rim_cells, _, rim_mask, rim_weights, fine_weights, fine_values, coarse_weights, coarse_values, middle, middle_pooled = results
    rim, messages, pooled = pl.pallas_call(
        make_mix_rim(count),
        in_specs=[SMEM] + [VMEM] * 12,
        out_specs=[VMEM] * 3,
        out_shape=[shaped(ROWS, RIM), shaped(count, 16, 512), shaped(ROWS, 768)],
        scratch_shapes=[
            pltpu.VMEM((4 * ROWS, RIM), BF),
            pltpu.VMEM((ROWS, 768), BF),
            pltpu.VMEM((4, ROWS, 128), BF),
            pltpu.VMEM((2, 16, 128), BF),
        ],
        compiler_params=PARAMS,
        cost_estimate=takes(3),
        name="mix_rim",
    )(
        table, *pieces, rim_cells, rim_mask, rim_weights, fine_weights, fine_values, pool, jnp.asarray(RIM_POOL),
        middle_pooled,
    )
    arrived = lax.all_to_all(messages, "tile", 0, 0, tiled=True)
    inner, middle_conv, pooled, taps = pl.pallas_call(
        conv_coarse,
        in_specs=[VMEM] * 3,
        out_specs=[VMEM] * 4,
        out_shape=[shaped(ROWS, 384, dtype=F32), shaped(ROWS, 256), shaped(ROWS, 640), shaped(49, ROWS, 128, dtype=F32)],
        scratch_shapes=[pltpu.VMEM((4, ROWS, 1024), F32), pltpu.VMEM((ROWS, 768), F32)],
        compiler_params=PARAMS,
        cost_estimate=takes(2),
        name="conv_coarse",
    )(pooled, depth_weight, depth_bias)
    conv = pl.pallas_call(
        border_coarse,
        in_specs=[SMEM] + [VMEM] * 3,
        out_specs=VMEM,
        out_shape=shaped(ROWS, 384),
        compiler_params=PARAMS,
        cost_estimate=takes(1),
        name="border_coarse",
    )(table, arrived, inner, taps)
    middle_across = lax.ppermute(middle_conv, "chan", pairs(2))
    middle_beside = lax.ppermute(middle_conv, "chan", pairs(1))
    middle_across, _ = lax.optimization_barrier((middle_across, conv))
    coarse_pieces = (middle_conv, middle_beside, middle_across, lax.ppermute(middle_across, "chan", pairs(1)))

    def back_in_rows(own):
        return pl.pallas_call(
            lambda after_ref, *refs: in_rows(*refs),
            in_specs=[VMEM] * 3,
            out_specs=[VMEM],
            out_shape=[shaped(ROWS, cells)],
            compiler_params=PARAMS,
            cost_estimate=takes(1),
            name="in_rows",
        )(own, rim, middle)

    def mix_coarse_cells(*results):
        return pl.pallas_call(
            mix_coarse_middle,
            in_specs=[VMEM] * 7,
            out_specs=[VMEM],
            out_shape=[shaped(ROWS, 256)],
            scratch_shapes=[pltpu.VMEM((4 * ROWS, 256), BF)],
            compiler_params=PARAMS,
            cost_estimate=takes(1),
            name="mix_coarse_middle",
        )(*coarse_pieces, pooled, coarse_weights, coarse_values)

    pieces, (fine, coarse_middle) = every_channel(conv, back_in_rows, mix_coarse_cells)
    return pl.pallas_call(
        mix_coarse,
        in_specs=[VMEM] * 12,
        out_specs=VMEM,
        out_shape=shaped(1, ROWS, cells),
        scratch_shapes=[pltpu.VMEM((4 * ROWS, 384), BF)],
        compiler_params=PARAMS,
        cost_estimate=takes(2),
        name="mix_coarse",
    )(*pieces, pooled, coarse_middle, fine, land_mask, coarse_weights, coarse_values, pool, jnp.asarray(COARSE_SPREAD))


def solution(mesh):
    placed = (
        P("tile", "chan", None),
        P("tile", None),
        P(),
        P(),
        P(None, "chan", None),
        P(None, "chan"),
        P(),
        P(),
        P(),
        P(),
        P(),
        P(),
        P(None, "chan"),
        P("chan", None),
        P("chan", None),
    )
    return jax.shard_map(
        per_device, mesh=mesh, in_specs=placed, out_specs=P("tile", "chan", None), check_vma=False
    )
```

```python
import jax
import jax.numpy as jnp
import ml_dtypes
import numpy as np
from jax import lax
from jax.experimental import pallas as pl
from jax.experimental.pallas import tpu as pltpu
from jax.sharding import PartitionSpec as P

TILE = 48
HALF = TILE // 2
GRID_Y = 4
GROUPS = 6
ROWS = 48
FINE_IN = 8 * TILE
RIM = 896
MIDDLE = 1664
BANDS = ((-1, -1), (-1, 0), (-1, 1), (0, -1), (0, 1), (1, -1), (1, 0), (1, 1))
norm_eps = 1e-06
BF = jnp.bfloat16
F32 = jnp.float32


def one_hot(shape, pairs):
    table = np.zeros(shape, np.float32)
    for source, target in pairs:
        table[source, target] = 1.0
    return table.astype(ml_dtypes.bfloat16)


def pool_table():
    return one_hot((384, 128), [(row * 48 + col, (row // 2) * 32 + 3 + col // 2) for row in range(8) for col in range(48)])


def coarse_spread_table():
    pairs = []
    for row in range(4):
        for col in range(HALF):
            if 4 <= col < 20:
                lane = 32 + row * 16 + col - 4
            else:
                lane = row * 8 + (col if col < 4 else col - 16)
            pairs += [(lane, (2 * row + u) * 48 + 2 * col + v) for u in range(2) for v in range(2)]
    return one_hot((128, 384), pairs)


POOL = pool_table()
COARSE_SPREAD = coarse_spread_table()


def dot(left, right):
    return jnp.dot(left, right, preferred_element_type=F32)


def stacked(value, width):
    return jnp.concatenate([value[:, i * width : (i + 1) * width] for i in range(GROUPS)], axis=0)


def lane_ids(shape):
    return lax.broadcasted_iota(jnp.int32, shape, 1)


def three_terms(row):
    high = row.astype(BF)
    rest = row - high.astype(F32)
    middle = rest.astype(BF)
    low = (rest - middle.astype(F32)).astype(BF)
    return jnp.concatenate([high, middle, low, jnp.zeros((13, row.shape[1]), BF)], axis=0)


def columns(row):
    return lax.dot_general(
        three_terms(row), jnp.ones((16, 128), BF), (((0,), (0,)), ((), ())), preferred_element_type=F32
    )


def wide(block, lanes):
    return jnp.concatenate([block] * (lanes // 128), axis=1)


def scan_tiles(count, step, carry):
    if count <= 16:
        for k in range(count):
            carry = step(k, carry)
        return carry
    return lax.fori_loop(0, count, step, carry)


def strip_table(pack_ref):
    shape = (FINE_IN, 256)
    source = lax.broadcasted_iota(jnp.int32, shape, 0)
    lane = lane_ids(shape)
    within = lane % 128
    wanted = (within // 3) * TILE + within % 3 + jnp.where(lane >= 128, TILE - 3, 0)
    pack_ref[...] = jnp.where((within < 24) & (source == wanted), 1.0, 0.0).astype(BF)


def quotient(value, divisor):
    if divisor & (divisor - 1) == 0:
        return lax.shift_right_logical(value, jnp.int32(divisor.bit_length() - 1))
    return lax.div(value, divisor)


def remainder(value, divisor):
    if divisor & (divisor - 1) == 0:
        return lax.bitwise_and(value, jnp.int32(divisor - 1))
    return lax.rem(value, divisor)


def make_prep(grid_x):
    def prep(slots_ref, dev_ref, x_ref, pack_ref, msg_ref, tab_ref, rows_ref, cols_ref, row_rest_ref, col_rest_ref):
        count = slots_ref.shape[0]
        me = lax.axis_index("tile")
        my_slot = scan_tiles(count, lambda k, c: c + jnp.where(dev_ref[k] == me, slots_ref[k], 0), jnp.int32(0))
        my_x = remainder(my_slot, grid_x)
        my_y = quotient(my_slot, grid_x)
        wanted = []
        for up_by, right_by in BANDS:
            near_x = remainder(my_x + (right_by + grid_x), grid_x)
            near_y = my_y + up_by
            folded = near_y >= GRID_Y
            from_x = jnp.where(folded, grid_x - 1 - near_x, near_x)
            from_y = jnp.where(folded, GRID_Y - 1, near_y)
            wanted.append(from_y * grid_x + from_x)

        def find(k, found):
            slot, dev = slots_ref[k], dev_ref[k]
            row_pick = jnp.where(quotient(slot, grid_x) + 1 == my_y, 0, 1)
            col_pick = jnp.where(remainder(slot, grid_x) == remainder(my_x + (grid_x - 1), grid_x), 0, 1)
            tab_ref[16 + dev] = 2 * row_pick + col_pick
            return tuple(jnp.where(slot == want, dev, old) for want, old in zip(wanted, found))

        found = scan_tiles(count, find, tuple(jnp.int32(-1) for _ in BANDS))
        for band in range(8):
            tab_ref[band] = found[band]
        tab_ref[8] = jnp.where(my_y == GRID_Y - 1, 2, 1)
        for spare in range(9, 16):
            tab_ref[spare] = 0

        x = x_ref[0]
        cols = dot(stacked(x, FINE_IN), pack_ref[...])
        lane = lane_ids((ROWS, 128))
        for side in range(2):
            part = cols[:, side * 128 : side * 128 + 128]
            main = part[0:ROWS]
            for i in range(1, 5):
                main = main + pltpu.roll(part[i * ROWS : (i + 1) * ROWS], 24 * i, 1)
            cols_ref[side] = main.astype(BF)
            rest = pltpu.roll(part[5 * ROWS : 6 * ROWS], 16, 1)
            col_rest_ref[side] = rest[0:16] + pltpu.roll(rest[16:32], 40, 1) + pltpu.roll(rest[32:48], 80, 1)
        rows_ref[0] = x[:, 0:128]
        rows_ref[1] = x[:, 2176:2304]
        ends = (x[:, 128:256].astype(F32), pltpu.roll(x[:, 2048:2176].astype(F32), 16, 1))
        for side in range(2):
            rest = jnp.where(lane < 16, ends[side], 0.0)
            row_rest_ref[side] = rest[0:16] + pltpu.roll(rest[16:32], 40, 1) + pltpu.roll(rest[32:48], 80, 1)

        def fill(dev, carry):
            row_pick = quotient(tab_ref[16 + dev], 2)
            col_pick = remainder(tab_ref[16 + dev], 2)
            for g in range(3):
                msg_ref[dev, :, 256 * g : 256 * g + 128] = rows_ref[row_pick, 16 * g : 16 * g + 16, :]
                msg_ref[dev, :, 256 * g + 128 : 256 * g + 256] = cols_ref[col_pick, 16 * g : 16 * g + 16, :]
            msg_ref[dev, :, 768:896] = (row_rest_ref[row_pick] + col_rest_ref[col_pick]).astype(BF)
            return carry

        scan_tiles(count, fill, jnp.int32(0))

    return prep


def band_source(tab_ref, band):
    source = tab_ref[band]
    return jnp.maximum(source, 0), jnp.where(source >= 0, 1.0, 0.0).astype(F32)


def lane_shifted(value, lanes):
    return pltpu.roll(value, value.shape[1] - lanes, 1)


def tall(row_block):
    return jnp.concatenate([row_block] * (ROWS // 8), axis=0)


def lanes_from(value, index):
    return jnp.take_along_axis(value, index, axis=1)


def conv_inner(x_ref, weight_ref, bias_ref, sum_ref, middle_ref, mirror_ref, wide_ref, pad_ref, odd_ref, total_ref):
    for tap in range(49):
        wide_ref[tap] = jnp.broadcast_to(weight_ref[0, :, tap : tap + 1], (ROWS, 128))
    mirrored_taps(wide_ref, mirror_ref)
    pad_ref[:, 0:256] = jnp.zeros((ROWS, 256), F32)
    pad_ref[:, 3328:3584] = jnp.zeros((ROWS, 256), F32)
    lane = lane_ids((8, 128))
    half, within = lane // 64, lane % 64
    valid = tall((within >= 3) & (within < 51))
    col = jnp.clip(within - 3, 0, 47)
    cells = [96 * k + 48 * half + col for k in range(4)]
    indices = [tall(cell % 128) for cell in cells]
    for i in range(GROUPS):
        tiles = [x_ref[0, :, 384 * i + 128 * m : 384 * i + 128 * m + 128].astype(F32) for m in range(3)]
        for k in range(4):
            first, final = (96 * k) // 128, (96 * k + 95) // 128
            value = lanes_from(tiles[first], indices[k])
            if final != first:
                value = jnp.where(tall(cells[k] < 128 * final), value, lanes_from(tiles[final], indices[k]))
            start = 256 + 512 * i + 128 * k
            pad_ref[:, start : start + 128] = jnp.where(valid, value, 0.0)
    odd_ref[...] = lane_shifted(pad_ref[...], 64)
    total_ref[...] = wide(columns(bias_ref[0:1, :]), 3072)

    def group(g, carry):
        here = pl.ds(pl.multiple_of(g * 8, 8), 8)
        for chunk in range(6):
            base = chunk * 512
            taken = []
            for a in range(1, 8):
                ref = odd_ref if a % 2 else pad_ref
                start = base + (a // 2) * 128
                taken.append([ref[here, start + 128 * j : start + 128 * j + 128] for j in range(4)])
            total = [total_ref[here, base + 128 * j : base + 128 * j + 128] for j in range(4)]
            for b in range(7):
                weights = [wide_ref[a * 7 + b, here, :] for a in range(7)]
                for j in range(4):
                    partial = weights[0] * taken[0][j]
                    for a in range(1, 7):
                        partial = partial + weights[a] * taken[a][j]
                    total[j] = total[j] + (pltpu.roll(partial, (3 - b) % 128, 1) if b != 3 else partial)
            for j in range(4):
                total_ref[here, base + 128 * j : base + 128 * j + 128] = total[j]
        return carry

    lax.fori_loop(0, ROWS // 8, group, 0)
    for m in range((RIM + MIDDLE) // 128):
        row, col = place_of(m)
        index = tall(row % 2 * 64 + 3 + col)
        value = None
        for pair in pairs_of(m):
            picked = lanes_from(total_ref[:, 128 * pair : 128 * pair + 128], index)
            value = picked if value is None else jnp.where(tall(row // 2 == pair), picked, value)
        if m < RIM // 128:
            sum_ref[:, 128 * m : 128 * m + 128] = value
        else:
            middle_ref[:, 128 * m - RIM : 128 * m - RIM + 128] = value.astype(BF)


def place_of(m, lane=None, ops=jnp):
    lane = lane_ids((8, 128)) if lane is None else lane
    if m < 4:
        return (2 * m if m < 2 else 40 + 2 * m) + lane // 64, ops.minimum(lane % 64, 47)
    if m < 7:
        col = lane % 8
        return ops.minimum(16 * m - 60 + lane // 8, 43), ops.where(col < 4, col, col + 40)
    cell = ops.minimum(128 * m - RIM + lane, 1599)
    return 4 + cell // 40, 4 + cell % 40


def pairs_of(m):
    return np.unique(place_of(m, np.arange(128), np)[0] // 2).tolist()


def sources_of(m):
    row, col = place_of(m, np.arange(128), np)
    return np.unique((row * 48 + col) // 128).tolist()


def lane_of(row, col, ops=jnp):
    ends = (row < 4) | (row >= 44)
    end = ops.where(row < 4, row, row - 40)
    side = (col < 4) | (col >= 44)
    cell = (row - 4) * 40 + col - 4
    tile = ops.where(ends, end // 2, ops.where(side, 4 + (row - 4) // 16, 7 + cell // 128))
    side_lane = (row - 4) % 16 * 8 + ops.where(col < 4, col, col - 40)
    return tile, ops.where(ends, end % 2 * 64 + col, ops.where(side, side_lane, cell % 128)) & 127


def collected(tiles, row, col, static_row, static_col, pick):
    tile, index = lane_of(row, col)
    value = None
    for m in np.unique(lane_of(static_row, static_col, np)[0]).tolist():
        if not pick(m):
            continue
        part = jnp.where(tall(tile == m), lanes_from(tiles(m), tall(index)), 0.0 if value is None else value)
        value = part
    return jnp.zeros((ROWS, 128), F32) if value is None else value


def coarse_from(i, sums, pick):
    def place(lane, ops):
        return 2 * (4 * i + lane // 32), 2 * ops.clip(lane % 32 - 3, 0, 23)

    lane = lane_ids((8, 128))
    inside = lane % 32
    row, col = place(lane, jnp)
    value = collected(sums, row, col, *place(np.arange(128), np), pick)
    return jnp.where(tall((inside >= 3) & (inside < 27)), value, 0.0)


def column_sums(beside, mirror_ref):
    total = [jnp.zeros((ROWS, 128), F32)] * 3
    for a in range(7):
        if mirror_ref.shape[0] == 49:
            low_half = tall(lane_ids((8, 128)) < 64)
            weights = [jnp.where(low_half, mirror_ref[7 * a + b], mirror_ref[7 * a + 6 - b]) for b in range(3)]
        else:
            weights = [mirror_ref[4 * a + b] for b in range(3)]
        for q in range(3):
            partial = weights[0] * beside[q]
            for j in range(q + 1, 3):
                partial = partial + weights[j - q] * beside[j]
            total[q] = total[q] + (pltpu.roll(partial, (3 - a) % 128, 1) if a != 3 else partial)
    return total


def row_sums(uses, mirror_ref):
    places = 1 + max(place for place, _, _ in uses)
    taps = {a: whole_row(mirror_ref, a) for _, a, _ in uses}
    total = [jnp.zeros((ROWS, 128), F32)] * places
    for b in range(7):
        partial = [None] * places
        for place, a, cells in uses:
            term = taps[a][b] * cells
            partial[place] = term if partial[place] is None else partial[place] + term
        for place in range(places):
            total[place] = total[place] + (pltpu.roll(partial[place], (3 - b) % 128, 1) if b != 3 else partial[place])
    return total


def mirrored_taps(wide_ref, mirror_ref):
    low_half = tall(lane_ids((8, 128)) < 64)
    for a in range(7):
        for b in range(3):
            mirror_ref[4 * a + b] = jnp.where(low_half, wide_ref[a * 7 + b], wide_ref[a * 7 + 6 - b])
        mirror_ref[4 * a + 3] = wide_ref[a * 7 + 3]


def whole_row(mirror_ref, a):
    if mirror_ref.shape[0] == 49:
        return [mirror_ref[7 * a + b] for b in range(7)]
    low_half = tall(lane_ids((8, 128)) < 64)
    ends = [(mirror_ref[4 * a + b], pltpu.roll(mirror_ref[4 * a + b], 64, 1)) for b in range(3)]
    first = [jnp.where(low_half, plain, turned) for plain, turned in ends]
    last = [jnp.where(low_half, turned, plain) for plain, turned in ends]
    return first + [mirror_ref[4 * a + 3]] + last[::-1]


def conv_border(tab_ref, recv_ref, sum_ref, mirror_ref, out_ref):
    lane = lane_ids((8, 128))
    half, within = lane // 64, lane % 64
    low_half = tall(lane < 64)

    group = lax.broadcasted_iota(jnp.int32, (ROWS, 128), 0) // 16

    def band_cells(band, offset):
        source, scale = band_source(tab_ref, band)
        main = jnp.concatenate([recv_ref[source, :, 256 * g + offset : 256 * g + offset + 128] for g in range(3)], axis=0)
        return main.astype(F32) * scale, recv_ref[source, :, 768:896].astype(F32) * scale

    def halo_rows(bands, folded, last, rest_side):
        sides = [band_cells(band, 0) for band in bands]
        first_columns = jnp.where((lane + jnp.where(last, 16, 0)) % 48 < 24, 1, 0)
        ends = jnp.where(tall(first_columns + jnp.where(folded, 1, 0) == 1), sides[2][0], sides[0][0])
        rest_lane = lane_ids((16, 128)) % 40
        rests = jnp.where(rest_lane < 20, sides[1][1], pltpu.roll(sides[rest_side][1], 20, 1))
        rests = jnp.concatenate([rests] * 3, axis=0)
        tiles = []
        for first_row in (0, 2):
            row = first_row + half
            inner = (within >= 3) & (within < 51)
            col = jnp.where(within < 3, 45 + within, jnp.where(within < 51, within - 3, within - 51))
            index = row * 48 + col
            index = jnp.where(folded, 143 - index, index)
            in_main = index - jnp.where(last, 16, 0)
            rest = (in_main < 0) | (in_main > 127)
            in_rest = jnp.where(in_main < 0, in_main + 16, in_main - 128) + jnp.where(inner, 0, 20)
            main_index, rest_index = tall(in_main & 127), (tall(in_rest) + 40 * group) & 127
            value = jnp.where(tall(inner), lanes_from(sides[1][0], main_index), lanes_from(ends, main_index))
            value = jnp.where(tall(rest), lanes_from(rests, rest_index), value)
            tiles.append(jnp.where(tall((within < 54) & (row < 3)), value, 0.0))
        return tiles

    def joined(first, second):
        return jnp.where(low_half, pltpu.roll(first, 64, 1), pltpu.roll(second, 64, 1))

    zeros = jnp.zeros((ROWS, 128), F32)
    below = halo_rows((0, 1, 2), False, True, 2)
    first_fix = row_sums(((0, 0, below[0]), (0, 1, joined(below[0], below[1])), (0, 2, below[1]), (1, 0, below[1])), mirror_ref)
    folded = tab_ref[8] == 2
    above = halo_rows((5, 6, 7), folded, folded, 0)
    edge = joined(zeros, above[0])
    last_fix = row_sums(((0, 6, edge), (1, 4, edge), (1, 5, above[0]), (1, 6, joined(above[0], above[1]))), mirror_ref)

    left, right = [(main, jnp.concatenate([rest] * 3, axis=0)) for main, rest in (band_cells(3, 128), band_cells(4, 128))]
    beside = []
    for j in range(3):
        which = jnp.where(half == 0, j, 2 - j)
        in_main = jnp.minimum(3 * within + which, 127)
        main_index, rest_index = tall(in_main), tall(jnp.clip(3 * (within - 40) + 16 + which, 0, 39)) + 40 * group
        picked = [
            jnp.where(tall(within < 40), lanes_from(main, main_index), lanes_from(rest, rest_index)) for main, rest in (left, right)
        ]
        beside.append(jnp.where(tall(within < 48), jnp.where(low_half, picked[0], picked[1]), 0.0))
    column_fix = column_sums(beside, mirror_ref)
    fixes = {0: first_fix[0], 1: first_fix[1], 22: last_fix[0], 23: last_fix[1]}
    for m in range(RIM // 128):
        row, col = place_of(m)
        index = tall(jnp.where(col < 24, row, 64 + row))
        value = sum_ref[:, 128 * m : 128 * m + 128]
        fix = zeros
        for q in range(3):
            fix = jnp.where(tall((col == q) | (col == 47 - q)), lanes_from(column_fix[q], index), fix)
        value = value + fix
        row_index = tall(row % 2 * 64 + 3 + col)
        for pair in pairs_of(m):
            if pair in fixes:
                value = value + jnp.where(tall(row // 2 == pair), lanes_from(fixes[pair], row_index), 0.0)
        out_ref[:, 128 * m : 128 * m + 128] = value.astype(BF)


def params(
    after_ref, x_ref, mask_ref, gain_ref, shift_ref, up_ref, up_bias_ref, down_ref, down_bias_ref, scale_ref, pool_weight_ref, spread_weight_ref,
    pool_ref, rim_cells_ref, middle_cells_ref, rim_mask_ref, rim_weights_ref, middle_weights_ref, *level_refs,
):
    me = lax.axis_index("chan")
    lane = lane_ids((192, 128))
    for level in range(2):
        weights_ref, values_ref = level_refs[2 * level : 2 * level + 2]
        row = slice(level, level + 1)
        spare = jnp.zeros((48, up_ref.shape[2]), BF)
        turned = jnp.concatenate([up_ref[level], three_terms(up_bias_ref[row, :]), spare], axis=0)
        weights_ref[0:768, :] = jnp.transpose(turned, (1, 0))
        own = down_ref[level, pl.ds(pl.multiple_of(me * ROWS, 16), ROWS), :]
        for j in range(3):
            weights_ref[768 + ROWS * j : 768 + ROWS * (j + 1), :] = own[:, 256 * j : 256 * j + 256]
        down_bias = columns(down_bias_ref[row, :])
        own = down_bias[0:ROWS]
        for k in range(1, down_bias.shape[0] // ROWS):
            own = jnp.where(me == k, down_bias[k * ROWS : (k + 1) * ROWS], own)
        rest = jnp.zeros((192 - ROWS, 128), F32)
        own, scale = [jnp.concatenate([value, rest], axis=0) for value in (own, columns(scale_ref[row, :]))]
        norm = jnp.where(lane == 0, columns(gain_ref[row, :]), columns(shift_ref[row, :]))
        values_ref[0:192, :] = jnp.where(lane < 2, norm, jnp.where(lane == 2, own, scale))
    fine_values_ref, coarse_values_ref = level_refs[1], level_refs[3]
    lane = lane_ids((ROWS, FINE_IN))
    spread = cell_weights(spread_weight_ref, lane // 48, lane % 48)
    for j in range(3):
        coarse_values_ref[240 + ROWS * j : 240 + ROWS * (j + 1), :] = spread[:, 128 * j : 128 * j + 128]
    lane = lane_ids((ROWS, 128))
    rim_weights_ref[:, 0:128] = cell_weights(pool_weight_ref, lane // 64, lane)
    rim_weights_ref[:, 128:256] = cell_weights(pool_weight_ref, lane // 8, lane)
    lane = lane_ids((ROWS, MIDDLE))
    middle_weights_ref[...] = cell_weights(pool_weight_ref, lane // 40, lane)

    masks = []
    for i in range(GROUPS):
        masks.append(jnp.broadcast_to(mask_ref[:, i * FINE_IN : (i + 1) * FINE_IN].astype(F32), (8, FINE_IN)))
    counts = dot(jnp.concatenate(masks, axis=0).astype(BF), pool_ref[...])
    small_mask = jnp.where(counts > 0.5, 1.0, 0.0)
    for m in range(5):
        coarse_values_ref[192 + 8 * m : 200 + 8 * m, :] = coarse_tile(m, lambda i: small_mask[8 * i : 8 * i + 8], lambda value: value)
    coarse_values_ref[232:240, :] = jnp.zeros((8, 128), F32)
    for m in range((RIM + MIDDLE) // 128):
        row, col = place_of(m)
        cell = row * 48 + col
        index, value, mask = cell % 128, None, None
        for tile in sources_of(m):
            lanes = slice(128 * tile, 128 * tile + 128)
            part = lanes_from(x_ref[0, :, lanes].astype(F32), tall(index))
            mask_part = lanes_from(jnp.broadcast_to(mask_ref[:, lanes].astype(F32), (8, 128)), index)
            value = part if value is None else jnp.where(tall(cell // 128 == tile), part, value)
            mask = mask_part if mask is None else jnp.where(cell // 128 == tile, mask_part, mask)
        if m < RIM // 128:
            rim_cells_ref[:, 128 * m : 128 * m + 128] = value.astype(BF)
            rim_mask_ref[:, 128 * m : 128 * m + 128] = mask
        else:
            t = m - RIM // 128
            middle_cells_ref[:, 128 * t : 128 * t + 128] = value.astype(BF)
            fine_values_ref[192 + 8 * t : 200 + 8 * t, :] = mask


def in_rows(rim_ref, middle_ref, out_ref):
    rim_tiles = RIM // 128

    def tiles(m):
        ref, t = (rim_ref, m) if m < rim_tiles else (middle_ref, m - rim_tiles)
        return ref[:, 128 * t : 128 * t + 128].astype(F32)

    for t in range(TILE * TILE // 128):
        cell, static = 128 * t + lane_ids((8, 128)), 128 * t + np.arange(128)
        value = collected(tiles, cell // 48, cell % 48, static // 48, static % 48, lambda m: True)
        out_ref[:, 128 * t : 128 * t + 128] = value.astype(BF)


def conv_coarse(x_ref, weight_ref, bias_ref, rim_ref, middle_ref, cells_ref, wide_ref, pad_ref, sum_ref):
    for tap in range(49):
        wide_ref[tap] = jnp.broadcast_to(weight_ref[1, :, tap : tap + 1], (ROWS, 128))
    pad_ref[0, :, 0:128] = jnp.zeros((ROWS, 128), F32)
    pad_ref[0, :, 896:1024] = jnp.zeros((ROWS, 128), F32)
    pad_ref[0, :, 128:896] = x_ref[...].astype(F32)
    padded = pad_ref[0]
    for turn in range(1, 4):
        pad_ref[turn] = lane_shifted(padded, 32 * turn)
    sum_ref[...] = wide(columns(bias_ref[1:2, :]), 768)

    def group(g, carry):
        rows = pl.ds(pl.multiple_of(g * 8, 8), 8)
        for chunk in range(2):
            base = chunk * 384
            taken = []
            for a in range(1, 8):
                start = base + (a // 4) * 128
                taken.append([pad_ref[a % 4, rows, start + 128 * j : start + 128 * j + 128] for j in range(3)])
            total = [sum_ref[rows, base + 128 * j : base + 128 * j + 128] for j in range(3)]
            for b in range(7):
                weights = [wide_ref[a * 7 + b, rows, :] for a in range(7)]
                for j in range(3):
                    partial = weights[0] * taken[0][j]
                    for a in range(1, 7):
                        partial = partial + weights[a] * taken[a][j]
                    total[j] = total[j] + (pltpu.roll(partial, (3 - b) % 128, 1) if b != 3 else partial)
            for j in range(3):
                sum_ref[rows, base + 128 * j : base + 128 * j + 128] = total[j]
        return carry

    lax.fori_loop(0, 6, group, 0)
    for m in range(5):
        here = slice(128 * m, 128 * m + 128)
        cells_ref[:, here] = coarse_tile(m, lambda i: x_ref[:, 128 * i : 128 * i + 128].astype(F32)).astype(BF)
        value = coarse_tile(m, lambda i: sum_ref[:, 128 * i : 128 * i + 128])
        if m < 3:
            rim_ref[:, here] = value
        else:
            middle_ref[:, 128 * m - 384 : 128 * m - 256] = value.astype(BF)


def coarse_place(m):
    lane = lane_ids((8, 128))
    if m < 2:
        return 20 * m + lane // 32, lane % 32 - 3
    if m == 2:
        col = lane % 8
        return 4 + lane // 8, jnp.where(col < 4, col, col + 16)
    return 4 + 8 * (m - 3) + lane // 16, 4 + lane % 16


def coarse_tile(m, group, spread=tall):
    if m < 2:
        return group(5 * m)
    row, col = coarse_place(m)
    index, value = spread(row % 4 * 32 + 3 + col), None
    for i in range(1, 5) if m == 2 else range(2 * m - 5, 2 * m - 3):
        picked = lanes_from(group(i), index)
        value = picked if value is None else jnp.where(spread(row // 4 == i), picked, value)
    return value


def border_coarse(tab_ref, recv_ref, sum_ref, mirror_ref, out_ref):
    lane = lane_ids((8, 128))
    half, within, segment, inside = lane // 64, lane % 64, lane // 32, lane % 32
    group = lax.broadcasted_iota(jnp.int32, (ROWS, 128), 0) // 16

    def band_main(band):
        source, scale = band_source(tab_ref, band)
        return jnp.concatenate([recv_ref[source, :, 128 * g : 128 * g + 128] for g in range(3)], axis=0).astype(F32) * scale

    def band_rest(band):
        source, scale = band_source(tab_ref, band)
        return jnp.concatenate([recv_ref[source, :, 384:512].astype(F32) * scale] * 3, axis=0)

    def halo_rows(bands, folded):
        col = jnp.where(inside < 3, 21 + inside, jnp.where(inside < 27, inside - 3, inside - 27))
        index = segment * 24 + col
        index = tall(jnp.where(folded, 71 - index, index) & 127)
        picked = [lanes_from(band_main(band), index) for band in bands]
        value = jnp.where(tall(inside < 3), picked[0], jnp.where(tall(inside < 27), picked[1], picked[2]))
        return jnp.where(tall((inside < 30) & (segment < 3)), value, 0.0)

    def turned(cells, lanes, kept):
        return jnp.where(tall(kept), pltpu.roll(cells, lanes, 1), 0.0)

    below = halo_rows((0, 1, 2), False)
    first_fix = row_sums(((0, 0, below), (0, 1, turned(below, 96, lane < 64)), (0, 2, turned(below, 64, lane < 32))), mirror_ref)[0]
    above = halo_rows((5, 6, 7), tab_ref[8] == 2)
    last_fix = row_sums(
        ((0, 6, turned(above, 32, lane >= 32)), (0, 5, turned(above, 64, lane >= 64)), (0, 4, turned(above, 96, lane >= 96))), mirror_ref
    )[0]
    sides = [(band_main(band), band_rest(band)) for band in (3, 4)]
    beside = []
    for j in range(3):
        which = jnp.where(half == 0, j, 2 - j)
        main_index = tall(jnp.minimum(72 + 3 * within + which, 127))
        rest_index = tall(jnp.clip(3 * (within - 16) + which, 0, 23)) + 24 * group
        picked = [
            jnp.where(tall(within < 16), lanes_from(main, main_index), lanes_from(rest, rest_index)) for main, rest in sides
        ]
        beside.append(jnp.where(tall(within < HALF), jnp.where(tall(half == 0), picked[0], picked[1]), 0.0))
    column_fix = column_sums(beside, mirror_ref)
    for m in range(3):
        row, col = coarse_place(m)
        index = tall(jnp.where(col < 12, row, 64 + row))
        value = sum_ref[:, 128 * m : 128 * m + 128]
        fix = jnp.zeros((ROWS, 128), F32)
        for q in range(3):
            fix = jnp.where(tall((col == q) | (col == 23 - q)), lanes_from(column_fix[q], index), fix)
        value = value + fix
        if m < 2:
            value = value + (first_fix, last_fix)[m]
        out_ref[:, 128 * m : 128 * m + 128] = value.astype(BF)


def gather_rows(pieces, cat_ref):
    me = lax.axis_index("chan")
    for k, piece in enumerate(pieces):
        first = pl.multiple_of(lax.bitwise_xor(me, k) * ROWS, 16)
        cat_ref[pl.ds(first, ROWS), :] = piece[...]


def make_branch(cat_ref, weights_ref, values_ref, block):
    def spread_lane(rows, lane):
        return wide(jnp.broadcast_to(values_ref[0:rows, lane : lane + 1], (rows, 128)), block)

    gain, shift, down_bias, scale = spread_lane(192, 0), spread_lane(192, 1), spread_lane(ROWS, 2), spread_lane(ROWS, 3)
    down = jnp.concatenate([weights_ref[768 + ROWS * j : 768 + ROWS * (j + 1), :] for j in range(3)], axis=1)
    inputs = 4 * ROWS

    def branch(start):
        values = cat_ref[0:inputs, start : start + block].astype(F32)
        mean = jnp.mean(values, axis=0, keepdims=True)
        centred = values - mean
        spread = jnp.mean(centred * centred, axis=0, keepdims=True)
        normed = (centred * lax.rsqrt(spread + norm_eps) * gain + shift).astype(BF)
        hidden = dot(weights_ref[0:768, 0 : inputs + 16], jnp.concatenate([normed, jnp.ones((16, block), BF)], axis=0))
        hidden = 0.5 * hidden * (1.0 + lax.erf(hidden * np.float32(0.5**0.5)))
        return scale * (dot(down, hidden.astype(BF)) + down_bias)

    return branch


def cell_weights(weight_ref, row, col):
    kind = 2 * (row % 2) + col % 2
    result = jnp.zeros(row.shape, F32)
    for k in range(4):
        result = jnp.where(kind == k, weight_ref[:, k : k + 1], result)
    return result


def make_mix_rim(count):
    def mix_rim(
        tab_ref, own_ref, p1_ref, p2_ref, p3_ref, x_ref, mask_ref, pool_cells_ref, weights_ref, values_ref,
        middle_pooled_ref, fine_ref, msg_ref, all_pooled_ref, cat_ref, mains_ref, rest_ref,
    ):
        gather_rows((own_ref, p1_ref, p2_ref, p3_ref), cat_ref)
        block = RIM
        branch = make_branch(cat_ref, weights_ref, values_ref, block)
        for start in range(0, RIM, block):
            here = slice(start, start + block)
            value = x_ref[:, here].astype(F32) + branch(start)
            fine_ref[:, here] = (mask_ref[0:1, here] * value).astype(BF)

        sums = []
        for m in range(RIM // 128):
            weights, step = (pool_cells_ref[:, 0:128], 64) if m < 4 else (pool_cells_ref[:, 128:256], 8)
            product = fine_ref[:, 128 * m : 128 * m + 128].astype(F32) * weights
            product = product + lane_shifted(product, 1)
            sums.append(product + lane_shifted(product, step))
        for i in range(GROUPS):
            here = slice(128 * i, 128 * i + 128)
            value = coarse_from(i, lambda m: sums[m], lambda m: m < RIM // 128)
            all_pooled_ref[:, here] = (value + middle_pooled_ref[:, here].astype(F32)).astype(BF)

        groups = [all_pooled_ref[:, 128 * i : 128 * i + 128].astype(F32) for i in range(GROUPS)]
        lane = lane_ids((8, 128))
        index = lane // 24 * 32 + 3 + lane % 24
        rows = [lanes_from(groups[0], tall(index & 127)), lanes_from(groups[5], tall((index + 32) & 127))]
        cell = jnp.clip(lane - 72, 0, 47)
        rest_cell = lane_ids((ROWS, 128)) - lax.broadcasted_iota(jnp.int32, (ROWS, 128), 0) // 16 * 24
        rest_valid = (rest_cell >= 0) & (rest_cell < 24)
        rest_cell = jnp.clip(rest_cell, 0, 23)
        for c in range(2):
            first = 24 if c else 3
            index = tall(cell // 3 % 4 * 32 + first + cell % 3)
            column = lanes_from(groups[0], index)
            for i in range(1, 4):
                column = jnp.where(tall(cell // 12 == i), lanes_from(groups[i], index), column)
            for r in range(2):
                mains_ref[2 * r + c] = jnp.where(tall(lane < 72), rows[r], column).astype(BF)
            index = rest_cell // 3 % 4 * 32 + first + rest_cell % 3
            rest = jnp.where(rest_cell < 12, lanes_from(groups[4], index), lanes_from(groups[5], index))
            rest = jnp.where(rest_valid, rest, 0.0)
            rest_ref[c] = (rest[0:16] + rest[16:32] + rest[32:48]).astype(BF)

        def fill(dev, carry):
            both = tab_ref[16 + dev]
            for g in range(3):
                msg_ref[dev, :, 128 * g : 128 * g + 128] = mains_ref[both, 16 * g : 16 * g + 16, :]
            msg_ref[dev, :, 384:512] = rest_ref[lax.bitwise_and(both, 1)]
            return carry

        scan_tiles(count, fill, jnp.int32(0))

    return mix_rim


def mix_middle(
    own_ref, p1_ref, p2_ref, p3_ref, x_ref, pool_cells_ref, weights_ref, values_ref, fine_ref, pooled_ref, cat_ref
):
    gather_rows((own_ref, p1_ref, p2_ref, p3_ref), cat_ref)
    value = x_ref[...].astype(F32) + make_branch(cat_ref, weights_ref, values_ref, MIDDLE)(0)
    mask = jnp.concatenate([values_ref[192 + 8 * t : 193 + 8 * t, :] for t in range(MIDDLE // 128)], axis=1)
    fine_ref[...] = (mask * value).astype(BF)
    sums = fine_ref[...].astype(F32) * pool_cells_ref[...]
    sums = sums + lane_shifted(sums, 1)
    sums = sums + lane_shifted(sums, 40)
    first = RIM // 128
    for i in range(GROUPS):
        value = coarse_from(i, lambda m: sums[:, 128 * (m - first) : 128 * (m - first) + 128], lambda m: m >= first)
        pooled_ref[:, 128 * i : 128 * i + 128] = value.astype(BF)


def coarse_cells(pieces, first, pooled_ref, weights_ref, values_ref, cat_ref):
    gather_rows(pieces, cat_ref)
    lanes = cat_ref.shape[1]
    value = pooled_ref[:, 128 * first : 128 * first + lanes].astype(F32) + make_branch(cat_ref, weights_ref, values_ref, lanes)(0)
    tiles = range(first, first + lanes // 128)
    return jnp.concatenate([values_ref[192 + 8 * m : 193 + 8 * m, :] for m in tiles], axis=1) * value


def mix_coarse_middle(own_ref, p1_ref, p2_ref, p3_ref, pooled_ref, weights_ref, values_ref, out_ref, cat_ref):
    out_ref[...] = coarse_cells((own_ref, p1_ref, p2_ref, p3_ref), 3, pooled_ref, weights_ref, values_ref, cat_ref).astype(BF)


def mix_coarse(
    own_ref, p1_ref, p2_ref, p3_ref, pooled_ref, middle_ref, fine_ref, mask_ref, weights_ref, values_ref, pool_ref, spread_ref, out_ref, cat_ref,
):
    rim = coarse_cells((own_ref, p1_ref, p2_ref, p3_ref), 0, pooled_ref, weights_ref, values_ref, cat_ref)
    ends = jnp.concatenate([rim[:, 0:128], rim[:, 128:256]], axis=0).astype(BF)
    ends = lax.dot_general(ends, pool_ref[...], (((1,), (1,)), ((), ())), preferred_element_type=F32)
    sides, lane = rim[:, 256:384], lane_ids((ROWS, 128))
    parts = []
    for i in range(4):
        middle = middle_ref[:, 128 * (i // 2) : 128 * (i // 2) + 128].astype(F32)
        side = pltpu.roll(sides, 128 - 32 * i, 1) if i else sides
        parts.append(jnp.where(lane < 32, side, pltpu.roll(middle, 96 if i % 2 else 32, 1)).astype(BF))
    inner = dot(jnp.concatenate(parts, axis=0), spread_ref[...])
    weights = jnp.concatenate([values_ref[240 + ROWS * j : 240 + ROWS * (j + 1), :] for j in range(3)], axis=1)
    for i in range(GROUPS):
        lanes = slice(i * FINE_IN, (i + 1) * FINE_IN)
        if i % 5 == 0:
            spread = ends[i // 5 * ROWS : (i // 5 + 1) * ROWS]
        else:
            spread = inner[(i - 1) * ROWS : i * ROWS]
        merged = fine_ref[:, lanes].astype(F32) + weights * spread
        out_ref[0, :, lanes] = (mask_ref[:, lanes].astype(F32) * merged).astype(BF)


VMEM = pl.BlockSpec(memory_space=pltpu.VMEM)
SMEM = pl.BlockSpec(memory_space=pltpu.SMEM)

def takes(microseconds):
    return pl.CostEstimate(flops=microseconds * 1_000_000_000, bytes_accessed=0, transcendentals=0)


def shaped(*shape, dtype=BF):
    return jax.ShapeDtypeStruct(shape, dtype)


PARAMS = pltpu.CompilerParams(vmem_limit_bytes=24 * 1024 * 1024)


def every_channel(own, first_work, later_work=lambda *results: ()):
    pairs = lambda bit: [(i, i ^ bit) for i in range(4)]
    across = lax.ppermute(own, "chan", pairs(2))
    near, *results = lax.optimization_barrier((own, *first_work(own)))
    beside = lax.ppermute(near, "chan", pairs(1))
    across, *results = lax.optimization_barrier((across, *results, *later_work(*results)))
    diagonal = lax.ppermute(across, "chan", pairs(1))
    return (own, beside, across, diagonal), results


def per_device(
    features, land_mask, wet_slots, device_of, depth_weight, depth_bias, norm_gain, norm_bias, up_weight, up_bias,
    down_weight, down_bias, layer_scale, pool_weight, spread_weight,
):
    count = wet_slots.shape[0]
    grid_x = 2 * count // GRID_Y
    cells = TILE * TILE
    pack = pl.pallas_call(
        strip_table, out_specs=VMEM, out_shape=shaped(FINE_IN, 256), compiler_params=PARAMS, cost_estimate=takes(2), name="strip_table"
    )()
    messages, table = pl.pallas_call(
        make_prep(grid_x),
        in_specs=[SMEM, SMEM, VMEM, VMEM],
        out_specs=[VMEM, SMEM],
        out_shape=[shaped(count, 16, 896), shaped(16 + count, dtype=jnp.int32)],
        scratch_shapes=[
            pltpu.VMEM((2, ROWS, 128), BF),
            pltpu.VMEM((2, ROWS, 128), BF),
            pltpu.VMEM((2, 16, 128), F32),
            pltpu.VMEM((2, 16, 128), F32),
        ],
        compiler_params=PARAMS,
        cost_estimate=takes(10),
        name="prep",
    )(wet_slots, device_of, features, pack)
    pool = jnp.asarray(POOL)
    arrived = lax.all_to_all(messages, "tile", 0, 0, tiled=True)
    inner, inner_middle, fine_taps = pl.pallas_call(
        lambda tab_ref, *refs: conv_inner(*refs),
        in_specs=[SMEM] + [VMEM] * 3,
        out_specs=[VMEM] * 3,
        out_shape=[shaped(ROWS, RIM, dtype=F32), shaped(ROWS, MIDDLE), shaped(28, ROWS, 128, dtype=F32)],
        scratch_shapes=[
            pltpu.VMEM((49, ROWS, 128), F32),
            pltpu.VMEM((ROWS, 3584), F32),
            pltpu.VMEM((ROWS, 3584), F32),
            pltpu.VMEM((ROWS, 3072), F32),
        ],
        compiler_params=PARAMS,
        cost_estimate=takes(4),
        name="conv_inner",
    )(table, features, depth_weight, depth_bias)
    conv = pl.pallas_call(
        conv_border,
        in_specs=[SMEM] + [VMEM] * 3,
        out_specs=VMEM,
        out_shape=shaped(ROWS, RIM),
        compiler_params=PARAMS,
        cost_estimate=takes(2),
        name="conv_border",
    )(table, arrived, inner, fine_taps)

    pairs = lambda bit: [(i, i ^ bit) for i in range(4)]
    middle_across = lax.ppermute(inner_middle, "chan", pairs(2))
    middle_beside = lax.ppermute(inner_middle, "chan", pairs(1))
    middle_across, _ = lax.optimization_barrier((middle_across, conv))
    middle_pieces = (inner_middle, middle_beside, middle_across, lax.ppermute(middle_across, "chan", pairs(1)))

    def mix_middle_cells(*results):
        return pl.pallas_call(
            mix_middle,
            in_specs=[VMEM] * 8,
            out_specs=[VMEM] * 2,
            out_shape=[shaped(ROWS, MIDDLE), shaped(ROWS, 768)],
            scratch_shapes=[pltpu.VMEM((4 * ROWS, MIDDLE), BF)],
            compiler_params=PARAMS,
            cost_estimate=takes(1),
            name="mix_middle",
        )(*middle_pieces, results[1], results[4], results[5], results[6])

    def spread_params(own):
        shapes = [
            ((ROWS, RIM), BF), ((ROWS, MIDDLE), BF), ((8, RIM), F32), ((ROWS, 256), F32), ((ROWS, MIDDLE), F32),
            ((912, 256), BF), ((296, 128), F32), ((912, 256), BF), ((384, 128), F32),
        ]
        return pl.pallas_call(
            params,
            in_specs=[VMEM] * 13,
            out_specs=[VMEM] * len(shapes),
            out_shape=[shaped(*shape, dtype=dtype) for shape, dtype in shapes],
            compiler_params=PARAMS,
            cost_estimate=takes(2),
            name="params",
        )(
            own, features, land_mask, norm_gain, norm_bias, jnp.swapaxes(up_weight, 1, 2), up_bias, down_weight, down_bias, layer_scale,
            pool_weight, spread_weight, pool,
        )

    pieces, results = every_channel(conv, spread_params, mix_middle_cells)
    rim_cells, _, rim_mask, rim_weights, _, fine_weights, fine_values, coarse_weights, coarse_values, middle, middle_pooled = results
    rim, messages, pooled = pl.pallas_call(
        make_mix_rim(count),
        in_specs=[SMEM] + [VMEM] * 10,
        out_specs=[VMEM] * 3,
        out_shape=[shaped(ROWS, RIM), shaped(count, 16, 512), shaped(ROWS, 768)],
        scratch_shapes=[
            pltpu.VMEM((4 * ROWS, RIM), BF),
            pltpu.VMEM((4, ROWS, 128), BF),
            pltpu.VMEM((2, 16, 128), BF),
        ],
        compiler_params=PARAMS,
        cost_estimate=takes(3),
        name="mix_rim",
    )(
        table, *pieces, rim_cells, rim_mask, rim_weights, fine_weights, fine_values, middle_pooled,
    )
    arrived = lax.all_to_all(messages, "tile", 0, 0, tiled=True)
    inner, middle_conv, pooled, taps = pl.pallas_call(
        conv_coarse,
        in_specs=[VMEM] * 3,
        out_specs=[VMEM] * 4,
        out_shape=[shaped(ROWS, 384, dtype=F32), shaped(ROWS, 256), shaped(ROWS, 640), shaped(49, ROWS, 128, dtype=F32)],
        scratch_shapes=[pltpu.VMEM((4, ROWS, 1024), F32), pltpu.VMEM((ROWS, 768), F32)],
        compiler_params=PARAMS,
        cost_estimate=takes(2),
        name="conv_coarse",
    )(pooled, depth_weight, depth_bias)
    conv = pl.pallas_call(
        border_coarse,
        in_specs=[SMEM] + [VMEM] * 3,
        out_specs=VMEM,
        out_shape=shaped(ROWS, 384),
        compiler_params=PARAMS,
        cost_estimate=takes(1),
        name="border_coarse",
    )(table, arrived, inner, taps)
    middle_across = lax.ppermute(middle_conv, "chan", pairs(2))
    middle_beside = lax.ppermute(middle_conv, "chan", pairs(1))
    middle_across, _ = lax.optimization_barrier((middle_across, conv))
    coarse_pieces = (middle_conv, middle_beside, middle_across, lax.ppermute(middle_across, "chan", pairs(1)))

    def back_in_rows(own):
        return pl.pallas_call(
            lambda after_ref, *refs: in_rows(*refs),
            in_specs=[VMEM] * 3,
            out_specs=[VMEM],
            out_shape=[shaped(ROWS, cells)],
            compiler_params=PARAMS,
            cost_estimate=takes(1),
            name="in_rows",
        )(own, rim, middle)

    def mix_coarse_cells(*results):
        return pl.pallas_call(
            mix_coarse_middle,
            in_specs=[VMEM] * 7,
            out_specs=[VMEM],
            out_shape=[shaped(ROWS, 256)],
            scratch_shapes=[pltpu.VMEM((4 * ROWS, 256), BF)],
            compiler_params=PARAMS,
            cost_estimate=takes(1),
            name="mix_coarse_middle",
        )(*coarse_pieces, pooled, coarse_weights, coarse_values)

    pieces, (fine, coarse_middle) = every_channel(conv, back_in_rows, mix_coarse_cells)
    return pl.pallas_call(
        mix_coarse,
        in_specs=[VMEM] * 12,
        out_specs=VMEM,
        out_shape=shaped(1, ROWS, cells),
        scratch_shapes=[pltpu.VMEM((4 * ROWS, 384), BF)],
        compiler_params=PARAMS,
        cost_estimate=takes(2),
        name="mix_coarse",
    )(*pieces, pooled, coarse_middle, fine, land_mask, coarse_weights, coarse_values, pool, jnp.asarray(COARSE_SPREAD))


def solution(mesh):
    placed = (
        P("tile", "chan", None),
        P("tile", None),
        P(),
        P(),
        P(None, "chan", None),
        P(None, "chan"),
        P(),
        P(),
        P(),
        P(),
        P(),
        P(),
        P(None, "chan"),
        P("chan", None),
        P("chan", None),
    )
    return jax.shard_map(
        per_device, mesh=mesh, in_specs=placed, out_specs=P("tile", "chan", None), check_vma=False
    )
```

```python
import jax
import jax.numpy as jnp
import ml_dtypes
import numpy as np
from jax import lax
from jax.experimental import pallas as pl
from jax.experimental.pallas import tpu as pltpu
from jax.sharding import PartitionSpec as P

TILE = 48
HALF = TILE // 2
GRID_Y = 4
GROUPS = 6
ROWS = 48
FINE_IN = 8 * TILE
RIM = 896
MIDDLE = 1664
BANDS = ((-1, -1), (-1, 0), (-1, 1), (0, -1), (0, 1), (1, -1), (1, 0), (1, 1))
norm_eps = 1e-06
BF = jnp.bfloat16
F32 = jnp.float32


def one_hot(shape, pairs):
    table = np.zeros(shape, np.float32)
    for source, target in pairs:
        table[source, target] = 1.0
    return table.astype(ml_dtypes.bfloat16)


def pool_table():
    return one_hot((384, 128), [(row * 48 + col, (row // 2) * 32 + 3 + col // 2) for row in range(8) for col in range(48)])


def coarse_spread_table():
    pairs = []
    for row in range(4):
        for col in range(HALF):
            if 4 <= col < 20:
                lane = 32 + row * 16 + col - 4
            else:
                lane = row * 8 + (col if col < 4 else col - 16)
            pairs += [(lane, (2 * row + u) * 48 + 2 * col + v) for u in range(2) for v in range(2)]
    return one_hot((128, 384), pairs)


POOL = pool_table()
COARSE_SPREAD = coarse_spread_table()


def dot(left, right):
    return jnp.dot(left, right, preferred_element_type=F32)


def stacked(value, width):
    return jnp.concatenate([value[:, i * width : (i + 1) * width] for i in range(GROUPS)], axis=0)


def lane_ids(shape):
    return lax.broadcasted_iota(jnp.int32, shape, 1)


def three_terms(row):
    high = row.astype(BF)
    rest = row - high.astype(F32)
    middle = rest.astype(BF)
    low = (rest - middle.astype(F32)).astype(BF)
    return jnp.concatenate([high, middle, low, jnp.zeros((13, row.shape[1]), BF)], axis=0)


def columns(row):
    return lax.dot_general(
        three_terms(row), jnp.ones((16, 128), BF), (((0,), (0,)), ((), ())), preferred_element_type=F32
    )


def wide(block, lanes):
    return jnp.concatenate([block] * (lanes // 128), axis=1)


def scan_tiles(count, step, carry):
    if count <= 16:
        for k in range(count):
            carry = step(k, carry)
        return carry
    return lax.fori_loop(0, count, step, carry)


def strip_table(pack_ref):
    shape = (FINE_IN, 256)
    source = lax.broadcasted_iota(jnp.int32, shape, 0)
    lane = lane_ids(shape)
    within = lane % 128
    wanted = (within // 3) * TILE + within % 3 + jnp.where(lane >= 128, TILE - 3, 0)
    pack_ref[...] = jnp.where((within < 24) & (source == wanted), 1.0, 0.0).astype(BF)


def quotient(value, divisor):
    if divisor & (divisor - 1) == 0:
        return lax.shift_right_logical(value, jnp.int32(divisor.bit_length() - 1))
    return lax.div(value, divisor)


def remainder(value, divisor):
    if divisor & (divisor - 1) == 0:
        return lax.bitwise_and(value, jnp.int32(divisor - 1))
    return lax.rem(value, divisor)


def make_prep(grid_x):
    def prep(slots_ref, dev_ref, x_ref, pack_ref, msg_ref, tab_ref, rows_ref, cols_ref, row_rest_ref, col_rest_ref):
        count = slots_ref.shape[0]
        me = lax.axis_index("tile")
        my_slot = scan_tiles(count, lambda k, c: c + jnp.where(dev_ref[k] == me, slots_ref[k], 0), jnp.int32(0))
        my_x = remainder(my_slot, grid_x)
        my_y = quotient(my_slot, grid_x)
        wanted = []
        for up_by, right_by in BANDS:
            near_x = remainder(my_x + (right_by + grid_x), grid_x)
            near_y = my_y + up_by
            folded = near_y >= GRID_Y
            from_x = jnp.where(folded, grid_x - 1 - near_x, near_x)
            from_y = jnp.where(folded, GRID_Y - 1, near_y)
            wanted.append(from_y * grid_x + from_x)

        def find(k, found):
            slot, dev = slots_ref[k], dev_ref[k]
            row_pick = jnp.where(quotient(slot, grid_x) + 1 == my_y, 0, 1)
            col_pick = jnp.where(remainder(slot, grid_x) == remainder(my_x + (grid_x - 1), grid_x), 0, 1)
            tab_ref[16 + dev] = 2 * row_pick + col_pick
            return tuple(jnp.where(slot == want, dev, old) for want, old in zip(wanted, found))

        found = scan_tiles(count, find, tuple(jnp.int32(-1) for _ in BANDS))
        for band in range(8):
            tab_ref[band] = found[band]
        tab_ref[8] = jnp.where(my_y == GRID_Y - 1, 2, 1)
        for spare in range(9, 16):
            tab_ref[spare] = 0

        x = x_ref[0]
        cols = dot(stacked(x, FINE_IN), pack_ref[...])
        lane = lane_ids((ROWS, 128))
        for side in range(2):
            part = cols[:, side * 128 : side * 128 + 128]
            main = part[0:ROWS]
            for i in range(1, 5):
                main = main + pltpu.roll(part[i * ROWS : (i + 1) * ROWS], 24 * i, 1)
            cols_ref[side] = main.astype(BF)
            rest = pltpu.roll(part[5 * ROWS : 6 * ROWS], 16, 1)
            col_rest_ref[side] = rest[0:16] + pltpu.roll(rest[16:32], 40, 1) + pltpu.roll(rest[32:48], 80, 1)
        rows_ref[0] = x[:, 0:128]
        rows_ref[1] = x[:, 2176:2304]
        ends = (x[:, 128:256].astype(F32), pltpu.roll(x[:, 2048:2176].astype(F32), 16, 1))
        for side in range(2):
            rest = jnp.where(lane < 16, ends[side], 0.0)
            row_rest_ref[side] = rest[0:16] + pltpu.roll(rest[16:32], 40, 1) + pltpu.roll(rest[32:48], 80, 1)

        def fill(dev, carry):
            row_pick = quotient(tab_ref[16 + dev], 2)
            col_pick = remainder(tab_ref[16 + dev], 2)
            for g in range(3):
                msg_ref[dev, :, 256 * g : 256 * g + 128] = rows_ref[row_pick, 16 * g : 16 * g + 16, :]
                msg_ref[dev, :, 256 * g + 128 : 256 * g + 256] = cols_ref[col_pick, 16 * g : 16 * g + 16, :]
            msg_ref[dev, :, 768:896] = (row_rest_ref[row_pick] + col_rest_ref[col_pick]).astype(BF)
            return carry

        scan_tiles(count, fill, jnp.int32(0))

    return prep


def band_source(tab_ref, band):
    source = tab_ref[band]
    return jnp.maximum(source, 0), jnp.where(source >= 0, 1.0, 0.0).astype(F32)


def lane_shifted(value, lanes):
    return pltpu.roll(value, value.shape[1] - lanes, 1)


def tall(row_block):
    return jnp.concatenate([row_block] * (ROWS // 8), axis=0)


def lanes_from(value, index):
    return jnp.take_along_axis(value, index, axis=1)


def conv_inner(x_ref, weight_ref, bias_ref, sum_ref, middle_ref, mirror_ref, wide_ref, pad_ref, odd_ref, total_ref):
    for tap in range(49):
        wide_ref[tap] = jnp.broadcast_to(weight_ref[0, :, tap : tap + 1], (ROWS, 128))
    mirrored_taps(wide_ref, mirror_ref)
    pad_ref[:, 0:256] = jnp.zeros((ROWS, 256), F32)
    pad_ref[:, 3328:3584] = jnp.zeros((ROWS, 256), F32)
    lane = lane_ids((8, 128))
    half, within = lane // 64, lane % 64
    valid = tall((within >= 3) & (within < 51))
    col = jnp.clip(within - 3, 0, 47)
    cells = [96 * k + 48 * half + col for k in range(4)]
    indices = [tall(cell % 128) for cell in cells]
    for i in range(GROUPS):
        tiles = [x_ref[0, :, 384 * i + 128 * m : 384 * i + 128 * m + 128].astype(F32) for m in range(3)]
        for k in range(4):
            first, final = (96 * k) // 128, (96 * k + 95) // 128
            value = lanes_from(tiles[first], indices[k])
            if final != first:
                value = jnp.where(tall(cells[k] < 128 * final), value, lanes_from(tiles[final], indices[k]))
            start = 256 + 512 * i + 128 * k
            pad_ref[:, start : start + 128] = jnp.where(valid, value, 0.0)
    odd_ref[...] = lane_shifted(pad_ref[...], 64)
    total_ref[...] = wide(columns(bias_ref[0:1, :]), 3072)

    def group(g, carry):
        here = pl.ds(pl.multiple_of(g * 8, 8), 8)
        for chunk in range(6):
            base = chunk * 512
            taken = []
            for a in range(1, 8):
                ref = odd_ref if a % 2 else pad_ref
                start = base + (a // 2) * 128
                taken.append([ref[here, start + 128 * j : start + 128 * j + 128] for j in range(4)])
            total = [total_ref[here, base + 128 * j : base + 128 * j + 128] for j in range(4)]
            for b in range(7):
                weights = [wide_ref[a * 7 + b, here, :] for a in range(7)]
                for j in range(4):
                    partial = weights[0] * taken[0][j]
                    for a in range(1, 7):
                        partial = partial + weights[a] * taken[a][j]
                    total[j] = total[j] + (pltpu.roll(partial, (3 - b) % 128, 1) if b != 3 else partial)
            for j in range(4):
                total_ref[here, base + 128 * j : base + 128 * j + 128] = total[j]
        return carry

    lax.fori_loop(0, ROWS // 8, group, 0)
    for m in range((RIM + MIDDLE) // 128):
        row, col = place_of(m)
        index = tall(row % 2 * 64 + 3 + col)
        value = None
        for pair in pairs_of(m):
            picked = lanes_from(total_ref[:, 128 * pair : 128 * pair + 128], index)
            value = picked if value is None else jnp.where(tall(row // 2 == pair), picked, value)
        if m < RIM // 128:
            sum_ref[:, 128 * m : 128 * m + 128] = value
        else:
            middle_ref[:, 128 * m - RIM : 128 * m - RIM + 128] = value.astype(BF)


def place_of(m, lane=None, ops=jnp):
    lane = lane_ids((8, 128)) if lane is None else lane
    if m < 4:
        return (2 * m if m < 2 else 40 + 2 * m) + lane // 64, ops.minimum(lane % 64, 47)
    if m < 7:
        col = lane % 8
        return ops.minimum(16 * m - 60 + lane // 8, 43), ops.where(col < 4, col, col + 40)
    cell = ops.minimum(128 * m - RIM + lane, 1599)
    return 4 + cell // 40, 4 + cell % 40


def pairs_of(m):
    return np.unique(place_of(m, np.arange(128), np)[0] // 2).tolist()


def sources_of(m):
    row, col = place_of(m, np.arange(128), np)
    return np.unique((row * 48 + col) // 128).tolist()


def lane_of(row, col, ops=jnp):
    ends = (row < 4) | (row >= 44)
    end = ops.where(row < 4, row, row - 40)
    side = (col < 4) | (col >= 44)
    cell = (row - 4) * 40 + col - 4
    tile = ops.where(ends, end // 2, ops.where(side, 4 + (row - 4) // 16, 7 + cell // 128))
    side_lane = (row - 4) % 16 * 8 + ops.where(col < 4, col, col - 40)
    return tile, ops.where(ends, end % 2 * 64 + col, ops.where(side, side_lane, cell % 128)) & 127


def collected(tiles, row, col, static_row, static_col, pick):
    tile, index = lane_of(row, col)
    value = None
    for m in np.unique(lane_of(static_row, static_col, np)[0]).tolist():
        if not pick(m):
            continue
        part = jnp.where(tall(tile == m), lanes_from(tiles(m), tall(index)), 0.0 if value is None else value)
        value = part
    return jnp.zeros((ROWS, 128), F32) if value is None else value


def coarse_from(i, sums, pick):
    def place(lane, ops):
        return 2 * (4 * i + lane // 32), 2 * ops.clip(lane % 32 - 3, 0, 23)

    lane = lane_ids((8, 128))
    inside = lane % 32
    row, col = place(lane, jnp)
    value = collected(sums, row, col, *place(np.arange(128), np), pick)
    return jnp.where(tall((inside >= 3) & (inside < 27)), value, 0.0)


def column_sums(beside, mirror_ref):
    total = [jnp.zeros((ROWS, 128), F32)] * 3
    for a in range(7):
        if mirror_ref.shape[0] == 49:
            low_half = tall(lane_ids((8, 128)) < 64)
            weights = [jnp.where(low_half, mirror_ref[7 * a + b], mirror_ref[7 * a + 6 - b]) for b in range(3)]
        else:
            weights = [mirror_ref[4 * a + b] for b in range(3)]
        for q in range(3):
            partial = weights[0] * beside[q]
            for j in range(q + 1, 3):
                partial = partial + weights[j - q] * beside[j]
            total[q] = total[q] + (pltpu.roll(partial, (3 - a) % 128, 1) if a != 3 else partial)
    return total


def row_sums(uses, mirror_ref):
    places = 1 + max(place for place, _, _ in uses)
    taps = {a: whole_row(mirror_ref, a) for _, a, _ in uses}
    total = [jnp.zeros((ROWS, 128), F32)] * places
    for b in range(7):
        partial = [None] * places
        for place, a, cells in uses:
            term = taps[a][b] * cells
            partial[place] = term if partial[place] is None else partial[place] + term
        for place in range(places):
            total[place] = total[place] + (pltpu.roll(partial[place], (3 - b) % 128, 1) if b != 3 else partial[place])
    return total


def mirrored_taps(wide_ref, mirror_ref):
    low_half = tall(lane_ids((8, 128)) < 64)
    for a in range(7):
        for b in range(3):
            mirror_ref[4 * a + b] = jnp.where(low_half, wide_ref[a * 7 + b], wide_ref[a * 7 + 6 - b])
        mirror_ref[4 * a + 3] = wide_ref[a * 7 + 3]


def whole_row(mirror_ref, a):
    if mirror_ref.shape[0] == 49:
        return [mirror_ref[7 * a + b] for b in range(7)]
    low_half = tall(lane_ids((8, 128)) < 64)
    ends = [(mirror_ref[4 * a + b], pltpu.roll(mirror_ref[4 * a + b], 64, 1)) for b in range(3)]
    first = [jnp.where(low_half, plain, turned) for plain, turned in ends]
    last = [jnp.where(low_half, turned, plain) for plain, turned in ends]
    return first + [mirror_ref[4 * a + 3]] + last[::-1]


def conv_border(tab_ref, recv_ref, sum_ref, mirror_ref, out_ref):
    lane = lane_ids((8, 128))
    half, within = lane // 64, lane % 64
    low_half = tall(lane < 64)

    group = lax.broadcasted_iota(jnp.int32, (ROWS, 128), 0) // 16

    def band_cells(band, offset):
        source, scale = band_source(tab_ref, band)
        main = jnp.concatenate([recv_ref[source, :, 256 * g + offset : 256 * g + offset + 128] for g in range(3)], axis=0)
        return main.astype(F32) * scale, recv_ref[source, :, 768:896].astype(F32) * scale

    def halo_rows(bands, folded, last, rest_side):
        sides = [band_cells(band, 0) for band in bands]
        first_columns = jnp.where((lane + jnp.where(last, 16, 0)) % 48 < 24, 1, 0)
        ends = jnp.where(tall(first_columns + jnp.where(folded, 1, 0) == 1), sides[2][0], sides[0][0])
        rest_lane = lane_ids((16, 128)) % 40
        rests = jnp.where(rest_lane < 20, sides[1][1], pltpu.roll(sides[rest_side][1], 20, 1))
        rests = jnp.concatenate([rests] * 3, axis=0)
        tiles = []
        for first_row in (0, 2):
            row = first_row + half
            inner = (within >= 3) & (within < 51)
            col = jnp.where(within < 3, 45 + within, jnp.where(within < 51, within - 3, within - 51))
            index = row * 48 + col
            index = jnp.where(folded, 143 - index, index)
            in_main = index - jnp.where(last, 16, 0)
            rest = (in_main < 0) | (in_main > 127)
            in_rest = jnp.where(in_main < 0, in_main + 16, in_main - 128) + jnp.where(inner, 0, 20)
            main_index, rest_index = tall(in_main & 127), (tall(in_rest) + 40 * group) & 127
            value = jnp.where(tall(inner), lanes_from(sides[1][0], main_index), lanes_from(ends, main_index))
            value = jnp.where(tall(rest), lanes_from(rests, rest_index), value)
            tiles.append(jnp.where(tall((within < 54) & (row < 3)), value, 0.0))
        return tiles

    def joined(first, second):
        return jnp.where(low_half, pltpu.roll(first, 64, 1), pltpu.roll(second, 64, 1))

    zeros = jnp.zeros((ROWS, 128), F32)
    below = halo_rows((0, 1, 2), False, True, 2)
    first_fix = row_sums(((0, 0, below[0]), (0, 1, joined(below[0], below[1])), (0, 2, below[1]), (1, 0, below[1])), mirror_ref)
    folded = tab_ref[8] == 2
    above = halo_rows((5, 6, 7), folded, folded, 0)
    edge = joined(zeros, above[0])
    last_fix = row_sums(((0, 6, edge), (1, 4, edge), (1, 5, above[0]), (1, 6, joined(above[0], above[1]))), mirror_ref)

    left, right = [(main, jnp.concatenate([rest] * 3, axis=0)) for main, rest in (band_cells(3, 128), band_cells(4, 128))]
    beside = []
    for j in range(3):
        which = jnp.where(half == 0, j, 2 - j)
        in_main = jnp.minimum(3 * within + which, 127)
        main_index, rest_index = tall(in_main), tall(jnp.clip(3 * (within - 40) + 16 + which, 0, 39)) + 40 * group
        picked = [
            jnp.where(tall(within < 40), lanes_from(main, main_index), lanes_from(rest, rest_index)) for main, rest in (left, right)
        ]
        beside.append(jnp.where(tall(within < 48), jnp.where(low_half, picked[0], picked[1]), 0.0))
    column_fix = column_sums(beside, mirror_ref)
    fixes = {0: first_fix[0], 1: first_fix[1], 22: last_fix[0], 23: last_fix[1]}
    for m in range(RIM // 128):
        row, col = place_of(m)
        index = tall(jnp.where(col < 24, row, 64 + row))
        value = sum_ref[:, 128 * m : 128 * m + 128]
        fix = zeros
        for q in range(3):
            fix = jnp.where(tall((col == q) | (col == 47 - q)), lanes_from(column_fix[q], index), fix)
        value = value + fix
        row_index = tall(row % 2 * 64 + 3 + col)
        for pair in pairs_of(m):
            if pair in fixes:
                value = value + jnp.where(tall(row // 2 == pair), lanes_from(fixes[pair], row_index), 0.0)
        out_ref[:, 128 * m : 128 * m + 128] = value.astype(BF)


def params(
    after_ref, x_ref, mask_ref, gain_ref, shift_ref, up_ref, up_bias_ref, down_ref, down_bias_ref, scale_ref, pool_weight_ref, spread_weight_ref,
    pool_ref, rim_cells_ref, middle_cells_ref, rim_mask_ref, rim_weights_ref, middle_weights_ref, *level_refs,
):
    me = lax.axis_index("chan")
    lane = lane_ids((192, 128))
    for level in range(2):
        weights_ref, values_ref = level_refs[2 * level : 2 * level + 2]
        row = slice(level, level + 1)
        spare = jnp.zeros((48, up_ref.shape[2]), BF)
        turned = jnp.concatenate([up_ref[level], three_terms(up_bias_ref[row, :]), spare], axis=0)
        weights_ref[0:768, :] = jnp.transpose(turned, (1, 0))
        own = down_ref[level, pl.ds(pl.multiple_of(me * ROWS, 16), ROWS), :]
        for j in range(3):
            weights_ref[768 + ROWS * j : 768 + ROWS * (j + 1), :] = own[:, 256 * j : 256 * j + 256]
        down_bias = columns(down_bias_ref[row, :])
        own = down_bias[0:ROWS]
        for k in range(1, down_bias.shape[0] // ROWS):
            own = jnp.where(me == k, down_bias[k * ROWS : (k + 1) * ROWS], own)
        rest = jnp.zeros((192 - ROWS, 128), F32)
        own, scale = [jnp.concatenate([value, rest], axis=0) for value in (own, columns(scale_ref[row, :]))]
        norm = jnp.where(lane == 0, columns(gain_ref[row, :]), columns(shift_ref[row, :]))
        values_ref[0:192, :] = jnp.where(lane < 2, norm, jnp.where(lane == 2, own, scale))
    fine_values_ref, coarse_values_ref = level_refs[1], level_refs[3]
    lane = lane_ids((ROWS, FINE_IN))
    spread = cell_weights(spread_weight_ref, lane // 48, lane % 48)
    for j in range(3):
        coarse_values_ref[240 + ROWS * j : 240 + ROWS * (j + 1), :] = spread[:, 128 * j : 128 * j + 128]
    lane = lane_ids((ROWS, 128))
    rim_weights_ref[:, 0:128] = cell_weights(pool_weight_ref, lane // 64, lane)
    rim_weights_ref[:, 128:256] = cell_weights(pool_weight_ref, lane // 8, lane)
    lane = lane_ids((ROWS, MIDDLE))
    middle_weights_ref[...] = cell_weights(pool_weight_ref, lane // 40, lane)

    masks = []
    for i in range(GROUPS):
        masks.append(jnp.broadcast_to(mask_ref[:, i * FINE_IN : (i + 1) * FINE_IN].astype(F32), (8, FINE_IN)))
    counts = dot(jnp.concatenate(masks, axis=0).astype(BF), pool_ref[...])
    small_mask = jnp.where(counts > 0.5, 1.0, 0.0)
    for m in range(5):
        coarse_values_ref[192 + 8 * m : 200 + 8 * m, :] = coarse_tile(m, lambda i: small_mask[8 * i : 8 * i + 8], lambda value: value)
    coarse_values_ref[232:240, :] = jnp.zeros((8, 128), F32)
    for m in range((RIM + MIDDLE) // 128):
        row, col = place_of(m)
        cell = row * 48 + col
        index, value, mask = cell % 128, None, None
        for tile in sources_of(m):
            lanes = slice(128 * tile, 128 * tile + 128)
            part = lanes_from(x_ref[0, :, lanes].astype(F32), tall(index))
            mask_part = lanes_from(jnp.broadcast_to(mask_ref[:, lanes].astype(F32), (8, 128)), index)
            value = part if value is None else jnp.where(tall(cell // 128 == tile), part, value)
            mask = mask_part if mask is None else jnp.where(cell // 128 == tile, mask_part, mask)
        if m < RIM // 128:
            rim_cells_ref[:, 128 * m : 128 * m + 128] = value.astype(BF)
            rim_mask_ref[:, 128 * m : 128 * m + 128] = mask
        else:
            t = m - RIM // 128
            middle_cells_ref[:, 128 * t : 128 * t + 128] = value.astype(BF)
            fine_values_ref[192 + 8 * t : 200 + 8 * t, :] = mask


def in_rows(rim_ref, middle_ref, out_ref):
    rim_tiles = RIM // 128

    def tiles(m):
        ref, t = (rim_ref, m) if m < rim_tiles else (middle_ref, m - rim_tiles)
        return ref[:, 128 * t : 128 * t + 128].astype(F32)

    for t in range(TILE * TILE // 128):
        cell, static = 128 * t + lane_ids((8, 128)), 128 * t + np.arange(128)
        value = collected(tiles, cell // 48, cell % 48, static // 48, static % 48, lambda m: True)
        out_ref[:, 128 * t : 128 * t + 128] = value.astype(BF)


def conv_coarse(x_ref, weight_ref, bias_ref, rim_ref, middle_ref, cells_ref, wide_ref, pad_ref, sum_ref):
    for tap in range(49):
        wide_ref[tap] = jnp.broadcast_to(weight_ref[1, :, tap : tap + 1], (ROWS, 128))
    pad_ref[0, :, 0:128] = jnp.zeros((ROWS, 128), F32)
    pad_ref[0, :, 896:1024] = jnp.zeros((ROWS, 128), F32)
    pad_ref[0, :, 128:896] = x_ref[...].astype(F32)
    padded = pad_ref[0]
    for turn in range(1, 4):
        pad_ref[turn] = lane_shifted(padded, 32 * turn)
    sum_ref[...] = wide(columns(bias_ref[1:2, :]), 768)

    def group(g, carry):
        rows = pl.ds(pl.multiple_of(g * 8, 8), 8)
        for chunk in range(2):
            base = chunk * 384
            taken = []
            for a in range(1, 8):
                start = base + (a // 4) * 128
                taken.append([pad_ref[a % 4, rows, start + 128 * j : start + 128 * j + 128] for j in range(3)])
            total = [sum_ref[rows, base + 128 * j : base + 128 * j + 128] for j in range(3)]
            for b in range(7):
                weights = [wide_ref[a * 7 + b, rows, :] for a in range(7)]
                for j in range(3):
                    partial = weights[0] * taken[0][j]
                    for a in range(1, 7):
                        partial = partial + weights[a] * taken[a][j]
                    total[j] = total[j] + (pltpu.roll(partial, (3 - b) % 128, 1) if b != 3 else partial)
            for j in range(3):
                sum_ref[rows, base + 128 * j : base + 128 * j + 128] = total[j]
        return carry

    lax.fori_loop(0, 6, group, 0)
    for m in range(5):
        here = slice(128 * m, 128 * m + 128)
        cells_ref[:, here] = coarse_tile(m, lambda i: x_ref[:, 128 * i : 128 * i + 128].astype(F32)).astype(BF)
        value = coarse_tile(m, lambda i: sum_ref[:, 128 * i : 128 * i + 128])
        if m < 3:
            rim_ref[:, here] = value
        else:
            middle_ref[:, 128 * m - 384 : 128 * m - 256] = value.astype(BF)


def coarse_place(m):
    lane = lane_ids((8, 128))
    if m < 2:
        return 20 * m + lane // 32, lane % 32 - 3
    if m == 2:
        col = lane % 8
        return 4 + lane // 8, jnp.where(col < 4, col, col + 16)
    return 4 + 8 * (m - 3) + lane // 16, 4 + lane % 16


def coarse_tile(m, group, spread=tall):
    if m < 2:
        return group(5 * m)
    row, col = coarse_place(m)
    index, value = spread(row % 4 * 32 + 3 + col), None
    for i in range(1, 5) if m == 2 else range(2 * m - 5, 2 * m - 3):
        picked = lanes_from(group(i), index)
        value = picked if value is None else jnp.where(spread(row // 4 == i), picked, value)
    return value


def border_coarse(tab_ref, recv_ref, sum_ref, mirror_ref, out_ref):
    lane = lane_ids((8, 128))
    half, within, segment, inside = lane // 64, lane % 64, lane // 32, lane % 32
    group = lax.broadcasted_iota(jnp.int32, (ROWS, 128), 0) // 16

    def band_main(band):
        source, scale = band_source(tab_ref, band)
        return jnp.concatenate([recv_ref[source, :, 128 * g : 128 * g + 128] for g in range(3)], axis=0).astype(F32) * scale

    def band_rest(band):
        source, scale = band_source(tab_ref, band)
        return jnp.concatenate([recv_ref[source, :, 384:512].astype(F32) * scale] * 3, axis=0)

    def halo_rows(bands, folded):
        col = jnp.where(inside < 3, 21 + inside, jnp.where(inside < 27, inside - 3, inside - 27))
        index = segment * 24 + col
        index = tall(jnp.where(folded, 71 - index, index) & 127)
        picked = [lanes_from(band_main(band), index) for band in bands]
        value = jnp.where(tall(inside < 3), picked[0], jnp.where(tall(inside < 27), picked[1], picked[2]))
        return jnp.where(tall((inside < 30) & (segment < 3)), value, 0.0)

    def turned(cells, lanes, kept):
        return jnp.where(tall(kept), pltpu.roll(cells, lanes, 1), 0.0)

    below = halo_rows((0, 1, 2), False)
    first_fix = row_sums(((0, 0, below), (0, 1, turned(below, 96, lane < 64)), (0, 2, turned(below, 64, lane < 32))), mirror_ref)[0]
    above = halo_rows((5, 6, 7), tab_ref[8] == 2)
    last_fix = row_sums(
        ((0, 6, turned(above, 32, lane >= 32)), (0, 5, turned(above, 64, lane >= 64)), (0, 4, turned(above, 96, lane >= 96))), mirror_ref
    )[0]
    sides = [(band_main(band), band_rest(band)) for band in (3, 4)]
    beside = []
    for j in range(3):
        which = jnp.where(half == 0, j, 2 - j)
        main_index = tall(jnp.minimum(72 + 3 * within + which, 127))
        rest_index = tall(jnp.clip(3 * (within - 16) + which, 0, 23)) + 24 * group
        picked = [
            jnp.where(tall(within < 16), lanes_from(main, main_index), lanes_from(rest, rest_index)) for main, rest in sides
        ]
        beside.append(jnp.where(tall(within < HALF), jnp.where(tall(half == 0), picked[0], picked[1]), 0.0))
    column_fix = column_sums(beside, mirror_ref)
    for m in range(3):
        row, col = coarse_place(m)
        index = tall(jnp.where(col < 12, row, 64 + row))
        value = sum_ref[:, 128 * m : 128 * m + 128]
        fix = jnp.zeros((ROWS, 128), F32)
        for q in range(3):
            fix = jnp.where(tall((col == q) | (col == 23 - q)), lanes_from(column_fix[q], index), fix)
        value = value + fix
        if m < 2:
            value = value + (first_fix, last_fix)[m]
        out_ref[:, 128 * m : 128 * m + 128] = value.astype(BF)


def gather_rows(pieces, cat_ref):
    me = lax.axis_index("chan")
    for k, piece in enumerate(pieces):
        first = pl.multiple_of(lax.bitwise_xor(me, k) * ROWS, 16)
        cat_ref[pl.ds(first, ROWS), :] = piece[...]


def make_branch(cat_ref, weights_ref, values_ref, block):
    def spread_lane(rows, lane):
        return wide(jnp.broadcast_to(values_ref[0:rows, lane : lane + 1], (rows, 128)), block)

    gain, shift, down_bias, scale = spread_lane(192, 0), spread_lane(192, 1), spread_lane(ROWS, 2), spread_lane(ROWS, 3)
    down = jnp.concatenate([weights_ref[768 + ROWS * j : 768 + ROWS * (j + 1), :] for j in range(3)], axis=1)
    inputs = 4 * ROWS

    def branch(start):
        values = cat_ref[0:inputs, start : start + block].astype(F32)
        mean = jnp.mean(values, axis=0, keepdims=True)
        centred = values - mean
        spread = jnp.mean(centred * centred, axis=0, keepdims=True)
        normed = (centred * lax.rsqrt(spread + norm_eps) * gain + shift).astype(BF)
        hidden = dot(weights_ref[0:768, 0 : inputs + 16], jnp.concatenate([normed, jnp.ones((16, block), BF)], axis=0))
        hidden = 0.5 * hidden * (1.0 + lax.erf(hidden * np.float32(0.5**0.5)))
        return scale * (dot(down, hidden.astype(BF)) + down_bias)

    return branch


def cell_weights(weight_ref, row, col):
    kind = 2 * (row % 2) + col % 2
    result = jnp.zeros(row.shape, F32)
    for k in range(4):
        result = jnp.where(kind == k, weight_ref[:, k : k + 1], result)
    return result


def make_mix_rim(count):
    def mix_rim(
        tab_ref, own_ref, p1_ref, p2_ref, p3_ref, x_ref, mask_ref, pool_cells_ref, weights_ref, values_ref,
        middle_pooled_ref, fine_ref, msg_ref, all_pooled_ref, cat_ref, mains_ref, rest_ref,
    ):
        gather_rows((own_ref, p1_ref, p2_ref, p3_ref), cat_ref)
        block = RIM
        branch = make_branch(cat_ref, weights_ref, values_ref, block)
        for start in range(0, RIM, block):
            here = slice(start, start + block)
            value = x_ref[:, here].astype(F32) + branch(start)
            fine_ref[:, here] = (mask_ref[0:1, here] * value).astype(BF)

        sums = []
        for m in range(RIM // 128):
            weights, step = (pool_cells_ref[:, 0:128], 64) if m < 4 else (pool_cells_ref[:, 128:256], 8)
            product = fine_ref[:, 128 * m : 128 * m + 128].astype(F32) * weights
            product = product + lane_shifted(product, 1)
            sums.append(product + lane_shifted(product, step))
        for i in range(GROUPS):
            here = slice(128 * i, 128 * i + 128)
            value = coarse_from(i, lambda m: sums[m], lambda m: m < RIM // 128)
            all_pooled_ref[:, here] = (value + middle_pooled_ref[:, here].astype(F32)).astype(BF)

        groups = [all_pooled_ref[:, 128 * i : 128 * i + 128].astype(F32) for i in range(GROUPS)]
        lane = lane_ids((8, 128))
        index = lane // 24 * 32 + 3 + lane % 24
        rows = [lanes_from(groups[0], tall(index & 127)), lanes_from(groups[5], tall((index + 32) & 127))]
        cell = jnp.clip(lane - 72, 0, 47)
        rest_cell = lane_ids((ROWS, 128)) - lax.broadcasted_iota(jnp.int32, (ROWS, 128), 0) // 16 * 24
        rest_valid = (rest_cell >= 0) & (rest_cell < 24)
        rest_cell = jnp.clip(rest_cell, 0, 23)
        for c in range(2):
            first = 24 if c else 3
            index = tall(cell // 3 % 4 * 32 + first + cell % 3)
            column = lanes_from(groups[0], index)
            for i in range(1, 4):
                column = jnp.where(tall(cell // 12 == i), lanes_from(groups[i], index), column)
            for r in range(2):
                mains_ref[2 * r + c] = jnp.where(tall(lane < 72), rows[r], column).astype(BF)
            index = rest_cell // 3 % 4 * 32 + first + rest_cell % 3
            rest = jnp.where(rest_cell < 12, lanes_from(groups[4], index), lanes_from(groups[5], index))
            rest = jnp.where(rest_valid, rest, 0.0)
            rest_ref[c] = (rest[0:16] + rest[16:32] + rest[32:48]).astype(BF)

        def fill(dev, carry):
            both = tab_ref[16 + dev]
            for g in range(3):
                msg_ref[dev, :, 128 * g : 128 * g + 128] = mains_ref[both, 16 * g : 16 * g + 16, :]
            msg_ref[dev, :, 384:512] = rest_ref[lax.bitwise_and(both, 1)]
            return carry

        scan_tiles(count, fill, jnp.int32(0))

    return mix_rim


def mix_middle(
    own_ref, p1_ref, p2_ref, p3_ref, x_ref, pool_cells_ref, weights_ref, values_ref, fine_ref, pooled_ref, cat_ref
):
    gather_rows((own_ref, p1_ref, p2_ref, p3_ref), cat_ref)
    value = x_ref[...].astype(F32) + make_branch(cat_ref, weights_ref, values_ref, MIDDLE)(0)
    mask = jnp.concatenate([values_ref[192 + 8 * t : 193 + 8 * t, :] for t in range(MIDDLE // 128)], axis=1)
    fine_ref[...] = (mask * value).astype(BF)
    sums = fine_ref[...].astype(F32) * pool_cells_ref[...]
    sums = sums + lane_shifted(sums, 1)
    sums = sums + lane_shifted(sums, 40)
    first = RIM // 128
    for i in range(GROUPS):
        value = coarse_from(i, lambda m: sums[:, 128 * (m - first) : 128 * (m - first) + 128], lambda m: m >= first)
        pooled_ref[:, 128 * i : 128 * i + 128] = value.astype(BF)


def coarse_cells(pieces, first, pooled_ref, weights_ref, values_ref, cat_ref):
    gather_rows(pieces, cat_ref)
    lanes = cat_ref.shape[1]
    value = pooled_ref[:, 128 * first : 128 * first + lanes].astype(F32) + make_branch(cat_ref, weights_ref, values_ref, lanes)(0)
    tiles = range(first, first + lanes // 128)
    return jnp.concatenate([values_ref[192 + 8 * m : 193 + 8 * m, :] for m in tiles], axis=1) * value


def mix_coarse_middle(own_ref, p1_ref, p2_ref, p3_ref, pooled_ref, weights_ref, values_ref, out_ref, cat_ref):
    out_ref[...] = coarse_cells((own_ref, p1_ref, p2_ref, p3_ref), 3, pooled_ref, weights_ref, values_ref, cat_ref).astype(BF)


def mix_coarse(
    own_ref, p1_ref, p2_ref, p3_ref, pooled_ref, middle_ref, fine_ref, mask_ref, weights_ref, values_ref, pool_ref, spread_ref, out_ref, cat_ref,
):
    rim = coarse_cells((own_ref, p1_ref, p2_ref, p3_ref), 0, pooled_ref, weights_ref, values_ref, cat_ref)
    ends = jnp.concatenate([rim[:, 0:128], rim[:, 128:256]], axis=0).astype(BF)
    ends = lax.dot_general(ends, pool_ref[...], (((1,), (1,)), ((), ())), preferred_element_type=F32)
    sides, lane = rim[:, 256:384], lane_ids((ROWS, 128))
    parts = []
    for i in range(4):
        middle = middle_ref[:, 128 * (i // 2) : 128 * (i // 2) + 128].astype(F32)
        side = pltpu.roll(sides, 128 - 32 * i, 1) if i else sides
        parts.append(jnp.where(lane < 32, side, pltpu.roll(middle, 96 if i % 2 else 32, 1)).astype(BF))
    inner = dot(jnp.concatenate(parts, axis=0), spread_ref[...])
    weights = jnp.concatenate([values_ref[240 + ROWS * j : 240 + ROWS * (j + 1), :] for j in range(3)], axis=1)
    for i in range(GROUPS):
        lanes = slice(i * FINE_IN, (i + 1) * FINE_IN)
        if i % 5 == 0:
            spread = ends[i // 5 * ROWS : (i // 5 + 1) * ROWS]
        else:
            spread = inner[(i - 1) * ROWS : i * ROWS]
        merged = fine_ref[:, lanes].astype(F32) + weights * spread
        out_ref[0, :, lanes] = (mask_ref[:, lanes].astype(F32) * merged).astype(BF)


VMEM = pl.BlockSpec(memory_space=pltpu.VMEM)
SMEM = pl.BlockSpec(memory_space=pltpu.SMEM)

def takes(microseconds):
    return pl.CostEstimate(flops=microseconds * 1_000_000_000, bytes_accessed=0, transcendentals=0)


def shaped(*shape, dtype=BF):
    return jax.ShapeDtypeStruct(shape, dtype)


PARAMS = pltpu.CompilerParams(vmem_limit_bytes=24 * 1024 * 1024)


def every_channel(own, first_work, later_work, direct):
    pairs = lambda bit: [(i, i ^ bit) for i in range(4)]
    across = lax.ppermute(own, "chan", pairs(2))
    if direct:
        diagonal = lax.ppermute(own, "chan", pairs(3))
    near, *results = lax.optimization_barrier((own, *first_work(own)))
    beside = lax.ppermute(near, "chan", pairs(1))
    if direct:
        across, diagonal, *results = lax.optimization_barrier((across, diagonal, *results, *later_work(*results)))
    else:
        across, *results = lax.optimization_barrier((across, *results, *later_work(*results)))
        diagonal = lax.ppermute(across, "chan", pairs(1))
    return (own, beside, across, diagonal), results


def per_device(
    features, land_mask, wet_slots, device_of, depth_weight, depth_bias, norm_gain, norm_bias, up_weight, up_bias,
    down_weight, down_bias, layer_scale, pool_weight, spread_weight,
):
    count = wet_slots.shape[0]
    grid_x = 2 * count // GRID_Y
    cells = TILE * TILE
    pack = pl.pallas_call(
        strip_table, out_specs=VMEM, out_shape=shaped(FINE_IN, 256), compiler_params=PARAMS, cost_estimate=takes(2), name="strip_table"
    )()
    messages, table = pl.pallas_call(
        make_prep(grid_x),
        in_specs=[SMEM, SMEM, VMEM, VMEM],
        out_specs=[VMEM, SMEM],
        out_shape=[shaped(count, 16, 896), shaped(16 + count, dtype=jnp.int32)],
        scratch_shapes=[
            pltpu.VMEM((2, ROWS, 128), BF),
            pltpu.VMEM((2, ROWS, 128), BF),
            pltpu.VMEM((2, 16, 128), F32),
            pltpu.VMEM((2, 16, 128), F32),
        ],
        compiler_params=PARAMS,
        cost_estimate=takes(10),
        name="prep",
    )(wet_slots, device_of, features, pack)
    pool = jnp.asarray(POOL)
    arrived = lax.all_to_all(messages, "tile", 0, 0, tiled=True)
    inner, inner_middle, fine_taps = pl.pallas_call(
        lambda tab_ref, *refs: conv_inner(*refs),
        in_specs=[SMEM] + [VMEM] * 3,
        out_specs=[VMEM] * 3,
        out_shape=[shaped(ROWS, RIM, dtype=F32), shaped(ROWS, MIDDLE), shaped(28, ROWS, 128, dtype=F32)],
        scratch_shapes=[
            pltpu.VMEM((49, ROWS, 128), F32),
            pltpu.VMEM((ROWS, 3584), F32),
            pltpu.VMEM((ROWS, 3584), F32),
            pltpu.VMEM((ROWS, 3072), F32),
        ],
        compiler_params=PARAMS,
        cost_estimate=takes(4),
        name="conv_inner",
    )(table, features, depth_weight, depth_bias)
    conv = pl.pallas_call(
        conv_border,
        in_specs=[SMEM] + [VMEM] * 3,
        out_specs=VMEM,
        out_shape=shaped(ROWS, RIM),
        compiler_params=PARAMS,
        cost_estimate=takes(2),
        name="conv_border",
    )(table, arrived, inner, fine_taps)

    pairs = lambda bit: [(i, i ^ bit) for i in range(4)]
    middle_across = lax.ppermute(inner_middle, "chan", pairs(2))
    middle_beside = lax.ppermute(inner_middle, "chan", pairs(1))
    middle_across, _ = lax.optimization_barrier((middle_across, conv))
    middle_pieces = (inner_middle, middle_beside, middle_across, lax.ppermute(middle_across, "chan", pairs(1)))

    def mix_middle_cells(*results):
        return pl.pallas_call(
            mix_middle,
            in_specs=[VMEM] * 8,
            out_specs=[VMEM] * 2,
            out_shape=[shaped(ROWS, MIDDLE), shaped(ROWS, 768)],
            scratch_shapes=[pltpu.VMEM((4 * ROWS, MIDDLE), BF)],
            compiler_params=PARAMS,
            cost_estimate=takes(1),
            name="mix_middle",
        )(*middle_pieces, results[1], results[4], results[5], results[6])

    def spread_params(own):
        shapes = [
            ((ROWS, RIM), BF), ((ROWS, MIDDLE), BF), ((8, RIM), F32), ((ROWS, 256), F32), ((ROWS, MIDDLE), F32),
            ((912, 256), BF), ((296, 128), F32), ((912, 256), BF), ((384, 128), F32),
        ]
        return pl.pallas_call(
            params,
            in_specs=[VMEM] * 13,
            out_specs=[VMEM] * len(shapes),
            out_shape=[shaped(*shape, dtype=dtype) for shape, dtype in shapes],
            compiler_params=PARAMS,
            cost_estimate=takes(2),
            name="params",
        )(
            own, features, land_mask, norm_gain, norm_bias, jnp.swapaxes(up_weight, 1, 2), up_bias, down_weight, down_bias, layer_scale,
            pool_weight, spread_weight, pool,
        )

    pieces, results = every_channel(conv, spread_params, mix_middle_cells, True)
    rim_cells, _, rim_mask, rim_weights, _, fine_weights, fine_values, coarse_weights, coarse_values, middle, middle_pooled = results
    rim, messages, pooled = pl.pallas_call(
        make_mix_rim(count),
        in_specs=[SMEM] + [VMEM] * 10,
        out_specs=[VMEM] * 3,
        out_shape=[shaped(ROWS, RIM), shaped(count, 16, 512), shaped(ROWS, 768)],
        scratch_shapes=[
            pltpu.VMEM((4 * ROWS, RIM), BF),
            pltpu.VMEM((4, ROWS, 128), BF),
            pltpu.VMEM((2, 16, 128), BF),
        ],
        compiler_params=PARAMS,
        cost_estimate=takes(3),
        name="mix_rim",
    )(
        table, *pieces, rim_cells, rim_mask, rim_weights, fine_weights, fine_values, middle_pooled,
    )
    arrived = lax.all_to_all(messages, "tile", 0, 0, tiled=True)
    inner, middle_conv, pooled, taps = pl.pallas_call(
        conv_coarse,
        in_specs=[VMEM] * 3,
        out_specs=[VMEM] * 4,
        out_shape=[shaped(ROWS, 384, dtype=F32), shaped(ROWS, 256), shaped(ROWS, 640), shaped(49, ROWS, 128, dtype=F32)],
        scratch_shapes=[pltpu.VMEM((4, ROWS, 1024), F32), pltpu.VMEM((ROWS, 768), F32)],
        compiler_params=PARAMS,
        cost_estimate=takes(2),
        name="conv_coarse",
    )(pooled, depth_weight, depth_bias)
    conv = pl.pallas_call(
        border_coarse,
        in_specs=[SMEM] + [VMEM] * 3,
        out_specs=VMEM,
        out_shape=shaped(ROWS, 384),
        compiler_params=PARAMS,
        cost_estimate=takes(1),
        name="border_coarse",
    )(table, arrived, inner, taps)
    middle_across = lax.ppermute(middle_conv, "chan", pairs(2))
    middle_beside = lax.ppermute(middle_conv, "chan", pairs(1))
    middle_across, _ = lax.optimization_barrier((middle_across, conv))
    coarse_pieces = (middle_conv, middle_beside, middle_across, lax.ppermute(middle_across, "chan", pairs(1)))

    def back_in_rows(own):
        return pl.pallas_call(
            lambda after_ref, *refs: in_rows(*refs),
            in_specs=[VMEM] * 3,
            out_specs=[VMEM],
            out_shape=[shaped(ROWS, cells)],
            compiler_params=PARAMS,
            cost_estimate=takes(1),
            name="in_rows",
        )(own, rim, middle)

    def mix_coarse_cells(*results):
        return pl.pallas_call(
            mix_coarse_middle,
            in_specs=[VMEM] * 7,
            out_specs=[VMEM],
            out_shape=[shaped(ROWS, 256)],
            scratch_shapes=[pltpu.VMEM((4 * ROWS, 256), BF)],
            compiler_params=PARAMS,
            cost_estimate=takes(1),
            name="mix_coarse_middle",
        )(*coarse_pieces, pooled, coarse_weights, coarse_values)

    pieces, (fine, coarse_middle) = every_channel(conv, back_in_rows, mix_coarse_cells, True)
    return pl.pallas_call(
        mix_coarse,
        in_specs=[VMEM] * 12,
        out_specs=VMEM,
        out_shape=shaped(1, ROWS, cells),
        scratch_shapes=[pltpu.VMEM((4 * ROWS, 384), BF)],
        compiler_params=PARAMS,
        cost_estimate=takes(2),
        name="mix_coarse",
    )(*pieces, pooled, coarse_middle, fine, land_mask, coarse_weights, coarse_values, pool, jnp.asarray(COARSE_SPREAD))


def solution(mesh):
    placed = (
        P("tile", "chan", None),
        P("tile", None),
        P(),
        P(),
        P(None, "chan", None),
        P(None, "chan"),
        P(),
        P(),
        P(),
        P(),
        P(),
        P(),
        P(None, "chan"),
        P("chan", None),
        P("chan", None),
    )
    return jax.shard_map(
        per_device, mesh=mesh, in_specs=placed, out_specs=P("tile", "chan", None), check_vma=False
    )
```

```python
import jax
import jax.numpy as jnp
import ml_dtypes
import numpy as np
from jax import lax
from jax.experimental import pallas as pl
from jax.experimental.pallas import tpu as pltpu
from jax.sharding import PartitionSpec as P

TILE = 48
HALF = TILE // 2
GRID_Y = 4
GROUPS = 6
ROWS = 48
FINE_IN = 8 * TILE
RIM = 896
MIDDLE = 1664
BANDS = ((-1, -1), (-1, 0), (-1, 1), (0, -1), (0, 1), (1, -1), (1, 0), (1, 1))
norm_eps = 1e-06
BF = jnp.bfloat16
F32 = jnp.float32


def one_hot(shape, pairs):
    table = np.zeros(shape, np.float32)
    for source, target in pairs:
        table[source, target] = 1.0
    return table.astype(ml_dtypes.bfloat16)


def pool_table():
    return one_hot((384, 128), [(row * 48 + col, (row // 2) * 32 + 3 + col // 2) for row in range(8) for col in range(48)])


def coarse_spread_table():
    pairs = []
    for row in range(4):
        for col in range(HALF):
            if 4 <= col < 20:
                lane = 32 + row * 16 + col - 4
            else:
                lane = row * 8 + (col if col < 4 else col - 16)
            pairs += [(lane, (2 * row + u) * 48 + 2 * col + v) for u in range(2) for v in range(2)]
    return one_hot((128, 384), pairs)


POOL = pool_table()
COARSE_SPREAD = coarse_spread_table()


def dot(left, right):
    return jnp.dot(left, right, preferred_element_type=F32)


def stacked(value, width):
    return jnp.concatenate([value[:, i * width : (i + 1) * width] for i in range(GROUPS)], axis=0)


def lane_ids(shape):
    return lax.broadcasted_iota(jnp.int32, shape, 1)


def three_terms(row):
    high = row.astype(BF)
    rest = row - high.astype(F32)
    middle = rest.astype(BF)
    low = (rest - middle.astype(F32)).astype(BF)
    return jnp.concatenate([high, middle, low, jnp.zeros((13, row.shape[1]), BF)], axis=0)


def columns(row):
    return lax.dot_general(
        three_terms(row), jnp.ones((16, 128), BF), (((0,), (0,)), ((), ())), preferred_element_type=F32
    )


def wide(block, lanes):
    return jnp.concatenate([block] * (lanes // 128), axis=1)


def scan_tiles(count, step, carry):
    if count <= 16:
        for k in range(count):
            carry = step(k, carry)
        return carry
    return lax.fori_loop(0, count, step, carry)


def strip_table(pack_ref):
    shape = (FINE_IN, 256)
    source = lax.broadcasted_iota(jnp.int32, shape, 0)
    lane = lane_ids(shape)
    within = lane % 128
    wanted = (within // 3) * TILE + within % 3 + jnp.where(lane >= 128, TILE - 3, 0)
    pack_ref[...] = jnp.where((within < 24) & (source == wanted), 1.0, 0.0).astype(BF)


def quotient(value, divisor):
    if divisor & (divisor - 1) == 0:
        return lax.shift_right_logical(value, jnp.int32(divisor.bit_length() - 1))
    return lax.div(value, divisor)


def remainder(value, divisor):
    if divisor & (divisor - 1) == 0:
        return lax.bitwise_and(value, jnp.int32(divisor - 1))
    return lax.rem(value, divisor)


def make_prep(grid_x):
    def prep(slots_ref, dev_ref, x_ref, pack_ref, msg_ref, tab_ref, rows_ref, cols_ref, row_rest_ref, col_rest_ref):
        count = slots_ref.shape[0]
        me = lax.axis_index("tile")
        my_slot = scan_tiles(count, lambda k, c: c + jnp.where(dev_ref[k] == me, slots_ref[k], 0), jnp.int32(0))
        my_x = remainder(my_slot, grid_x)
        my_y = quotient(my_slot, grid_x)
        wanted = []
        for up_by, right_by in BANDS:
            near_x = remainder(my_x + (right_by + grid_x), grid_x)
            near_y = my_y + up_by
            folded = near_y >= GRID_Y
            from_x = jnp.where(folded, grid_x - 1 - near_x, near_x)
            from_y = jnp.where(folded, GRID_Y - 1, near_y)
            wanted.append(from_y * grid_x + from_x)

        def find(k, found):
            slot, dev = slots_ref[k], dev_ref[k]
            row_pick = jnp.where(quotient(slot, grid_x) + 1 == my_y, 0, 1)
            col_pick = jnp.where(remainder(slot, grid_x) == remainder(my_x + (grid_x - 1), grid_x), 0, 1)
            tab_ref[16 + dev] = 2 * row_pick + col_pick
            return tuple(jnp.where(slot == want, dev, old) for want, old in zip(wanted, found))

        found = scan_tiles(count, find, tuple(jnp.int32(-1) for _ in BANDS))
        for band in range(8):
            tab_ref[band] = found[band]
        tab_ref[8] = jnp.where(my_y == GRID_Y - 1, 2, 1)
        for spare in range(9, 16):
            tab_ref[spare] = 0

        x = x_ref[0]
        cols = dot(stacked(x, FINE_IN), pack_ref[...])
        lane = lane_ids((ROWS, 128))
        for side in range(2):
            part = cols[:, side * 128 : side * 128 + 128]
            main = part[0:ROWS]
            for i in range(1, 5):
                main = main + pltpu.roll(part[i * ROWS : (i + 1) * ROWS], 24 * i, 1)
            cols_ref[side] = main.astype(BF)
            rest = pltpu.roll(part[5 * ROWS : 6 * ROWS], 16, 1)
            col_rest_ref[side] = rest[0:16] + pltpu.roll(rest[16:32], 40, 1) + pltpu.roll(rest[32:48], 80, 1)
        rows_ref[0] = x[:, 0:128]
        rows_ref[1] = x[:, 2176:2304]
        ends = (x[:, 128:256].astype(F32), pltpu.roll(x[:, 2048:2176].astype(F32), 16, 1))
        for side in range(2):
            rest = jnp.where(lane < 16, ends[side], 0.0)
            row_rest_ref[side] = rest[0:16] + pltpu.roll(rest[16:32], 40, 1) + pltpu.roll(rest[32:48], 80, 1)

        def fill(dev, carry):
            row_pick = quotient(tab_ref[16 + dev], 2)
            col_pick = remainder(tab_ref[16 + dev], 2)
            for g in range(3):
                msg_ref[dev, :, 256 * g : 256 * g + 128] = rows_ref[row_pick, 16 * g : 16 * g + 16, :]
                msg_ref[dev, :, 256 * g + 128 : 256 * g + 256] = cols_ref[col_pick, 16 * g : 16 * g + 16, :]
            msg_ref[dev, :, 768:896] = (row_rest_ref[row_pick] + col_rest_ref[col_pick]).astype(BF)
            return carry

        scan_tiles(count, fill, jnp.int32(0))

    return prep


def band_source(tab_ref, band):
    source = tab_ref[band]
    return jnp.maximum(source, 0), jnp.where(source >= 0, 1.0, 0.0).astype(F32)


def lane_shifted(value, lanes):
    return pltpu.roll(value, value.shape[1] - lanes, 1)


def tall(row_block):
    return jnp.concatenate([row_block] * (ROWS // 8), axis=0)


def lanes_from(value, index):
    return jnp.take_along_axis(value, index, axis=1)


def conv_inner(x_ref, weight_ref, bias_ref, sum_ref, middle_ref, mirror_ref, wide_ref, pad_ref, odd_ref, total_ref):
    for tap in range(49):
        wide_ref[tap] = jnp.broadcast_to(weight_ref[0, :, tap : tap + 1], (ROWS, 128))
    mirrored_taps(wide_ref, mirror_ref)
    pad_ref[:, 0:256] = jnp.zeros((ROWS, 256), F32)
    pad_ref[:, 3328:3584] = jnp.zeros((ROWS, 256), F32)
    lane = lane_ids((8, 128))
    half, within = lane // 64, lane % 64
    valid = tall((within >= 3) & (within < 51))
    col = jnp.clip(within - 3, 0, 47)
    cells = [96 * k + 48 * half + col for k in range(4)]
    indices = [tall(cell % 128) for cell in cells]
    for i in range(GROUPS):
        tiles = [x_ref[0, :, 384 * i + 128 * m : 384 * i + 128 * m + 128].astype(F32) for m in range(3)]
        for k in range(4):
            first, final = (96 * k) // 128, (96 * k + 95) // 128
            value = lanes_from(tiles[first], indices[k])
            if final != first:
                value = jnp.where(tall(cells[k] < 128 * final), value, lanes_from(tiles[final], indices[k]))
            start = 256 + 512 * i + 128 * k
            pad_ref[:, start : start + 128] = jnp.where(valid, value, 0.0)
    odd_ref[...] = lane_shifted(pad_ref[...], 64)
    total_ref[...] = wide(columns(bias_ref[0:1, :]), 3072)

    def group(g, carry):
        here = pl.ds(pl.multiple_of(g * 8, 8), 8)
        for chunk in range(6):
            base = chunk * 512
            taken = []
            for a in range(1, 8):
                ref = odd_ref if a % 2 else pad_ref
                start = base + (a // 2) * 128
                taken.append([ref[here, start + 128 * j : start + 128 * j + 128] for j in range(4)])
            total = [total_ref[here, base + 128 * j : base + 128 * j + 128] for j in range(4)]
            for b in range(7):
                weights = [wide_ref[a * 7 + b, here, :] for a in range(7)]
                for j in range(4):
                    partial = weights[0] * taken[0][j]
                    for a in range(1, 7):
                        partial = partial + weights[a] * taken[a][j]
                    total[j] = total[j] + (pltpu.roll(partial, (3 - b) % 128, 1) if b != 3 else partial)
            for j in range(4):
                total_ref[here, base + 128 * j : base + 128 * j + 128] = total[j]
        return carry

    lax.fori_loop(0, ROWS // 8, group, 0)
    for m in range((RIM + MIDDLE) // 128):
        row, col = place_of(m)
        index = tall(row % 2 * 64 + 3 + col)
        value = None
        for pair in pairs_of(m):
            picked = lanes_from(total_ref[:, 128 * pair : 128 * pair + 128], index)
            value = picked if value is None else jnp.where(tall(row // 2 == pair), picked, value)
        if m < RIM // 128:
            sum_ref[:, 128 * m : 128 * m + 128] = value
        else:
            middle_ref[:, 128 * m - RIM : 128 * m - RIM + 128] = value.astype(BF)


def place_of(m, lane=None, ops=jnp):
    lane = lane_ids((8, 128)) if lane is None else lane
    if m < 4:
        return (2 * m if m < 2 else 40 + 2 * m) + lane // 64, ops.minimum(lane % 64, 47)
    if m < 7:
        col = lane % 8
        return ops.minimum(16 * m - 60 + lane // 8, 43), ops.where(col < 4, col, col + 40)
    cell = ops.minimum(128 * m - RIM + lane, 1599)
    return 4 + cell // 40, 4 + cell % 40


def pairs_of(m):
    return np.unique(place_of(m, np.arange(128), np)[0] // 2).tolist()


def sources_of(m):
    row, col = place_of(m, np.arange(128), np)
    return np.unique((row * 48 + col) // 128).tolist()


def lane_of(row, col, ops=jnp):
    ends = (row < 4) | (row >= 44)
    end = ops.where(row < 4, row, row - 40)
    side = (col < 4) | (col >= 44)
    cell = (row - 4) * 40 + col - 4
    tile = ops.where(ends, end // 2, ops.where(side, 4 + (row - 4) // 16, 7 + cell // 128))
    side_lane = (row - 4) % 16 * 8 + ops.where(col < 4, col, col - 40)
    return tile, ops.where(ends, end % 2 * 64 + col, ops.where(side, side_lane, cell % 128)) & 127


def collected(tiles, row, col, static_row, static_col, pick):
    tile, index = lane_of(row, col)
    value = None
    for m in np.unique(lane_of(static_row, static_col, np)[0]).tolist():
        if not pick(m):
            continue
        part = jnp.where(tall(tile == m), lanes_from(tiles(m), tall(index)), 0.0 if value is None else value)
        value = part
    return jnp.zeros((ROWS, 128), F32) if value is None else value


def coarse_from(i, sums, pick):
    def place(lane, ops):
        return 2 * (4 * i + lane // 32), 2 * ops.clip(lane % 32 - 3, 0, 23)

    lane = lane_ids((8, 128))
    inside = lane % 32
    row, col = place(lane, jnp)
    value = collected(sums, row, col, *place(np.arange(128), np), pick)
    return jnp.where(tall((inside >= 3) & (inside < 27)), value, 0.0)


def column_sums(beside, mirror_ref):
    total = [jnp.zeros((ROWS, 128), F32)] * 3
    for a in range(7):
        if mirror_ref.shape[0] == 49:
            low_half = tall(lane_ids((8, 128)) < 64)
            weights = [jnp.where(low_half, mirror_ref[7 * a + b], mirror_ref[7 * a + 6 - b]) for b in range(3)]
        else:
            weights = [mirror_ref[4 * a + b] for b in range(3)]
        for q in range(3):
            partial = weights[0] * beside[q]
            for j in range(q + 1, 3):
                partial = partial + weights[j - q] * beside[j]
            total[q] = total[q] + (pltpu.roll(partial, (3 - a) % 128, 1) if a != 3 else partial)
    return total


def row_sums(uses, mirror_ref):
    places = 1 + max(place for place, _, _ in uses)
    taps = {a: whole_row(mirror_ref, a) for _, a, _ in uses}
    total = [jnp.zeros((ROWS, 128), F32)] * places
    for b in range(7):
        partial = [None] * places
        for place, a, cells in uses:
            term = taps[a][b] * cells
            partial[place] = term if partial[place] is None else partial[place] + term
        for place in range(places):
            total[place] = total[place] + (pltpu.roll(partial[place], (3 - b) % 128, 1) if b != 3 else partial[place])
    return total


def mirrored_taps(wide_ref, mirror_ref):
    low_half = tall(lane_ids((8, 128)) < 64)
    for a in range(7):
        for b in range(3):
            mirror_ref[4 * a + b] = jnp.where(low_half, wide_ref[a * 7 + b], wide_ref[a * 7 + 6 - b])
        mirror_ref[4 * a + 3] = wide_ref[a * 7 + 3]


def whole_row(mirror_ref, a):
    if mirror_ref.shape[0] == 49:
        return [mirror_ref[7 * a + b] for b in range(7)]
    low_half = tall(lane_ids((8, 128)) < 64)
    ends = [(mirror_ref[4 * a + b], pltpu.roll(mirror_ref[4 * a + b], 64, 1)) for b in range(3)]
    first = [jnp.where(low_half, plain, turned) for plain, turned in ends]
    last = [jnp.where(low_half, turned, plain) for plain, turned in ends]
    return first + [mirror_ref[4 * a + 3]] + last[::-1]


def conv_border(tab_ref, recv_ref, sum_ref, mirror_ref, out_ref):
    lane = lane_ids((8, 128))
    half, within = lane // 64, lane % 64
    low_half = tall(lane < 64)

    group = lax.broadcasted_iota(jnp.int32, (ROWS, 128), 0) // 16

    def band_cells(band, offset):
        source, scale = band_source(tab_ref, band)
        main = jnp.concatenate([recv_ref[source, :, 256 * g + offset : 256 * g + offset + 128] for g in range(3)], axis=0)
        return main.astype(F32) * scale, recv_ref[source, :, 768:896].astype(F32) * scale

    def halo_rows(bands, folded, last, rest_side):
        sides = [band_cells(band, 0) for band in bands]
        first_columns = jnp.where((lane + jnp.where(last, 16, 0)) % 48 < 24, 1, 0)
        ends = jnp.where(tall(first_columns + jnp.where(folded, 1, 0) == 1), sides[2][0], sides[0][0])
        rest_lane = lane_ids((16, 128)) % 40
        rests = jnp.where(rest_lane < 20, sides[1][1], pltpu.roll(sides[rest_side][1], 20, 1))
        rests = jnp.concatenate([rests] * 3, axis=0)
        tiles = []
        for first_row in (0, 2):
            row = first_row + half
            inner = (within >= 3) & (within < 51)
            col = jnp.where(within < 3, 45 + within, jnp.where(within < 51, within - 3, within - 51))
            index = row * 48 + col
            index = jnp.where(folded, 143 - index, index)
            in_main = index - jnp.where(last, 16, 0)
            rest = (in_main < 0) | (in_main > 127)
            in_rest = jnp.where(in_main < 0, in_main + 16, in_main - 128) + jnp.where(inner, 0, 20)
            main_index, rest_index = tall(in_main & 127), (tall(in_rest) + 40 * group) & 127
            value = jnp.where(tall(inner), lanes_from(sides[1][0], main_index), lanes_from(ends, main_index))
            value = jnp.where(tall(rest), lanes_from(rests, rest_index), value)
            tiles.append(jnp.where(tall((within < 54) & (row < 3)), value, 0.0))
        return tiles

    def joined(first, second):
        return jnp.where(low_half, pltpu.roll(first, 64, 1), pltpu.roll(second, 64, 1))

    zeros = jnp.zeros((ROWS, 128), F32)
    below = halo_rows((0, 1, 2), False, True, 2)
    first_fix = row_sums(((0, 0, below[0]), (0, 1, joined(below[0], below[1])), (0, 2, below[1]), (1, 0, below[1])), mirror_ref)
    folded = tab_ref[8] == 2
    above = halo_rows((5, 6, 7), folded, folded, 0)
    edge = joined(zeros, above[0])
    last_fix = row_sums(((0, 6, edge), (1, 4, edge), (1, 5, above[0]), (1, 6, joined(above[0], above[1]))), mirror_ref)

    left, right = [(main, jnp.concatenate([rest] * 3, axis=0)) for main, rest in (band_cells(3, 128), band_cells(4, 128))]
    beside = []
    for j in range(3):
        which = jnp.where(half == 0, j, 2 - j)
        in_main = jnp.minimum(3 * within + which, 127)
        main_index, rest_index = tall(in_main), tall(jnp.clip(3 * (within - 40) + 16 + which, 0, 39)) + 40 * group
        picked = [
            jnp.where(tall(within < 40), lanes_from(main, main_index), lanes_from(rest, rest_index)) for main, rest in (left, right)
        ]
        beside.append(jnp.where(tall(within < 48), jnp.where(low_half, picked[0], picked[1]), 0.0))
    column_fix = column_sums(beside, mirror_ref)
    fixes = {0: first_fix[0], 1: first_fix[1], 22: last_fix[0], 23: last_fix[1]}
    for m in range(RIM // 128):
        row, col = place_of(m)
        index = tall(jnp.where(col < 24, row, 64 + row))
        value = sum_ref[:, 128 * m : 128 * m + 128]
        fix = zeros
        for q in range(3):
            fix = jnp.where(tall((col == q) | (col == 47 - q)), lanes_from(column_fix[q], index), fix)
        value = value + fix
        row_index = tall(row % 2 * 64 + 3 + col)
        for pair in pairs_of(m):
            if pair in fixes:
                value = value + jnp.where(tall(row // 2 == pair), lanes_from(fixes[pair], row_index), 0.0)
        out_ref[:, 128 * m : 128 * m + 128] = value.astype(BF)


def params(
    after_ref, x_ref, mask_ref, gain_ref, shift_ref, up_ref, up_bias_ref, down_ref, down_bias_ref, scale_ref, pool_weight_ref, spread_weight_ref,
    pool_ref, rim_cells_ref, middle_cells_ref, rim_mask_ref, rim_weights_ref, middle_weights_ref, *level_refs,
):
    me = lax.axis_index("chan")
    lane = lane_ids((192, 128))
    for level in range(2):
        weights_ref, values_ref = level_refs[2 * level : 2 * level + 2]
        row = slice(level, level + 1)
        spare = jnp.zeros((48, up_ref.shape[2]), BF)
        turned = jnp.concatenate([up_ref[level], three_terms(up_bias_ref[row, :]), spare], axis=0)
        weights_ref[0:768, :] = jnp.transpose(turned, (1, 0))
        own = down_ref[level, pl.ds(pl.multiple_of(me * ROWS, 16), ROWS), :]
        for j in range(3):
            weights_ref[768 + ROWS * j : 768 + ROWS * (j + 1), :] = own[:, 256 * j : 256 * j + 256]
        down_bias = columns(down_bias_ref[row, :])
        own = down_bias[0:ROWS]
        for k in range(1, down_bias.shape[0] // ROWS):
            own = jnp.where(me == k, down_bias[k * ROWS : (k + 1) * ROWS], own)
        rest = jnp.zeros((192 - ROWS, 128), F32)
        own, scale = [jnp.concatenate([value, rest], axis=0) for value in (own, columns(scale_ref[row, :]))]
        norm = jnp.where(lane == 0, columns(gain_ref[row, :]), columns(shift_ref[row, :]))
        values_ref[0:192, :] = jnp.where(lane < 2, norm, jnp.where(lane == 2, own, scale))
    fine_values_ref, coarse_values_ref = level_refs[1], level_refs[3]
    lane = lane_ids((8, FINE_IN))
    spread = cell_weights(spread_weight_ref, lane // 48, lane % 48)
    for j in range(3):
        coarse_values_ref[240 + ROWS * j : 240 + ROWS * (j + 1), :] = spread[:, 128 * j : 128 * j + 128]
    lane = lane_ids((8, 128))
    rim_weights_ref[:, 0:128] = cell_weights(pool_weight_ref, lane // 64, lane)
    rim_weights_ref[:, 128:256] = cell_weights(pool_weight_ref, lane // 8, lane)
    lane = lane_ids((8, MIDDLE))
    middle_weights_ref[...] = cell_weights(pool_weight_ref, lane // 40, lane)

    masks = []
    for i in range(GROUPS):
        masks.append(jnp.broadcast_to(mask_ref[:, i * FINE_IN : (i + 1) * FINE_IN].astype(F32), (8, FINE_IN)))
    counts = dot(jnp.concatenate(masks, axis=0).astype(BF), pool_ref[...])
    small_mask = jnp.where(counts > 0.5, 1.0, 0.0)
    for m in range(5):
        coarse_values_ref[192 + 8 * m : 200 + 8 * m, :] = coarse_tile(m, lambda i: small_mask[8 * i : 8 * i + 8], lambda value: value)
    coarse_values_ref[232:240, :] = jnp.zeros((8, 128), F32)
    for m in range((RIM + MIDDLE) // 128):
        row, col = place_of(m)
        cell = row * 48 + col
        index, value, mask = cell % 128, None, None
        for tile in sources_of(m):
            lanes = slice(128 * tile, 128 * tile + 128)
            part = lanes_from(x_ref[0, :, lanes].astype(F32), tall(index))
            mask_part = lanes_from(jnp.broadcast_to(mask_ref[:, lanes].astype(F32), (8, 128)), index)
            value = part if value is None else jnp.where(tall(cell // 128 == tile), part, value)
            mask = mask_part if mask is None else jnp.where(cell // 128 == tile, mask_part, mask)
        if m < RIM // 128:
            rim_cells_ref[:, 128 * m : 128 * m + 128] = value.astype(BF)
            rim_mask_ref[:, 128 * m : 128 * m + 128] = mask
        else:
            t = m - RIM // 128
            middle_cells_ref[:, 128 * t : 128 * t + 128] = value.astype(BF)
            fine_values_ref[192 + 8 * t : 200 + 8 * t, :] = mask


def in_rows(rim_ref, middle_ref, out_ref):
    rim_tiles = RIM // 128

    def tiles(m):
        ref, t = (rim_ref, m) if m < rim_tiles else (middle_ref, m - rim_tiles)
        return ref[:, 128 * t : 128 * t + 128].astype(F32)

    for t in range(TILE * TILE // 128):
        cell, static = 128 * t + lane_ids((8, 128)), 128 * t + np.arange(128)
        value = collected(tiles, cell // 48, cell % 48, static // 48, static % 48, lambda m: True)
        out_ref[:, 128 * t : 128 * t + 128] = value.astype(BF)


def conv_coarse(x_ref, weight_ref, bias_ref, rim_ref, middle_ref, cells_ref, wide_ref, pad_ref, sum_ref):
    for tap in range(49):
        wide_ref[tap] = jnp.broadcast_to(weight_ref[1, :, tap : tap + 1], (ROWS, 128))
    pad_ref[0, :, 0:128] = jnp.zeros((ROWS, 128), F32)
    pad_ref[0, :, 896:1024] = jnp.zeros((ROWS, 128), F32)
    pad_ref[0, :, 128:896] = x_ref[...].astype(F32)
    padded = pad_ref[0]
    for turn in range(1, 4):
        pad_ref[turn] = lane_shifted(padded, 32 * turn)
    sum_ref[...] = wide(columns(bias_ref[1:2, :]), 768)

    def group(g, carry):
        rows = pl.ds(pl.multiple_of(g * 8, 8), 8)
        for chunk in range(2):
            base = chunk * 384
            taken = []
            for a in range(1, 8):
                start = base + (a // 4) * 128
                taken.append([pad_ref[a % 4, rows, start + 128 * j : start + 128 * j + 128] for j in range(3)])
            total = [sum_ref[rows, base + 128 * j : base + 128 * j + 128] for j in range(3)]
            for b in range(7):
                weights = [wide_ref[a * 7 + b, rows, :] for a in range(7)]
                for j in range(3):
                    partial = weights[0] * taken[0][j]
                    for a in range(1, 7):
                        partial = partial + weights[a] * taken[a][j]
                    total[j] = total[j] + (pltpu.roll(partial, (3 - b) % 128, 1) if b != 3 else partial)
            for j in range(3):
                sum_ref[rows, base + 128 * j : base + 128 * j + 128] = total[j]
        return carry

    lax.fori_loop(0, 6, group, 0)
    for m in range(5):
        here = slice(128 * m, 128 * m + 128)
        cells_ref[:, here] = coarse_tile(m, lambda i: x_ref[:, 128 * i : 128 * i + 128].astype(F32)).astype(BF)
        value = coarse_tile(m, lambda i: sum_ref[:, 128 * i : 128 * i + 128])
        if m < 3:
            rim_ref[:, here] = value
        else:
            middle_ref[:, 128 * m - 384 : 128 * m - 256] = value.astype(BF)


def coarse_place(m):
    lane = lane_ids((8, 128))
    if m < 2:
        return 20 * m + lane // 32, lane % 32 - 3
    if m == 2:
        col = lane % 8
        return 4 + lane // 8, jnp.where(col < 4, col, col + 16)
    return 4 + 8 * (m - 3) + lane // 16, 4 + lane % 16


def coarse_tile(m, group, spread=tall):
    if m < 2:
        return group(5 * m)
    row, col = coarse_place(m)
    index, value = spread(row % 4 * 32 + 3 + col), None
    for i in range(1, 5) if m == 2 else range(2 * m - 5, 2 * m - 3):
        picked = lanes_from(group(i), index)
        value = picked if value is None else jnp.where(spread(row // 4 == i), picked, value)
    return value


def border_coarse(tab_ref, recv_ref, sum_ref, mirror_ref, out_ref):
    lane = lane_ids((8, 128))
    half, within, segment, inside = lane // 64, lane % 64, lane // 32, lane % 32
    group = lax.broadcasted_iota(jnp.int32, (ROWS, 128), 0) // 16

    def band_main(band):
        source, scale = band_source(tab_ref, band)
        return jnp.concatenate([recv_ref[source, :, 128 * g : 128 * g + 128] for g in range(3)], axis=0).astype(F32) * scale

    def band_rest(band):
        source, scale = band_source(tab_ref, band)
        return jnp.concatenate([recv_ref[source, :, 384:512].astype(F32) * scale] * 3, axis=0)

    def halo_rows(bands, folded):
        col = jnp.where(inside < 3, 21 + inside, jnp.where(inside < 27, inside - 3, inside - 27))
        index = segment * 24 + col
        index = tall(jnp.where(folded, 71 - index, index) & 127)
        picked = [lanes_from(band_main(band), index) for band in bands]
        value = jnp.where(tall(inside < 3), picked[0], jnp.where(tall(inside < 27), picked[1], picked[2]))
        return jnp.where(tall((inside < 30) & (segment < 3)), value, 0.0)

    def turned(cells, lanes, kept):
        return jnp.where(tall(kept), pltpu.roll(cells, lanes, 1), 0.0)

    below = halo_rows((0, 1, 2), False)
    first_fix = row_sums(((0, 0, below), (0, 1, turned(below, 96, lane < 64)), (0, 2, turned(below, 64, lane < 32))), mirror_ref)[0]
    above = halo_rows((5, 6, 7), tab_ref[8] == 2)
    last_fix = row_sums(
        ((0, 6, turned(above, 32, lane >= 32)), (0, 5, turned(above, 64, lane >= 64)), (0, 4, turned(above, 96, lane >= 96))), mirror_ref
    )[0]
    sides = [(band_main(band), band_rest(band)) for band in (3, 4)]
    beside = []
    for j in range(3):
        which = jnp.where(half == 0, j, 2 - j)
        main_index = tall(jnp.minimum(72 + 3 * within + which, 127))
        rest_index = tall(jnp.clip(3 * (within - 16) + which, 0, 23)) + 24 * group
        picked = [
            jnp.where(tall(within < 16), lanes_from(main, main_index), lanes_from(rest, rest_index)) for main, rest in sides
        ]
        beside.append(jnp.where(tall(within < HALF), jnp.where(tall(half == 0), picked[0], picked[1]), 0.0))
    column_fix = column_sums(beside, mirror_ref)
    for m in range(3):
        row, col = coarse_place(m)
        index = tall(jnp.where(col < 12, row, 64 + row))
        value = sum_ref[:, 128 * m : 128 * m + 128]
        fix = jnp.zeros((ROWS, 128), F32)
        for q in range(3):
            fix = jnp.where(tall((col == q) | (col == 23 - q)), lanes_from(column_fix[q], index), fix)
        value = value + fix
        if m < 2:
            value = value + (first_fix, last_fix)[m]
        out_ref[:, 128 * m : 128 * m + 128] = value.astype(BF)


def gather_rows(pieces, cat_ref):
    me = lax.axis_index("chan")
    for k, piece in enumerate(pieces):
        first = pl.multiple_of(lax.bitwise_xor(me, k) * ROWS, 16)
        cat_ref[pl.ds(first, ROWS), :] = piece[...]


def make_branch(cat_ref, weights_ref, values_ref, block):
    def spread_lane(rows, lane):
        return wide(jnp.broadcast_to(values_ref[0:rows, lane : lane + 1], (rows, 128)), block)

    gain, shift, down_bias, scale = spread_lane(192, 0), spread_lane(192, 1), spread_lane(ROWS, 2), spread_lane(ROWS, 3)
    down = jnp.concatenate([weights_ref[768 + ROWS * j : 768 + ROWS * (j + 1), :] for j in range(3)], axis=1)
    inputs = 4 * ROWS

    def branch(start):
        values = cat_ref[0:inputs, start : start + block].astype(F32)
        mean = jnp.mean(values, axis=0, keepdims=True)
        centred = values - mean
        spread = jnp.mean(centred * centred, axis=0, keepdims=True)
        normed = (centred * lax.rsqrt(spread + norm_eps) * gain + shift).astype(BF)
        hidden = dot(weights_ref[0:768, 0 : inputs + 16], jnp.concatenate([normed, jnp.ones((16, block), BF)], axis=0))
        hidden = 0.5 * hidden * (1.0 + lax.erf(hidden * np.float32(0.5**0.5)))
        return scale * (dot(down, hidden.astype(BF)) + down_bias)

    return branch


def cell_weights(weight_ref, row, col):
    kind = tall(2 * (row % 2) + col % 2)
    result = jnp.zeros(kind.shape, F32)
    for k in range(4):
        result = jnp.where(kind == k, weight_ref[:, k : k + 1], result)
    return result


def make_mix_rim(count):
    def mix_rim(
        tab_ref, own_ref, p1_ref, p2_ref, p3_ref, x_ref, mask_ref, pool_cells_ref, weights_ref, values_ref,
        middle_pooled_ref, fine_ref, msg_ref, all_pooled_ref, cat_ref, mains_ref, rest_ref,
    ):
        gather_rows((own_ref, p1_ref, p2_ref, p3_ref), cat_ref)
        block = RIM
        branch = make_branch(cat_ref, weights_ref, values_ref, block)
        for start in range(0, RIM, block):
            here = slice(start, start + block)
            value = x_ref[:, here].astype(F32) + branch(start)
            fine_ref[:, here] = (mask_ref[0:1, here] * value).astype(BF)

        sums = []
        for m in range(RIM // 128):
            weights, step = (pool_cells_ref[:, 0:128], 64) if m < 4 else (pool_cells_ref[:, 128:256], 8)
            product = fine_ref[:, 128 * m : 128 * m + 128].astype(F32) * weights
            product = product + lane_shifted(product, 1)
            sums.append(product + lane_shifted(product, step))
        for i in range(GROUPS):
            here = slice(128 * i, 128 * i + 128)
            value = coarse_from(i, lambda m: sums[m], lambda m: m < RIM // 128)
            all_pooled_ref[:, here] = (value + middle_pooled_ref[:, here].astype(F32)).astype(BF)

        groups = [all_pooled_ref[:, 128 * i : 128 * i + 128].astype(F32) for i in range(GROUPS)]
        lane = lane_ids((8, 128))
        index = lane // 24 * 32 + 3 + lane % 24
        rows = [lanes_from(groups[0], tall(index & 127)), lanes_from(groups[5], tall((index + 32) & 127))]
        cell = jnp.clip(lane - 72, 0, 47)
        rest_cell = lane_ids((ROWS, 128)) - lax.broadcasted_iota(jnp.int32, (ROWS, 128), 0) // 16 * 24
        rest_valid = (rest_cell >= 0) & (rest_cell < 24)
        rest_cell = jnp.clip(rest_cell, 0, 23)
        for c in range(2):
            first = 24 if c else 3
            index = tall(cell // 3 % 4 * 32 + first + cell % 3)
            column = lanes_from(groups[0], index)
            for i in range(1, 4):
                column = jnp.where(tall(cell // 12 == i), lanes_from(groups[i], index), column)
            for r in range(2):
                mains_ref[2 * r + c] = jnp.where(tall(lane < 72), rows[r], column).astype(BF)
            index = rest_cell // 3 % 4 * 32 + first + rest_cell % 3
            rest = jnp.where(rest_cell < 12, lanes_from(groups[4], index), lanes_from(groups[5], index))
            rest = jnp.where(rest_valid, rest, 0.0)
            rest_ref[c] = (rest[0:16] + rest[16:32] + rest[32:48]).astype(BF)

        def fill(dev, carry):
            both = tab_ref[16 + dev]
            for g in range(3):
                msg_ref[dev, :, 128 * g : 128 * g + 128] = mains_ref[both, 16 * g : 16 * g + 16, :]
            msg_ref[dev, :, 384:512] = rest_ref[lax.bitwise_and(both, 1)]
            return carry

        scan_tiles(count, fill, jnp.int32(0))

    return mix_rim


def mix_middle(
    own_ref, p1_ref, p2_ref, p3_ref, x_ref, pool_cells_ref, weights_ref, values_ref, fine_ref, pooled_ref, cat_ref
):
    gather_rows((own_ref, p1_ref, p2_ref, p3_ref), cat_ref)
    value = x_ref[...].astype(F32) + make_branch(cat_ref, weights_ref, values_ref, MIDDLE)(0)
    mask = jnp.concatenate([values_ref[192 + 8 * t : 193 + 8 * t, :] for t in range(MIDDLE // 128)], axis=1)
    fine_ref[...] = (mask * value).astype(BF)
    sums = fine_ref[...].astype(F32) * pool_cells_ref[...]
    sums = sums + lane_shifted(sums, 1)
    sums = sums + lane_shifted(sums, 40)
    first = RIM // 128
    for i in range(GROUPS):
        value = coarse_from(i, lambda m: sums[:, 128 * (m - first) : 128 * (m - first) + 128], lambda m: m >= first)
        pooled_ref[:, 128 * i : 128 * i + 128] = value.astype(BF)


def coarse_cells(pieces, first, pooled_ref, weights_ref, values_ref, cat_ref):
    gather_rows(pieces, cat_ref)
    lanes = cat_ref.shape[1]
    value = pooled_ref[:, 128 * first : 128 * first + lanes].astype(F32) + make_branch(cat_ref, weights_ref, values_ref, lanes)(0)
    tiles = range(first, first + lanes // 128)
    return jnp.concatenate([values_ref[192 + 8 * m : 193 + 8 * m, :] for m in tiles], axis=1) * value


def mix_coarse_middle(own_ref, p1_ref, p2_ref, p3_ref, pooled_ref, weights_ref, values_ref, out_ref, cat_ref):
    out_ref[...] = coarse_cells((own_ref, p1_ref, p2_ref, p3_ref), 3, pooled_ref, weights_ref, values_ref, cat_ref).astype(BF)


def mix_coarse(
    own_ref, p1_ref, p2_ref, p3_ref, pooled_ref, middle_ref, fine_ref, mask_ref, weights_ref, values_ref, pool_ref, spread_ref, out_ref, cat_ref,
):
    rim = coarse_cells((own_ref, p1_ref, p2_ref, p3_ref), 0, pooled_ref, weights_ref, values_ref, cat_ref)
    ends = jnp.concatenate([rim[:, 0:128], rim[:, 128:256]], axis=0).astype(BF)
    ends = lax.dot_general(ends, pool_ref[...], (((1,), (1,)), ((), ())), preferred_element_type=F32)
    sides, lane = rim[:, 256:384], lane_ids((ROWS, 128))
    parts = []
    for i in range(4):
        middle = middle_ref[:, 128 * (i // 2) : 128 * (i // 2) + 128].astype(F32)
        side = pltpu.roll(sides, 128 - 32 * i, 1) if i else sides
        parts.append(jnp.where(lane < 32, side, pltpu.roll(middle, 96 if i % 2 else 32, 1)).astype(BF))
    inner = dot(jnp.concatenate(parts, axis=0), spread_ref[...])
    weights = jnp.concatenate([values_ref[240 + ROWS * j : 240 + ROWS * (j + 1), :] for j in range(3)], axis=1)
    for i in range(GROUPS):
        lanes = slice(i * FINE_IN, (i + 1) * FINE_IN)
        if i % 5 == 0:
            spread = ends[i // 5 * ROWS : (i // 5 + 1) * ROWS]
        else:
            spread = inner[(i - 1) * ROWS : i * ROWS]
        merged = fine_ref[:, lanes].astype(F32) + weights * spread
        out_ref[0, :, lanes] = (mask_ref[:, lanes].astype(F32) * merged).astype(BF)


VMEM = pl.BlockSpec(memory_space=pltpu.VMEM)
SMEM = pl.BlockSpec(memory_space=pltpu.SMEM)

def takes(microseconds):
    return pl.CostEstimate(flops=microseconds * 1_000_000_000, bytes_accessed=0, transcendentals=0)


def shaped(*shape, dtype=BF):
    return jax.ShapeDtypeStruct(shape, dtype)


PARAMS = pltpu.CompilerParams(vmem_limit_bytes=24 * 1024 * 1024)


def every_channel(own, first_work, later_work, direct):
    pairs = lambda bit: [(i, i ^ bit) for i in range(4)]
    across = lax.ppermute(own, "chan", pairs(2))
    if direct:
        diagonal = lax.ppermute(own, "chan", pairs(3))
    near, *results = lax.optimization_barrier((own, *first_work(own)))
    beside = lax.ppermute(near, "chan", pairs(1))
    if direct:
        across, diagonal, *results = lax.optimization_barrier((across, diagonal, *results, *later_work(*results)))
    else:
        across, *results = lax.optimization_barrier((across, *results, *later_work(*results)))
        diagonal = lax.ppermute(across, "chan", pairs(1))
    return (own, beside, across, diagonal), results


def per_device(
    features, land_mask, wet_slots, device_of, depth_weight, depth_bias, norm_gain, norm_bias, up_weight, up_bias,
    down_weight, down_bias, layer_scale, pool_weight, spread_weight,
):
    count = wet_slots.shape[0]
    grid_x = 2 * count // GRID_Y
    cells = TILE * TILE
    pack = pl.pallas_call(
        strip_table, out_specs=VMEM, out_shape=shaped(FINE_IN, 256), compiler_params=PARAMS, cost_estimate=takes(2), name="strip_table"
    )()
    messages, table = pl.pallas_call(
        make_prep(grid_x),
        in_specs=[SMEM, SMEM, VMEM, VMEM],
        out_specs=[VMEM, SMEM],
        out_shape=[shaped(count, 16, 896), shaped(16 + count, dtype=jnp.int32)],
        scratch_shapes=[
            pltpu.VMEM((2, ROWS, 128), BF),
            pltpu.VMEM((2, ROWS, 128), BF),
            pltpu.VMEM((2, 16, 128), F32),
            pltpu.VMEM((2, 16, 128), F32),
        ],
        compiler_params=PARAMS,
        cost_estimate=takes(10),
        name="prep",
    )(wet_slots, device_of, features, pack)
    pool = jnp.asarray(POOL)
    arrived = lax.all_to_all(messages, "tile", 0, 0, tiled=True)
    inner, inner_middle, fine_taps = pl.pallas_call(
        lambda tab_ref, *refs: conv_inner(*refs),
        in_specs=[SMEM] + [VMEM] * 3,
        out_specs=[VMEM] * 3,
        out_shape=[shaped(ROWS, RIM, dtype=F32), shaped(ROWS, MIDDLE), shaped(28, ROWS, 128, dtype=F32)],
        scratch_shapes=[
            pltpu.VMEM((49, ROWS, 128), F32),
            pltpu.VMEM((ROWS, 3584), F32),
            pltpu.VMEM((ROWS, 3584), F32),
            pltpu.VMEM((ROWS, 3072), F32),
        ],
        compiler_params=PARAMS,
        cost_estimate=takes(4),
        name="conv_inner",
    )(table, features, depth_weight, depth_bias)
    conv = pl.pallas_call(
        conv_border,
        in_specs=[SMEM] + [VMEM] * 3,
        out_specs=VMEM,
        out_shape=shaped(ROWS, RIM),
        compiler_params=PARAMS,
        cost_estimate=takes(2),
        name="conv_border",
    )(table, arrived, inner, fine_taps)

    pairs = lambda bit: [(i, i ^ bit) for i in range(4)]
    middle_across = lax.ppermute(inner_middle, "chan", pairs(2))
    middle_beside = lax.ppermute(inner_middle, "chan", pairs(1))
    middle_across, _ = lax.optimization_barrier((middle_across, conv))
    middle_pieces = (inner_middle, middle_beside, middle_across, lax.ppermute(middle_across, "chan", pairs(1)))

    def mix_middle_cells(*results):
        return pl.pallas_call(
            mix_middle,
            in_specs=[VMEM] * 8,
            out_specs=[VMEM] * 2,
            out_shape=[shaped(ROWS, MIDDLE), shaped(ROWS, 768)],
            scratch_shapes=[pltpu.VMEM((4 * ROWS, MIDDLE), BF)],
            compiler_params=PARAMS,
            cost_estimate=takes(1),
            name="mix_middle",
        )(*middle_pieces, results[1], results[4], results[5], results[6])

    def spread_params(own):
        shapes = [
            ((ROWS, RIM), BF), ((ROWS, MIDDLE), BF), ((8, RIM), F32), ((ROWS, 256), F32), ((ROWS, MIDDLE), F32),
            ((912, 256), BF), ((296, 128), F32), ((912, 256), BF), ((384, 128), F32),
        ]
        return pl.pallas_call(
            params,
            in_specs=[VMEM] * 13,
            out_specs=[VMEM] * len(shapes),
            out_shape=[shaped(*shape, dtype=dtype) for shape, dtype in shapes],
            compiler_params=PARAMS,
            cost_estimate=takes(2),
            name="params",
        )(
            own, features, land_mask, norm_gain, norm_bias, jnp.swapaxes(up_weight, 1, 2), up_bias, down_weight, down_bias, layer_scale,
            pool_weight, spread_weight, pool,
        )

    pieces, results = every_channel(conv, spread_params, mix_middle_cells, True)
    rim_cells, _, rim_mask, rim_weights, _, fine_weights, fine_values, coarse_weights, coarse_values, middle, middle_pooled = results
    rim, messages, pooled = pl.pallas_call(
        make_mix_rim(count),
        in_specs=[SMEM] + [VMEM] * 10,
        out_specs=[VMEM] * 3,
        out_shape=[shaped(ROWS, RIM), shaped(count, 16, 512), shaped(ROWS, 768)],
        scratch_shapes=[
            pltpu.VMEM((4 * ROWS, RIM), BF),
            pltpu.VMEM((4, ROWS, 128), BF),
            pltpu.VMEM((2, 16, 128), BF),
        ],
        compiler_params=PARAMS,
        cost_estimate=takes(3),
        name="mix_rim",
    )(
        table, *pieces, rim_cells, rim_mask, rim_weights, fine_weights, fine_values, middle_pooled,
    )
    arrived = lax.all_to_all(messages, "tile", 0, 0, tiled=True)
    inner, middle_conv, pooled, taps = pl.pallas_call(
        conv_coarse,
        in_specs=[VMEM] * 3,
        out_specs=[VMEM] * 4,
        out_shape=[shaped(ROWS, 384, dtype=F32), shaped(ROWS, 256), shaped(ROWS, 640), shaped(49, ROWS, 128, dtype=F32)],
        scratch_shapes=[pltpu.VMEM((4, ROWS, 1024), F32), pltpu.VMEM((ROWS, 768), F32)],
        compiler_params=PARAMS,
        cost_estimate=takes(2),
        name="conv_coarse",
    )(pooled, depth_weight, depth_bias)
    conv = pl.pallas_call(
        border_coarse,
        in_specs=[SMEM] + [VMEM] * 3,
        out_specs=VMEM,
        out_shape=shaped(ROWS, 384),
        compiler_params=PARAMS,
        cost_estimate=takes(1),
        name="border_coarse",
    )(table, arrived, inner, taps)
    middle_across = lax.ppermute(middle_conv, "chan", pairs(2))
    middle_beside = lax.ppermute(middle_conv, "chan", pairs(1))
    middle_across, _ = lax.optimization_barrier((middle_across, conv))
    coarse_pieces = (middle_conv, middle_beside, middle_across, lax.ppermute(middle_across, "chan", pairs(1)))

    def back_in_rows(own):
        return pl.pallas_call(
            lambda after_ref, *refs: in_rows(*refs),
            in_specs=[VMEM] * 3,
            out_specs=[VMEM],
            out_shape=[shaped(ROWS, cells)],
            compiler_params=PARAMS,
            cost_estimate=takes(1),
            name="in_rows",
        )(own, rim, middle)

    def mix_coarse_cells(*results):
        return pl.pallas_call(
            mix_coarse_middle,
            in_specs=[VMEM] * 7,
            out_specs=[VMEM],
            out_shape=[shaped(ROWS, 256)],
            scratch_shapes=[pltpu.VMEM((4 * ROWS, 256), BF)],
            compiler_params=PARAMS,
            cost_estimate=takes(1),
            name="mix_coarse_middle",
        )(*coarse_pieces, pooled, coarse_weights, coarse_values)

    pieces, (fine, coarse_middle) = every_channel(conv, back_in_rows, mix_coarse_cells, True)
    return pl.pallas_call(
        mix_coarse,
        in_specs=[VMEM] * 12,
        out_specs=VMEM,
        out_shape=shaped(1, ROWS, cells),
        scratch_shapes=[pltpu.VMEM((4 * ROWS, 384), BF)],
        compiler_params=PARAMS,
        cost_estimate=takes(2),
        name="mix_coarse",
    )(*pieces, pooled, coarse_middle, fine, land_mask, coarse_weights, coarse_values, pool, jnp.asarray(COARSE_SPREAD))


def solution(mesh):
    placed = (
        P("tile", "chan", None),
        P("tile", None),
        P(),
        P(),
        P(None, "chan", None),
        P(None, "chan"),
        P(),
        P(),
        P(),
        P(),
        P(),
        P(),
        P(None, "chan"),
        P("chan", None),
        P("chan", None),
    )
    return jax.shard_map(
        per_device, mesh=mesh, in_specs=placed, out_specs=P("tile", "chan", None), check_vma=False
    )
```
